32 devices in a mesh: seq: 8 (over y, x, core), res: 4 (over z).
Axes of the slice: x: 2, y: 2, z: 4, core: 2. Of those that a mesh axis runs over, the one named last changes fastest.
Arguments:
- alignment_embedding: bfloat16 [32, 256, 256], P('seq', 'res'), may hold values from -6 to 6
- coupling_embedding: bfloat16 [256, 256, 128], P('seq', 'res'), may hold values from -6 to 6
- vertex_embedding: float32 [256, 64], replicated, may hold values from -6 to 6
- atom_locations: float32 [3, 256], replicated, may hold values from -6 to 6
- chain_existence_flags: int32 [32], replicated, may hold values from 0 to 1
- closest_aminos: int32 [256, 64], P('seq'), may hold values from 0 to 255, all different within a row
- softmax_mixer_scale_factor: float32 [256], replicated, may hold values from 0.1 to 1.9
- attender_stacked_matrix: bfloat16 [256, 1024], replicated, may hold values from -0.375 to 0.375
- softmax_mixer_exit_matrix: bfloat16 [256, 256], replicated, may hold values from -1.5 to 1.5
- tensor_mean_scale_factor: float32 [256], replicated, may hold values from 0.1 to 1.9
- tensor_mean_entry_matrix: bfloat16 [256, 64], replicated, may hold values from -0.375 to 0.375
- tensor_mean_exit_matrix: bfloat16 [1024, 128], replicated, may hold values from -0.5 to 0.5
- outbound_entry_scale: float32 [128], replicated, may hold values from 0.1 to 1.9
- outbound_entry_matrix: bfloat16 [128, 640], replicated, may hold values from -0.5 to 0.5
- outbound_exit_scale: float32 [128], replicated, may hold values from 0.1 to 1.9
- outbound_exit_matrix: bfloat16 [128, 128], replicated, may hold values from -0.5 to 0.5
- inbound_entry_scale: float32 [128], replicated, may hold values from 0.1 to 1.9
- inbound_entry_matrix: bfloat16 [128, 640], replicated, may hold values from -0.5 to 0.5
- inbound_exit_scale: float32 [128], replicated, may hold values from 0.1 to 1.9
- inbound_exit_matrix: bfloat16 [128, 128], replicated, may hold values from -0.5 to 0.5
- vertex_mapping_matrix: bfloat16 [64, 128], replicated, may hold values from -0.75 to 0.75
- bond_mapping_matrix: bfloat16 [128, 64], replicated, may hold values from -0.5 to 0.5
- distance_basis_matrix: float32 [64], replicated, may hold values from -3 to 3
- signal_matrix: bfloat16 [64, 64], replicated, may hold values from -0.75 to 0.75
- signal_location_matrix: float32 [64], replicated, may hold values from -1.5 to 1.5
- vertex_change_matrix: bfloat16 [64, 64], replicated, may hold values from -0.75 to 0.75
- alignment_adjoint: bfloat16 [32, 256, 256], P('seq', 'res'), may hold values from -6 to 6
- coupling_adjoint: bfloat16 [256, 256, 128], P('seq', 'res'), may hold values from -6 to 6
- vertex_adjoint: float32 [256, 64], P('seq'), may hold values from -6 to 6
- location_adjoint: float32 [3, 256], P(None, 'seq'), may hold values from -6 to 6
Outputs:
- msa_out: bfloat16 [32, 256, 256], P('seq', 'res')
- pair_out: bfloat16 [256, 256, 128], P('seq', 'res')
- single_out: float32 [256, 64], P('seq')
- coords_out: float32 [3, 256], P(None, 'seq')
- alignment_sensitivity: float32 [32, 256, 256], P('seq', 'res')
- pair_grad: float32 [256, 256, 128], P('seq', 'res')
- single_grad: float32 [256, 64], P('seq')
- coords_grad: float32 [3, 256], P(None, 'seq')
- msa_gain_grad: float32 [256], replicated
- w_qkvg_grad: float32 [256, 1024], replicated
- w_attn_out_grad: float32 [256, 256], replicated
- opm_gain_grad: float32 [256], replicated
- w_opm_in_grad: float32 [256, 64], replicated
- w_opm_out_grad: float32 [1024, 128], replicated
- tri_gain_grad: float32 [128], replicated
- w_tri_in_grad: float32 [128, 640], replicated
- tri_out_gain_grad: float32 [128], replicated
- w_tri_out_grad: float32 [128, 128], replicated
- inc_gain_grad: float32 [128], replicated
- w_inc_in_grad: float32 [128, 640], replicated
- inc_out_gain_grad: float32 [128], replicated
- w_inc_out_grad: float32 [128, 128], replicated
- w_node_grad: float32 [64, 128], replicated
- w_edge_grad: float32 [128, 64], replicated
- dist_weight_grad: float32 [64], replicated
- w_msg_grad: float32 [64, 64], replicated
- coord_weight_grad: float32 [64], replicated
- w_update_grad: float32 [64, 64], replicated
The draws below stay inside these ranges and needn't reach their ends.
Inputs may be any that keep to these rules, and one draw needn't show every extreme that they name: `closest_aminos`: each row names 64 different residues.
All inputs are finite; a program needn't handle non-finite values.
Results may differ from the reference program's by a relative error of at most 0.03.
Values may be sent and summed in bfloat16 or wider, within the bound.
A program may use at most 192 MiB of HBM per device.

```python
from functools import partial
import jax
import jax.numpy as jnp
from jax import lax

ALIGNMENT_DIM = 256
HEADS = 8
TENSOR_MEAN_DIM = 32
COUPLING_DIM = 128
C_TRI = 128
C_S = 64
K = 64
WINDOW_AMINOS = 256
ALIGNED_CHAINS = 32


def draw_chain_existence_flags(key, part):
    key = jax.random.fold_in(key, 7)
    random_seed_alpha, random_seed_beta, random_seed_gamma = jax.random.split(key, 3)
    layer_count_alpha = jax.random.randint(random_seed_alpha, (), 1, ALIGNED_CHAINS + 1)
    layer_count_beta = jax.random.randint(random_seed_beta, (), 1, ALIGNED_CHAINS + 1)
    sampled_layering = layer_count_alpha * layer_count_beta // ALIGNED_CHAINS
    spatial_places = jnp.arange(ALIGNED_CHAINS)
    distributed_sums = jax.random.randint(random_seed_gamma, (ALIGNED_CHAINS,), 0, 8) == 0
    return ((spatial_places <= sampled_layering) | distributed_sums).astype(jnp.int32)


def levels(stream_key, extent, cuts, low, high):
    loudness = 1.0
    for dim, shards_of in cuts:
        heights = jax.random.uniform(jax.random.fold_in(jax.random.fold_in(stream_key, 6), dim), (shards_of,), jnp.float32, low / len(cuts), high / len(cuts))
        loudness = loudness * jnp.repeat(jnp.exp(heights), extent[dim] // shards_of).reshape((-1,) + (1,) * (len(extent) - 1 - dim))
    return loudness


def picks_of(own_key, rows, amount, top, lift):
    order = jax.random.permutation(jax.random.fold_in(own_key, 1), amount)
    pull = order
    for power in range(3):
        pull = pull * pull // amount
    pull = pull * lift // amount
    lots = jax.random.randint(jax.random.fold_in(own_key, 2), (rows, amount), 0, 4096) + pull
    fixed_rows = jax.random.permutation(jax.random.fold_in(own_key, 3), rows)[jnp.arange(amount) % rows]
    lots = jnp.where(jnp.arange(rows)[:, None] == fixed_rows[None, :], 1 << 14, lots)
    score = lots * amount + jnp.arange(amount)
    return lax.top_k(score.astype(jnp.int32), top)[1].astype(jnp.int32)


def bell_draw(stream_key, shape, scale, most, cuts=(), kind=jnp.bfloat16):
    result = jax.random.normal(stream_key, shape, jnp.float32) * scale
    if len(cuts) > 0:
        result = levels(stream_key, shape, cuts, -0.22, 0.18) * result
    return jnp.clip(result, min=-most, max=most).astype(kind)


def setup_inputs(seed: int = 0) -> dict:
    arg_keys = jax.random.split(jax.random.key(seed), 31)
    alignment_embedding = bell_draw(arg_keys[0], (ALIGNED_CHAINS, WINDOW_AMINOS, ALIGNMENT_DIM), 1.0, 6.0, ((0, 8), (1, 4)))
    coupling_embedding = bell_draw(arg_keys[1], (WINDOW_AMINOS, WINDOW_AMINOS, COUPLING_DIM), 1.0, 6.0, ((0, 8), (1, 4)))
    vertex_embedding = bell_draw(arg_keys[2], (WINDOW_AMINOS, C_S), 1.0, 6.0, (), jnp.float32)
    atom_locations = bell_draw(arg_keys[3], (3, WINDOW_AMINOS), 1.0, 6.0, (), jnp.float32)
    chain_existence_flags = draw_chain_existence_flags(jax.random.fold_in(arg_keys[30], 71), 0)
    closest_aminos = picks_of(arg_keys[5], WINDOW_AMINOS, WINDOW_AMINOS, K, 0)
    softmax_mixer_scale_factor = jnp.clip(1.0 + 0.18 * jax.random.normal(arg_keys[6], (ALIGNMENT_DIM,), jnp.float32), 0.1, 1.9)
    attender_stacked_matrix = bell_draw(arg_keys[7], (ALIGNMENT_DIM, 4 * ALIGNMENT_DIM), ALIGNMENT_DIM ** -0.5, 0.375)
    softmax_mixer_exit_matrix = bell_draw(arg_keys[8], (ALIGNMENT_DIM, ALIGNMENT_DIM), (max(1, 2 * ALIGNMENT_DIM // ALIGNED_CHAINS)) ** -0.5, 1.5)
    tensor_mean_scale_factor = jnp.clip(1.0 + 0.18 * jax.random.normal(arg_keys[9], (ALIGNMENT_DIM,), jnp.float32), 0.1, 1.9)
    tensor_mean_entry_matrix = bell_draw(arg_keys[10], (ALIGNMENT_DIM, 2 * TENSOR_MEAN_DIM), ALIGNMENT_DIM ** -0.5, 0.375)
    tensor_mean_exit_matrix = bell_draw(arg_keys[11], (TENSOR_MEAN_DIM * TENSOR_MEAN_DIM, COUPLING_DIM), (max(1, 4 * TENSOR_MEAN_DIM * TENSOR_MEAN_DIM // ALIGNED_CHAINS)) ** -0.5, 0.5)
    outbound_entry_scale = jnp.clip(1.0 + 0.18 * jax.random.normal(arg_keys[12], (COUPLING_DIM,), jnp.float32), 0.1, 1.9)
    outbound_entry_matrix = bell_draw(arg_keys[13], (COUPLING_DIM, 4 * C_TRI + COUPLING_DIM), COUPLING_DIM ** -0.5, 0.5)
    outbound_exit_scale = jnp.clip(1.0 + 0.18 * jax.random.normal(arg_keys[14], (C_TRI,), jnp.float32), 0.1, 1.9)
    outbound_exit_matrix = bell_draw(arg_keys[15], (C_TRI, COUPLING_DIM), C_TRI ** -0.5, 0.5)
    inbound_entry_scale = jnp.clip(1.0 + 0.18 * jax.random.normal(arg_keys[16], (COUPLING_DIM,), jnp.float32), 0.1, 1.9)
    inbound_entry_matrix = bell_draw(arg_keys[17], (COUPLING_DIM, 4 * C_TRI + COUPLING_DIM), COUPLING_DIM ** -0.5, 0.5)
    inbound_exit_scale = jnp.clip(1.0 + 0.18 * jax.random.normal(arg_keys[18], (C_TRI,), jnp.float32), 0.1, 1.9)
    inbound_exit_matrix = bell_draw(arg_keys[19], (C_TRI, COUPLING_DIM), C_TRI ** -0.5, 0.5)
    vertex_mapping_matrix = bell_draw(arg_keys[20], (C_S, 2 * C_S), C_S ** -0.5, 0.75)
    bond_mapping_matrix = bell_draw(arg_keys[21], (COUPLING_DIM, C_S), COUPLING_DIM ** -0.5, 0.5)
    distance_basis_matrix = bell_draw(arg_keys[22], (C_S,), 0.5, 3.0, (), jnp.float32)
    signal_matrix = bell_draw(arg_keys[23], (C_S, C_S), C_S ** -0.5, 0.75)
    signal_location_matrix = bell_draw(arg_keys[24], (C_S,), (max(1, C_S // 4)) ** -0.5, 1.5, (), jnp.float32)
    vertex_change_matrix = bell_draw(arg_keys[25], (C_S, C_S), C_S ** -0.5, 0.75)
    alignment_adjoint = bell_draw(arg_keys[26], (ALIGNED_CHAINS, WINDOW_AMINOS, ALIGNMENT_DIM), 1.0, 6.0, ((0, 8), (1, 4)))
    coupling_adjoint = bell_draw(arg_keys[27], (WINDOW_AMINOS, WINDOW_AMINOS, COUPLING_DIM), 1.0, 6.0, ((0, 8), (1, 4)))
    vertex_adjoint = bell_draw(arg_keys[28], (WINDOW_AMINOS, C_S), 1.0, 6.0, ((0, 8),), jnp.float32)
    location_adjoint = bell_draw(arg_keys[29], (3, WINDOW_AMINOS), 1.0, 6.0, ((1, 8),), jnp.float32)
    return dict(alignment_embedding=alignment_embedding, coupling_embedding=coupling_embedding, vertex_embedding=vertex_embedding, atom_locations=atom_locations, chain_existence_flags=chain_existence_flags, closest_aminos=closest_aminos, softmax_mixer_scale_factor=softmax_mixer_scale_factor, attender_stacked_matrix=attender_stacked_matrix, softmax_mixer_exit_matrix=softmax_mixer_exit_matrix, tensor_mean_scale_factor=tensor_mean_scale_factor, tensor_mean_entry_matrix=tensor_mean_entry_matrix, tensor_mean_exit_matrix=tensor_mean_exit_matrix, outbound_entry_scale=outbound_entry_scale, outbound_entry_matrix=outbound_entry_matrix, outbound_exit_scale=outbound_exit_scale, outbound_exit_matrix=outbound_exit_matrix, inbound_entry_scale=inbound_entry_scale, inbound_entry_matrix=inbound_entry_matrix, inbound_exit_scale=inbound_exit_scale, inbound_exit_matrix=inbound_exit_matrix, vertex_mapping_matrix=vertex_mapping_matrix, bond_mapping_matrix=bond_mapping_matrix, distance_basis_matrix=distance_basis_matrix, signal_matrix=signal_matrix, signal_location_matrix=signal_location_matrix, vertex_change_matrix=vertex_change_matrix, alignment_adjoint=alignment_adjoint, coupling_adjoint=coupling_adjoint, vertex_adjoint=vertex_adjoint, location_adjoint=location_adjoint)


@jax.custom_vjp
def reduced_accuracy(v):
    return lax.optimization_barrier(v.astype(jnp.bfloat16)).astype(jnp.float32)

@jax.custom_vjp
def reduced_accuracy_reverse(v):
    return v

def low_keep(v):
    return (reduced_accuracy(v), None)

def low_pass(kept, grad):
    return (grad,)

def back_keep(v):
    return (v, None)

def back_low(kept, grad):
    return (reduced_accuracy(grad),)
reduced_accuracy.defvjp(low_keep, low_pass)
reduced_accuracy_reverse.defvjp(back_keep, back_low)
EPS = 1e-05
HIGH = lax.Precision.HIGHEST

def standardize_lines(value, gain):
    row_mean = lax.optimization_barrier(jnp.mean(value, -1, keepdims=True))
    centred = value - row_mean
    spread = lax.optimization_barrier(jnp.mean(centred * centred, -1, keepdims=True))
    return centred * lax.rsqrt(spread + EPS) * gain

def matrix_multiply(value, weight):
    return jnp.einsum('...c,cd->...d', value, weight, precision=HIGH)

def evaluate_model(alignment_embedding, coupling_embedding, vertex_embedding, atom_locations, softmax_mixer_scale_factor, attender_stacked_matrix, softmax_mixer_exit_matrix, tensor_mean_scale_factor, tensor_mean_entry_matrix, tensor_mean_exit_matrix, outbound_entry_scale, outbound_entry_matrix, outbound_exit_scale, outbound_exit_matrix, inbound_entry_scale, inbound_entry_matrix, inbound_exit_scale, inbound_exit_matrix, vertex_mapping_matrix, bond_mapping_matrix, distance_basis_matrix, signal_matrix, signal_location_matrix, vertex_change_matrix, chain_exists, closest_aminos):
    block_tally, span_overall, breadth_overall = alignment_embedding.shape
    head_size = breadth_overall // HEADS
    standardized_lines = reduced_accuracy(standardize_lines(alignment_embedding, softmax_mixer_scale_factor))
    projected = reduced_accuracy_reverse(matrix_multiply(standardized_lines, attender_stacked_matrix))
    query = reduced_accuracy(projected[..., :breadth_overall]).reshape(block_tally, span_overall, HEADS, head_size)
    keys = reduced_accuracy(projected[..., breadth_overall:2 * breadth_overall]).reshape(block_tally, span_overall, HEADS, head_size)
    values = reduced_accuracy(projected[..., 2 * breadth_overall:3 * breadth_overall]).reshape(block_tally, span_overall, HEADS, head_size)
    gate_lin = projected[..., 3 * breadth_overall:]
    scores = reduced_accuracy_reverse(jnp.einsum('qlhd,klhd->lhqk', query, keys, precision=HIGH)) * head_size ** (-0.5)
    scores = jnp.where(chain_exists[None, None, None, :] > 0, scores, -1e+30)
    probs = reduced_accuracy(jax.nn.softmax(scores, axis=-1))
    attended = reduced_accuracy_reverse(jnp.einsum('lhqk,klhd->qlhd', probs, values, precision=HIGH)).reshape(block_tally, span_overall, breadth_overall)
    sigmoid_scaled_entries = reduced_accuracy(jax.nn.sigmoid(gate_lin) * attended)
    alignment_later = alignment_embedding + reduced_accuracy_reverse(matrix_multiply(sigmoid_scaled_entries, softmax_mixer_exit_matrix))
    line_indicator_entries = (chain_exists > 0).astype(alignment_embedding.dtype)
    opm_width = tensor_mean_entry_matrix.shape[1] // 2
    standardized_lines2 = reduced_accuracy(standardize_lines(alignment_later, tensor_mean_scale_factor))
    outer_in = reduced_accuracy(reduced_accuracy_reverse(matrix_multiply(standardized_lines2, tensor_mean_entry_matrix))) * line_indicator_entries[:, None, None]
    left = outer_in[..., :opm_width]
    right = outer_in[..., opm_width:]
    count = jnp.sum(line_indicator_entries)
    block_rows = 32
    blocks = left.reshape(block_tally, span_overall // block_rows, block_rows, opm_width).transpose(1, 0, 2, 3)

    def outer_block(left_block):
        outer = jnp.einsum('sic,sjd->ijcd', left_block, right, precision=HIGH)
        outer = reduced_accuracy(reduced_accuracy_reverse(outer.reshape(block_rows, span_overall, opm_width * opm_width)))
        return reduced_accuracy_reverse(matrix_multiply(outer, tensor_mean_exit_matrix))
    pair_opm = lax.map(jax.checkpoint(outer_block), blocks).reshape(span_overall, span_overall, -1)
    pair1 = coupling_embedding + pair_opm / count
    tri_width = outbound_exit_matrix.shape[0]
    normed3 = reduced_accuracy(standardize_lines(pair1, outbound_entry_scale))
    tri = reduced_accuracy_reverse(matrix_multiply(normed3, outbound_entry_matrix))
    left_t = reduced_accuracy(jax.nn.sigmoid(tri[..., tri_width:2 * tri_width]) * tri[..., :tri_width])
    right_t = reduced_accuracy(jax.nn.sigmoid(tri[..., 3 * tri_width:4 * tri_width]) * tri[..., 2 * tri_width:3 * tri_width])
    triangle = reduced_accuracy_reverse(jnp.einsum('ikc,jkc->ijc', left_t, right_t, precision=HIGH))
    normed4 = reduced_accuracy(standardize_lines(triangle, outbound_exit_scale))
    update = reduced_accuracy_reverse(matrix_multiply(normed4, outbound_exit_matrix))
    pair2 = pair1 + jax.nn.sigmoid(tri[..., 4 * tri_width:]) * update
    normed5 = reduced_accuracy(standardize_lines(pair2, inbound_entry_scale))
    tri2 = reduced_accuracy_reverse(matrix_multiply(normed5, inbound_entry_matrix))
    left_i = reduced_accuracy(jax.nn.sigmoid(tri2[..., tri_width:2 * tri_width]) * tri2[..., :tri_width])
    right_i = reduced_accuracy(jax.nn.sigmoid(tri2[..., 3 * tri_width:4 * tri_width]) * tri2[..., 2 * tri_width:3 * tri_width])
    triangle2 = reduced_accuracy_reverse(jnp.einsum('kic,kjc->ijc', left_i, right_i, precision=HIGH))
    normed6 = reduced_accuracy(standardize_lines(triangle2, inbound_exit_scale))
    update2 = reduced_accuracy_reverse(matrix_multiply(normed6, inbound_exit_matrix))
    coupling_later3 = pair2 + jax.nn.sigmoid(tri2[..., 4 * tri_width:]) * update2
    node_width = signal_matrix.shape[0]
    edges = jnp.take_along_axis(reduced_accuracy(coupling_later3), closest_aminos[:, :, None], axis=1)
    node_proj = reduced_accuracy_reverse(matrix_multiply(reduced_accuracy(vertex_embedding), vertex_mapping_matrix))
    other_near = node_proj[:, node_width:][closest_aminos]
    diff = atom_locations[:, :, None] - atom_locations[:, closest_aminos]
    radial = jnp.log(1.0 + lax.optimization_barrier(jnp.sum(diff * diff, 0)))
    edge_lin = reduced_accuracy_reverse(matrix_multiply(edges, bond_mapping_matrix))
    hidden = reduced_accuracy(jax.nn.silu(node_proj[:, None, :node_width] + other_near + edge_lin + radial[..., None] * distance_basis_matrix))
    message = jax.nn.silu(reduced_accuracy_reverse(matrix_multiply(hidden, signal_matrix)))
    turn = jnp.tanh(matrix_multiply(message, signal_location_matrix[:, None])[..., 0])
    mean_msg = reduced_accuracy(lax.optimization_barrier(jnp.mean(message, 1)))
    vertex_later = vertex_embedding + reduced_accuracy_reverse(matrix_multiply(mean_msg, vertex_change_matrix))
    locations_later = atom_locations + lax.optimization_barrier(jnp.mean(diff * turn[None], 2))
    return (alignment_later, coupling_later3, vertex_later, locations_later)

def reference(alignment_embedding, coupling_embedding, vertex_embedding, atom_locations, chain_existence_flags, closest_aminos, softmax_mixer_scale_factor, attender_stacked_matrix, softmax_mixer_exit_matrix, tensor_mean_scale_factor, tensor_mean_entry_matrix, tensor_mean_exit_matrix, outbound_entry_scale, outbound_entry_matrix, outbound_exit_scale, outbound_exit_matrix, inbound_entry_scale, inbound_entry_matrix, inbound_exit_scale, inbound_exit_matrix, vertex_mapping_matrix, bond_mapping_matrix, distance_basis_matrix, signal_matrix, signal_location_matrix, vertex_change_matrix, alignment_adjoint, coupling_adjoint, vertex_adjoint, location_adjoint):
    real_tally = (alignment_embedding.astype(jnp.float32), coupling_embedding.astype(jnp.float32), vertex_embedding, atom_locations, softmax_mixer_scale_factor, attender_stacked_matrix.astype(jnp.float32), softmax_mixer_exit_matrix.astype(jnp.float32), tensor_mean_scale_factor, tensor_mean_entry_matrix.astype(jnp.float32), tensor_mean_exit_matrix.astype(jnp.float32), outbound_entry_scale, outbound_entry_matrix.astype(jnp.float32), outbound_exit_scale, outbound_exit_matrix.astype(jnp.float32), inbound_entry_scale, inbound_entry_matrix.astype(jnp.float32), inbound_exit_scale, inbound_exit_matrix.astype(jnp.float32), vertex_mapping_matrix.astype(jnp.float32), bond_mapping_matrix.astype(jnp.float32), distance_basis_matrix, signal_matrix.astype(jnp.float32), signal_location_matrix, vertex_change_matrix.astype(jnp.float32))
    outputs, adjoint_mapping = jax.vjp(partial(evaluate_model, chain_exists=chain_existence_flags, closest_aminos=closest_aminos), *real_tally)
    derivative_bundle = adjoint_mapping((alignment_adjoint.astype(jnp.float32), coupling_adjoint.astype(jnp.float32), vertex_adjoint, location_adjoint))
    return (outputs[0].astype(jnp.bfloat16), outputs[1].astype(jnp.bfloat16), outputs[2], outputs[3], derivative_bundle[0], derivative_bundle[1], derivative_bundle[2], derivative_bundle[3], derivative_bundle[4], derivative_bundle[5], derivative_bundle[6], derivative_bundle[7], derivative_bundle[8], derivative_bundle[9], derivative_bundle[10], derivative_bundle[11], derivative_bundle[12], derivative_bundle[13], derivative_bundle[14], derivative_bundle[15], derivative_bundle[16], derivative_bundle[17], derivative_bundle[18], derivative_bundle[19], derivative_bundle[20], derivative_bundle[21], derivative_bundle[22], derivative_bundle[23])
```

```python
import functools
from types import SimpleNamespace

import jax
import jax.numpy as jnp
from jax import lax
from jax.experimental import pallas as pl
from jax.experimental.pallas import tpu as pltpu
from jax.sharding import PartitionSpec as P

HEADS = 8


EPS = 1e-05
HIGH = lax.Precision.HIGHEST


def spread_2(value, axis, source):
    kept = jnp.where(lax.axis_index(axis) == source, value, 0).astype(value.dtype)
    return lax.psum(kept, axis)


def standardize_lines(value, gain):
    row_mean = jnp.mean(value, -1, keepdims=True)
    centred = value - row_mean
    spread = jnp.mean(centred * centred, -1, keepdims=True)
    return centred * lax.rsqrt(spread + EPS) * gain


def tensor_mean_answer(left, right):
    return jnp.einsum("...c,cd->...d", left, right, preferred_element_type=jnp.float32)


def product_back(grad, right):
    return jnp.einsum("...d,cd->...c", grad, right, preferred_element_type=jnp.float32)


def weight_back(left, grad):
    flat_left = left.reshape(-1, left.shape[-1])
    flat_grad = grad.reshape(-1, grad.shape[-1])
    return jnp.einsum("nc,nd->cd", flat_left, flat_grad, preferred_element_type=jnp.float32)


def attn_scores(query, keys, allowed, scale):
    raw_scores = (
        jnp.einsum("qlhd,klhd->lhqk", query, keys, preferred_element_type=jnp.float32) * scale
    )
    return jnp.where(allowed, raw_scores, -1e30)


def tri_gates(tri_lin):
    quarter = tri_lin.shape[-1] // 4
    left_part = jax.nn.sigmoid(tri_lin[..., quarter : 2 * quarter]) * tri_lin[..., :quarter]
    right_part = (
        jax.nn.sigmoid(tri_lin[..., 3 * quarter :]) * tri_lin[..., 2 * quarter : 3 * quarter]
    )
    return (left_part, right_part)


def edge_front(own_rows, other_near, edge_lin, diff, distance_basis_matrix):
    radial = jnp.log(1.0 + jnp.sum(diff * diff, 0))
    return jax.nn.silu(
        own_rows[:, None, :] + other_near + edge_lin + radial[..., None] * distance_basis_matrix
    )


def edge_finish(msg_lin, signal_location_matrix, diff):
    message = jax.nn.silu(msg_lin)
    turn = jnp.tanh(jnp.einsum("ikc,c->ik", message, signal_location_matrix, precision=HIGH))
    return (jnp.mean(message, 1), jnp.mean(diff * turn[None], 2))


def gather_rows(value):
    return lax.all_gather(value, "seq", axis=0, tiled=True)


def across_res(value):
    return lax.psum(value.astype(jnp.bfloat16), "res").astype(jnp.float32)


def owners_sum(value):
    return lax.psum_scatter(value, "seq", scatter_dimension=0, tiled=True)


def place_home(rows_part, col_width, offset, keep_home):
    empty = jnp.zeros((rows_part.shape[0], col_width, rows_part.shape[2]), jnp.float32)
    return lax.dynamic_update_slice_in_dim(empty, rows_part, offset, 1) * keep_home


def sum_flat(parts):
    flat = jnp.concatenate([jnp.ravel(member) for member in parts])
    summed = lax.psum(flat, ("seq", "res"))
    pieces = []
    offset = 0
    for member in parts:
        pieces.append(summed[offset : offset + member.size].reshape(member.shape))
        offset = offset + member.size
    return pieces


def shards(
    alignment_embedding,
    coupling_embedding,
    vertex_embedding,
    atom_locations,
    chain_existence_flags,
    closest_aminos,
    softmax_mixer_scale_factor,
    attender_stacked_matrix,
    softmax_mixer_exit_matrix,
    tensor_mean_scale_factor,
    tensor_mean_entry_matrix,
    tensor_mean_exit_matrix,
    outbound_entry_scale,
    outbound_entry_matrix,
    outbound_exit_scale,
    outbound_exit_matrix,
    inbound_entry_scale,
    inbound_entry_matrix,
    inbound_exit_scale,
    inbound_exit_matrix,
    vertex_mapping_matrix,
    bond_mapping_matrix,
    distance_basis_matrix,
    signal_matrix,
    signal_location_matrix,
    vertex_change_matrix,
    alignment_adjoint,
    coupling_adjoint,
    vertex_adjoint,
    location_adjoint,
):
    seq_index = lax.axis_index("seq")
    res_index = lax.axis_index("res")
    n_seq = lax.axis_size("seq")
    n_res = lax.axis_size("res")
    chain_shard_piece, vertical_shard_piece, breadth_overall = alignment_embedding.shape
    rows_dev = coupling_embedding.shape[0]
    span_overall, node_width = vertex_embedding.shape
    block_tally = chain_existence_flags.shape[0]
    head_size = breadth_overall // HEADS
    scale = head_size ** (-0.5)
    opm_width = tensor_mean_entry_matrix.shape[1] // 2
    tri_width = outbound_exit_matrix.shape[0]
    chain_exists = (chain_existence_flags > 0).astype(jnp.float32)
    line_indicator_entries = lax.dynamic_slice_in_dim(
        chain_exists, seq_index * chain_shard_piece, chain_shard_piece
    )
    first_res = (res_index == 0).astype(jnp.float32)
    home = seq_index * rows_dev // vertical_shard_piece
    offset = seq_index * rows_dev - home * vertical_shard_piece
    keep_home = (home == res_index).astype(jnp.float32)
    alignment_real_lines = alignment_embedding.astype(jnp.float32)
    standardized_lines, standardize_reverse_alpha = jax.vjp(
        standardize_lines, alignment_real_lines, softmax_mixer_scale_factor
    )
    normed_b = standardized_lines.astype(jnp.bfloat16)
    projected = tensor_mean_answer(normed_b, attender_stacked_matrix)
    query = projected[..., :breadth_overall].astype(jnp.bfloat16)
    keyval = projected[..., breadth_overall : 3 * breadth_overall].astype(jnp.bfloat16)
    attn_gate = jax.nn.sigmoid(projected[..., 3 * breadth_overall :])
    all_keyval = lax.all_gather(keyval, "seq", axis=0, tiled=True)
    query4 = query.reshape(chain_shard_piece, vertical_shard_piece, HEADS, head_size)
    keys4 = all_keyval[..., :breadth_overall].reshape(
        block_tally, vertical_shard_piece, HEADS, head_size
    )
    values4 = all_keyval[..., breadth_overall:].reshape(
        block_tally, vertical_shard_piece, HEADS, head_size
    )
    allowed = chain_exists[None, None, None, :] > 0
    scores = attn_scores(query4, keys4, allowed, scale)
    score_peak = jnp.max(scores, -1, keepdims=True)
    exp_scores = jnp.exp(scores - score_peak)
    exp_total = jnp.sum(exp_scores, -1, keepdims=True)
    log_total = score_peak + jnp.log(exp_total)
    probs_b = (exp_scores / exp_total).astype(jnp.bfloat16)
    attended = jnp.einsum(
        "lhqk,klhd->qlhd", probs_b, values4, preferred_element_type=jnp.float32
    ).reshape(chain_shard_piece, vertical_shard_piece, breadth_overall)
    sigmoid_scaled_lines = (attn_gate * attended).astype(jnp.bfloat16)
    alignment_later = alignment_real_lines + tensor_mean_answer(
        sigmoid_scaled_lines, softmax_mixer_exit_matrix
    )
    standardized_lines2, standardize_reverse_beta = jax.vjp(
        standardize_lines, alignment_later, tensor_mean_scale_factor
    )
    normed2_b = standardized_lines2.astype(jnp.bfloat16)
    outer_in = (
        tensor_mean_answer(normed2_b, tensor_mean_entry_matrix)
        * line_indicator_entries[:, None, None]
    ).astype(jnp.bfloat16)
    everyone = lax.all_gather(outer_in, ("seq", "res"), axis=0, tiled=True)
    blocks = everyone.reshape(n_seq, n_res, chain_shard_piece, vertical_shard_piece, 2 * opm_width)
    home_block = lax.dynamic_index_in_dim(blocks, home, 1, keepdims=False)
    left_rows = lax.dynamic_slice_in_dim(home_block, offset, rows_dev, 2)[..., :opm_width]
    left_rows = left_rows.reshape(block_tally, rows_dev, opm_width)
    right_cols = lax.dynamic_index_in_dim(blocks, res_index, 1, keepdims=False)[..., opm_width:]
    right_cols = right_cols.reshape(block_tally, vertical_shard_piece, opm_width)
    outer_b = jnp.einsum("sic,sjd->ijcd", left_rows, right_cols, preferred_element_type=jnp.float32)
    outer_b = outer_b.reshape(rows_dev, vertical_shard_piece, opm_width * opm_width).astype(
        jnp.bfloat16
    )
    count = jnp.sum(chain_exists)
    pair1 = (
        coupling_embedding.astype(jnp.float32)
        + tensor_mean_answer(outer_b, tensor_mean_exit_matrix) / count
    )
    normed3, norm_back3 = jax.vjp(standardize_lines, pair1, outbound_entry_scale)
    normed3_b = normed3.astype(jnp.bfloat16)
    tri = tensor_mean_answer(normed3_b, outbound_entry_matrix)
    (left_t, right_t), gates_back = jax.vjp(tri_gates, tri[..., : 4 * tri_width])
    left_b = left_t.astype(jnp.bfloat16)
    right_b = right_t.astype(jnp.bfloat16)
    right_all = gather_rows(right_b)
    partial_tri = jnp.einsum("ikc,jkc->ijc", left_b, right_all, preferred_element_type=jnp.float32)
    triangle = lax.psum_scatter(
        partial_tri.astype(jnp.bfloat16), "res", scatter_dimension=1, tiled=True
    ).astype(jnp.float32)
    normed4, norm_back4 = jax.vjp(standardize_lines, triangle, outbound_exit_scale)
    normed4_b = normed4.astype(jnp.bfloat16)
    update = tensor_mean_answer(normed4_b, outbound_exit_matrix)
    out_gate = jax.nn.sigmoid(tri[..., 4 * tri_width :])
    pair2 = pair1 + out_gate * update
    normed5, norm_back5 = jax.vjp(standardize_lines, pair2, inbound_entry_scale)
    normed5_b = normed5.astype(jnp.bfloat16)
    tri2 = tensor_mean_answer(normed5_b, inbound_entry_matrix)
    (left_i, right_i), gates_back2 = jax.vjp(tri_gates, tri2[..., : 4 * tri_width])
    both_local = jnp.concatenate([left_i.astype(jnp.bfloat16), right_i.astype(jnp.bfloat16)], -1)
    both_all = gather_rows(both_local)
    right_all2 = both_all[..., tri_width:]
    left_cand = lax.dynamic_slice_in_dim(both_all[..., :tri_width], offset, rows_dev, 1)
    left_sel = spread_2(left_cand, "res", home)
    triangle2 = jnp.einsum("kic,kjc->ijc", left_sel, right_all2, preferred_element_type=jnp.float32)
    normed6, norm_back6 = jax.vjp(standardize_lines, triangle2, inbound_exit_scale)
    normed6_b = normed6.astype(jnp.bfloat16)
    update2 = tensor_mean_answer(normed6_b, inbound_exit_matrix)
    out_gate2 = jax.nn.sigmoid(tri2[..., 4 * tri_width :])
    coupling_later3 = pair2 + out_gate2 * update2
    pair3_b = coupling_later3.astype(jnp.bfloat16)
    rows_all = lax.all_gather(pair3_b, "res", axis=1, tiled=True)
    nbr_hot = closest_aminos[:, :, None] == jnp.arange(span_overall, dtype=jnp.int32)[None, None, :]
    hot_float = nbr_hot.astype(jnp.float32)
    edges_b = jnp.einsum(
        "ikl,ilc->ikc", nbr_hot.astype(jnp.bfloat16), rows_all, preferred_element_type=jnp.float32
    ).astype(jnp.bfloat16)
    single_b = vertex_embedding.astype(jnp.bfloat16)
    node_proj = tensor_mean_answer(single_b, vertex_mapping_matrix)
    own_rows = lax.dynamic_slice_in_dim(node_proj[:, :node_width], seq_index * rows_dev, rows_dev)
    other_near = jnp.einsum("ikl,lc->ikc", hot_float, node_proj[:, node_width:], precision=HIGH)
    coords_own = lax.dynamic_slice_in_dim(atom_locations, seq_index * rows_dev, rows_dev, 1)
    coords_near = jnp.einsum("ikl,xl->xik", hot_float, atom_locations, precision=HIGH)
    diff = coords_own[:, :, None] - coords_near
    edge_lin = tensor_mean_answer(edges_b, bond_mapping_matrix)
    hidden, front_back = jax.vjp(
        edge_front, own_rows, other_near, edge_lin, diff, distance_basis_matrix
    )
    hidden_b = hidden.astype(jnp.bfloat16)
    msg_lin = tensor_mean_answer(hidden_b, signal_matrix)
    (mean_msg, shift), finish_back = jax.vjp(edge_finish, msg_lin, signal_location_matrix, diff)
    mean_b = mean_msg.astype(jnp.bfloat16)
    single_rows = lax.dynamic_slice_in_dim(vertex_embedding, seq_index * rows_dev, rows_dev)
    single_out = single_rows + tensor_mean_answer(mean_b, vertex_change_matrix)
    coords_out = coords_own + shift
    d_update_b = vertex_adjoint.astype(jnp.bfloat16)
    g_update = weight_back(mean_b, d_update_b)
    d_mean = product_back(d_update_b, vertex_change_matrix)
    d_msg_lin, g_coord, d_diff_finish = finish_back((d_mean, location_adjoint))
    d_msg_b = d_msg_lin.astype(jnp.bfloat16)
    g_msg = weight_back(hidden_b, d_msg_b)
    d_hidden = product_back(d_msg_b, signal_matrix)
    d_own, d_other_near, d_edge_lin, d_diff_front, g_dist = front_back(d_hidden)
    d_edge_b = d_edge_lin.astype(jnp.bfloat16)
    g_edge = weight_back(edges_b, d_edge_b)
    d_edges = product_back(d_edge_b, bond_mapping_matrix)
    d_rows = jnp.einsum("ikl,ikc->ilc", hot_float, d_edges, precision=HIGH)
    d_pair3 = coupling_adjoint.astype(jnp.float32) + lax.dynamic_slice_in_dim(
        d_rows, res_index * vertical_shard_piece, vertical_shard_piece, 1
    )
    d_diff = d_diff_front + d_diff_finish
    d_coords_own = jnp.sum(d_diff, 2)
    d_coords_near = jnp.einsum("ikl,xik->xl", hot_float, -d_diff, precision=HIGH)
    d_other_all = jnp.einsum("ikl,ikc->lc", hot_float, d_other_near, precision=HIGH)
    d_other_rows, d_near_rows = (
        lax.psum_scatter(d_other_all, "seq", scatter_dimension=0, tiled=True),
        lax.psum_scatter(d_coords_near, "seq", scatter_dimension=1, tiled=True),
    )
    d_node_b = jnp.concatenate([d_own, d_other_rows], -1).astype(jnp.bfloat16)
    g_node = weight_back(
        lax.dynamic_slice_in_dim(single_b, seq_index * rows_dev, rows_dev), d_node_b
    )
    single_grad = vertex_adjoint + product_back(d_node_b, vertex_mapping_matrix)
    coords_grad = location_adjoint + d_coords_own + d_near_rows
    layer_two = [
        g_node * first_res,
        g_edge * first_res,
        g_dist * first_res,
        g_msg * first_res,
        g_coord * first_res,
        g_update * first_res,
    ]
    d_inc_b = (d_pair3 * out_gate2).astype(jnp.bfloat16)
    d_gate_out2 = d_pair3 * update2 * out_gate2 * (1.0 - out_gate2)
    g_inc_out = weight_back(normed6_b, d_inc_b)
    d_normed6 = product_back(d_inc_b, inbound_exit_matrix)
    d_triangle2, g_inc_out_gain = norm_back6(d_normed6)
    d_tri2_b = d_triangle2.astype(jnp.bfloat16)
    d_left_sel = jnp.einsum(
        "ijc,kjc->kic", d_tri2_b, right_all2, preferred_element_type=jnp.float32
    )
    d_right_all2 = jnp.einsum(
        "ijc,kic->kjc", d_tri2_b, left_sel, preferred_element_type=jnp.float32
    )
    d_left_total = across_res(d_left_sel)
    d_both2 = owners_sum(
        jnp.concatenate(
            [place_home(d_left_total, vertical_shard_piece, offset, keep_home), d_right_all2], -1
        )
    )
    (d_gates2,) = gates_back2((d_both2[..., :tri_width], d_both2[..., tri_width:]))
    d_tri2_in_b = jnp.concatenate([d_gates2, d_gate_out2], -1).astype(jnp.bfloat16)
    g_inc_in = weight_back(normed5_b, d_tri2_in_b)
    d_normed5 = product_back(d_tri2_in_b, inbound_entry_matrix)
    d_pair2_norm, g_inc_gain = norm_back5(d_normed5)
    d_pair2 = d_pair3 + d_pair2_norm
    d_tri_out_b = (d_pair2 * out_gate).astype(jnp.bfloat16)
    d_gate_out = d_pair2 * update * out_gate * (1.0 - out_gate)
    g_tri_out = weight_back(normed4_b, d_tri_out_b)
    d_normed4 = product_back(d_tri_out_b, outbound_exit_matrix)
    d_triangle, g_tri_out_gain = norm_back4(d_normed4)
    d_triangle_b = d_triangle.astype(jnp.bfloat16)
    d_tri_all = lax.all_gather(d_triangle_b, "res", axis=1, tiled=True)
    d_left = jnp.einsum("ijc,jkc->ikc", d_tri_all, right_all, preferred_element_type=jnp.float32)
    d_right_part = jnp.einsum("ijc,ikc->jkc", d_tri_all, left_b, preferred_element_type=jnp.float32)
    d_right = owners_sum(d_right_part)
    (d_gates_in,) = gates_back((d_left, d_right))
    d_tri_b = jnp.concatenate([d_gates_in, d_gate_out], -1).astype(jnp.bfloat16)
    g_tri_in = weight_back(normed3_b, d_tri_b)
    d_normed3 = product_back(d_tri_b, outbound_entry_matrix)
    d_pair1_norm, g_tri_gain = norm_back3(d_normed3)
    pair_grad = d_pair2 + d_pair1_norm
    d_opm_b = (pair_grad / count).astype(jnp.bfloat16)
    g_opm_out = weight_back(outer_b, d_opm_b)
    d_outer = product_back(d_opm_b, tensor_mean_exit_matrix).astype(jnp.bfloat16)
    d_outer = d_outer.reshape(rows_dev, vertical_shard_piece, opm_width, opm_width)
    d_left_rows = jnp.einsum(
        "ijcd,sjd->sic", d_outer, right_cols, preferred_element_type=jnp.float32
    )
    d_right_cols = jnp.einsum(
        "ijcd,sic->sjd", d_outer, left_rows, preferred_element_type=jnp.float32
    )
    d_left_sum = across_res(d_left_rows)
    d_outer_in = owners_sum(
        jnp.concatenate(
            [place_home(d_left_sum, vertical_shard_piece, offset, keep_home), d_right_cols], -1
        )
    )
    d_outer_in_b = (d_outer_in * line_indicator_entries[:, None, None]).astype(jnp.bfloat16)
    g_opm_in = weight_back(normed2_b, d_outer_in_b)
    standardized_sens2 = product_back(d_outer_in_b, tensor_mean_entry_matrix)
    alignment_standard_sens, tensor_mean_scale_sens = standardize_reverse_beta(standardized_sens2)
    alignment_later_sens = alignment_adjoint.astype(jnp.float32) + alignment_standard_sens
    softmax_mixer_sens_lines = alignment_later_sens.astype(jnp.bfloat16)
    g_attn_out = weight_back(sigmoid_scaled_lines, softmax_mixer_sens_lines)
    d_gated = product_back(softmax_mixer_sens_lines, softmax_mixer_exit_matrix)
    d_attended_b = (d_gated * attn_gate).astype(jnp.bfloat16)
    d_gate_lin = d_gated * attended * attn_gate * (1.0 - attn_gate)
    probs_full = jnp.exp(attn_scores(query4, keys4, allowed, scale) - log_total)
    d_attended4 = d_attended_b.reshape(chain_shard_piece, vertical_shard_piece, HEADS, head_size)
    d_probs = jnp.einsum(
        "qlhd,klhd->lhqk", d_attended4, values4, preferred_element_type=jnp.float32
    )
    softmax_total = jnp.sum(probs_full * d_probs, -1, keepdims=True)
    d_scores_b = (probs_full * (d_probs - softmax_total) * scale).astype(jnp.bfloat16)
    d_query = jnp.einsum(
        "lhqk,klhd->qlhd", d_scores_b, keys4, preferred_element_type=jnp.float32
    ).reshape(chain_shard_piece, vertical_shard_piece, breadth_overall)
    d_keys = jnp.einsum("lhqk,qlhd->klhd", d_scores_b, query4, preferred_element_type=jnp.float32)
    d_values = jnp.einsum(
        "lhqk,qlhd->klhd",
        probs_full.astype(jnp.bfloat16),
        d_attended4,
        preferred_element_type=jnp.float32,
    )
    d_keyval = jnp.concatenate(
        [
            d_keys.reshape(block_tally, vertical_shard_piece, breadth_overall),
            d_values.reshape(block_tally, vertical_shard_piece, breadth_overall),
        ],
        -1,
    )
    d_keyval_own = lax.psum_scatter(d_keyval, "seq", scatter_dimension=0, tiled=True)
    d_proj_b = jnp.concatenate([d_query, d_keyval_own, d_gate_lin], -1).astype(jnp.bfloat16)
    g_qkvg = weight_back(normed_b, d_proj_b)
    standardized_sens = product_back(d_proj_b, attender_stacked_matrix)
    alignment_early_sens, alignment_scale_sens = standardize_reverse_alpha(standardized_sens)
    alignment_sensitivity = alignment_later_sens + alignment_early_sens
    layer_one = [
        alignment_scale_sens,
        g_qkvg,
        g_attn_out,
        tensor_mean_scale_sens,
        g_opm_in,
        g_opm_out,
        g_tri_gain,
        g_tri_in,
        g_tri_out_gain,
        g_tri_out,
        g_inc_gain,
        g_inc_in,
        g_inc_out_gain,
        g_inc_out,
    ]
    summed_all = sum_flat(layer_one + layer_two)
    layer_one = summed_all[:14]
    layer_two = summed_all[14:]
    return (
        alignment_later.astype(jnp.bfloat16),
        pair3_b,
        single_out,
        coords_out,
        alignment_sensitivity,
        pair_grad,
        single_grad,
        coords_grad,
        layer_one[0],
        layer_one[1],
        layer_one[2],
        layer_one[3],
        layer_one[4],
        layer_one[5],
        layer_one[6],
        layer_one[7],
        layer_one[8],
        layer_one[9],
        layer_one[10],
        layer_one[11],
        layer_one[12],
        layer_one[13],
        layer_two[0],
        layer_two[1],
        layer_two[2],
        layer_two[3],
        layer_two[4],
        layer_two[5],
    )


F32 = jnp.float32
BF16 = jnp.bfloat16
MESH = pl.DeviceIdType.MESH
LANES = 128
CHUNK = 256


def dot_nn(a, b):
    return jnp.dot(a, b, preferred_element_type=F32)


def dot_nt(a, b):
    return lax.dot_general(a, b, (((1,), (1,)), ((), ())), preferred_element_type=F32)


def dot_tn(a, b):
    return lax.dot_general(a, b, (((0,), (0,)), ((), ())), preferred_element_type=F32)


def split_terms(value, terms):
    parts = []
    for _ in range(terms):
        part = value.astype(BF16)
        parts.append(part)
        value = value - part.astype(F32)
    return parts


def pick_nn(value, hot, terms):
    return sum(dot_nn(part, hot) for part in split_terms(value, terms))


def pick_nt(value, hot, terms):
    return sum(dot_nt(part, hot) for part in split_terms(value, terms))


def iota(shape, axis):
    return lax.broadcasted_iota(jnp.int32, shape, axis)


def hot_bf16(cond):
    return jnp.where(cond, 1.0, 0.0).astype(BF16)


def sigmoid(value):
    return 0.5 * jnp.tanh(0.5 * value) + 0.5


def norm(value, axis):
    centred = value - jnp.mean(value, axis, keepdims=True)
    rstd = lax.rsqrt(jnp.mean(centred * centred, axis, keepdims=True) + EPS)
    return centred * rstd, rstd


def norm_back(grad, gain, hat, rstd, axis):
    scaled = grad * gain
    first = jnp.mean(scaled, axis, keepdims=True)
    second = jnp.mean(scaled * hat, axis, keepdims=True)
    return rstd * (scaled - first - hat * second)


def column(row):
    size = row.shape[1]
    eye = iota((size, size), 0) == iota((size, size), 1)
    return jnp.sum(jnp.where(eye, row, 0.0), 1, keepdims=True)


def lane_group(ref, j):
    return jnp.concatenate(
        [ref[pl.ds(2 * j + q, LANES, stride=16), :] for q in range(2)], axis=1
    )


def lane_ungroup(ref, j, value):
    for q in range(2):
        ref[pl.ds(2 * j + q, LANES, stride=16), :] = value[:, q * LANES : (q + 1) * LANES]


def chunk_at(j):
    return pl.ds(pl.multiple_of(j * CHUNK, CHUNK), CHUNK)


def all_peers(D, t):
    return lax.rem(D.s + t // D.nr, D.ns), lax.rem(D.r + t % D.nr, D.nr)


def seq_peers(D, t):
    return lax.rem(D.s + t, D.ns), D.r


def res_peers(D, t):
    return D.s, lax.rem(D.r + t, D.nr)


def remote(src, dst, sems, slot, peer):
    return pltpu.make_async_remote_copy(
        src_ref=src,
        dst_ref=dst,
        send_sem=sems[0].at[slot],
        recv_sem=sems[1].at[slot],
        device_id=peer,
        device_id_type=MESH,
    )


def swap(D, src_at, dst_at, sems, count, peers, index, me):
    def copy(t):
        peer = peers(D, t)
        return remote(src_at(index(*peer)), dst_at(me), sems, t, peer)

    @pl.loop(1, count)
    def _(t):
        copy(t).start()

    return copy


def swap_wait(copy, count):
    @pl.loop(1, count)
    def _(t):
        copy(t).wait()


def swap_all(R, D, src, dst, sems):
    n = D.ns * D.nr
    me = D.s * D.nr + D.r
    copy = swap(
        D,
        lambda i: src.at[i],
        lambda i: dst.at[i],
        sems,
        n,
        all_peers,
        lambda ps, pr: ps * D.nr + pr,
        me,
    )
    dst[me] = src[me]
    swap_wait(copy, n)


def p_pack(R, D):
    for q in range(4):
        rows = R.x[q].astype(F32)
        adjoint = R.adj_a[q].astype(F32)
        for d in range(8):
            both = jnp.concatenate([rows[8 * d : 8 * d + 8], adjoint[8 * d : 8 * d + 8]], 0)
            R.xsend[d, q] = both.astype(BF16)


def p_spread(R, D, sems):
    copy = swap(
        D,
        lambda i: R.xsend.at[i],
        lambda i: R.xrecv.at[i],
        sems,
        D.ns,
        seq_peers,
        lambda ps, pr: ps,
        D.s,
    )
    R.xrecv[D.s] = R.xsend[D.s]
    swap_wait(copy, D.ns)
    for d in range(8):
        for q in range(4):
            both = R.xrecv[d, q].astype(F32)
            rows = pl.ds(4 * d + q, 8, stride=32)
            for half, stages in ((0, (R.sp0, R.sp2)), (1, (R.sp1, R.sp3))):
                lanes = slice(LANES * half, LANES * half + LANES)
                stages[0][rows, :] = both[:8, lanes]
                stages[1][rows, :] = both[8:, lanes]
    R.xc[...] = jnp.concatenate([R.sp0[...], R.sp1[...]], 1)
    R.ac[...] = jnp.concatenate([R.sp2[...], R.sp3[...]], 1)


def flag_column(flags):
    here = iota((256, 32), 0) % 32 == iota((256, 32), 1)
    return jnp.sum(jnp.where(here, flags, 0.0), 1, keepdims=True)


def head_probs(keys, query, flag_rows, head):
    lanes = iota((1, 256), 1) // 32
    mine = hot_bf16(lanes == head)
    scores = dot_nt(keys, query * mine) * (32 ** (-0.5))
    same = iota((256, 256), 0) // 32 == iota((256, 256), 1) // 32
    scores = jnp.where(same, jnp.where(flag_rows > 0, scores, -1e30), -3e38)
    weights = jnp.exp(scores - jnp.max(scores, 0, keepdims=True))
    return weights / jnp.sum(weights, 0, keepdims=True)


def p_attention(R, D):
    flag_rows = flag_column(R.fl[...].astype(F32))
    hat, _ = norm(R.xc[...], -1)
    normed = (hat * R.g1[...]).astype(BF16)
    projected = dot_nn(normed, R.w_qkvg[...])
    R.qkv[...] = projected[:, :768].astype(BF16)
    R.gl[...] = projected[:, 768:]
    R.att[...] = jnp.zeros((256, 256), F32)

    @pl.loop(0, 8)
    def _(head):
        probs = head_probs(R.qkv[:, 256:512], R.qkv[:, :256], flag_rows, head).astype(BF16)
        lanes = iota((1, 256), 1) // 32
        R.att[...] += jnp.where(lanes == head, dot_tn(probs, R.qkv[:, 512:768]), 0.0)

    gated = (sigmoid(R.gl[...]) * R.att[...]).astype(BF16)
    later = R.xc[...] + dot_nn(gated, R.w_ao[...])
    R.msan[...] = later
    hat2, _ = norm(later, -1)
    normed2 = (hat2 * R.g2[...]).astype(BF16)
    outer_in = (dot_nt(normed2, R.w_oit[...]) * (flag_rows > 0).astype(F32)).astype(BF16)
    wide = jnp.concatenate([outer_in.astype(F32), jnp.zeros((256, 64), F32)], 1)
    R.lsend[...] = wide.T[:32].astype(BF16)
    spread = hot_bf16(iota((64, 1024), 0) == 32 + iota((64, 1024), 1) // 32)
    kept = iota((256, 1024), 0) % 32 == iota((256, 1024), 1) % 32
    rows = jnp.where(kept, dot_nn(outer_in, spread), 0.0).astype(BF16)
    R.rsend[...] = dot_nn(hot_bf16(iota((8, 256), 0) == iota((8, 256), 1) // 32), rows)


def p_outer_exchange(R, D, sems):
    owner = 2 * D.r + D.s // 4
    slot = D.s % 4

    def left(k):
        return remote(R.lsend, R.lall.at[slot], sems, k, (owner, k))

    for k in range(4):
        mine = (owner == D.s) & (D.r == k)

        @pl.when(jnp.logical_not(mine))
        def _():
            pltpu.make_async_remote_copy(
                src_ref=R.lsend,
                dst_ref=R.lall.at[slot],
                send_sem=sems[0].at[k],
                recv_sem=sems[1].at[slot],
                device_id=(owner, k),
                device_id_type=MESH,
            ).start()

        @pl.when(mine)
        def _():
            R.lall[slot] = R.lsend[...]

    here = pl.ds(pl.multiple_of(8 * D.s, 8), 8)

    def right(t):
        return remote(R.rsend, R.rall.at[here], sems, 4 + t, seq_peers(D, t))

    @pl.loop(1, 8)
    def _(t):
        right(t).start()

    R.rall[here, :] = R.rsend[...]

    for k in range(4):
        mine = (owner == D.s) & (D.r == k)
        theirs = (4 * (D.s % 2) + k == D.s) & (D.s // 2 == D.r)
        token = pltpu.make_async_remote_copy(
            src_ref=R.lsend,
            dst_ref=R.lall.at[k],
            send_sem=sems[0].at[k],
            recv_sem=sems[1].at[k],
            device_id=(owner, k),
            device_id_type=MESH,
        )

        @pl.when(jnp.logical_not(mine))
        def _():
            token.wait_send()

        @pl.when(jnp.logical_not(theirs))
        def _():
            token.wait_recv()

    @pl.loop(1, 8)
    def _(t):
        right(t).wait()


def stage_outer_weight(R):
    R.st0[0:1024, :] = R.w_oo[...].astype(F32)


def outer_weight(R, d):
    return R.st0[pl.ds(d, 32, stride=32), :].astype(BF16)


def count_of(R):
    return jnp.sum(R.fl[...].astype(F32), 1, keepdims=True)


def p_outer(R, D):
    stage_outer_weight(R)
    for q in range(4):
        wide = jnp.concatenate([R.lall[q].astype(F32), jnp.zeros((96, 256), F32)], 0)
        R.l2[256 * q : 256 * q + 256, :] = wide.T[:, :32].astype(BF16)

    @pl.loop(0, 32)
    def _(d):
        part = dot_nn(R.l2[...], outer_weight(R, d)).astype(BF16)
        at = pl.ds(pl.multiple_of(32 * d, 32), 32)
        for i in range(32):
            R.zb[i, at, :] = part[32 * i : 32 * i + 32]

    inverse = 1.0 / count_of(R)

    @pl.loop(0, 16)
    def _(m):
        right = R.rall[...].astype(BF16)
        halves = []
        for h in range(2):
            i = 16 * h + m
            halves.append(dot_nn(right, R.zb[i]) * inverse + R.pe[i].astype(F32))
        R.pair1[:, pl.ds(pl.multiple_of(m * LANES, LANES), LANES)] = jnp.concatenate(halves, 0).T


def entry_chunk(R, pair, gain, w_t, nb, j):
    hat, _ = norm(pair, 0)
    nb_here = (hat * gain).astype(BF16)
    nb[:, chunk_at(j)] = nb_here
    for k, stage in ((0, R.st0), (1, R.st1)):
        linear = dot_nn(w_t[256 * k : 256 * k + 256, :], nb_here)
        lane_ungroup(stage, j, sigmoid(linear[128:]) * linear[:128])


def pack_both(R, send):
    @pl.loop(0, 32)
    def _(d):
        at = pl.ds(pl.multiple_of(64 * d, 64), 64)
        send[d, 0:64, :] = R.st0[at, :].astype(BF16)
        send[d, 64:128, :] = R.st1[at, :].astype(BF16)


def p_entry1(R, D):
    R.w1t[...] = R.w_ti[...].astype(F32).T.astype(BF16)
    gain = column(R.g3[...])

    @pl.loop(0, 8)
    def _(j):
        entry_chunk(R, R.pair1[:, chunk_at(j)], gain, R.w1t, R.nb3, j)

    pack_both(R, R.lrs)


def gather_mats(recv, mats, first, rows, at):
    @pl.loop(0, 8)
    def _(s):
        top = pl.ds(pl.multiple_of(32 * s, 32), 16)
        low = pl.ds(pl.multiple_of(32 * s + 16, 16), 16)
        for c in range(4):
            off = first + 16 * c
            for p in range(2):
                a = recv[4 * s + 2 * p, off : off + 16, :]
                b = recv[4 * s + 2 * p + 1, off : off + 16, :]
                lanes = slice(LANES * p, LANES * p + LANES)
                mats[at + c, top, lanes] = jnp.concatenate([a[:, :64], b[:, :64]], 1)
                mats[at + c, low, lanes] = jnp.concatenate([a[:, 64:], b[:, 64:]], 1)


def scatter_mat(mat, send, off):
    @pl.loop(0, 8)
    def _(s):
        for p in range(2):
            lanes = slice(LANES * p, LANES * p + LANES)
            a = mat[pl.ds(pl.multiple_of(32 * s, 32), 16), lanes]
            b = mat[pl.ds(pl.multiple_of(32 * s + 16, 16), 16), lanes]
            send[4 * s + 2 * p, off : off + 16, :] = jnp.concatenate([a[:, :64], b[:, :64]], 1)
            send[4 * s + 2 * p + 1, off : off + 16, :] = jnp.concatenate([a[:, 64:], b[:, 64:]], 1)


def tri_forward(R, mats, send, product):
    for c in range(4):
        R.tm[...] = product(mats[c], mats[4 + c]).astype(BF16)
        scatter_mat(R.tm, send, 16 * c)


def tri_backward(R, recv, mats, send, products):
    gather_mats(recv, R.dm, 0, 64, 0)
    for c in range(4):
        for k in range(2):
            R.tm[...] = products[k](mats[c], mats[4 + c], R.dm[c]).astype(BF16)
            scatter_mat(R.tm, send, 64 * k + 16 * c)


def p_tri1(R, D, sems):
    swap_all(R, D, R.lrs, R.lr1r, sems[0:2])
    gather_mats(R.lr1r, R.mats1, 0, 64, 0)
    gather_mats(R.lr1r, R.mats1, 64, 64, 4)
    tri_forward(R, R.mats1, R.ts, dot_nt)
    swap_all(R, D, R.ts, R.t1r, sems[2:4])


def stage_single(recv, stage):
    @pl.loop(0, 32)
    def _(d):
        stage[pl.ds(pl.multiple_of(64 * d, 64), 64), :] = recv[d].astype(F32)


def stage_both(recv, first, second):
    @pl.loop(0, 32)
    def _(d):
        at = pl.ds(pl.multiple_of(64 * d, 64), 64)
        first[at, :] = recv[d, 0:64, :].astype(F32)
        second[at, :] = recv[d, 64:128, :].astype(F32)


def p_middle(R, D):
    stage_single(R.t1r, R.st2)
    R.w2t[...] = R.w_ii[...].astype(F32).T.astype(BF16)
    R.wo1t[...] = R.w_to[...].astype(F32).T.astype(BF16)
    gain4 = column(R.g4[...])
    gain5 = column(R.g5[...])

    @pl.loop(0, 8)
    def _(j):
        hat, _ = norm(lane_group(R.st2, j), 0)
        nb4 = (hat * gain4).astype(BF16)
        R.nb4[:, chunk_at(j)] = nb4
        update = dot_nn(R.wo1t[...], nb4)
        gate = sigmoid(dot_nn(R.w1t[512:, :], R.nb3[:, chunk_at(j)]))
        pair2 = R.pair1[:, chunk_at(j)] + gate * update
        R.pair2[:, chunk_at(j)] = pair2
        entry_chunk(R, pair2, gain5, R.w2t, R.nb5, j)

    pack_both(R, R.lrs)


def p_tri2(R, D, sems):
    swap_all(R, D, R.lrs, R.lr2r, sems[0:2])
    gather_mats(R.lr2r, R.mats2, 0, 64, 0)
    gather_mats(R.lr2r, R.mats2, 64, 64, 4)
    tri_forward(R, R.mats2, R.ts, dot_tn)
    swap_all(R, D, R.ts, R.t2r, sems[2:4])


def p_turn(R, D):
    stage_single(R.t2r, R.st2)
    R.wo2t[...] = R.w_io[...].astype(F32).T.astype(BF16)
    gain6 = column(R.g6[...])
    dist = column(R.w_ds[...])
    turn_weight = column(R.w_sl[...])
    inv_k = 1.0 / R.ca.shape[1]
    R.at8[...] = jnp.zeros((8, 256), F32)
    R.at8[0:3, :] = R.at[...]
    R.la8[...] = jnp.zeros((8, 32), F32)
    R.la8[0:3, :] = R.adj_l[...]
    node = dot_tn(R.vet[...].astype(BF16), R.w_nd[...])
    R.nodet[...] = node.T
    R.dmean[...] = dot_nt(R.w_up[...], R.adj_v[...].astype(BF16))
    near = hot_bf16(iota((256, CHUNK), 0) == 64 * D.r + iota((256, CHUNK), 1) % 64)
    R.nbase[...] = pick_nn(R.nodet[64:, :], near, 2)
    R.cbase[...] = pick_nn(R.at8[...], near, 3)
    for acc in (R.s_mean, R.s_own, R.s_other):
        acc[...] = jnp.zeros(acc.shape, F32)
    R.s_xyz[...] = jnp.zeros((16, 256), F32)
    R.a_g6[...] = jnp.zeros((128, CHUNK), F32)
    R.a_dist[...] = jnp.zeros((64, CHUNK), F32)
    R.a_coord[...] = jnp.zeros((64, CHUNK), F32)
    R.nb_f[...] = R.ca[...].astype(F32)

    @pl.loop(0, 8)
    def _(j):
        here = chunk_at(j)
        hat, rstd = norm(lane_group(R.st2, j), 0)
        nb6 = (hat * gain6).astype(BF16)
        R.nb6[:, here] = nb6
        update2 = dot_nn(R.wo2t[...], nb6)
        gate2 = sigmoid(dot_nn(R.w2t[512:, :], R.nb5[:, here]))
        pair3 = R.pair2[:, here] + gate2 * update2
        po_b = pair3.astype(BF16)
        R.po[:, here] = po_b
        lane = iota((1, CHUNK), 1)
        local_row = 16 * ((lane % LANES) // 64) + 2 * j + lane // LANES
        mine = hot_bf16(iota((32, CHUNK), 0) == local_row)
        row = hot_bf16(iota((256, CHUNK), 0) == 32 * D.s + local_row)
        named = dot_tn(R.nb_f[...].astype(BF16), mine)
        target = (64 * D.r + lane % 64).astype(F32)
        mask = jnp.max(jnp.where(named == target, 1.0, 0.0), 0, keepdims=True) * inv_k
        diff = pick_nn(R.at8[...], row, 3) - R.cbase[...]
        square = 1.0 + jnp.sum(diff * diff, 0, keepdims=True)
        radial = jnp.log(square)
        edge = dot_nn(R.w_edt[...], po_b)
        pre = pick_nn(R.nodet[0:64, :], row, 2) + R.nbase[...] + edge + radial * dist
        sig_pre = sigmoid(pre)
        hidden = (pre * sig_pre).astype(BF16)
        R.hid[:, here] = hidden
        msg = dot_tn(R.w_ms[...], hidden)
        sig_msg = sigmoid(msg)
        message = msg * sig_msg
        turn = jnp.tanh(jnp.sum(message * turn_weight, 0, keepdims=True))
        R.s_mean[...] += pick_nt(message * mask, row, 2)
        locadj = pick_nn(R.la8[...], mine, 3)
        d_turn = jnp.sum(locadj * diff, 0, keepdims=True) * mask * (1.0 - turn * turn)
        d_message = pick_nn(R.dmean[...], mine, 2) * mask + turn_weight * d_turn
        R.a_coord[...] += message * d_turn
        d_msg = (d_message * sig_msg * (1.0 + msg * (1.0 - sig_msg))).astype(BF16)
        R.dmsg[:, here] = d_msg
        d_pre = dot_nn(R.w_ms[...], d_msg) * sig_pre * (1.0 + pre * (1.0 - sig_pre))
        R.a_dist[...] += d_pre * radial
        d_edge = d_pre.astype(BF16)
        R.dedge[:, here] = d_edge
        R.s_own[...] += pick_nt(d_pre, row, 2)
        R.s_other[...] += pick_nt(d_pre, near, 2)
        d_radial = jnp.sum(d_pre * dist, 0, keepdims=True)
        d_diff = (2.0 * d_radial / square) * diff + locadj * (turn * mask)
        R.s_xyz[0:8, :] += pick_nt(diff * (turn * mask), row, 2)
        R.s_xyz[8:16, :] += pick_nt(d_diff, row, 2) - pick_nt(d_diff, near, 2)
        d_po = dot_tn(R.w_edt[...], d_edge)
        adjoint = []
        for q in range(2):
            m = 2 * j + q
            both = jnp.concatenate([R.adj_c[m], R.adj_c[16 + m]], 0).astype(F32)
            adjoint.append(both.T)
            out = pair3[:, q * LANES : (q + 1) * LANES].T.astype(BF16)
            R.pair_out[m] = out[:64]
            R.pair_out[16 + m] = out[64:]
        d_pair3 = jnp.concatenate(adjoint, 1) + d_po
        R.dpair[:, here] = d_pair3
        d_up = (d_pair3 * gate2).astype(BF16)
        R.dup2[:, here] = d_up
        R.dtri2[512:, here] = (d_pair3 * update2 * gate2 * (1.0 - gate2)).astype(BF16)
        d_nb = dot_nn(R.w_io[...], d_up)
        R.a_g6[...] += d_nb * hat
        lane_ungroup(R.st0, j, norm_back(d_nb, gain6, hat, rstd, 0))

    R.g_io[...] = dot_nt(R.nb6[...], R.dup2[...])
    R.g_ed[...] = dot_nt(R.dedge[...], R.po[...])
    R.g_ms[...] = dot_nt(R.hid[...], R.dmsg[...])
    R.gg6[...] = jnp.sum(R.a_g6[...], 1, keepdims=True)
    R.g_ds[...] = jnp.sum(R.a_dist[...], 1, keepdims=True)
    R.g_sl[...] = jnp.sum(R.a_coord[...], 1, keepdims=True)
    pack_single(R, R.ts)


def pack_single(R, send):
    @pl.loop(0, 32)
    def _(d):
        send[d] = R.st0[pl.ds(pl.multiple_of(64 * d, 64), 64), :].astype(BF16)


def p_back2(R, D, sems):
    swap_all(R, D, R.ts, R.dt2r, sems[0:2])
    tri_backward(
        R,
        R.dt2r,
        R.mats2,
        R.lrs,
        (lambda a, b, d: dot_nt(b, d), lambda a, b, d: dot_nn(a, d)),
    )
    swap_all(R, D, R.lrs, R.dlr2r, sems[2:4])


def gates_back(R, d_tri, w_t, nb_here, j):
    here = chunk_at(j)
    for k, stage in ((0, R.st0), (1, R.st1)):
        grad = lane_group(stage, j)
        linear = dot_nn(w_t[256 * k : 256 * k + 256, :], nb_here)
        gate = sigmoid(linear[128:])
        d_first = grad * gate
        d_tri[256 * k : 256 * k + 128, here] = d_first.astype(BF16)
        d_tri[256 * k + 128 : 256 * k + 256, here] = (
            d_first * linear[:128] * (1.0 - gate)
        ).astype(BF16)


def p_between(R, D):
    stage_both(R.dlr2r, R.st0, R.st1)
    stage_single(R.t1r, R.st2)
    gain4 = column(R.g4[...])
    gain5 = column(R.g5[...])
    R.a_g4[...] = jnp.zeros((128, CHUNK), F32)
    R.a_g5[...] = jnp.zeros((128, CHUNK), F32)

    @pl.loop(0, 8)
    def _(j):
        here = chunk_at(j)
        gates_back(R, R.dtri2, R.w2t, R.nb5[:, here], j)
        d_nb5 = dot_nn(R.w_ii[...], R.dtri2[:, here])
        hat5, rstd5 = norm(R.pair2[:, here], 0)
        R.a_g5[...] += d_nb5 * hat5
        d_pair2 = R.dpair[:, here] + norm_back(d_nb5, gain5, hat5, rstd5, 0)
        R.dpair[:, here] = d_pair2
        gate = sigmoid(dot_nn(R.w1t[512:, :], R.nb3[:, here]))
        update = dot_nn(R.wo1t[...], R.nb4[:, here])
        d_up = (d_pair2 * gate).astype(BF16)
        R.dup1[:, here] = d_up
        R.dtri1[512:, here] = (d_pair2 * update * gate * (1.0 - gate)).astype(BF16)
        d_nb4 = dot_nn(R.w_to[...], d_up)
        hat4, rstd4 = norm(lane_group(R.st2, j), 0)
        R.a_g4[...] += d_nb4 * hat4
        lane_ungroup(R.st3, j, norm_back(d_nb4, gain4, hat4, rstd4, 0))

    R.g_ii[...] = dot_nt(R.nb5[...], R.dtri2[...])
    R.g_to[...] = dot_nt(R.nb4[...], R.dup1[...])
    R.gg5[...] = jnp.sum(R.a_g5[...], 1, keepdims=True)
    R.gg4[...] = jnp.sum(R.a_g4[...], 1, keepdims=True)

    @pl.loop(0, 32)
    def _(d):
        R.ts[d] = R.st3[pl.ds(pl.multiple_of(64 * d, 64), 64), :].astype(BF16)


def p_back1(R, D, sems):
    swap_all(R, D, R.ts, R.dt1r, sems[0:2])
    tri_backward(
        R,
        R.dt1r,
        R.mats1,
        R.lrs,
        (lambda a, b, d: dot_nn(d, b), lambda a, b, d: dot_tn(d, a)),
    )
    swap_all(R, D, R.lrs, R.dlr1r, sems[2:4])


def p_pair_end(R, D):
    stage_both(R.dlr1r, R.st0, R.st1)
    gain3 = column(R.g3[...])
    R.a_g3[...] = jnp.zeros((128, CHUNK), F32)
    inverse = 1.0 / count_of(R)

    @pl.loop(0, 8)
    def _(j):
        here = chunk_at(j)
        gates_back(R, R.dtri1, R.w1t, R.nb3[:, here], j)
        d_nb3 = dot_nn(R.w_ti[...], R.dtri1[:, here])
        hat3, rstd3 = norm(R.pair1[:, here], 0)
        R.a_g3[...] += d_nb3 * hat3
        d_pair1 = R.dpair[:, here] + norm_back(d_nb3, gain3, hat3, rstd3, 0)
        for q in range(2):
            m = 2 * j + q
            out = d_pair1[:, q * LANES : (q + 1) * LANES].T
            R.pair_grad[m] = out[:64]
            R.pair_grad[16 + m] = out[64:]
            small = (out * inverse).astype(BF16)
            R.dopm[m] = small[:64]
            R.dopm[16 + m] = small[64:]

    R.g_ti[...] = dot_nt(R.nb3[...], R.dtri1[...])
    R.gg3[...] = jnp.sum(R.a_g3[...], 1, keepdims=True)


def p_outer_back(R, D):
    stage_outer_weight(R)
    R.rt[...] = R.rall[...].T.astype(BF16)
    R.dright[...] = jnp.zeros((64, 1024), F32)
    R.dleft[...] = jnp.zeros((32, 1024), F32)
    for q in range(4):

        @pl.loop(0, 8)
        def _(k):
            i = 8 * q + k
            grad = R.dopm[i]
            R.yb[k] = dot_nn(R.rt[...], grad).astype(BF16)
            R.dright[...] += dot_nt(grad, R.zb[i])

        @pl.loop(0, 32)
        def _(d):
            at = pl.ds(pl.multiple_of(32 * d, 32), 32)
            rows = R.yb[:, at, :].reshape(256, LANES)
            lanes = slice(256 * q, 256 * q + 256)
            R.dleft[:, lanes] += dot_nt(outer_weight(R, d), rows)
            total = dot_nn(R.lall[q], rows)
            here = pl.ds(d, 32, stride=32)
            if q:
                total += R.st1[here, :]
            R.st1[here, :] = total

    R.g_oo[...] = R.st1[0:1024, :]
    for q in range(4):
        R.dls[q] = R.dleft[:, 256 * q : 256 * q + 256].astype(BF16)


def p_outer_return(R, D, sems):
    column_res = D.s // 2
    owner = 2 * D.r + D.s // 4

    def left(q, slot):
        return pltpu.make_async_remote_copy(
            src_ref=R.dls.at[q],
            dst_ref=R.dlr.at[slot],
            send_sem=sems[0].at[q],
            recv_sem=sems[1].at[slot],
            device_id=(4 * (D.s % 2) + q, column_res),
            device_id_type=MESH,
        )

    for q in range(4):
        mine = (4 * (D.s % 2) + q == D.s) & (column_res == D.r)

        @pl.when(jnp.logical_not(mine))
        def _():
            left(q, D.r).start()

        @pl.when(mine)
        def _():
            R.dlr[D.r] = R.dls[q]

    def right(t):
        peer = seq_peers(D, t)
        at = pl.ds(pl.multiple_of(8 * peer[0], 8), 8)
        return remote(R.dright.at[at], R.drr.at[D.s], sems, 4 + t, peer)

    @pl.loop(1, 8)
    def _(t):
        right(t).start()

    R.drr[D.s] = R.dright[pl.ds(pl.multiple_of(8 * D.s, 8), 8), :]

    for q in range(4):
        mine = (4 * (D.s % 2) + q == D.s) & (column_res == D.r)
        theirs = (owner == D.s) & (D.r == q)

        @pl.when(jnp.logical_not(mine))
        def _():
            left(q, q).wait_send()

        @pl.when(jnp.logical_not(theirs))
        def _():
            left(q, q).wait_recv()

    @pl.loop(1, 8)
    def _(t):
        right(t).wait()


def p_attention_back(R, D):
    flag_rows = flag_column(R.fl[...].astype(F32))
    live = (flag_rows > 0).astype(F32)
    left = R.dlr[0].astype(F32)
    for k in range(1, 4):
        left += R.dlr[k].astype(F32)
    right = R.drr[0]
    for k in range(1, 8):
        right += R.drr[k]
    wide = jnp.concatenate([left, jnp.zeros((96, 256), F32)], 0).T
    spread = dot_nn(
        hot_bf16(iota((256, 8), 0) // 32 == iota((256, 8), 1)), right.astype(BF16)
    )
    kept = iota((256, 1024), 0) % 32 == iota((256, 1024), 1) % 32
    spread = jnp.where(kept, spread, 0.0).astype(BF16)
    back = hot_bf16(32 + iota((1024, LANES), 0) // 32 == iota((1024, LANES), 1))
    d_in = ((wide + dot_nn(spread, back)) * live).astype(BF16)[:, :64]
    hat2, rstd2 = norm(R.msan[...], -1)
    normed2 = (hat2 * R.g2[...]).astype(BF16)
    R.g_oi[...] = dot_tn(d_in, normed2)
    d_normed2 = dot_nn(d_in, R.w_oit[...])
    R.gg2[...] = jnp.sum(d_normed2 * hat2, 0, keepdims=True)
    d_later = R.ac[...] + norm_back(d_normed2, R.g2[...], hat2, rstd2, -1)
    R.dlater[...] = d_later
    d_exit = d_later.astype(BF16)
    gate = sigmoid(R.gl[...])
    gated = (gate * R.att[...]).astype(BF16)
    R.g_ao[...] = dot_tn(gated, d_exit)
    d_gated = dot_nt(d_exit, R.w_ao[...])
    R.datt[...] = (d_gated * gate).astype(BF16)
    R.dproj[:, 768:] = (d_gated * R.att[...] * gate * (1.0 - gate)).astype(BF16)
    R.dqkv[...] = jnp.zeros((256, 768), F32)

    @pl.loop(0, 8)
    def _(head):
        lanes = iota((1, 256), 1) // 32
        mine = lanes == head
        hot = hot_bf16(mine)
        query = R.qkv[:, 0:256]
        keys = R.qkv[:, 256:512]
        probs = head_probs(keys, query, flag_rows, head)
        d_att = R.datt[...]
        d_probs = dot_nt(R.qkv[:, 512:768], d_att * hot)
        total = jnp.sum(probs * d_probs, 0, keepdims=True)
        d_scores = (probs * (d_probs - total) * (32 ** (-0.5))).astype(BF16)
        R.dqkv[:, 0:256] += jnp.where(mine, dot_tn(d_scores, keys), 0.0)
        R.dqkv[:, 256:512] += jnp.where(mine, dot_nn(d_scores, query), 0.0)
        R.dqkv[:, 512:768] += jnp.where(mine, dot_nn(probs.astype(BF16), d_att), 0.0)

    R.dproj[:, :768] = R.dqkv[...].astype(BF16)
    hat, rstd = norm(R.xc[...], -1)
    normed = (hat * R.g1[...]).astype(BF16)
    R.g_qkvg[...] = dot_tn(normed, R.dproj[...])
    d_normed = dot_nt(R.dproj[...], R.w_qkvg[...])
    R.gg1[...] = jnp.sum(d_normed * hat, 0, keepdims=True)
    R.dlater[...] += norm_back(d_normed, R.g1[...], hat, rstd, -1)

    R.sp0[...] = R.msan[:, :LANES]
    R.sp1[...] = R.msan[:, LANES:]
    R.sp2[...] = R.dlater[:, :LANES]
    R.sp3[...] = R.dlater[:, LANES:]
    for d in range(8):
        for q in range(4):
            rows = pl.ds(4 * d + q, 8, stride=32)
            value = jnp.concatenate([R.sp0[rows, :], R.sp1[rows, :]], 1)
            grad = jnp.concatenate([R.sp2[rows, :], R.sp3[rows, :]], 1)
            R.osend[d, q] = jnp.concatenate([value, grad], 0).astype(BF16)


def p_collect(R, D, sems):
    copy = swap(
        D,
        lambda i: R.osend.at[i],
        lambda i: R.orecv.at[i],
        sems,
        D.ns,
        seq_peers,
        lambda ps, pr: ps,
        D.s,
    )
    R.orecv[D.s] = R.osend[D.s]
    swap_wait(copy, D.ns)
    for q in range(4):
        blocks = [R.orecv[d, q].astype(F32) for d in range(8)]
        R.msa_out[q] = jnp.concatenate([b[:8] for b in blocks], 0).astype(BF16)
        R.msa_grad[q] = jnp.concatenate([b[8:] for b in blocks], 0)


def payload_layout():
    layout = []
    start = 0
    shapes = dict(
        g_qkvg=(256, 1024),
        g_ao=(256, 256),
        g_oo=(1024, 128),
        g_ti=(128, 640),
        g_ii=(128, 640),
        g_to=(128, 128),
        g_io=(128, 128),
        s_mean=(64, 256),
        s_own=(64, 256),
        s_other=(64, 256),
        s_vadj=(64, 256),
        s_xyz=(16, 256),
        g_oi=(64, 256),
        g_ed=(64, 128),
        g_ms=(64, 64),
        small=(128, 128),
    )
    for name, (rows, cols) in shapes.items():
        for lane in range(0, cols, LANES):
            layout.append((name, start, rows, lane, min(LANES, cols - lane)))
            start += rows
    return layout, -(-start // 512) * 512


def p_sum_pack(R, D):
    rows = iota((32, 256), 0)
    place = hot_bf16(iota((32, 256), 1) == 32 * D.s + rows)
    first = jnp.where(D.r == 0, 1.0, 0.0)
    R.s_vadj[...] = dot_tn(R.adj_v[...].astype(BF16), place) * first
    R.small[...] = jnp.zeros((128, LANES), F32)
    for k, name in enumerate(("gg3", "gg4", "gg5", "gg6", "g_ds", "g_sl")):
        value = getattr(R, name)
        R.small[0 : value.shape[0], k : k + 1] = value[...]
    for k, name in enumerate(("gg1", "gg2")):
        value = getattr(R, name)
        for half in range(2):
            R.small[:, 8 + 2 * k + half : 9 + 2 * k + half] = column(
                value[:, LANES * half : LANES * half + LANES]
            )
    layout, total = payload_layout()
    for name, start, count, lane, width in layout:
        R.pay[start : start + count, 0:width] = getattr(R, name)[:, lane : lane + width].astype(
            BF16
        )
    last = layout[-1]
    end = last[1] + last[2]
    if end < total:
        R.pay[end:total, :] = jnp.zeros((total - end, LANES), BF16)


def p_sum(R, D, sems):
    eighth = R.pay.shape[0] // 8
    part = eighth // 4

    def rows(ref, index, size):
        return ref.at[pl.ds(pl.multiple_of(index * size, size), size)]

    copy = swap(
        D,
        lambda i: rows(R.pay, i, eighth),
        lambda i: R.sum_a.at[i],
        sems[0:2],
        D.ns,
        seq_peers,
        lambda ps, pr: ps,
        D.s,
    )
    swap_wait(copy, D.ns)
    R.sum_a[D.s] = R.pay[pl.ds(pl.multiple_of(D.s * eighth, eighth), eighth), :]
    total = R.sum_a[0].astype(F32)
    for k in range(1, 8):
        total += R.sum_a[k].astype(F32)
    R.sum_b[...] = total.astype(BF16)
    copy = swap(
        D,
        lambda i: rows(R.sum_b, i, part),
        lambda i: R.sum_c.at[i],
        sems[2:4],
        D.nr,
        res_peers,
        lambda ps, pr: pr,
        D.r,
    )
    swap_wait(copy, D.nr)
    R.sum_c[D.r] = R.sum_b[pl.ds(pl.multiple_of(D.r * part, part), part), :]
    total = R.sum_c[0].astype(F32)
    for k in range(1, 4):
        total += R.sum_c[k].astype(F32)
    R.sum_d[...] = total.astype(BF16)
    mine = pl.ds(pl.multiple_of(D.s * eighth + D.r * part, part), part)
    R.full[mine, :] = R.sum_d[...]
    copy = swap(
        D,
        lambda i: R.sum_d,
        lambda i: R.full.at[mine],
        sems[4:6],
        D.nr,
        res_peers,
        lambda ps, pr: pr,
        D.r,
    )
    swap_wait(copy, D.nr)
    copy = swap(
        D,
        lambda i: rows(R.full, D.s, eighth),
        lambda i: rows(R.full, i, eighth),
        sems[6:8],
        D.ns,
        seq_peers,
        lambda ps, pr: ps,
        D.s,
    )
    swap_wait(copy, D.ns)


def p_finish(R, D):
    layout, _ = payload_layout()
    held = {}
    for name, start, count, lane, width in layout:
        value = R.full[start : start + count, 0:width].astype(F32)
        if name.startswith("g_"):
            getattr(R, "o_" + name)[:, lane : lane + width] = value
        else:
            held.setdefault(name, []).append(value)
    held = {name: jnp.concatenate(parts, 1) for name, parts in held.items()}
    small = held["small"].T
    for k, name in enumerate(("gg3", "gg4", "gg5", "gg6")):
        getattr(R, "o_" + name)[...] = small[k : k + 1, :]
    R.o_g_ds[...] = small[4:5, :64]
    R.o_g_sl[...] = small[5:6, :64]
    for k, name in enumerate(("gg1", "gg2")):
        for half in range(2):
            at = 8 + 2 * k + half
            getattr(R, "o_" + name)[:, LANES * half : LANES * half + LANES] = small[at : at + 1]
    mean_b = held["s_mean"].astype(BF16)
    R.o_g_up[...] = dot_nt(mean_b, held["s_vadj"].astype(BF16))
    d_node = jnp.concatenate([held["s_own"], held["s_other"]], 0).astype(BF16)
    R.o_g_nd[...] = dot_nt(R.vet[...].astype(BF16), d_node)
    step = dot_tn(R.w_up[...], mean_b)
    grad = dot_nn(R.w_nd[...], d_node)
    R.rows_f[...] = jnp.concatenate([step + R.vet[...], grad], 0).T
    here = pl.ds(pl.multiple_of(32 * D.s, 32), 32)
    mine = R.rows_f[here, :]
    R.single_out[...] = mine[:, :64]
    R.single_grad[...] = R.adj_v[...] + mine[:, 64:]
    R.xyz[...] = jnp.zeros((128, 256), F32)
    R.xyz[0:16, :] = held["s_xyz"]
    R.xyz[16:19, :] = R.at[...]
    R.rows_g[...] = R.xyz[...].T
    turned = R.rows_g[here, :]
    back = jnp.concatenate([turned, jnp.zeros((96, 128), F32)], 0).T
    R.coords_out[...] = back[16:19, 0:32] + back[0:3, 0:32]
    R.coords_grad[...] = R.adj_l[...] + back[8:11, 0:32]


KEPT = dict(
    xsend=((8, 4, 16, 256), BF16),
    xrecv=((8, 4, 16, 256), BF16),
    xc=((256, 256), F32),
    ac=((256, 256), F32),
    sp0=((256, 128), F32),
    sp1=((256, 128), F32),
    sp2=((256, 128), F32),
    sp3=((256, 128), F32),
    qkv=((256, 768), BF16),
    gl=((256, 256), F32),
    att=((256, 256), F32),
    msan=((256, 256), F32),
    lsend=((32, 256), BF16),
    rsend=((8, 1024), F32),
    lall=((4, 32, 256), BF16),
    rall=((64, 1024), F32),
    st0=((2048, 128), F32),
    st1=((2048, 128), F32),
    st2=((2048, 128), F32),
    st3=((2048, 128), F32),
    l2=((1024, 32), BF16),
    zb=((32, 1024, 128), BF16),
    yb=((8, 1024, 128), BF16),
    pair1=((128, 2048), F32),
    pair2=((128, 2048), F32),
    dpair=((128, 2048), F32),
    w1t=((640, 128), BF16),
    w2t=((640, 128), BF16),
    wo1t=((128, 128), BF16),
    wo2t=((128, 128), BF16),
    nb3=((128, 2048), BF16),
    nb4=((128, 2048), BF16),
    nb5=((128, 2048), BF16),
    nb6=((128, 2048), BF16),
    po=((128, 2048), BF16),
    hid=((64, 2048), BF16),
    dmsg=((64, 2048), BF16),
    dedge=((64, 2048), BF16),
    dup1=((128, 2048), BF16),
    dup2=((128, 2048), BF16),
    dtri1=((640, 2048), BF16),
    dtri2=((640, 2048), BF16),
    mats1=((8, 256, 256), BF16),
    mats2=((8, 256, 256), BF16),
    dm=((4, 256, 256), BF16),
    tm=((256, 256), BF16),
    lrs=((32, 128, 128), BF16),
    lr1r=((32, 128, 128), BF16),
    lr2r=((32, 128, 128), BF16),
    dlr1r=((32, 128, 128), BF16),
    dlr2r=((32, 128, 128), BF16),
    ts=((32, 64, 128), BF16),
    t1r=((32, 64, 128), BF16),
    t2r=((32, 64, 128), BF16),
    dt1r=((32, 64, 128), BF16),
    dt2r=((32, 64, 128), BF16),
    at8=((8, 256), F32),
    la8=((8, 32), F32),
    nodet=((128, 256), F32),
    dmean=((64, 32), F32),
    nbase=((64, 256), F32),
    cbase=((8, 256), F32),
    nb_f=((32, 64), F32),
    s_mean=((64, 256), F32),
    s_own=((64, 256), F32),
    s_other=((64, 256), F32),
    s_vadj=((64, 256), F32),
    s_xyz=((16, 256), F32),
    a_g3=((128, 256), F32),
    a_g4=((128, 256), F32),
    a_g5=((128, 256), F32),
    a_g6=((128, 256), F32),
    a_dist=((64, 256), F32),
    a_coord=((64, 256), F32),
    gg3=((128, 1), F32),
    gg4=((128, 1), F32),
    gg5=((128, 1), F32),
    gg6=((128, 1), F32),
    gg1=((1, 256), F32),
    gg2=((1, 256), F32),
    g_ds=((64, 1), F32),
    g_sl=((64, 1), F32),
    g_io=((128, 128), F32),
    g_to=((128, 128), F32),
    g_ti=((128, 640), F32),
    g_ii=((128, 640), F32),
    g_ed=((64, 128), F32),
    g_ms=((64, 64), F32),
    g_oo=((1024, 128), F32),
    g_oi=((64, 256), F32),
    g_ao=((256, 256), F32),
    g_qkvg=((256, 1024), F32),
    small=((128, 128), F32),
    dopm=((32, 64, 128), BF16),
    rt=((1024, 64), BF16),
    dright=((64, 1024), F32),
    dleft=((32, 1024), F32),
    dls=((4, 32, 256), BF16),
    dlr=((4, 32, 256), BF16),
    drr=((8, 8, 1024), F32),
    dlater=((256, 256), F32),
    datt=((256, 256), BF16),
    dproj=((256, 1024), BF16),
    dqkv=((256, 768), F32),
    osend=((8, 4, 16, 256), BF16),
    orecv=((8, 4, 16, 256), BF16),
)
PAYLOAD = payload_layout()[1]
KEPT.update(
    pay=((PAYLOAD, 128), BF16),
    sum_a=((8, PAYLOAD // 8, 128), BF16),
    sum_b=((PAYLOAD // 8, 128), BF16),
    sum_c=((4, PAYLOAD // 32, 128), BF16),
    sum_d=((PAYLOAD // 32, 128), BF16),
)
LAST_ONLY = ()
LARGE = ("msa_out", "pair_out", "msa_grad", "pair_grad")
FINISH = ("full", "vet", "w_up", "w_nd", "adj_v", "at", "adj_l")
FINISH_KEPT = dict(
    rows_f=((256, 128), F32), rows_g=((256, 128), F32), xyz=((128, 256), F32)
)
MIDDLE = dict(full=((PAYLOAD, 128), BF16))
RESULTS = dict(
    msa_out=((4, 64, 256), BF16),
    pair_out=((32, 64, 128), BF16),
    single_out=((32, 64), F32),
    coords_out=((3, 32), F32),
    msa_grad=((4, 64, 256), F32),
    pair_grad=((32, 64, 128), F32),
    single_grad=((32, 64), F32),
    coords_grad=((3, 32), F32),
    o_gg1=((1, 256), F32),
    o_g_qkvg=((256, 1024), F32),
    o_g_ao=((256, 256), F32),
    o_gg2=((1, 256), F32),
    o_g_oi=((64, 256), F32),
    o_g_oo=((1024, 128), F32),
    o_gg3=((1, 128), F32),
    o_g_ti=((128, 640), F32),
    o_gg4=((1, 128), F32),
    o_g_to=((128, 128), F32),
    o_gg5=((1, 128), F32),
    o_g_ii=((128, 640), F32),
    o_gg6=((1, 128), F32),
    o_g_io=((128, 128), F32),
    o_g_nd=((64, 128), F32),
    o_g_ed=((64, 128), F32),
    o_g_ds=((1, 64), F32),
    o_g_ms=((64, 64), F32),
    o_g_sl=((1, 64), F32),
    o_g_up=((64, 64), F32),
)

STEPS = (
    (p_pack, 0),
    (p_spread, 1),
    (p_attention, 0),
    (p_outer_exchange, 1),
    (p_outer, 0),
    (p_entry1, 0),
    (p_tri1, 2),
    (p_middle, 0),
    (p_tri2, 2),
    (p_turn, 0),
    (p_back2, 2),
    (p_between, 0),
    (p_back1, 2),
    (p_pair_end, 0),
    (p_outer_back, 0),
    (p_outer_return, 1),
    (p_attention_back, 0),
    (p_collect, 1),
    (p_sum_pack, 0),
    (p_sum, 4),
)


def first_kernel(n_seq, n_res, names, exchanges, *refs):
    R = SimpleNamespace(**dict(zip(names, refs)))
    sems = refs[len(names) :]
    D = SimpleNamespace(s=lax.axis_index("seq"), r=lax.axis_index("res"), ns=n_seq, nr=n_res)
    barrier = pltpu.get_barrier_semaphore()

    @pl.loop(1, n_seq * n_res)
    def _(t):
        pl.semaphore_signal(barrier, inc=1, device_id=all_peers(D, t), device_id_type=MESH)

    used = 0
    for step, count in STEPS:
        if count:
            if not used:
                pl.semaphore_wait(barrier, n_seq * n_res - 1)
            step(R, D, sems[2 * used : 2 * used + 2 * count])
            used += count
        else:
            step(R, D)


def last_kernel(n_seq, n_res, names, *refs):
    R = SimpleNamespace(**dict(zip(names, refs)))
    D = SimpleNamespace(s=lax.axis_index("seq"), r=lax.axis_index("res"), ns=n_seq, nr=n_res)
    p_finish(R, D)


ARGS = dict(
    x=(4, 64, 256),
    pe=(32, 64, 128),
    vet=(256, 64),
    at=(3, 256),
    fl=(32,),
    ca=(32, 64),
    g1=(256,),
    w_qkvg=(256, 1024),
    w_ao=(256, 256),
    g2=(256,),
    w_oit=(256, 64),
    w_oo=(1024, 128),
    g3=(128,),
    w_ti=(128, 640),
    g4=(128,),
    w_to=(128, 128),
    g5=(128,),
    w_ii=(128, 640),
    g6=(128,),
    w_io=(128, 128),
    w_nd=(64, 128),
    w_edt=(128, 64),
    w_ds=(64,),
    w_ms=(64, 64),
    w_sl=(64,),
    w_up=(64, 64),
    adj_a=(4, 64, 256),
    adj_c=(32, 64, 128),
    adj_v=(32, 64),
    adj_l=(3, 32),
)


def fits(n_seq, n_res, args):
    shapes = tuple(tuple(arg.shape) for arg in args)
    return (n_seq, n_res) == (8, 4) and shapes == tuple(ARGS.values())


def fast_shards(n_seq, n_res, *args):
    env = dict(zip(ARGS, args))
    for name, value in tuple(env.items()):
        if value.ndim == 1:
            env[name] = value.reshape(1, -1)
    env.update(vet=env["vet"].T, w_oit=env["w_oit"].T, w_edt=env["w_edt"].T)
    space = pl.BlockSpec(memory_space=pltpu.VMEM)
    exchanges = sum(count for _, count in STEPS)
    slots = n_seq * n_res

    def shapes(table):
        return [jax.ShapeDtypeStruct(*entry) for entry in table.values()]

    large = {name: RESULTS[name] for name in LARGE}
    middle = dict(**large, **MIDDLE)
    inputs = [name for name in env if name not in LAST_ONLY]
    values = pl.pallas_call(
        functools.partial(first_kernel, n_seq, n_res, (*inputs, *middle, *KEPT), exchanges),
        out_shape=shapes(middle),
        in_specs=[space] * len(inputs),
        out_specs=[space] * len(middle),
        scratch_shapes=[pltpu.VMEM(*entry) for entry in KEPT.values()]
        + [pltpu.SemaphoreType.DMA((slots,))] * (2 * exchanges),
        compiler_params=pltpu.CompilerParams(
            vmem_limit_bytes=60 * 2**20, collective_id=0, has_side_effects=True
        ),
    )(*[env[name] for name in inputs])
    env.update(zip(middle, values))
    small = {name: entry for name, entry in RESULTS.items() if name not in large}
    inputs = [*FINISH]
    values = pl.pallas_call(
        functools.partial(last_kernel, n_seq, n_res, (*inputs, *small, *FINISH_KEPT)),
        out_shape=shapes(small),
        in_specs=[space] * len(inputs),
        out_specs=[space] * len(small),
        scratch_shapes=[pltpu.VMEM(*entry) for entry in FINISH_KEPT.values()],
        compiler_params=pltpu.CompilerParams(vmem_limit_bytes=60 * 2**20),
    )(*[env[name] for name in inputs])
    env.update(zip(small, values))
    results = [env[name] for name in RESULTS]
    for index, value in enumerate(results):
        if value.shape[0] == 1:
            results[index] = value.reshape(-1)
    for index in (12, 23):
        results[index] = results[index].T
    return tuple(results)


def solution(mesh):
    n_seq, n_res = mesh.shape["seq"], mesh.shape["res"]

    def body(*args):
        if fits(n_seq, n_res, args):
            return fast_shards(n_seq, n_res, *args)
        return shards(*args)

    return jax.shard_map(
        body,
        mesh=mesh,
        in_specs=(
            P("seq", "res", None),
            P("seq", "res", None),
            P(),
            P(),
            P(),
            P("seq", None),
            P(),
            P(),
            P(),
            P(),
            P(),
            P(),
            P(),
            P(),
            P(),
            P(),
            P(),
            P(),
            P(),
            P(),
            P(),
            P(),
            P(),
            P(),
            P(),
            P(),
            P("seq", "res", None),
            P("seq", "res", None),
            P("seq", None),
            P(None, "seq"),
        ),
        out_specs=(
            P("seq", "res", None),
            P("seq", "res", None),
            P("seq", None),
            P(None, "seq"),
            P("seq", "res", None),
            P("seq", "res", None),
            P("seq", None),
            P(None, "seq"),
            P(),
            P(),
            P(),
            P(),
            P(),
            P(),
            P(),
            P(),
            P(),
            P(),
            P(),
            P(),
            P(),
            P(),
            P(),
            P(),
            P(),
            P(),
            P(),
            P(),
        ),
        check_vma=False,
    )
```

```python
import functools
from types import SimpleNamespace

import jax
import jax.numpy as jnp
from jax import lax
from jax.experimental import pallas as pl
from jax.experimental.pallas import tpu as pltpu
from jax.sharding import PartitionSpec as P

HEADS = 8


EPS = 1e-05
HIGH = lax.Precision.HIGHEST


def spread_2(value, axis, source):
    kept = jnp.where(lax.axis_index(axis) == source, value, 0).astype(value.dtype)
    return lax.psum(kept, axis)


def standardize_lines(value, gain):
    row_mean = jnp.mean(value, -1, keepdims=True)
    centred = value - row_mean
    spread = jnp.mean(centred * centred, -1, keepdims=True)
    return centred * lax.rsqrt(spread + EPS) * gain


def tensor_mean_answer(left, right):
    return jnp.einsum("...c,cd->...d", left, right, preferred_element_type=jnp.float32)


def product_back(grad, right):
    return jnp.einsum("...d,cd->...c", grad, right, preferred_element_type=jnp.float32)


def weight_back(left, grad):
    flat_left = left.reshape(-1, left.shape[-1])
    flat_grad = grad.reshape(-1, grad.shape[-1])
    return jnp.einsum("nc,nd->cd", flat_left, flat_grad, preferred_element_type=jnp.float32)


def attn_scores(query, keys, allowed, scale):
    raw_scores = (
        jnp.einsum("qlhd,klhd->lhqk", query, keys, preferred_element_type=jnp.float32) * scale
    )
    return jnp.where(allowed, raw_scores, -1e30)


def tri_gates(tri_lin):
    quarter = tri_lin.shape[-1] // 4
    left_part = jax.nn.sigmoid(tri_lin[..., quarter : 2 * quarter]) * tri_lin[..., :quarter]
    right_part = (
        jax.nn.sigmoid(tri_lin[..., 3 * quarter :]) * tri_lin[..., 2 * quarter : 3 * quarter]
    )
    return (left_part, right_part)


def edge_front(own_rows, other_near, edge_lin, diff, distance_basis_matrix):
    radial = jnp.log(1.0 + jnp.sum(diff * diff, 0))
    return jax.nn.silu(
        own_rows[:, None, :] + other_near + edge_lin + radial[..., None] * distance_basis_matrix
    )


def edge_finish(msg_lin, signal_location_matrix, diff):
    message = jax.nn.silu(msg_lin)
    turn = jnp.tanh(jnp.einsum("ikc,c->ik", message, signal_location_matrix, precision=HIGH))
    return (jnp.mean(message, 1), jnp.mean(diff * turn[None], 2))


def gather_rows(value):
    return lax.all_gather(value, "seq", axis=0, tiled=True)


def across_res(value):
    return lax.psum(value.astype(jnp.bfloat16), "res").astype(jnp.float32)


def owners_sum(value):
    return lax.psum_scatter(value, "seq", scatter_dimension=0, tiled=True)


def place_home(rows_part, col_width, offset, keep_home):
    empty = jnp.zeros((rows_part.shape[0], col_width, rows_part.shape[2]), jnp.float32)
    return lax.dynamic_update_slice_in_dim(empty, rows_part, offset, 1) * keep_home


def sum_flat(parts):
    flat = jnp.concatenate([jnp.ravel(member) for member in parts])
    summed = lax.psum(flat, ("seq", "res"))
    pieces = []
    offset = 0
    for member in parts:
        pieces.append(summed[offset : offset + member.size].reshape(member.shape))
        offset = offset + member.size
    return pieces


def shards(
    alignment_embedding,
    coupling_embedding,
    vertex_embedding,
    atom_locations,
    chain_existence_flags,
    closest_aminos,
    softmax_mixer_scale_factor,
    attender_stacked_matrix,
    softmax_mixer_exit_matrix,
    tensor_mean_scale_factor,
    tensor_mean_entry_matrix,
    tensor_mean_exit_matrix,
    outbound_entry_scale,
    outbound_entry_matrix,
    outbound_exit_scale,
    outbound_exit_matrix,
    inbound_entry_scale,
    inbound_entry_matrix,
    inbound_exit_scale,
    inbound_exit_matrix,
    vertex_mapping_matrix,
    bond_mapping_matrix,
    distance_basis_matrix,
    signal_matrix,
    signal_location_matrix,
    vertex_change_matrix,
    alignment_adjoint,
    coupling_adjoint,
    vertex_adjoint,
    location_adjoint,
):
    seq_index = lax.axis_index("seq")
    res_index = lax.axis_index("res")
    n_seq = lax.axis_size("seq")
    n_res = lax.axis_size("res")
    chain_shard_piece, vertical_shard_piece, breadth_overall = alignment_embedding.shape
    rows_dev = coupling_embedding.shape[0]
    span_overall, node_width = vertex_embedding.shape
    block_tally = chain_existence_flags.shape[0]
    head_size = breadth_overall // HEADS
    scale = head_size ** (-0.5)
    opm_width = tensor_mean_entry_matrix.shape[1] // 2
    tri_width = outbound_exit_matrix.shape[0]
    chain_exists = (chain_existence_flags > 0).astype(jnp.float32)
    line_indicator_entries = lax.dynamic_slice_in_dim(
        chain_exists, seq_index * chain_shard_piece, chain_shard_piece
    )
    first_res = (res_index == 0).astype(jnp.float32)
    home = seq_index * rows_dev // vertical_shard_piece
    offset = seq_index * rows_dev - home * vertical_shard_piece
    keep_home = (home == res_index).astype(jnp.float32)
    alignment_real_lines = alignment_embedding.astype(jnp.float32)
    standardized_lines, standardize_reverse_alpha = jax.vjp(
        standardize_lines, alignment_real_lines, softmax_mixer_scale_factor
    )
    normed_b = standardized_lines.astype(jnp.bfloat16)
    projected = tensor_mean_answer(normed_b, attender_stacked_matrix)
    query = projected[..., :breadth_overall].astype(jnp.bfloat16)
    keyval = projected[..., breadth_overall : 3 * breadth_overall].astype(jnp.bfloat16)
    attn_gate = jax.nn.sigmoid(projected[..., 3 * breadth_overall :])
    all_keyval = lax.all_gather(keyval, "seq", axis=0, tiled=True)
    query4 = query.reshape(chain_shard_piece, vertical_shard_piece, HEADS, head_size)
    keys4 = all_keyval[..., :breadth_overall].reshape(
        block_tally, vertical_shard_piece, HEADS, head_size
    )
    values4 = all_keyval[..., breadth_overall:].reshape(
        block_tally, vertical_shard_piece, HEADS, head_size
    )
    allowed = chain_exists[None, None, None, :] > 0
    scores = attn_scores(query4, keys4, allowed, scale)
    score_peak = jnp.max(scores, -1, keepdims=True)
    exp_scores = jnp.exp(scores - score_peak)
    exp_total = jnp.sum(exp_scores, -1, keepdims=True)
    log_total = score_peak + jnp.log(exp_total)
    probs_b = (exp_scores / exp_total).astype(jnp.bfloat16)
    attended = jnp.einsum(
        "lhqk,klhd->qlhd", probs_b, values4, preferred_element_type=jnp.float32
    ).reshape(chain_shard_piece, vertical_shard_piece, breadth_overall)
    sigmoid_scaled_lines = (attn_gate * attended).astype(jnp.bfloat16)
    alignment_later = alignment_real_lines + tensor_mean_answer(
        sigmoid_scaled_lines, softmax_mixer_exit_matrix
    )
    standardized_lines2, standardize_reverse_beta = jax.vjp(
        standardize_lines, alignment_later, tensor_mean_scale_factor
    )
    normed2_b = standardized_lines2.astype(jnp.bfloat16)
    outer_in = (
        tensor_mean_answer(normed2_b, tensor_mean_entry_matrix)
        * line_indicator_entries[:, None, None]
    ).astype(jnp.bfloat16)
    everyone = lax.all_gather(outer_in, ("seq", "res"), axis=0, tiled=True)
    blocks = everyone.reshape(n_seq, n_res, chain_shard_piece, vertical_shard_piece, 2 * opm_width)
    home_block = lax.dynamic_index_in_dim(blocks, home, 1, keepdims=False)
    left_rows = lax.dynamic_slice_in_dim(home_block, offset, rows_dev, 2)[..., :opm_width]
    left_rows = left_rows.reshape(block_tally, rows_dev, opm_width)
    right_cols = lax.dynamic_index_in_dim(blocks, res_index, 1, keepdims=False)[..., opm_width:]
    right_cols = right_cols.reshape(block_tally, vertical_shard_piece, opm_width)
    outer_b = jnp.einsum("sic,sjd->ijcd", left_rows, right_cols, preferred_element_type=jnp.float32)
    outer_b = outer_b.reshape(rows_dev, vertical_shard_piece, opm_width * opm_width).astype(
        jnp.bfloat16
    )
    count = jnp.sum(chain_exists)
    pair1 = (
        coupling_embedding.astype(jnp.float32)
        + tensor_mean_answer(outer_b, tensor_mean_exit_matrix) / count
    )
    normed3, norm_back3 = jax.vjp(standardize_lines, pair1, outbound_entry_scale)
    normed3_b = normed3.astype(jnp.bfloat16)
    tri = tensor_mean_answer(normed3_b, outbound_entry_matrix)
    (left_t, right_t), gates_back = jax.vjp(tri_gates, tri[..., : 4 * tri_width])
    left_b = left_t.astype(jnp.bfloat16)
    right_b = right_t.astype(jnp.bfloat16)
    right_all = gather_rows(right_b)
    partial_tri = jnp.einsum("ikc,jkc->ijc", left_b, right_all, preferred_element_type=jnp.float32)
    triangle = lax.psum_scatter(
        partial_tri.astype(jnp.bfloat16), "res", scatter_dimension=1, tiled=True
    ).astype(jnp.float32)
    normed4, norm_back4 = jax.vjp(standardize_lines, triangle, outbound_exit_scale)
    normed4_b = normed4.astype(jnp.bfloat16)
    update = tensor_mean_answer(normed4_b, outbound_exit_matrix)
    out_gate = jax.nn.sigmoid(tri[..., 4 * tri_width :])
    pair2 = pair1 + out_gate * update
    normed5, norm_back5 = jax.vjp(standardize_lines, pair2, inbound_entry_scale)
    normed5_b = normed5.astype(jnp.bfloat16)
    tri2 = tensor_mean_answer(normed5_b, inbound_entry_matrix)
    (left_i, right_i), gates_back2 = jax.vjp(tri_gates, tri2[..., : 4 * tri_width])
    both_local = jnp.concatenate([left_i.astype(jnp.bfloat16), right_i.astype(jnp.bfloat16)], -1)
    both_all = gather_rows(both_local)
    right_all2 = both_all[..., tri_width:]
    left_cand = lax.dynamic_slice_in_dim(both_all[..., :tri_width], offset, rows_dev, 1)
    left_sel = spread_2(left_cand, "res", home)
    triangle2 = jnp.einsum("kic,kjc->ijc", left_sel, right_all2, preferred_element_type=jnp.float32)
    normed6, norm_back6 = jax.vjp(standardize_lines, triangle2, inbound_exit_scale)
    normed6_b = normed6.astype(jnp.bfloat16)
    update2 = tensor_mean_answer(normed6_b, inbound_exit_matrix)
    out_gate2 = jax.nn.sigmoid(tri2[..., 4 * tri_width :])
    coupling_later3 = pair2 + out_gate2 * update2
    pair3_b = coupling_later3.astype(jnp.bfloat16)
    rows_all = lax.all_gather(pair3_b, "res", axis=1, tiled=True)
    nbr_hot = closest_aminos[:, :, None] == jnp.arange(span_overall, dtype=jnp.int32)[None, None, :]
    hot_float = nbr_hot.astype(jnp.float32)
    edges_b = jnp.einsum(
        "ikl,ilc->ikc", nbr_hot.astype(jnp.bfloat16), rows_all, preferred_element_type=jnp.float32
    ).astype(jnp.bfloat16)
    single_b = vertex_embedding.astype(jnp.bfloat16)
    node_proj = tensor_mean_answer(single_b, vertex_mapping_matrix)
    own_rows = lax.dynamic_slice_in_dim(node_proj[:, :node_width], seq_index * rows_dev, rows_dev)
    other_near = jnp.einsum("ikl,lc->ikc", hot_float, node_proj[:, node_width:], precision=HIGH)
    coords_own = lax.dynamic_slice_in_dim(atom_locations, seq_index * rows_dev, rows_dev, 1)
    coords_near = jnp.einsum("ikl,xl->xik", hot_float, atom_locations, precision=HIGH)
    diff = coords_own[:, :, None] - coords_near
    edge_lin = tensor_mean_answer(edges_b, bond_mapping_matrix)
    hidden, front_back = jax.vjp(
        edge_front, own_rows, other_near, edge_lin, diff, distance_basis_matrix
    )
    hidden_b = hidden.astype(jnp.bfloat16)
    msg_lin = tensor_mean_answer(hidden_b, signal_matrix)
    (mean_msg, shift), finish_back = jax.vjp(edge_finish, msg_lin, signal_location_matrix, diff)
    mean_b = mean_msg.astype(jnp.bfloat16)
    single_rows = lax.dynamic_slice_in_dim(vertex_embedding, seq_index * rows_dev, rows_dev)
    single_out = single_rows + tensor_mean_answer(mean_b, vertex_change_matrix)
    coords_out = coords_own + shift
    d_update_b = vertex_adjoint.astype(jnp.bfloat16)
    g_update = weight_back(mean_b, d_update_b)
    d_mean = product_back(d_update_b, vertex_change_matrix)
    d_msg_lin, g_coord, d_diff_finish = finish_back((d_mean, location_adjoint))
    d_msg_b = d_msg_lin.astype(jnp.bfloat16)
    g_msg = weight_back(hidden_b, d_msg_b)
    d_hidden = product_back(d_msg_b, signal_matrix)
    d_own, d_other_near, d_edge_lin, d_diff_front, g_dist = front_back(d_hidden)
    d_edge_b = d_edge_lin.astype(jnp.bfloat16)
    g_edge = weight_back(edges_b, d_edge_b)
    d_edges = product_back(d_edge_b, bond_mapping_matrix)
    d_rows = jnp.einsum("ikl,ikc->ilc", hot_float, d_edges, precision=HIGH)
    d_pair3 = coupling_adjoint.astype(jnp.float32) + lax.dynamic_slice_in_dim(
        d_rows, res_index * vertical_shard_piece, vertical_shard_piece, 1
    )
    d_diff = d_diff_front + d_diff_finish
    d_coords_own = jnp.sum(d_diff, 2)
    d_coords_near = jnp.einsum("ikl,xik->xl", hot_float, -d_diff, precision=HIGH)
    d_other_all = jnp.einsum("ikl,ikc->lc", hot_float, d_other_near, precision=HIGH)
    d_other_rows, d_near_rows = (
        lax.psum_scatter(d_other_all, "seq", scatter_dimension=0, tiled=True),
        lax.psum_scatter(d_coords_near, "seq", scatter_dimension=1, tiled=True),
    )
    d_node_b = jnp.concatenate([d_own, d_other_rows], -1).astype(jnp.bfloat16)
    g_node = weight_back(
        lax.dynamic_slice_in_dim(single_b, seq_index * rows_dev, rows_dev), d_node_b
    )
    single_grad = vertex_adjoint + product_back(d_node_b, vertex_mapping_matrix)
    coords_grad = location_adjoint + d_coords_own + d_near_rows
    layer_two = [
        g_node * first_res,
        g_edge * first_res,
        g_dist * first_res,
        g_msg * first_res,
        g_coord * first_res,
        g_update * first_res,
    ]
    d_inc_b = (d_pair3 * out_gate2).astype(jnp.bfloat16)
    d_gate_out2 = d_pair3 * update2 * out_gate2 * (1.0 - out_gate2)
    g_inc_out = weight_back(normed6_b, d_inc_b)
    d_normed6 = product_back(d_inc_b, inbound_exit_matrix)
    d_triangle2, g_inc_out_gain = norm_back6(d_normed6)
    d_tri2_b = d_triangle2.astype(jnp.bfloat16)
    d_left_sel = jnp.einsum(
        "ijc,kjc->kic", d_tri2_b, right_all2, preferred_element_type=jnp.float32
    )
    d_right_all2 = jnp.einsum(
        "ijc,kic->kjc", d_tri2_b, left_sel, preferred_element_type=jnp.float32
    )
    d_left_total = across_res(d_left_sel)
    d_both2 = owners_sum(
        jnp.concatenate(
            [place_home(d_left_total, vertical_shard_piece, offset, keep_home), d_right_all2], -1
        )
    )
    (d_gates2,) = gates_back2((d_both2[..., :tri_width], d_both2[..., tri_width:]))
    d_tri2_in_b = jnp.concatenate([d_gates2, d_gate_out2], -1).astype(jnp.bfloat16)
    g_inc_in = weight_back(normed5_b, d_tri2_in_b)
    d_normed5 = product_back(d_tri2_in_b, inbound_entry_matrix)
    d_pair2_norm, g_inc_gain = norm_back5(d_normed5)
    d_pair2 = d_pair3 + d_pair2_norm
    d_tri_out_b = (d_pair2 * out_gate).astype(jnp.bfloat16)
    d_gate_out = d_pair2 * update * out_gate * (1.0 - out_gate)
    g_tri_out = weight_back(normed4_b, d_tri_out_b)
    d_normed4 = product_back(d_tri_out_b, outbound_exit_matrix)
    d_triangle, g_tri_out_gain = norm_back4(d_normed4)
    d_triangle_b = d_triangle.astype(jnp.bfloat16)
    d_tri_all = lax.all_gather(d_triangle_b, "res", axis=1, tiled=True)
    d_left = jnp.einsum("ijc,jkc->ikc", d_tri_all, right_all, preferred_element_type=jnp.float32)
    d_right_part = jnp.einsum("ijc,ikc->jkc", d_tri_all, left_b, preferred_element_type=jnp.float32)
    d_right = owners_sum(d_right_part)
    (d_gates_in,) = gates_back((d_left, d_right))
    d_tri_b = jnp.concatenate([d_gates_in, d_gate_out], -1).astype(jnp.bfloat16)
    g_tri_in = weight_back(normed3_b, d_tri_b)
    d_normed3 = product_back(d_tri_b, outbound_entry_matrix)
    d_pair1_norm, g_tri_gain = norm_back3(d_normed3)
    pair_grad = d_pair2 + d_pair1_norm
    d_opm_b = (pair_grad / count).astype(jnp.bfloat16)
    g_opm_out = weight_back(outer_b, d_opm_b)
    d_outer = product_back(d_opm_b, tensor_mean_exit_matrix).astype(jnp.bfloat16)
    d_outer = d_outer.reshape(rows_dev, vertical_shard_piece, opm_width, opm_width)
    d_left_rows = jnp.einsum(
        "ijcd,sjd->sic", d_outer, right_cols, preferred_element_type=jnp.float32
    )
    d_right_cols = jnp.einsum(
        "ijcd,sic->sjd", d_outer, left_rows, preferred_element_type=jnp.float32
    )
    d_left_sum = across_res(d_left_rows)
    d_outer_in = owners_sum(
        jnp.concatenate(
            [place_home(d_left_sum, vertical_shard_piece, offset, keep_home), d_right_cols], -1
        )
    )
    d_outer_in_b = (d_outer_in * line_indicator_entries[:, None, None]).astype(jnp.bfloat16)
    g_opm_in = weight_back(normed2_b, d_outer_in_b)
    standardized_sens2 = product_back(d_outer_in_b, tensor_mean_entry_matrix)
    alignment_standard_sens, tensor_mean_scale_sens = standardize_reverse_beta(standardized_sens2)
    alignment_later_sens = alignment_adjoint.astype(jnp.float32) + alignment_standard_sens
    softmax_mixer_sens_lines = alignment_later_sens.astype(jnp.bfloat16)
    g_attn_out = weight_back(sigmoid_scaled_lines, softmax_mixer_sens_lines)
    d_gated = product_back(softmax_mixer_sens_lines, softmax_mixer_exit_matrix)
    d_attended_b = (d_gated * attn_gate).astype(jnp.bfloat16)
    d_gate_lin = d_gated * attended * attn_gate * (1.0 - attn_gate)
    probs_full = jnp.exp(attn_scores(query4, keys4, allowed, scale) - log_total)
    d_attended4 = d_attended_b.reshape(chain_shard_piece, vertical_shard_piece, HEADS, head_size)
    d_probs = jnp.einsum(
        "qlhd,klhd->lhqk", d_attended4, values4, preferred_element_type=jnp.float32
    )
    softmax_total = jnp.sum(probs_full * d_probs, -1, keepdims=True)
    d_scores_b = (probs_full * (d_probs - softmax_total) * scale).astype(jnp.bfloat16)
    d_query = jnp.einsum(
        "lhqk,klhd->qlhd", d_scores_b, keys4, preferred_element_type=jnp.float32
    ).reshape(chain_shard_piece, vertical_shard_piece, breadth_overall)
    d_keys = jnp.einsum("lhqk,qlhd->klhd", d_scores_b, query4, preferred_element_type=jnp.float32)
    d_values = jnp.einsum(
        "lhqk,qlhd->klhd",
        probs_full.astype(jnp.bfloat16),
        d_attended4,
        preferred_element_type=jnp.float32,
    )
    d_keyval = jnp.concatenate(
        [
            d_keys.reshape(block_tally, vertical_shard_piece, breadth_overall),
            d_values.reshape(block_tally, vertical_shard_piece, breadth_overall),
        ],
        -1,
    )
    d_keyval_own = lax.psum_scatter(d_keyval, "seq", scatter_dimension=0, tiled=True)
    d_proj_b = jnp.concatenate([d_query, d_keyval_own, d_gate_lin], -1).astype(jnp.bfloat16)
    g_qkvg = weight_back(normed_b, d_proj_b)
    standardized_sens = product_back(d_proj_b, attender_stacked_matrix)
    alignment_early_sens, alignment_scale_sens = standardize_reverse_alpha(standardized_sens)
    alignment_sensitivity = alignment_later_sens + alignment_early_sens
    layer_one = [
        alignment_scale_sens,
        g_qkvg,
        g_attn_out,
        tensor_mean_scale_sens,
        g_opm_in,
        g_opm_out,
        g_tri_gain,
        g_tri_in,
        g_tri_out_gain,
        g_tri_out,
        g_inc_gain,
        g_inc_in,
        g_inc_out_gain,
        g_inc_out,
    ]
    summed_all = sum_flat(layer_one + layer_two)
    layer_one = summed_all[:14]
    layer_two = summed_all[14:]
    return (
        alignment_later.astype(jnp.bfloat16),
        pair3_b,
        single_out,
        coords_out,
        alignment_sensitivity,
        pair_grad,
        single_grad,
        coords_grad,
        layer_one[0],
        layer_one[1],
        layer_one[2],
        layer_one[3],
        layer_one[4],
        layer_one[5],
        layer_one[6],
        layer_one[7],
        layer_one[8],
        layer_one[9],
        layer_one[10],
        layer_one[11],
        layer_one[12],
        layer_one[13],
        layer_two[0],
        layer_two[1],
        layer_two[2],
        layer_two[3],
        layer_two[4],
        layer_two[5],
    )


F32 = jnp.float32
BF16 = jnp.bfloat16
MESH = pl.DeviceIdType.MESH
LANES = 128
CHUNK = 256


def dot_nn(a, b):
    return jnp.dot(a, b, preferred_element_type=F32)


def dot_nt(a, b):
    return lax.dot_general(a, b, (((1,), (1,)), ((), ())), preferred_element_type=F32)


def dot_tn(a, b):
    return lax.dot_general(a, b, (((0,), (0,)), ((), ())), preferred_element_type=F32)


def split_terms(value, terms):
    parts = []
    for _ in range(terms):
        part = value.astype(BF16)
        parts.append(part)
        value = value - part.astype(F32)
    return parts


def pick_nn(value, hot, terms):
    return sum(dot_nn(part, hot) for part in split_terms(value, terms))


def pick_nt(value, hot, terms):
    return sum(dot_nt(part, hot) for part in split_terms(value, terms))


def iota(shape, axis):
    return lax.broadcasted_iota(jnp.int32, shape, axis)


def hot_bf16(cond):
    return jnp.where(cond, 1.0, 0.0).astype(BF16)


def sigmoid(value):
    return 0.5 * jnp.tanh(0.5 * value) + 0.5


def norm(value, axis):
    centred = value - jnp.mean(value, axis, keepdims=True)
    rstd = lax.rsqrt(jnp.mean(centred * centred, axis, keepdims=True) + EPS)
    return centred * rstd, rstd


def norm_back(grad, gain, hat, rstd, axis):
    scaled = grad * gain
    first = jnp.mean(scaled, axis, keepdims=True)
    second = jnp.mean(scaled * hat, axis, keepdims=True)
    return rstd * (scaled - first - hat * second)


def column(row):
    size = row.shape[1]
    eye = iota((size, size), 0) == iota((size, size), 1)
    return jnp.sum(jnp.where(eye, row, 0.0), 1, keepdims=True)


def lane_group(ref, j):
    return jnp.concatenate(
        [ref[pl.ds(2 * j + q, LANES, stride=16), :] for q in range(2)], axis=1
    )


def lane_ungroup(ref, j, value):
    for q in range(2):
        ref[pl.ds(2 * j + q, LANES, stride=16), :] = value[:, q * LANES : (q + 1) * LANES]


def chunk_at(j):
    return pl.ds(pl.multiple_of(j * CHUNK, CHUNK), CHUNK)


def all_peers(D, t):
    return lax.rem(D.s + t // D.nr, D.ns), lax.rem(D.r + t % D.nr, D.nr)


def seq_peers(D, t):
    return lax.rem(D.s + t, D.ns), D.r


def res_peers(D, t):
    return D.s, lax.rem(D.r + t, D.nr)


def remote(src, dst, sems, slot, peer):
    return pltpu.make_async_remote_copy(
        src_ref=src,
        dst_ref=dst,
        send_sem=sems[0].at[slot],
        recv_sem=sems[1].at[slot],
        device_id=peer,
        device_id_type=MESH,
    )


def swap(D, src_at, dst_at, sems, count, peers, index, me):
    def copy(t):
        peer = peers(D, t)
        return remote(src_at(index(*peer)), dst_at(me), sems, t, peer)

    @pl.loop(1, count)
    def _(t):
        copy(t).start()

    return copy


def swap_wait(copy, count):
    @pl.loop(1, count)
    def _(t):
        copy(t).wait()


def start_all(D, src, dst, first, size):
    n = D.ns * D.nr
    me = D.s * D.nr + D.r
    rows = pl.ds(first, size)
    copy = swap(
        D,
        lambda i: src.at[i, rows],
        lambda i: dst.at[i, rows],
        D.take(),
        n,
        all_peers,
        lambda ps, pr: ps * D.nr + pr,
        me,
    )
    dst[me, rows, :] = src[me, rows, :]
    return lambda: swap_wait(copy, n)


def start_seq(D, src_at, dst_at):
    copy = swap(D, src_at, dst_at, D.take(), D.ns, seq_peers, lambda ps, pr: ps, D.s)
    return lambda: swap_wait(copy, D.ns)


def start_res(D, src_at, dst_at):
    copy = swap(D, src_at, dst_at, D.take(), D.nr, res_peers, lambda ps, pr: pr, D.r)
    return lambda: swap_wait(copy, D.nr)


def pack_columns(value, send):
    for q in range(2):
        first = value[2 * q].astype(F32)
        second = value[2 * q + 1].astype(F32)
        for d in range(8):
            at = slice(8 * d, 8 * d + 8)
            send[d, q] = jnp.concatenate([first[at], second[at]], 0).astype(BF16)


def start_columns(D, send, recv):
    recv[D.s] = send[D.s]
    return start_seq(D, lambda i: send.at[i], lambda i: recv.at[i])


def unpack_columns(R, recv, target):
    for d in range(8):
        for q in range(2):
            both = recv[d, q].astype(F32)
            for k in range(2):
                rows = pl.ds(4 * d + 2 * q + k, 8, stride=32)
                R.sp0[rows, :] = both[8 * k : 8 * k + 8, :LANES]
                R.sp1[rows, :] = both[8 * k : 8 * k + 8, LANES:]
    target[...] = jnp.concatenate([R.sp0[...], R.sp1[...]], 1)


def p_spread(R, D):
    pack_columns(R.x, R.xsend)
    D.ready()
    wait = start_columns(D, R.xsend, R.xrecv)
    pack_columns(R.adj_a, R.asend)
    R.wait_adjoint = start_columns(D, R.asend, R.arecv)
    R.w1t[...] = R.w_ti[...].astype(F32).T.astype(BF16)
    R.w2t[...] = R.w_ii[...].astype(F32).T.astype(BF16)
    R.wo1t[...] = R.w_to[...].astype(F32).T.astype(BF16)
    R.wo2t[...] = R.w_io[...].astype(F32).T.astype(BF16)
    stage_outer_weight(R)
    wait()
    unpack_columns(R, R.xrecv, R.xc)


def flag_column(flags):
    here = iota((256, 32), 0) % 32 == iota((256, 32), 1)
    return jnp.sum(jnp.where(here, flags, 0.0), 1, keepdims=True)


def head_probs(keys, query, flag_rows, head):
    lanes = iota((1, 256), 1) // 32
    mine = hot_bf16(lanes == head)
    scores = dot_nt(keys, query * mine) * (32 ** (-0.5))
    same = iota((256, 256), 0) // 32 == iota((256, 256), 1) // 32
    scores = jnp.where(same, jnp.where(flag_rows > 0, scores, -1e30), -3e38)
    weights = jnp.exp(scores - jnp.max(scores, 0, keepdims=True))
    return weights / jnp.sum(weights, 0, keepdims=True)


def p_attention(R, D):
    flag_rows = flag_column(R.fl[...].astype(F32))
    hat, _ = norm(R.xc[...], -1)
    normed = (hat * R.g1[...]).astype(BF16)
    projected = dot_nn(normed, R.w_qkvg[...])
    R.qkv[...] = projected[:, :768].astype(BF16)
    R.gl[...] = projected[:, 768:]
    R.att[...] = jnp.zeros((256, 256), F32)

    @pl.loop(0, 8, unroll=4)
    def _(head):
        probs = head_probs(R.qkv[:, 256:512], R.qkv[:, :256], flag_rows, head).astype(BF16)
        lanes = iota((1, 256), 1) // 32
        R.att[...] += jnp.where(lanes == head, dot_tn(probs, R.qkv[:, 512:768]), 0.0)

    gated = (sigmoid(R.gl[...]) * R.att[...]).astype(BF16)
    later = R.xc[...] + dot_nn(gated, R.w_ao[...])
    R.msan[...] = later
    hat2, _ = norm(later, -1)
    normed2 = (hat2 * R.g2[...]).astype(BF16)
    outer_in = (dot_nt(normed2, R.w_oit[...]) * (flag_rows > 0).astype(F32)).astype(BF16)
    wide = jnp.concatenate([outer_in.astype(F32), jnp.zeros((256, 64), F32)], 1)
    R.lsend[...] = wide.T[:32].astype(BF16)
    spread = hot_bf16(iota((64, 1024), 0) == 32 + iota((64, 1024), 1) // 32)
    kept = iota((256, 1024), 0) % 32 == iota((256, 1024), 1) % 32
    rows = jnp.where(kept, dot_nn(outer_in, spread), 0.0).astype(BF16)
    R.rsend[...] = dot_nn(hot_bf16(iota((8, 256), 0) == iota((8, 256), 1) // 32), rows)


def p_outer_exchange(R, D):
    sems = D.take()
    owner = 2 * D.r + D.s // 4
    slot = D.s % 4

    def left(k):
        return remote(R.lsend, R.lall.at[slot], sems, k, (owner, k))

    for k in range(4):
        mine = (owner == D.s) & (D.r == k)

        @pl.when(jnp.logical_not(mine))
        def _():
            pltpu.make_async_remote_copy(
                src_ref=R.lsend,
                dst_ref=R.lall.at[slot],
                send_sem=sems[0].at[k],
                recv_sem=sems[1].at[slot],
                device_id=(owner, k),
                device_id_type=MESH,
            ).start()

        @pl.when(mine)
        def _():
            R.lall[slot] = R.lsend[...]

    here = pl.ds(pl.multiple_of(8 * D.s, 8), 8)

    def right(t):
        return remote(R.rsend, R.rall.at[here], sems, 4 + t, seq_peers(D, t))

    @pl.loop(1, 8)
    def _(t):
        right(t).start()

    R.rall[here, :] = R.rsend[...]

    for k in range(4):
        mine = (owner == D.s) & (D.r == k)
        theirs = (4 * (D.s % 2) + k == D.s) & (D.s // 2 == D.r)
        token = pltpu.make_async_remote_copy(
            src_ref=R.lsend,
            dst_ref=R.lall.at[k],
            send_sem=sems[0].at[k],
            recv_sem=sems[1].at[k],
            device_id=(owner, k),
            device_id_type=MESH,
        )

        @pl.when(jnp.logical_not(mine))
        def _():
            token.wait_send()

        @pl.when(jnp.logical_not(theirs))
        def _():
            token.wait_recv()

    @pl.loop(1, 8)
    def _(t):
        right(t).wait()


def stage_outer_weight(R):
    R.wst[...] = R.w_oo[...].astype(F32)


def outer_weight(R, d):
    return R.wst[pl.ds(d, 32, stride=32), :].astype(BF16)


def count_of(R):
    return jnp.sum(R.fl[...].astype(F32), 1, keepdims=True)


def p_outer(R, D):
    for q in range(4):
        wide = jnp.concatenate([R.lall[q].astype(F32), jnp.zeros((96, 256), F32)], 0)
        R.l2[256 * q : 256 * q + 256, :] = wide.T[:, :32].astype(BF16)
        R.lt[:, 256 * q : 256 * q + 256] = R.lall[q]

    @pl.loop(0, 8)
    def _(e):
        weights = jnp.concatenate([outer_weight(R, 4 * e + u) for u in range(4)], 1)
        part = dot_nn(R.l2[...], weights).astype(BF16)
        for u in range(4):
            at = pl.ds(pl.multiple_of(32 * (4 * e + u), 32), 32)
            for i in range(32):
                R.zb[i, at, :] = part[32 * i : 32 * i + 32, LANES * u : LANES * u + LANES]

    inverse = 1.0 / count_of(R)
    right = R.rall[...].astype(BF16)

    @pl.loop(0, 16, unroll=4)
    def _(m):
        both = dot_nn(right, jnp.concatenate([R.zb[m], R.zb[16 + m]], 1)) * inverse
        rows = [
            both[:, LANES * h : LANES * h + LANES] + R.pe[16 * h + m].astype(F32) for h in range(2)
        ]
        R.pair1[:, pl.ds(pl.multiple_of(m * LANES, LANES), LANES)] = jnp.concatenate(rows, 0).T


def entry_chunk(R, pair, gain, w_t, nb, j):
    hat, _ = norm(pair, 0)
    nb_here = (hat * gain).astype(BF16)
    nb[:, chunk_at(j)] = nb_here
    for k, stage in ((0, R.st0), (1, R.st1)):
        linear = dot_nn(w_t[256 * k : 256 * k + 256, :], nb_here)
        lane_ungroup(stage, j, sigmoid(linear[128:]) * linear[:128])


def pack_both(R, send):
    @pl.loop(0, 32, unroll=4)
    def _(d):
        at = pl.ds(pl.multiple_of(64 * d, 64), 64)
        first = R.st0[at, :].astype(BF16)
        second = R.st1[at, :].astype(BF16)
        for c in range(4):
            send[d, 32 * c : 32 * c + 16, :] = first[16 * c : 16 * c + 16]
            send[d, 32 * c + 16 : 32 * c + 32, :] = second[16 * c : 16 * c + 16]


def p_entry1(R, D):
    gain = column(R.g3[...])

    @pl.loop(0, 8, unroll=4)
    def _(j):
        entry_chunk(R, R.pair1[:, chunk_at(j)], gain, R.w1t, R.nb3, j)

    pack_both(R, R.lrs)


def gather_mat(recv, off, mats, at):
    @pl.loop(0, 8, unroll=4)
    def _(s):
        top = pl.ds(pl.multiple_of(32 * s, 32), 16)
        low = pl.ds(pl.multiple_of(32 * s + 16, 16), 16)
        for p in range(2):
            a = recv[4 * s + 2 * p, off : off + 16, :]
            b = recv[4 * s + 2 * p + 1, off : off + 16, :]
            lanes = slice(LANES * p, LANES * p + LANES)
            mats[at, top, lanes] = jnp.concatenate([a[:, :64], b[:, :64]], 1)
            mats[at, low, lanes] = jnp.concatenate([a[:, 64:], b[:, 64:]], 1)


def scatter_mat(mat, send, off):
    @pl.loop(0, 8, unroll=4)
    def _(s):
        for p in range(2):
            lanes = slice(LANES * p, LANES * p + LANES)
            a = mat[pl.ds(pl.multiple_of(32 * s, 32), 16), lanes]
            b = mat[pl.ds(pl.multiple_of(32 * s + 16, 16), 16), lanes]
            send[4 * s + 2 * p, off : off + 16, :] = jnp.concatenate([a[:, :64], b[:, :64]], 1)
            send[4 * s + 2 * p + 1, off : off + 16, :] = jnp.concatenate([a[:, 64:], b[:, 64:]], 1)


def tri_forward(R, D, recv, mats, back, product, meanwhile):
    size = 4 // PARTS
    waits = [start_all(D, R.lrs, recv, 32 * size * h, 32 * size) for h in range(PARTS)]
    meanwhile(R, D)
    later = []
    for h in range(PARTS):
        waits[h]()
        for c in range(size * h, size * h + size):
            gather_mat(recv, 32 * c, mats, c)
            gather_mat(recv, 32 * c + 16, mats, 4 + c)
            R.tm[c] = product(mats[c], mats[4 + c]).astype(BF16)
            scatter_mat(R.tm.at[c], R.ts, 16 * c)
        later.append(start_all(D, R.ts, back, 16 * size * h, 16 * size))
    for wait in later:
        wait()


def tri_backward(R, D, recv, mats, back, products, meanwhile):
    size = 4 // PARTS
    waits = [start_all(D, R.ts, recv, 16 * size * h, 16 * size) for h in range(PARTS)]
    meanwhile(R, D)
    later = []
    for h in range(PARTS):
        waits[h]()
        for c in range(size * h, size * h + size):
            gather_mat(recv, 16 * c, R.dm, c)
            for k in range(2):
                R.tm[c] = products[k](mats[c], mats[4 + c], R.dm[c]).astype(BF16)
                scatter_mat(R.tm.at[c], R.lrs, 32 * c + 16 * k)
        later.append(start_all(D, R.lrs, back, 32 * size * h, 32 * size))
    for wait in later:
        wait()


def nothing(R, D):
    pass


def p_tri1(R, D):
    tri_forward(R, D, R.lr1r, R.mats1, R.t1r, dot_nt, p_still)


def stage_single(recv, stage):
    @pl.loop(0, 32, unroll=4)
    def _(d):
        stage[pl.ds(pl.multiple_of(64 * d, 64), 64), :] = recv[d].astype(F32)


def stage_both(recv, first, second):
    @pl.loop(0, 32, unroll=4)
    def _(d):
        at = pl.ds(pl.multiple_of(64 * d, 64), 64)
        both = recv[d].astype(F32)
        first[at, :] = jnp.concatenate([both[32 * c : 32 * c + 16] for c in range(4)], 0)
        second[at, :] = jnp.concatenate([both[32 * c + 16 : 32 * c + 32] for c in range(4)], 0)


def p_middle(R, D):
    stage_single(R.t1r, R.st2)
    gain4 = column(R.g4[...])
    gain5 = column(R.g5[...])

    @pl.loop(0, 8, unroll=4)
    def _(j):
        hat, _ = norm(lane_group(R.st2, j), 0)
        nb4 = (hat * gain4).astype(BF16)
        R.nb4[:, chunk_at(j)] = nb4
        update = dot_nn(R.wo1t[...], nb4)
        gate = sigmoid(dot_nn(R.w1t[512:, :], R.nb3[:, chunk_at(j)]))
        pair2 = R.pair1[:, chunk_at(j)] + gate * update
        R.pair2[:, chunk_at(j)] = pair2
        entry_chunk(R, pair2, gain5, R.w2t, R.nb5, j)

    pack_both(R, R.lrs)


def p_tri2(R, D):
    tri_forward(R, D, R.lr2r, R.mats2, R.t2r, dot_tn, nothing)


def chunk_rows(D, j):
    lane = iota((1, CHUNK), 1)
    local = 16 * ((lane % LANES) // 64) + 2 * j + lane // LANES
    return local, hot_bf16(iota((256, CHUNK), 0) == 32 * D.s + local)


def near_rows(D):
    return hot_bf16(iota((256, CHUNK), 0) == 64 * D.r + iota((256, CHUNK), 1) % 64)


def p_still(R, D):
    dist = column(R.w_ds[...])
    inv_k = 1.0 / R.ca.shape[1]
    R.at8[...] = jnp.zeros((8, 256), F32)
    R.at8[0:3, :] = R.at[...]
    R.la8[...] = jnp.zeros((8, 32), F32)
    R.la8[0:3, :] = R.adj_l[...]
    R.nodet[...] = dot_tn(R.vet[...].astype(BF16), R.w_nd[...]).T
    R.dmean[...] = dot_nt(R.w_up[...], R.adj_v[...].astype(BF16))
    near = near_rows(D)
    R.nbase[...] = pick_nn(R.nodet[64:, :], near, 2)
    R.cbase[...] = pick_nn(R.at8[...], near, 3)
    R.nb_f[...] = R.ca[...].astype(F32)

    @pl.loop(0, 8, unroll=2)
    def _(j):
        here = chunk_at(j)
        local, row = chunk_rows(D, j)
        mine = hot_bf16(iota((32, CHUNK), 0) == local)
        named = dot_tn(R.nb_f[...].astype(BF16), mine)
        target = (64 * D.r + iota((1, CHUNK), 1) % 64).astype(F32)
        mask = jnp.max(jnp.where(named == target, 1.0, 0.0), 0, keepdims=True) * inv_k
        diff = pick_nn(R.at8[...], row, 3) - R.cbase[...]
        square = 1.0 + jnp.sum(diff * diff, 0, keepdims=True)
        radial = jnp.log(square)
        R.geo[0:8, here] = diff
        R.geo[8:16, here] = pick_nn(R.la8[...], mine, 3)
        R.geo[16:17, here] = radial
        R.geo[17:18, here] = mask
        R.geo[18:19, here] = 2.0 / square
        R.pre[0:64, here] = pick_nn(R.nodet[0:64, :], row, 2) + R.nbase[...] + radial * dist
        R.pre[64:128, here] = pick_nn(R.dmean[...], mine, 2) * mask
        for q in range(2):
            m = 2 * j + q
            both = jnp.concatenate([R.adj_c[m], R.adj_c[16 + m]], 0).astype(F32)
            R.dpair[:, pl.ds(pl.multiple_of(m * LANES, LANES), LANES)] = both.T


def p_turn(R, D):
    stage_single(R.t2r, R.st2)
    gain6 = column(R.g6[...])
    dist = column(R.w_ds[...])
    turn_weight = column(R.w_sl[...])
    R.a_g6[...] = jnp.zeros((128, CHUNK), F32)

    @pl.loop(0, 8, unroll=4)
    def _(j):
        here = chunk_at(j)
        hat, rstd = norm(lane_group(R.st2, j), 0)
        nb6 = (hat * gain6).astype(BF16)
        R.nb6[:, here] = nb6
        update2 = dot_nn(R.wo2t[...], nb6)
        gate2 = sigmoid(dot_nn(R.w2t[512:, :], R.nb5[:, here]))
        pair3 = R.pair2[:, here] + gate2 * update2
        po_b = pair3.astype(BF16)
        R.po[:, here] = po_b
        pre = R.pre[0:64, here] + dot_nn(R.w_edt[...], po_b)
        sig_pre = sigmoid(pre)
        hidden = (pre * sig_pre).astype(BF16)
        R.hid[:, here] = hidden
        msg = dot_tn(R.w_ms[...], hidden)
        sig_msg = sigmoid(msg)
        message = msg * sig_msg
        turn = jnp.tanh(jnp.sum(message * turn_weight, 0, keepdims=True))
        diff = R.geo[0:8, here]
        locadj = R.geo[8:16, here]
        mask = R.geo[17:18, here]
        d_turn = jnp.sum(locadj * diff, 0, keepdims=True) * mask * (1.0 - turn * turn)
        d_message = R.pre[64:128, here] + turn_weight * d_turn
        d_msg = (d_message * sig_msg * (1.0 + msg * (1.0 - sig_msg))).astype(BF16)
        R.dmsg[:, here] = d_msg
        d_pre = dot_nn(R.w_ms[...], d_msg) * sig_pre * (1.0 + pre * (1.0 - sig_pre))
        d_edge = d_pre.astype(BF16)
        R.dedge[:, here] = d_edge
        d_radial = jnp.sum(d_pre * dist, 0, keepdims=True)
        R.pre[0:64, here] = message
        R.pre[64:128, here] = d_pre
        R.geo[19:20, here] = turn * mask
        R.geo[20:21, here] = d_turn
        R.geo[24:32, here] = (d_radial * R.geo[18:19, here]) * diff + locadj * (turn * mask)
        d_pair3 = R.dpair[:, here] + dot_tn(R.w_edt[...], d_edge)
        R.dpair[:, here] = d_pair3
        d_up = (d_pair3 * gate2).astype(BF16)
        R.dup2[:, here] = d_up
        R.dtri2[512:, here] = (d_pair3 * update2 * gate2 * (1.0 - gate2)).astype(BF16)
        d_nb = dot_nn(R.w_io[...], d_up)
        R.a_g6[...] += d_nb * hat
        lane_ungroup(R.st0, j, norm_back(d_nb, gain6, hat, rstd, 0))

    pack_single(R, R.ts)


def p_turn_grads(R, D):
    R.g_io[...] = dot_nt(R.nb6[...], R.dup2[...])
    R.g_ed[...] = dot_nt(R.dedge[...], R.po[...])
    R.g_ms[...] = dot_nt(R.hid[...], R.dmsg[...])
    R.gg6[...] = jnp.sum(R.a_g6[...], 1, keepdims=True)
    R.g_ds[...] = jnp.sum(R.pre[64:128, :] * R.geo[16:17, :], 1, keepdims=True)
    R.g_sl[...] = jnp.sum(R.pre[0:64, :] * R.geo[20:21, :], 1, keepdims=True)
    for acc in (R.s_mean, R.s_own, R.s_other):
        acc[...] = jnp.zeros(acc.shape, F32)
    R.s_xyz[...] = jnp.zeros((16, 256), F32)

    @pl.loop(0, 8, unroll=2)
    def _(j):
        here = chunk_at(j)
        _, row = chunk_rows(D, j)
        near = near_rows(D)
        d_pre = R.pre[64:128, here]
        d_diff = R.geo[24:32, here]
        R.s_mean[...] += pick_nt(R.pre[0:64, here] * R.geo[17:18, here], row, 2)
        R.s_own[...] += pick_nt(d_pre, row, 2)
        R.s_other[...] += pick_nt(d_pre, near, 2)
        R.s_xyz[0:8, :] += pick_nt(R.geo[0:8, here] * R.geo[19:20, here], row, 2)
        R.s_xyz[8:16, :] += pick_nt(d_diff, row, 2) - pick_nt(d_diff, near, 2)
        for q in range(2):
            m = 2 * j + q
            at = pl.ds(pl.multiple_of(m * LANES, LANES), LANES)
            out = R.po[:, at].astype(F32).T.astype(BF16)
            R.pair_out[m] = out[:64]
            R.pair_out[16 + m] = out[64:]


def pack_single(R, send):
    @pl.loop(0, 32, unroll=4)
    def _(d):
        send[d] = R.st0[pl.ds(pl.multiple_of(64 * d, 64), 64), :].astype(BF16)


def p_back2(R, D):
    tri_backward(
        R,
        D,
        R.dt2r,
        R.mats2,
        R.dlr2r,
        (lambda a, b, d: dot_nt(b, d), lambda a, b, d: dot_nn(a, d)),
        p_turn_grads,
    )


def gates_back(R, d_tri, w_t, nb_here, j):
    here = chunk_at(j)
    for k, stage in ((0, R.st0), (1, R.st1)):
        grad = lane_group(stage, j)
        linear = dot_nn(w_t[256 * k : 256 * k + 256, :], nb_here)
        gate = sigmoid(linear[128:])
        d_first = grad * gate
        d_tri[256 * k : 256 * k + 128, here] = d_first.astype(BF16)
        d_tri[256 * k + 128 : 256 * k + 256, here] = (
            d_first * linear[:128] * (1.0 - gate)
        ).astype(BF16)


def p_between(R, D):
    stage_both(R.dlr2r, R.st0, R.st1)
    stage_single(R.t1r, R.st2)
    gain4 = column(R.g4[...])
    gain5 = column(R.g5[...])
    R.a_g4[...] = jnp.zeros((128, CHUNK), F32)
    R.a_g5[...] = jnp.zeros((128, CHUNK), F32)

    @pl.loop(0, 8, unroll=4)
    def _(j):
        here = chunk_at(j)
        gates_back(R, R.dtri2, R.w2t, R.nb5[:, here], j)
        d_nb5 = dot_nn(R.w_ii[...], R.dtri2[:, here])
        hat5, rstd5 = norm(R.pair2[:, here], 0)
        R.a_g5[...] += d_nb5 * hat5
        d_pair2 = R.dpair[:, here] + norm_back(d_nb5, gain5, hat5, rstd5, 0)
        R.dpair[:, here] = d_pair2
        gate = sigmoid(dot_nn(R.w1t[512:, :], R.nb3[:, here]))
        update = dot_nn(R.wo1t[...], R.nb4[:, here])
        d_up = (d_pair2 * gate).astype(BF16)
        R.dup1[:, here] = d_up
        R.dtri1[512:, here] = (d_pair2 * update * gate * (1.0 - gate)).astype(BF16)
        d_nb4 = dot_nn(R.w_to[...], d_up)
        hat4, rstd4 = norm(lane_group(R.st2, j), 0)
        R.a_g4[...] += d_nb4 * hat4
        lane_ungroup(R.st3, j, norm_back(d_nb4, gain4, hat4, rstd4, 0))

    @pl.loop(0, 32, unroll=4)
    def _(d):
        R.ts[d] = R.st3[pl.ds(pl.multiple_of(64 * d, 64), 64), :].astype(BF16)


def p_between_grads(R, D):
    R.g_ii[...] = dot_nt(R.nb5[...], R.dtri2[...])
    R.g_to[...] = dot_nt(R.nb4[...], R.dup1[...])
    R.gg5[...] = jnp.sum(R.a_g5[...], 1, keepdims=True)
    R.gg4[...] = jnp.sum(R.a_g4[...], 1, keepdims=True)


def p_back1(R, D):
    tri_backward(
        R,
        D,
        R.dt1r,
        R.mats1,
        R.dlr1r,
        (lambda a, b, d: dot_nn(d, b), lambda a, b, d: dot_tn(d, a)),
        p_between_grads,
    )


def p_pair_end(R, D):
    stage_both(R.dlr1r, R.st0, R.st1)
    gain3 = column(R.g3[...])
    R.a_g3[...] = jnp.zeros((128, CHUNK), F32)
    inverse = 1.0 / count_of(R)

    @pl.loop(0, 8, unroll=4)
    def _(j):
        here = chunk_at(j)
        gates_back(R, R.dtri1, R.w1t, R.nb3[:, here], j)
        d_nb3 = dot_nn(R.w_ti[...], R.dtri1[:, here])
        hat3, rstd3 = norm(R.pair1[:, here], 0)
        R.a_g3[...] += d_nb3 * hat3
        d_pair1 = R.dpair[:, here] + norm_back(d_nb3, gain3, hat3, rstd3, 0)
        for q in range(2):
            m = 2 * j + q
            out = d_pair1[:, q * LANES : (q + 1) * LANES].T
            R.pair_grad[m] = out[:64]
            R.pair_grad[16 + m] = out[64:]
            small = (out * inverse).astype(BF16)
            R.dopm[m] = small[:64]
            R.dopm[16 + m] = small[64:]

    R.g_ti[...] = dot_nt(R.nb3[...], R.dtri1[...])
    R.gg3[...] = jnp.sum(R.a_g3[...], 1, keepdims=True)


def p_outer_back(R, D):
    R.rt[...] = R.rall[...].T.astype(BF16)
    R.dright[...] = jnp.zeros((64, 1024), F32)
    R.dleft[...] = jnp.zeros((32, 1024), F32)

    @pl.loop(0, 4)
    def _(k):
        grad = jnp.concatenate([R.dopm[8 * k + u] for u in range(8)], 1)
        R.dright[...] += dot_nt(grad, jnp.concatenate([R.zb[8 * k + u] for u in range(8)], 1))

    @pl.loop(0, 4)
    def _(g):
        right = R.rt[pl.ds(pl.multiple_of(256 * g, 256), 256), :]

        @pl.loop(0, 16, unroll=16)
        def _(k):
            grad = jnp.concatenate([R.dopm[2 * k], R.dopm[2 * k + 1]], 1)
            both = dot_nn(right, grad).astype(BF16)
            R.yg[:, 2 * k] = both[:, :LANES].reshape(8, 32, LANES)
            R.yg[:, 2 * k + 1] = both[:, LANES:].reshape(8, 32, LANES)

        weights = jnp.concatenate([outer_weight(R, 8 * g + u) for u in range(8)], 1)
        rows = jnp.concatenate([R.yg[u].reshape(1024, LANES) for u in range(8)], 1)
        R.dleft[...] += dot_nt(weights, rows)
        total = dot_nn(R.lt[...], rows)
        for u in range(8):
            R.st1[pl.ds(8 * g + u, 32, stride=32), :] = total[:, LANES * u : LANES * u + LANES]

    R.g_oo[...] = R.st1[0:1024, :]
    for q in range(4):
        R.dls[q] = R.dleft[:, 256 * q : 256 * q + 256].astype(BF16)


def p_outer_return(R, D):
    sems = D.take()
    column_res = D.s // 2
    owner = 2 * D.r + D.s // 4

    def left(q, slot):
        return pltpu.make_async_remote_copy(
            src_ref=R.dls.at[q],
            dst_ref=R.dlr.at[slot],
            send_sem=sems[0].at[q],
            recv_sem=sems[1].at[slot],
            device_id=(4 * (D.s % 2) + q, column_res),
            device_id_type=MESH,
        )

    for q in range(4):
        mine = (4 * (D.s % 2) + q == D.s) & (column_res == D.r)

        @pl.when(jnp.logical_not(mine))
        def _():
            left(q, D.r).start()

        @pl.when(mine)
        def _():
            R.dlr[D.r] = R.dls[q]

    def right(t):
        peer = seq_peers(D, t)
        at = pl.ds(pl.multiple_of(8 * peer[0], 8), 8)
        return remote(R.dright.at[at], R.drr.at[D.s], sems, 4 + t, peer)

    @pl.loop(1, 8)
    def _(t):
        right(t).start()

    R.drr[D.s] = R.dright[pl.ds(pl.multiple_of(8 * D.s, 8), 8), :]

    for q in range(4):
        mine = (4 * (D.s % 2) + q == D.s) & (column_res == D.r)
        theirs = (owner == D.s) & (D.r == q)

        @pl.when(jnp.logical_not(mine))
        def _():
            left(q, q).wait_send()

        @pl.when(jnp.logical_not(theirs))
        def _():
            left(q, q).wait_recv()

    @pl.loop(1, 8)
    def _(t):
        right(t).wait()


def p_attention_back(R, D):
    next(R.sum0)
    flag_rows = flag_column(R.fl[...].astype(F32))
    live = (flag_rows > 0).astype(F32)
    left = R.dlr[0].astype(F32)
    for k in range(1, 4):
        left += R.dlr[k].astype(F32)
    right = R.drr[0]
    for k in range(1, 8):
        right += R.drr[k]
    wide = jnp.concatenate([left, jnp.zeros((96, 256), F32)], 0).T
    spread = dot_nn(
        hot_bf16(iota((256, 8), 0) // 32 == iota((256, 8), 1)), right.astype(BF16)
    )
    kept = iota((256, 1024), 0) % 32 == iota((256, 1024), 1) % 32
    spread = jnp.where(kept, spread, 0.0).astype(BF16)
    back = hot_bf16(32 + iota((1024, LANES), 0) // 32 == iota((1024, LANES), 1))
    d_in = ((wide + dot_nn(spread, back)) * live).astype(BF16)[:, :64]
    hat2, rstd2 = norm(R.msan[...], -1)
    normed2 = (hat2 * R.g2[...]).astype(BF16)
    R.g_oi[...] = dot_tn(d_in, normed2)
    d_normed2 = dot_nn(d_in, R.w_oit[...])
    R.gg2[...] = jnp.sum(d_normed2 * hat2, 0, keepdims=True)
    d_later = R.ac[...] + norm_back(d_normed2, R.g2[...], hat2, rstd2, -1)
    R.dlater[...] = d_later
    d_exit = d_later.astype(BF16)
    gate = sigmoid(R.gl[...])
    gated = (gate * R.att[...]).astype(BF16)
    R.g_ao[...] = dot_tn(gated, d_exit)
    d_gated = dot_nt(d_exit, R.w_ao[...])
    R.datt[...] = (d_gated * gate).astype(BF16)
    R.dproj[:, 768:] = (d_gated * R.att[...] * gate * (1.0 - gate)).astype(BF16)
    R.dqkv[...] = jnp.zeros((256, 768), F32)

    @pl.loop(0, 8, unroll=4)
    def _(head):
        lanes = iota((1, 256), 1) // 32
        mine = lanes == head
        hot = hot_bf16(mine)
        query = R.qkv[:, 0:256]
        keys = R.qkv[:, 256:512]
        probs = head_probs(keys, query, flag_rows, head)
        d_att = R.datt[...]
        d_probs = dot_nt(R.qkv[:, 512:768], d_att * hot)
        total = jnp.sum(probs * d_probs, 0, keepdims=True)
        d_scores = (probs * (d_probs - total) * (32 ** (-0.5))).astype(BF16)
        R.dqkv[:, 0:256] += jnp.where(mine, dot_tn(d_scores, keys), 0.0)
        R.dqkv[:, 256:512] += jnp.where(mine, dot_nn(d_scores, query), 0.0)
        R.dqkv[:, 512:768] += jnp.where(mine, dot_nn(probs.astype(BF16), d_att), 0.0)

    R.dproj[:, :768] = R.dqkv[...].astype(BF16)
    hat, rstd = norm(R.xc[...], -1)
    normed = (hat * R.g1[...]).astype(BF16)
    R.g_qkvg[...] = dot_tn(normed, R.dproj[...])
    d_normed = dot_nt(R.dproj[...], R.w_qkvg[...])
    R.gg1[...] = jnp.sum(d_normed * hat, 0, keepdims=True)
    R.dlater[...] += norm_back(d_normed, R.g1[...], hat, rstd, -1)
    group_columns(R, R.dlater, R.gsend)


def group_columns(R, value, send):
    R.sp0[...] = value[:, :LANES]
    R.sp1[...] = value[:, LANES:]
    for d in range(8):
        for q in range(2):
            parts = []
            for k in range(2):
                rows = pl.ds(4 * d + 2 * q + k, 8, stride=32)
                parts.append(jnp.concatenate([R.sp0[rows, :], R.sp1[rows, :]], 1))
            send[d, q] = jnp.concatenate(parts, 0).astype(BF16)


def ungroup_columns(recv, target):
    for q in range(2):
        blocks = [recv[d, q].astype(F32) for d in range(8)]
        for k in range(2):
            rows = jnp.concatenate([block[8 * k : 8 * k + 8] for block in blocks], 0)
            target[2 * q + k] = rows.astype(target.dtype)


def p_send_value(R, D):
    group_columns(R, R.msan, R.osend)
    R.wait_value = start_columns(D, R.osend, R.orecv)


def p_take_value(R, D):
    R.wait_value()
    ungroup_columns(R.orecv, R.msa_out)
    R.wait_adjoint()
    unpack_columns(R, R.arecv, R.ac)


SEGMENTS = (
    dict(
        g_ti=(128, 640),
        g_ii=(128, 640),
        g_to=(128, 128),
        g_io=(128, 128),
        s_mean=(64, 256),
        s_own=(64, 256),
        s_other=(64, 256),
        s_vadj=(64, 256),
        s_xyz=(16, 256),
        g_ed=(64, 128),
        g_ms=(64, 64),
        small0=(16, 128),
    ),
    dict(g_oo=(1024, 128)),
    dict(g_qkvg=(256, 1024), g_ao=(256, 256), g_oi=(64, 256), small1=(16, 128)),
)


def segment_layout(index):
    layout = []
    start = 0
    for name, (rows, cols) in SEGMENTS[index].items():
        for lane in range(0, cols, LANES):
            layout.append((name, start, rows, lane, min(LANES, cols - lane)))
            start += rows
    return layout, -(-start // 512) * 512


def pack_segment(R, index):
    layout, total = segment_layout(index)
    pay = R.pay[index]
    for name, start, count, lane, width in layout:
        value = getattr(R, name)[:, lane : lane + width]
        pay[start : start + count, 0:width] = value.astype(BF16)
    end = layout[-1][1] + layout[-1][2]
    if end < total:
        pay[end:total, :] = jnp.zeros((total - end, LANES), BF16)


def rows_of(index, size):
    return pl.ds(pl.multiple_of(index * size, size), size)


def sum_segment(R, D, index):
    pay, full = R.pay[index], R.full[index]
    first, second, third, fourth = (table[index] for table in R.parts)
    eighth = pay.shape[0] // 8
    part = eighth // 4
    pack_segment(R, index)
    first[D.s] = pay[rows_of(D.s, eighth), :]
    wait = start_seq(D, lambda i: pay.at[rows_of(i, eighth)], lambda i: first.at[i])
    yield
    wait()
    total = first[0].astype(F32)
    for k in range(1, 8):
        total += first[k].astype(F32)
    second[...] = total.astype(BF16)
    third[D.r] = second[rows_of(D.r, part), :]
    wait = start_res(D, lambda i: second.at[rows_of(i, part)], lambda i: third.at[i])
    yield
    wait()
    total = third[0].astype(F32)
    for k in range(1, 4):
        total += third[k].astype(F32)
    fourth[...] = total.astype(BF16)
    mine = pl.ds(pl.multiple_of(D.s * eighth + D.r * part, part), part)
    full[mine, :] = fourth[...]
    wait = start_res(D, lambda i: fourth, lambda i: full.at[mine])
    yield
    wait()
    wait = start_seq(
        D, lambda i: full.at[rows_of(D.s, eighth)], lambda i: full.at[rows_of(i, eighth)]
    )
    yield
    wait()


def p_sum0(R, D):
    place = hot_bf16(iota((32, 256), 1) == 32 * D.s + iota((32, 256), 0))
    first = jnp.where(D.r == 0, 1.0, 0.0)
    R.s_vadj[...] = dot_tn(R.adj_v[...].astype(BF16), place) * first
    R.small[...] = jnp.zeros((128, LANES), F32)
    for k, value in enumerate((R.gg3, R.gg4, R.gg5, R.gg6, R.g_ds, R.g_sl)):
        R.small[0 : value.shape[0], k : k + 1] = value[...]
    R.small0[...] = R.small[...].T[:16]
    R.sum0 = sum_segment(R, D, 0)
    next(R.sum0)


def p_sum1(R, D):
    R.sum1 = sum_segment(R, D, 1)
    next(R.sum1)


def p_sum2(R, D):
    R.small1[...] = jnp.zeros((16, LANES), F32)
    for k, value in enumerate((R.gg1, R.gg2)):
        for half in range(2):
            at = 2 * k + half
            R.small1[at : at + 1, :] = value[:, LANES * half : LANES * half + LANES]
    R.sum2 = sum_segment(R, D, 2)
    next(R.sum2)


def p_sums(R, D):
    wait = start_columns(D, R.gsend, R.grecv)
    sums = [R.sum0, R.sum1, R.sum2]
    while sums:
        sums = [each for each in sums if next(each, D) is not D]
        if wait:
            wait()
            ungroup_columns(R.grecv, R.msa_grad)
            wait = None


def p_finish(R, D):
    held = {}
    for index in range(len(SEGMENTS)):
        for name, start, count, lane, width in segment_layout(index)[0]:
            value = R.full[index][start : start + count, 0:width].astype(F32)
            if name.startswith("g_"):
                getattr(R, "o_" + name)[:, lane : lane + width] = value
            else:
                held.setdefault(name, []).append(value)
    held = {name: jnp.concatenate(parts, 1) for name, parts in held.items()}
    small = held["small0"]
    for k, target in enumerate((R.o_gg3, R.o_gg4, R.o_gg5, R.o_gg6)):
        target[...] = small[k : k + 1, :]
    R.o_g_ds[...] = small[4:5, :64]
    R.o_g_sl[...] = small[5:6, :64]
    small = held["small1"]
    for k, target in enumerate((R.o_gg1, R.o_gg2)):
        for half in range(2):
            at = 2 * k + half
            target[:, LANES * half : LANES * half + LANES] = small[at : at + 1]
    mean_b = held["s_mean"].astype(BF16)
    R.o_g_up[...] = dot_nt(mean_b, held["s_vadj"].astype(BF16))
    d_node = jnp.concatenate([held["s_own"], held["s_other"]], 0).astype(BF16)
    R.o_g_nd[...] = dot_nt(R.vet[...].astype(BF16), d_node)
    step = dot_tn(R.w_up[...], mean_b)
    grad = dot_nn(R.w_nd[...], d_node)
    R.rows_f[...] = jnp.concatenate([step + R.vet[...], grad], 0).T
    here = pl.ds(pl.multiple_of(32 * D.s, 32), 32)
    mine = R.rows_f[here, :]
    R.single_out[...] = mine[:, :64]
    R.single_grad[...] = R.adj_v[...] + mine[:, 64:]
    R.xyz[...] = jnp.zeros((128, 256), F32)
    R.xyz[0:16, :] = held["s_xyz"]
    R.xyz[16:19, :] = R.at[...]
    R.rows_g[...] = R.xyz[...].T
    turned = R.rows_g[here, :]
    back = jnp.concatenate([turned, jnp.zeros((96, 128), F32)], 0).T
    R.coords_out[...] = back[16:19, 0:32] + back[0:3, 0:32]
    R.coords_grad[...] = R.adj_l[...] + back[8:11, 0:32]


KEPT = dict(
    xsend=((8, 2, 16, 256), BF16),
    xrecv=((8, 2, 16, 256), BF16),
    asend=((8, 2, 16, 256), BF16),
    arecv=((8, 2, 16, 256), BF16),
    osend=((8, 2, 16, 256), BF16),
    orecv=((8, 2, 16, 256), BF16),
    gsend=((8, 2, 16, 256), BF16),
    grecv=((8, 2, 16, 256), BF16),
    wst=((1024, 128), F32),
    lt=((32, 1024), BF16),
    yg=((8, 32, 32, 128), BF16),
    tm=((4, 256, 256), BF16),
    geo=((32, 2048), F32),
    pre=((128, 2048), F32),
    small0=((16, 128), F32),
    small1=((16, 128), F32),
    xc=((256, 256), F32),
    ac=((256, 256), F32),
    sp0=((256, 128), F32),
    sp1=((256, 128), F32),
    qkv=((256, 768), BF16),
    gl=((256, 256), F32),
    att=((256, 256), F32),
    msan=((256, 256), F32),
    lsend=((32, 256), BF16),
    rsend=((8, 1024), F32),
    lall=((4, 32, 256), BF16),
    rall=((64, 1024), F32),
    st0=((2048, 128), F32),
    st1=((2048, 128), F32),
    st2=((2048, 128), F32),
    st3=((2048, 128), F32),
    l2=((1024, 32), BF16),
    zb=((32, 1024, 128), BF16),
    pair1=((128, 2048), F32),
    pair2=((128, 2048), F32),
    dpair=((128, 2048), F32),
    w1t=((640, 128), BF16),
    w2t=((640, 128), BF16),
    wo1t=((128, 128), BF16),
    wo2t=((128, 128), BF16),
    nb3=((128, 2048), BF16),
    nb4=((128, 2048), BF16),
    nb5=((128, 2048), BF16),
    nb6=((128, 2048), BF16),
    po=((128, 2048), BF16),
    hid=((64, 2048), BF16),
    dmsg=((64, 2048), BF16),
    dedge=((64, 2048), BF16),
    dup1=((128, 2048), BF16),
    dup2=((128, 2048), BF16),
    dtri1=((640, 2048), BF16),
    dtri2=((640, 2048), BF16),
    mats1=((8, 256, 256), BF16),
    mats2=((8, 256, 256), BF16),
    dm=((4, 256, 256), BF16),
    lrs=((32, 128, 128), BF16),
    lr1r=((32, 128, 128), BF16),
    lr2r=((32, 128, 128), BF16),
    dlr1r=((32, 128, 128), BF16),
    dlr2r=((32, 128, 128), BF16),
    ts=((32, 64, 128), BF16),
    t1r=((32, 64, 128), BF16),
    t2r=((32, 64, 128), BF16),
    dt1r=((32, 64, 128), BF16),
    dt2r=((32, 64, 128), BF16),
    at8=((8, 256), F32),
    la8=((8, 32), F32),
    nodet=((128, 256), F32),
    dmean=((64, 32), F32),
    nbase=((64, 256), F32),
    cbase=((8, 256), F32),
    nb_f=((32, 64), F32),
    s_mean=((64, 256), F32),
    s_own=((64, 256), F32),
    s_other=((64, 256), F32),
    s_vadj=((64, 256), F32),
    s_xyz=((16, 256), F32),
    a_g3=((128, 256), F32),
    a_g4=((128, 256), F32),
    a_g5=((128, 256), F32),
    a_g6=((128, 256), F32),
    gg3=((128, 1), F32),
    gg4=((128, 1), F32),
    gg5=((128, 1), F32),
    gg6=((128, 1), F32),
    gg1=((1, 256), F32),
    gg2=((1, 256), F32),
    g_ds=((64, 1), F32),
    g_sl=((64, 1), F32),
    g_io=((128, 128), F32),
    g_to=((128, 128), F32),
    g_ti=((128, 640), F32),
    g_ii=((128, 640), F32),
    g_ed=((64, 128), F32),
    g_ms=((64, 64), F32),
    g_oo=((1024, 128), F32),
    g_oi=((64, 256), F32),
    g_ao=((256, 256), F32),
    g_qkvg=((256, 1024), F32),
    small=((128, 128), F32),
    dopm=((32, 64, 128), BF16),
    rt=((1024, 64), BF16),
    dright=((64, 1024), F32),
    dleft=((32, 1024), F32),
    dls=((4, 32, 256), BF16),
    dlr=((4, 32, 256), BF16),
    drr=((8, 8, 1024), F32),
    dlater=((256, 256), F32),
    datt=((256, 256), BF16),
    dproj=((256, 1024), BF16),
    dqkv=((256, 768), F32),
)
SIZES = [segment_layout(index)[1] for index in range(len(SEGMENTS))]
PAYLOADS = [((size, 128), BF16) for size in SIZES]
PARTIAL = (
    [((8, size // 8, 128), BF16) for size in SIZES]
    + [((size // 8, 128), BF16) for size in SIZES]
    + [((4, size // 32, 128), BF16) for size in SIZES]
    + [((size // 32, 128), BF16) for size in SIZES]
)
LARGE = ("msa_out", "pair_out", "msa_grad", "pair_grad")
FINISH = ("vet", "w_up", "w_nd", "adj_v", "at", "adj_l")
FINISH_KEPT = dict(
    rows_f=((256, 128), F32), rows_g=((256, 128), F32), xyz=((128, 256), F32)
)
RESULTS = dict(
    msa_out=((4, 64, 256), BF16),
    pair_out=((32, 64, 128), BF16),
    single_out=((32, 64), F32),
    coords_out=((3, 32), F32),
    msa_grad=((4, 64, 256), F32),
    pair_grad=((32, 64, 128), F32),
    single_grad=((32, 64), F32),
    coords_grad=((3, 32), F32),
    o_gg1=((1, 256), F32),
    o_g_qkvg=((256, 1024), F32),
    o_g_ao=((256, 256), F32),
    o_gg2=((1, 256), F32),
    o_g_oi=((64, 256), F32),
    o_g_oo=((1024, 128), F32),
    o_gg3=((1, 128), F32),
    o_g_ti=((128, 640), F32),
    o_gg4=((1, 128), F32),
    o_g_to=((128, 128), F32),
    o_gg5=((1, 128), F32),
    o_g_ii=((128, 640), F32),
    o_gg6=((1, 128), F32),
    o_g_io=((128, 128), F32),
    o_g_nd=((64, 128), F32),
    o_g_ed=((64, 128), F32),
    o_g_ds=((1, 64), F32),
    o_g_ms=((64, 64), F32),
    o_g_sl=((1, 64), F32),
    o_g_up=((64, 64), F32),
)

STEPS = (
    p_spread,
    p_attention,
    p_outer_exchange,
    p_send_value,
    p_outer,
    p_take_value,
    p_entry1,
    p_tri1,
    p_middle,
    p_tri2,
    p_turn,
    p_back2,
    p_between,
    p_back1,
    p_pair_end,
    p_sum0,
    p_outer_back,
    p_sum1,
    p_outer_return,
    p_attention_back,
    p_sum2,
    p_sums,
)
EXCHANGES = 35
PARTS = 2


class Device:
    def __init__(self, n_seq, n_res, sems):
        self.s, self.r = lax.axis_index("seq"), lax.axis_index("res")
        self.ns, self.nr = n_seq, n_res
        self.sems = list(sems)

    def take(self):
        return self.sems.pop(0), self.sems.pop(0)

    def ready(self):
        pl.semaphore_wait(pltpu.get_barrier_semaphore(), self.ns * self.nr - 1)


def first_kernel(n_seq, n_res, names, *refs):
    refs = list(refs)
    R = SimpleNamespace(**{name: refs.pop(0) for name in names})
    R.full = [refs.pop(0) for _ in SIZES]
    R.__dict__.update({name: refs.pop(0) for name in KEPT})
    tables = [[refs.pop(0) for _ in SIZES] for _ in range(5)]
    R.pay, R.parts = tables[0], tables[1:]
    D = Device(n_seq, n_res, refs)
    barrier = pltpu.get_barrier_semaphore()

    @pl.loop(1, n_seq * n_res)
    def _(t):
        pl.semaphore_signal(barrier, inc=1, device_id=all_peers(D, t), device_id_type=MESH)

    for step in STEPS:
        step(R, D)


def last_kernel(n_seq, n_res, names, *refs):
    refs = list(refs)
    full = [refs.pop(0) for _ in SIZES]
    R = SimpleNamespace(full=full, **dict(zip(names, refs)))
    p_finish(R, Device(n_seq, n_res, ()))


ARGS = dict(
    x=(4, 64, 256),
    pe=(32, 64, 128),
    vet=(256, 64),
    at=(3, 256),
    fl=(32,),
    ca=(32, 64),
    g1=(256,),
    w_qkvg=(256, 1024),
    w_ao=(256, 256),
    g2=(256,),
    w_oit=(256, 64),
    w_oo=(1024, 128),
    g3=(128,),
    w_ti=(128, 640),
    g4=(128,),
    w_to=(128, 128),
    g5=(128,),
    w_ii=(128, 640),
    g6=(128,),
    w_io=(128, 128),
    w_nd=(64, 128),
    w_edt=(128, 64),
    w_ds=(64,),
    w_ms=(64, 64),
    w_sl=(64,),
    w_up=(64, 64),
    adj_a=(4, 64, 256),
    adj_c=(32, 64, 128),
    adj_v=(32, 64),
    adj_l=(3, 32),
)


def fits(n_seq, n_res, args):
    shapes = tuple(tuple(arg.shape) for arg in args)
    return (n_seq, n_res) == (8, 4) and shapes == tuple(ARGS.values())


def fast_shards(n_seq, n_res, *args):
    env = dict(zip(ARGS, args))
    for name, value in tuple(env.items()):
        if value.ndim == 1:
            env[name] = value.reshape(1, -1)
    env.update(vet=env["vet"].T, w_oit=env["w_oit"].T, w_edt=env["w_edt"].T)
    space = pl.BlockSpec(memory_space=pltpu.VMEM)
    slots = n_seq * n_res

    def shapes(entries):
        return [jax.ShapeDtypeStruct(*entry) for entry in entries]

    large = {name: RESULTS[name] for name in LARGE}
    values = pl.pallas_call(
        functools.partial(first_kernel, n_seq, n_res, (*env, *large)),
        out_shape=shapes((*large.values(), *PAYLOADS)),
        in_specs=[space] * len(env),
        out_specs=[space] * (len(large) + len(PAYLOADS)),
        scratch_shapes=[pltpu.VMEM(*entry) for entry in (*KEPT.values(), *PAYLOADS, *PARTIAL)]
        + [pltpu.SemaphoreType.DMA((slots,))] * (2 * EXCHANGES),
        compiler_params=pltpu.CompilerParams(
            vmem_limit_bytes=62 * 2**20, collective_id=0, has_side_effects=True
        ),
    )(*env.values())
    full = values[len(large) :]
    env.update(zip(large, values))
    small = {name: entry for name, entry in RESULTS.items() if name not in large}
    values = pl.pallas_call(
        functools.partial(last_kernel, n_seq, n_res, (*FINISH, *small, *FINISH_KEPT)),
        out_shape=shapes(small.values()),
        in_specs=[space] * (len(full) + len(FINISH)),
        out_specs=[space] * len(small),
        scratch_shapes=[pltpu.VMEM(*entry) for entry in FINISH_KEPT.values()],
        compiler_params=pltpu.CompilerParams(vmem_limit_bytes=60 * 2**20),
    )(*full, *[env[name] for name in FINISH])
    env.update(zip(small, values))
    results = [env[name] for name in RESULTS]
    for index, value in enumerate(results):
        if value.shape[0] == 1:
            results[index] = value.reshape(-1)
    for index in (12, 23):
        results[index] = results[index].T
    return tuple(results)


def solution(mesh):
    n_seq, n_res = mesh.shape["seq"], mesh.shape["res"]

    def body(*args):
        if fits(n_seq, n_res, args):
            return fast_shards(n_seq, n_res, *args)
        return shards(*args)

    return jax.shard_map(
        body,
        mesh=mesh,
        in_specs=(
            P("seq", "res", None),
            P("seq", "res", None),
            P(),
            P(),
            P(),
            P("seq", None),
            P(),
            P(),
            P(),
            P(),
            P(),
            P(),
            P(),
            P(),
            P(),
            P(),
            P(),
            P(),
            P(),
            P(),
            P(),
            P(),
            P(),
            P(),
            P(),
            P(),
            P("seq", "res", None),
            P("seq", "res", None),
            P("seq", None),
            P(None, "seq"),
        ),
        out_specs=(
            P("seq", "res", None),
            P("seq", "res", None),
            P("seq", None),
            P(None, "seq"),
            P("seq", "res", None),
            P("seq", "res", None),
            P("seq", None),
            P(None, "seq"),
            P(),
            P(),
            P(),
            P(),
            P(),
            P(),
            P(),
            P(),
            P(),
            P(),
            P(),
            P(),
            P(),
            P(),
            P(),
            P(),
            P(),
            P(),
            P(),
            P(),
        ),
        check_vma=False,
    )
```

```python
import functools
from types import SimpleNamespace

import jax
import jax.numpy as jnp
from jax import lax
from jax.experimental import pallas as pl
from jax.experimental.pallas import tpu as pltpu
from jax.sharding import PartitionSpec as P

HEADS = 8


EPS = 1e-05
HIGH = lax.Precision.HIGHEST


def spread_2(value, axis, source):
    kept = jnp.where(lax.axis_index(axis) == source, value, 0).astype(value.dtype)
    return lax.psum(kept, axis)


def standardize_lines(value, gain):
    row_mean = jnp.mean(value, -1, keepdims=True)
    centred = value - row_mean
    spread = jnp.mean(centred * centred, -1, keepdims=True)
    return centred * lax.rsqrt(spread + EPS) * gain


def tensor_mean_answer(left, right):
    return jnp.einsum("...c,cd->...d", left, right, preferred_element_type=jnp.float32)


def product_back(grad, right):
    return jnp.einsum("...d,cd->...c", grad, right, preferred_element_type=jnp.float32)


def weight_back(left, grad):
    flat_left = left.reshape(-1, left.shape[-1])
    flat_grad = grad.reshape(-1, grad.shape[-1])
    return jnp.einsum("nc,nd->cd", flat_left, flat_grad, preferred_element_type=jnp.float32)


def attn_scores(query, keys, allowed, scale):
    raw_scores = (
        jnp.einsum("qlhd,klhd->lhqk", query, keys, preferred_element_type=jnp.float32) * scale
    )
    return jnp.where(allowed, raw_scores, -1e30)


def tri_gates(tri_lin):
    quarter = tri_lin.shape[-1] // 4
    left_part = jax.nn.sigmoid(tri_lin[..., quarter : 2 * quarter]) * tri_lin[..., :quarter]
    right_part = (
        jax.nn.sigmoid(tri_lin[..., 3 * quarter :]) * tri_lin[..., 2 * quarter : 3 * quarter]
    )
    return (left_part, right_part)


def edge_front(own_rows, other_near, edge_lin, diff, distance_basis_matrix):
    radial = jnp.log(1.0 + jnp.sum(diff * diff, 0))
    return jax.nn.silu(
        own_rows[:, None, :] + other_near + edge_lin + radial[..., None] * distance_basis_matrix
    )


def edge_finish(msg_lin, signal_location_matrix, diff):
    message = jax.nn.silu(msg_lin)
    turn = jnp.tanh(jnp.einsum("ikc,c->ik", message, signal_location_matrix, precision=HIGH))
    return (jnp.mean(message, 1), jnp.mean(diff * turn[None], 2))


def gather_rows(value):
    return lax.all_gather(value, "seq", axis=0, tiled=True)


def across_res(value):
    return lax.psum(value.astype(jnp.bfloat16), "res").astype(jnp.float32)


def owners_sum(value):
    return lax.psum_scatter(value, "seq", scatter_dimension=0, tiled=True)


def place_home(rows_part, col_width, offset, keep_home):
    empty = jnp.zeros((rows_part.shape[0], col_width, rows_part.shape[2]), jnp.float32)
    return lax.dynamic_update_slice_in_dim(empty, rows_part, offset, 1) * keep_home


def sum_flat(parts):
    flat = jnp.concatenate([jnp.ravel(member) for member in parts])
    summed = lax.psum(flat, ("seq", "res"))
    pieces = []
    offset = 0
    for member in parts:
        pieces.append(summed[offset : offset + member.size].reshape(member.shape))
        offset = offset + member.size
    return pieces


def shards(
    alignment_embedding,
    coupling_embedding,
    vertex_embedding,
    atom_locations,
    chain_existence_flags,
    closest_aminos,
    softmax_mixer_scale_factor,
    attender_stacked_matrix,
    softmax_mixer_exit_matrix,
    tensor_mean_scale_factor,
    tensor_mean_entry_matrix,
    tensor_mean_exit_matrix,
    outbound_entry_scale,
    outbound_entry_matrix,
    outbound_exit_scale,
    outbound_exit_matrix,
    inbound_entry_scale,
    inbound_entry_matrix,
    inbound_exit_scale,
    inbound_exit_matrix,
    vertex_mapping_matrix,
    bond_mapping_matrix,
    distance_basis_matrix,
    signal_matrix,
    signal_location_matrix,
    vertex_change_matrix,
    alignment_adjoint,
    coupling_adjoint,
    vertex_adjoint,
    location_adjoint,
):
    seq_index = lax.axis_index("seq")
    res_index = lax.axis_index("res")
    n_seq = lax.axis_size("seq")
    n_res = lax.axis_size("res")
    chain_shard_piece, vertical_shard_piece, breadth_overall = alignment_embedding.shape
    rows_dev = coupling_embedding.shape[0]
    span_overall, node_width = vertex_embedding.shape
    block_tally = chain_existence_flags.shape[0]
    head_size = breadth_overall // HEADS
    scale = head_size ** (-0.5)
    opm_width = tensor_mean_entry_matrix.shape[1] // 2
    tri_width = outbound_exit_matrix.shape[0]
    chain_exists = (chain_existence_flags > 0).astype(jnp.float32)
    line_indicator_entries = lax.dynamic_slice_in_dim(
        chain_exists, seq_index * chain_shard_piece, chain_shard_piece
    )
    first_res = (res_index == 0).astype(jnp.float32)
    home = seq_index * rows_dev // vertical_shard_piece
    offset = seq_index * rows_dev - home * vertical_shard_piece
    keep_home = (home == res_index).astype(jnp.float32)
    alignment_real_lines = alignment_embedding.astype(jnp.float32)
    standardized_lines, standardize_reverse_alpha = jax.vjp(
        standardize_lines, alignment_real_lines, softmax_mixer_scale_factor
    )
    normed_b = standardized_lines.astype(jnp.bfloat16)
    projected = tensor_mean_answer(normed_b, attender_stacked_matrix)
    query = projected[..., :breadth_overall].astype(jnp.bfloat16)
    keyval = projected[..., breadth_overall : 3 * breadth_overall].astype(jnp.bfloat16)
    attn_gate = jax.nn.sigmoid(projected[..., 3 * breadth_overall :])
    all_keyval = lax.all_gather(keyval, "seq", axis=0, tiled=True)
    query4 = query.reshape(chain_shard_piece, vertical_shard_piece, HEADS, head_size)
    keys4 = all_keyval[..., :breadth_overall].reshape(
        block_tally, vertical_shard_piece, HEADS, head_size
    )
    values4 = all_keyval[..., breadth_overall:].reshape(
        block_tally, vertical_shard_piece, HEADS, head_size
    )
    allowed = chain_exists[None, None, None, :] > 0
    scores = attn_scores(query4, keys4, allowed, scale)
    score_peak = jnp.max(scores, -1, keepdims=True)
    exp_scores = jnp.exp(scores - score_peak)
    exp_total = jnp.sum(exp_scores, -1, keepdims=True)
    log_total = score_peak + jnp.log(exp_total)
    probs_b = (exp_scores / exp_total).astype(jnp.bfloat16)
    attended = jnp.einsum(
        "lhqk,klhd->qlhd", probs_b, values4, preferred_element_type=jnp.float32
    ).reshape(chain_shard_piece, vertical_shard_piece, breadth_overall)
    sigmoid_scaled_lines = (attn_gate * attended).astype(jnp.bfloat16)
    alignment_later = alignment_real_lines + tensor_mean_answer(
        sigmoid_scaled_lines, softmax_mixer_exit_matrix
    )
    standardized_lines2, standardize_reverse_beta = jax.vjp(
        standardize_lines, alignment_later, tensor_mean_scale_factor
    )
    normed2_b = standardized_lines2.astype(jnp.bfloat16)
    outer_in = (
        tensor_mean_answer(normed2_b, tensor_mean_entry_matrix)
        * line_indicator_entries[:, None, None]
    ).astype(jnp.bfloat16)
    everyone = lax.all_gather(outer_in, ("seq", "res"), axis=0, tiled=True)
    blocks = everyone.reshape(n_seq, n_res, chain_shard_piece, vertical_shard_piece, 2 * opm_width)
    home_block = lax.dynamic_index_in_dim(blocks, home, 1, keepdims=False)
    left_rows = lax.dynamic_slice_in_dim(home_block, offset, rows_dev, 2)[..., :opm_width]
    left_rows = left_rows.reshape(block_tally, rows_dev, opm_width)
    right_cols = lax.dynamic_index_in_dim(blocks, res_index, 1, keepdims=False)[..., opm_width:]
    right_cols = right_cols.reshape(block_tally, vertical_shard_piece, opm_width)
    outer_b = jnp.einsum("sic,sjd->ijcd", left_rows, right_cols, preferred_element_type=jnp.float32)
    outer_b = outer_b.reshape(rows_dev, vertical_shard_piece, opm_width * opm_width).astype(
        jnp.bfloat16
    )
    count = jnp.sum(chain_exists)
    pair1 = (
        coupling_embedding.astype(jnp.float32)
        + tensor_mean_answer(outer_b, tensor_mean_exit_matrix) / count
    )
    normed3, norm_back3 = jax.vjp(standardize_lines, pair1, outbound_entry_scale)
    normed3_b = normed3.astype(jnp.bfloat16)
    tri = tensor_mean_answer(normed3_b, outbound_entry_matrix)
    (left_t, right_t), gates_back = jax.vjp(tri_gates, tri[..., : 4 * tri_width])
    left_b = left_t.astype(jnp.bfloat16)
    right_b = right_t.astype(jnp.bfloat16)
    right_all = gather_rows(right_b)
    partial_tri = jnp.einsum("ikc,jkc->ijc", left_b, right_all, preferred_element_type=jnp.float32)
    triangle = lax.psum_scatter(
        partial_tri.astype(jnp.bfloat16), "res", scatter_dimension=1, tiled=True
    ).astype(jnp.float32)
    normed4, norm_back4 = jax.vjp(standardize_lines, triangle, outbound_exit_scale)
    normed4_b = normed4.astype(jnp.bfloat16)
    update = tensor_mean_answer(normed4_b, outbound_exit_matrix)
    out_gate = jax.nn.sigmoid(tri[..., 4 * tri_width :])
    pair2 = pair1 + out_gate * update
    normed5, norm_back5 = jax.vjp(standardize_lines, pair2, inbound_entry_scale)
    normed5_b = normed5.astype(jnp.bfloat16)
    tri2 = tensor_mean_answer(normed5_b, inbound_entry_matrix)
    (left_i, right_i), gates_back2 = jax.vjp(tri_gates, tri2[..., : 4 * tri_width])
    both_local = jnp.concatenate([left_i.astype(jnp.bfloat16), right_i.astype(jnp.bfloat16)], -1)
    both_all = gather_rows(both_local)
    right_all2 = both_all[..., tri_width:]
    left_cand = lax.dynamic_slice_in_dim(both_all[..., :tri_width], offset, rows_dev, 1)
    left_sel = spread_2(left_cand, "res", home)
    triangle2 = jnp.einsum("kic,kjc->ijc", left_sel, right_all2, preferred_element_type=jnp.float32)
    normed6, norm_back6 = jax.vjp(standardize_lines, triangle2, inbound_exit_scale)
    normed6_b = normed6.astype(jnp.bfloat16)
    update2 = tensor_mean_answer(normed6_b, inbound_exit_matrix)
    out_gate2 = jax.nn.sigmoid(tri2[..., 4 * tri_width :])
    coupling_later3 = pair2 + out_gate2 * update2
    pair3_b = coupling_later3.astype(jnp.bfloat16)
    rows_all = lax.all_gather(pair3_b, "res", axis=1, tiled=True)
    nbr_hot = closest_aminos[:, :, None] == jnp.arange(span_overall, dtype=jnp.int32)[None, None, :]
    hot_float = nbr_hot.astype(jnp.float32)
    edges_b = jnp.einsum(
        "ikl,ilc->ikc", nbr_hot.astype(jnp.bfloat16), rows_all, preferred_element_type=jnp.float32
    ).astype(jnp.bfloat16)
    single_b = vertex_embedding.astype(jnp.bfloat16)
    node_proj = tensor_mean_answer(single_b, vertex_mapping_matrix)
    own_rows = lax.dynamic_slice_in_dim(node_proj[:, :node_width], seq_index * rows_dev, rows_dev)
    other_near = jnp.einsum("ikl,lc->ikc", hot_float, node_proj[:, node_width:], precision=HIGH)
    coords_own = lax.dynamic_slice_in_dim(atom_locations, seq_index * rows_dev, rows_dev, 1)
    coords_near = jnp.einsum("ikl,xl->xik", hot_float, atom_locations, precision=HIGH)
    diff = coords_own[:, :, None] - coords_near
    edge_lin = tensor_mean_answer(edges_b, bond_mapping_matrix)
    hidden, front_back = jax.vjp(
        edge_front, own_rows, other_near, edge_lin, diff, distance_basis_matrix
    )
    hidden_b = hidden.astype(jnp.bfloat16)
    msg_lin = tensor_mean_answer(hidden_b, signal_matrix)
    (mean_msg, shift), finish_back = jax.vjp(edge_finish, msg_lin, signal_location_matrix, diff)
    mean_b = mean_msg.astype(jnp.bfloat16)
    single_rows = lax.dynamic_slice_in_dim(vertex_embedding, seq_index * rows_dev, rows_dev)
    single_out = single_rows + tensor_mean_answer(mean_b, vertex_change_matrix)
    coords_out = coords_own + shift
    d_update_b = vertex_adjoint.astype(jnp.bfloat16)
    g_update = weight_back(mean_b, d_update_b)
    d_mean = product_back(d_update_b, vertex_change_matrix)
    d_msg_lin, g_coord, d_diff_finish = finish_back((d_mean, location_adjoint))
    d_msg_b = d_msg_lin.astype(jnp.bfloat16)
    g_msg = weight_back(hidden_b, d_msg_b)
    d_hidden = product_back(d_msg_b, signal_matrix)
    d_own, d_other_near, d_edge_lin, d_diff_front, g_dist = front_back(d_hidden)
    d_edge_b = d_edge_lin.astype(jnp.bfloat16)
    g_edge = weight_back(edges_b, d_edge_b)
    d_edges = product_back(d_edge_b, bond_mapping_matrix)
    d_rows = jnp.einsum("ikl,ikc->ilc", hot_float, d_edges, precision=HIGH)
    d_pair3 = coupling_adjoint.astype(jnp.float32) + lax.dynamic_slice_in_dim(
        d_rows, res_index * vertical_shard_piece, vertical_shard_piece, 1
    )
    d_diff = d_diff_front + d_diff_finish
    d_coords_own = jnp.sum(d_diff, 2)
    d_coords_near = jnp.einsum("ikl,xik->xl", hot_float, -d_diff, precision=HIGH)
    d_other_all = jnp.einsum("ikl,ikc->lc", hot_float, d_other_near, precision=HIGH)
    d_other_rows, d_near_rows = (
        lax.psum_scatter(d_other_all, "seq", scatter_dimension=0, tiled=True),
        lax.psum_scatter(d_coords_near, "seq", scatter_dimension=1, tiled=True),
    )
    d_node_b = jnp.concatenate([d_own, d_other_rows], -1).astype(jnp.bfloat16)
    g_node = weight_back(
        lax.dynamic_slice_in_dim(single_b, seq_index * rows_dev, rows_dev), d_node_b
    )
    single_grad = vertex_adjoint + product_back(d_node_b, vertex_mapping_matrix)
    coords_grad = location_adjoint + d_coords_own + d_near_rows
    layer_two = [
        g_node * first_res,
        g_edge * first_res,
        g_dist * first_res,
        g_msg * first_res,
        g_coord * first_res,
        g_update * first_res,
    ]
    d_inc_b = (d_pair3 * out_gate2).astype(jnp.bfloat16)
    d_gate_out2 = d_pair3 * update2 * out_gate2 * (1.0 - out_gate2)
    g_inc_out = weight_back(normed6_b, d_inc_b)
    d_normed6 = product_back(d_inc_b, inbound_exit_matrix)
    d_triangle2, g_inc_out_gain = norm_back6(d_normed6)
    d_tri2_b = d_triangle2.astype(jnp.bfloat16)
    d_left_sel = jnp.einsum(
        "ijc,kjc->kic", d_tri2_b, right_all2, preferred_element_type=jnp.float32
    )
    d_right_all2 = jnp.einsum(
        "ijc,kic->kjc", d_tri2_b, left_sel, preferred_element_type=jnp.float32
    )
    d_left_total = across_res(d_left_sel)
    d_both2 = owners_sum(
        jnp.concatenate(
            [place_home(d_left_total, vertical_shard_piece, offset, keep_home), d_right_all2], -1
        )
    )
    (d_gates2,) = gates_back2((d_both2[..., :tri_width], d_both2[..., tri_width:]))
    d_tri2_in_b = jnp.concatenate([d_gates2, d_gate_out2], -1).astype(jnp.bfloat16)
    g_inc_in = weight_back(normed5_b, d_tri2_in_b)
    d_normed5 = product_back(d_tri2_in_b, inbound_entry_matrix)
    d_pair2_norm, g_inc_gain = norm_back5(d_normed5)
    d_pair2 = d_pair3 + d_pair2_norm
    d_tri_out_b = (d_pair2 * out_gate).astype(jnp.bfloat16)
    d_gate_out = d_pair2 * update * out_gate * (1.0 - out_gate)
    g_tri_out = weight_back(normed4_b, d_tri_out_b)
    d_normed4 = product_back(d_tri_out_b, outbound_exit_matrix)
    d_triangle, g_tri_out_gain = norm_back4(d_normed4)
    d_triangle_b = d_triangle.astype(jnp.bfloat16)
    d_tri_all = lax.all_gather(d_triangle_b, "res", axis=1, tiled=True)
    d_left = jnp.einsum("ijc,jkc->ikc", d_tri_all, right_all, preferred_element_type=jnp.float32)
    d_right_part = jnp.einsum("ijc,ikc->jkc", d_tri_all, left_b, preferred_element_type=jnp.float32)
    d_right = owners_sum(d_right_part)
    (d_gates_in,) = gates_back((d_left, d_right))
    d_tri_b = jnp.concatenate([d_gates_in, d_gate_out], -1).astype(jnp.bfloat16)
    g_tri_in = weight_back(normed3_b, d_tri_b)
    d_normed3 = product_back(d_tri_b, outbound_entry_matrix)
    d_pair1_norm, g_tri_gain = norm_back3(d_normed3)
    pair_grad = d_pair2 + d_pair1_norm
    d_opm_b = (pair_grad / count).astype(jnp.bfloat16)
    g_opm_out = weight_back(outer_b, d_opm_b)
    d_outer = product_back(d_opm_b, tensor_mean_exit_matrix).astype(jnp.bfloat16)
    d_outer = d_outer.reshape(rows_dev, vertical_shard_piece, opm_width, opm_width)
    d_left_rows = jnp.einsum(
        "ijcd,sjd->sic", d_outer, right_cols, preferred_element_type=jnp.float32
    )
    d_right_cols = jnp.einsum(
        "ijcd,sic->sjd", d_outer, left_rows, preferred_element_type=jnp.float32
    )
    d_left_sum = across_res(d_left_rows)
    d_outer_in = owners_sum(
        jnp.concatenate(
            [place_home(d_left_sum, vertical_shard_piece, offset, keep_home), d_right_cols], -1
        )
    )
    d_outer_in_b = (d_outer_in * line_indicator_entries[:, None, None]).astype(jnp.bfloat16)
    g_opm_in = weight_back(normed2_b, d_outer_in_b)
    standardized_sens2 = product_back(d_outer_in_b, tensor_mean_entry_matrix)
    alignment_standard_sens, tensor_mean_scale_sens = standardize_reverse_beta(standardized_sens2)
    alignment_later_sens = alignment_adjoint.astype(jnp.float32) + alignment_standard_sens
    softmax_mixer_sens_lines = alignment_later_sens.astype(jnp.bfloat16)
    g_attn_out = weight_back(sigmoid_scaled_lines, softmax_mixer_sens_lines)
    d_gated = product_back(softmax_mixer_sens_lines, softmax_mixer_exit_matrix)
    d_attended_b = (d_gated * attn_gate).astype(jnp.bfloat16)
    d_gate_lin = d_gated * attended * attn_gate * (1.0 - attn_gate)
    probs_full = jnp.exp(attn_scores(query4, keys4, allowed, scale) - log_total)
    d_attended4 = d_attended_b.reshape(chain_shard_piece, vertical_shard_piece, HEADS, head_size)
    d_probs = jnp.einsum(
        "qlhd,klhd->lhqk", d_attended4, values4, preferred_element_type=jnp.float32
    )
    softmax_total = jnp.sum(probs_full * d_probs, -1, keepdims=True)
    d_scores_b = (probs_full * (d_probs - softmax_total) * scale).astype(jnp.bfloat16)
    d_query = jnp.einsum(
        "lhqk,klhd->qlhd", d_scores_b, keys4, preferred_element_type=jnp.float32
    ).reshape(chain_shard_piece, vertical_shard_piece, breadth_overall)
    d_keys = jnp.einsum("lhqk,qlhd->klhd", d_scores_b, query4, preferred_element_type=jnp.float32)
    d_values = jnp.einsum(
        "lhqk,qlhd->klhd",
        probs_full.astype(jnp.bfloat16),
        d_attended4,
        preferred_element_type=jnp.float32,
    )
    d_keyval = jnp.concatenate(
        [
            d_keys.reshape(block_tally, vertical_shard_piece, breadth_overall),
            d_values.reshape(block_tally, vertical_shard_piece, breadth_overall),
        ],
        -1,
    )
    d_keyval_own = lax.psum_scatter(d_keyval, "seq", scatter_dimension=0, tiled=True)
    d_proj_b = jnp.concatenate([d_query, d_keyval_own, d_gate_lin], -1).astype(jnp.bfloat16)
    g_qkvg = weight_back(normed_b, d_proj_b)
    standardized_sens = product_back(d_proj_b, attender_stacked_matrix)
    alignment_early_sens, alignment_scale_sens = standardize_reverse_alpha(standardized_sens)
    alignment_sensitivity = alignment_later_sens + alignment_early_sens
    layer_one = [
        alignment_scale_sens,
        g_qkvg,
        g_attn_out,
        tensor_mean_scale_sens,
        g_opm_in,
        g_opm_out,
        g_tri_gain,
        g_tri_in,
        g_tri_out_gain,
        g_tri_out,
        g_inc_gain,
        g_inc_in,
        g_inc_out_gain,
        g_inc_out,
    ]
    summed_all = sum_flat(layer_one + layer_two)
    layer_one = summed_all[:14]
    layer_two = summed_all[14:]
    return (
        alignment_later.astype(jnp.bfloat16),
        pair3_b,
        single_out,
        coords_out,
        alignment_sensitivity,
        pair_grad,
        single_grad,
        coords_grad,
        layer_one[0],
        layer_one[1],
        layer_one[2],
        layer_one[3],
        layer_one[4],
        layer_one[5],
        layer_one[6],
        layer_one[7],
        layer_one[8],
        layer_one[9],
        layer_one[10],
        layer_one[11],
        layer_one[12],
        layer_one[13],
        layer_two[0],
        layer_two[1],
        layer_two[2],
        layer_two[3],
        layer_two[4],
        layer_two[5],
    )


F32 = jnp.float32
BF16 = jnp.bfloat16
MESH = pl.DeviceIdType.MESH
LANES = 128
CHUNK = 256


def dot_nn(a, b):
    return jnp.dot(a, b, preferred_element_type=F32)


def dot_nt(a, b):
    return lax.dot_general(a, b, (((1,), (1,)), ((), ())), preferred_element_type=F32)


def dot_tn(a, b):
    return lax.dot_general(a, b, (((0,), (0,)), ((), ())), preferred_element_type=F32)


def split_terms(value, terms):
    parts = []
    for _ in range(terms):
        part = value.astype(BF16)
        parts.append(part)
        value = value - part.astype(F32)
    return parts


def pick_nn(value, hot, terms):
    return sum(dot_nn(part, hot) for part in split_terms(value, terms))


def pick_nt(value, hot, terms):
    return sum(dot_nt(part, hot) for part in split_terms(value, terms))


def iota(shape, axis):
    return lax.broadcasted_iota(jnp.int32, shape, axis)


def hot_bf16(cond):
    return jnp.where(cond, 1.0, 0.0).astype(BF16)


def sigmoid(value):
    return 0.5 * jnp.tanh(0.5 * value) + 0.5


def norm(value, axis):
    centred = value - jnp.mean(value, axis, keepdims=True)
    rstd = lax.rsqrt(jnp.mean(centred * centred, axis, keepdims=True) + EPS)
    return centred * rstd, rstd


def norm_back(grad, gain, hat, rstd, axis):
    scaled = grad * gain
    first = jnp.mean(scaled, axis, keepdims=True)
    second = jnp.mean(scaled * hat, axis, keepdims=True)
    return rstd * (scaled - first - hat * second)


def column(row):
    size = row.shape[1]
    eye = iota((size, size), 0) == iota((size, size), 1)
    return jnp.sum(jnp.where(eye, row, 0.0), 1, keepdims=True)


def lane_group(ref, j):
    return jnp.concatenate(
        [ref[pl.ds(2 * j + q, LANES, stride=16), :] for q in range(2)], axis=1
    )


def lane_ungroup(ref, j, value):
    for q in range(2):
        ref[pl.ds(2 * j + q, LANES, stride=16), :] = value[:, q * LANES : (q + 1) * LANES]


def chunk_at(j):
    return pl.ds(pl.multiple_of(j * CHUNK, CHUNK), CHUNK)


def all_peers(D, t):
    return lax.rem(D.s + t // D.nr, D.ns), lax.rem(D.r + t % D.nr, D.nr)


def seq_peers(D, t):
    return lax.rem(D.s + t, D.ns), D.r


def res_peers(D, t):
    return D.s, lax.rem(D.r + t, D.nr)


def remote(src, dst, send, recv, peer):
    return pltpu.make_async_remote_copy(
        src_ref=src,
        dst_ref=dst,
        send_sem=send,
        recv_sem=recv,
        device_id=peer,
        device_id_type=MESH,
    )


def swap(D, src_at, dst_at, count, peers, index, me, like):
    send, recv = D.take()

    @pl.loop(1, count)
    def _(t):
        peer = peers(D, t)
        remote(src_at(index(*peer)), dst_at(me), send, recv, peer).start()

    def wait():
        done = remote(like, like, send, recv, peers(D, 1))
        done.wait_send()
        done.wait_recv()

    return wait


def start_all(D, src, dst, first, size):
    n = D.ns * D.nr
    me = D.s * D.nr + D.r
    rows = pl.ds(first, size)
    dst[me, rows, :] = src[me, rows, :]
    return swap(
        D,
        lambda i: src.at[i, rows],
        lambda i: dst.at[i, rows],
        n,
        all_peers,
        lambda ps, pr: ps * D.nr + pr,
        me,
        dst.at[pl.ds(0, n - 1), rows],
    )


def start_seq(D, src_at, dst_at, like):
    return swap(D, src_at, dst_at, D.ns, seq_peers, lambda ps, pr: ps, D.s, like)


def start_res(D, src_at, dst_at, like):
    return swap(D, src_at, dst_at, D.nr, res_peers, lambda ps, pr: pr, D.r, like)


def pack_columns(value, send):
    for q in range(2):
        first = value[2 * q].astype(F32)
        second = value[2 * q + 1].astype(F32)
        for d in range(8):
            at = slice(8 * d, 8 * d + 8)
            send[d, q] = jnp.concatenate([first[at], second[at]], 0).astype(BF16)


def start_columns(D, send, recv):
    recv[D.s] = send[D.s]
    return start_seq(D, lambda i: send.at[i], lambda i: recv.at[i], recv.at[pl.ds(0, D.ns - 1)])


def unpack_columns(R, recv, target):
    for d in range(8):
        for q in range(2):
            both = recv[d, q].astype(F32)
            for k in range(2):
                rows = pl.ds(4 * d + 2 * q + k, 8, stride=32)
                R.sp0[rows, :] = both[8 * k : 8 * k + 8, :LANES]
                R.sp1[rows, :] = both[8 * k : 8 * k + 8, LANES:]
    target[...] = jnp.concatenate([R.sp0[...], R.sp1[...]], 1)


def p_spread(R, D):
    pack_columns(R.x, R.xsend)
    D.ready()
    wait = start_columns(D, R.xsend, R.xrecv)
    R.arrived("adj_a")
    pack_columns(R.adj_a, R.asend)
    R.wait_adjoint = start_columns(D, R.asend, R.arecv)
    R.arrived("w_ti", "w_ii", "w_oo", "w_qkvg", "w_ao", "pe", "adj_c")
    R.w1t[...] = R.w_ti[...].astype(F32).T.astype(BF16)
    R.w2t[...] = R.w_ii[...].astype(F32).T.astype(BF16)
    R.wo1t[...] = R.w_to[...].astype(F32).T.astype(BF16)
    R.wo2t[...] = R.w_io[...].astype(F32).T.astype(BF16)
    stage_outer_weight(R)
    wait()
    unpack_columns(R, R.xrecv, R.xc)


def flag_column(flags):
    here = iota((256, 32), 0) % 32 == iota((256, 32), 1)
    return jnp.sum(jnp.where(here, flags, 0.0), 1, keepdims=True)


def head_probs(keys, query, flag_rows, head):
    lanes = iota((1, 256), 1) // 32
    mine = hot_bf16(lanes == head)
    scores = dot_nt(keys, query * mine) * (32 ** (-0.5))
    same = iota((256, 256), 0) // 32 == iota((256, 256), 1) // 32
    scores = jnp.where(same, jnp.where(flag_rows > 0, scores, -1e30), -3e38)
    weights = jnp.exp(scores - jnp.max(scores, 0, keepdims=True))
    return weights / jnp.sum(weights, 0, keepdims=True)


def p_attention(R, D):
    flag_rows = flag_column(R.fl[...].astype(F32))
    hat, _ = norm(R.xc[...], -1)
    normed = (hat * R.g1[...]).astype(BF16)
    projected = dot_nn(normed, R.w_qkvg[...])
    R.qkv[...] = projected[:, :768].astype(BF16)
    R.gl[...] = projected[:, 768:]
    R.att[...] = jnp.zeros((256, 256), F32)

    @pl.loop(0, 8, unroll=4)
    def _(head):
        probs = head_probs(R.qkv[:, 256:512], R.qkv[:, :256], flag_rows, head).astype(BF16)
        lanes = iota((1, 256), 1) // 32
        R.att[...] += jnp.where(lanes == head, dot_tn(probs, R.qkv[:, 512:768]), 0.0)

    gated = (sigmoid(R.gl[...]) * R.att[...]).astype(BF16)
    later = R.xc[...] + dot_nn(gated, R.w_ao[...])
    R.msan[...] = later
    hat2, _ = norm(later, -1)
    normed2 = (hat2 * R.g2[...]).astype(BF16)
    outer_in = (dot_nt(normed2, R.w_oit[...]) * (flag_rows > 0).astype(F32)).astype(BF16)
    wide = jnp.concatenate([outer_in.astype(F32), jnp.zeros((256, 64), F32)], 1)
    R.lsend[...] = wide.T[:32].astype(BF16)
    spread = hot_bf16(iota((64, 1024), 0) == 32 + iota((64, 1024), 1) // 32)
    kept = iota((256, 1024), 0) % 32 == iota((256, 1024), 1) % 32
    rows = jnp.where(kept, dot_nn(outer_in, spread), 0.0).astype(BF16)
    R.rsend[...] = dot_nn(hot_bf16(iota((8, 256), 0) == iota((8, 256), 1) // 32), rows)


def p_outer_exchange(R, D):
    send, recv = R.out_send, R.out_recv
    D.all_ready()
    owner = 2 * D.r + D.s // 4
    slot = D.s % 4

    def left(k, to):
        return remote(R.lsend, R.lall.at[to], send.at[k], recv.at[to], (owner, k))

    for k in range(4):
        mine = (owner == D.s) & (D.r == k)

        @pl.when(jnp.logical_not(mine))
        def _():
            left(k, slot).start()

        @pl.when(mine)
        def _():
            R.lall[slot] = R.lsend[...]

    here = pl.ds(pl.multiple_of(8 * D.s, 8), 8)

    def right(t):
        return remote(R.rsend, R.rall.at[here], send.at[4 + t], recv.at[4 + t], seq_peers(D, t))

    @pl.loop(1, 8)
    def _(t):
        right(t).start()

    R.rall[here, :] = R.rsend[...]

    for k in range(4):
        mine = (owner == D.s) & (D.r == k)
        theirs = (4 * (D.s % 2) + k == D.s) & (D.s // 2 == D.r)

        @pl.when(jnp.logical_not(mine))
        def _():
            left(k, k).wait_send()

        @pl.when(jnp.logical_not(theirs))
        def _():
            left(k, k).wait_recv()

    @pl.loop(1, 8)
    def _(t):
        right(t).wait()


def stage_outer_weight(R):
    R.wst[...] = R.w_oo[...].astype(F32)


def outer_weight(R, d):
    return R.wst[pl.ds(d, 32, stride=32), :].astype(BF16)


def count_of(R):
    return jnp.sum(R.fl[...].astype(F32), 1, keepdims=True)


def p_outer(R, D):
    for q in range(4):
        wide = jnp.concatenate([R.lall[q].astype(F32), jnp.zeros((96, 256), F32)], 0)
        R.l2[256 * q : 256 * q + 256, :] = wide.T[:, :32].astype(BF16)
        R.lt[:, 256 * q : 256 * q + 256] = R.lall[q]

    @pl.loop(0, 8)
    def _(e):
        weights = jnp.concatenate([outer_weight(R, 4 * e + u) for u in range(4)], 1)
        part = dot_nn(R.l2[...], weights).astype(BF16)
        for u in range(4):
            at = pl.ds(pl.multiple_of(32 * (4 * e + u), 32), 32)
            for i in range(32):
                R.zb[i, at, :] = part[32 * i : 32 * i + 32, LANES * u : LANES * u + LANES]

    inverse = 1.0 / count_of(R)
    right = R.rall[...].astype(BF16)

    @pl.loop(0, 16, unroll=4)
    def _(m):
        both = dot_nn(right, jnp.concatenate([R.zb[m], R.zb[16 + m]], 1)) * inverse
        rows = [
            both[:, LANES * h : LANES * h + LANES] + R.pe[16 * h + m].astype(F32) for h in range(2)
        ]
        R.pair1[:, pl.ds(pl.multiple_of(m * LANES, LANES), LANES)] = jnp.concatenate(rows, 0).T


def entry_chunk(R, pair, gain, w_t, nb, j):
    hat, _ = norm(pair, 0)
    nb_here = (hat * gain).astype(BF16)
    nb[:, chunk_at(j)] = nb_here
    for k, stage in ((0, R.st0), (1, R.st1)):
        linear = dot_nn(w_t[256 * k : 256 * k + 256, :], nb_here)
        lane_ungroup(stage, j, sigmoid(linear[128:]) * linear[:128])


def pack_both(R, send):
    @pl.loop(0, 32, unroll=4)
    def _(d):
        at = pl.ds(pl.multiple_of(64 * d, 64), 64)
        first = R.st0[at, :].astype(BF16)
        second = R.st1[at, :].astype(BF16)
        for c in range(4):
            send[d, 32 * c : 32 * c + 16, :] = first[16 * c : 16 * c + 16]
            send[d, 32 * c + 16 : 32 * c + 32, :] = second[16 * c : 16 * c + 16]


def p_entry1(R, D):
    gain = column(R.g3[...])

    @pl.loop(0, 8, unroll=4)
    def _(j):
        entry_chunk(R, R.pair1[:, chunk_at(j)], gain, R.w1t, R.nb3, j)

    pack_both(R, R.lrs)


def gather_mat(recv, off, mats, at):
    @pl.loop(0, 8, unroll=4)
    def _(s):
        top = pl.ds(pl.multiple_of(32 * s, 32), 16)
        low = pl.ds(pl.multiple_of(32 * s + 16, 16), 16)
        for p in range(2):
            a = recv[4 * s + 2 * p, off : off + 16, :]
            b = recv[4 * s + 2 * p + 1, off : off + 16, :]
            lanes = slice(LANES * p, LANES * p + LANES)
            mats[at, top, lanes] = jnp.concatenate([a[:, :64], b[:, :64]], 1)
            mats[at, low, lanes] = jnp.concatenate([a[:, 64:], b[:, 64:]], 1)


def scatter_mat(mat, send, off):
    @pl.loop(0, 8, unroll=4)
    def _(s):
        for p in range(2):
            lanes = slice(LANES * p, LANES * p + LANES)
            a = mat[pl.ds(pl.multiple_of(32 * s, 32), 16), lanes]
            b = mat[pl.ds(pl.multiple_of(32 * s + 16, 16), 16), lanes]
            send[4 * s + 2 * p, off : off + 16, :] = jnp.concatenate([a[:, :64], b[:, :64]], 1)
            send[4 * s + 2 * p + 1, off : off + 16, :] = jnp.concatenate([a[:, 64:], b[:, 64:]], 1)


def tri_forward(R, D, recv, mats, back, product, meanwhile):
    size = 4 // PARTS
    waits = [start_all(D, R.lrs, recv, 32 * size * h, 32 * size) for h in range(PARTS)]
    meanwhile(R, D)
    later = []
    for h in range(PARTS):
        waits[h]()
        for c in range(size * h, size * h + size):
            gather_mat(recv, 32 * c, mats, c)
            gather_mat(recv, 32 * c + 16, mats, 4 + c)
            R.tm[c] = product(mats[c], mats[4 + c]).astype(BF16)
            scatter_mat(R.tm.at[c], R.ts, 16 * c)
        later.append(start_all(D, R.ts, back, 16 * size * h, 16 * size))
    for wait in later:
        wait()


def tri_backward(R, D, recv, mats, back, products, meanwhile):
    size = 4 // PARTS
    waits = [start_all(D, R.ts, recv, 16 * size * h, 16 * size) for h in range(PARTS)]
    meanwhile(R, D)
    later = []
    for h in range(PARTS):
        waits[h]()
        for c in range(size * h, size * h + size):
            gather_mat(recv, 16 * c, R.dm, c)
            for k in range(2):
                R.tm[c] = products[k](mats[c], mats[4 + c], R.dm[c]).astype(BF16)
                scatter_mat(R.tm.at[c], R.lrs, 32 * c + 16 * k)
        later.append(start_all(D, R.lrs, back, 32 * size * h, 32 * size))
    for wait in later:
        wait()


def nothing(R, D):
    pass


def p_tri1(R, D):
    tri_forward(R, D, R.lr1r, R.mats1, R.t1r, dot_nt, p_still)


def stage_single(recv, stage):
    @pl.loop(0, 32, unroll=4)
    def _(d):
        stage[pl.ds(pl.multiple_of(64 * d, 64), 64), :] = recv[d].astype(F32)


def stage_both(recv, first, second):
    @pl.loop(0, 32, unroll=4)
    def _(d):
        at = pl.ds(pl.multiple_of(64 * d, 64), 64)
        both = recv[d].astype(F32)
        first[at, :] = jnp.concatenate([both[32 * c : 32 * c + 16] for c in range(4)], 0)
        second[at, :] = jnp.concatenate([both[32 * c + 16 : 32 * c + 32] for c in range(4)], 0)


def p_middle(R, D):
    stage_single(R.t1r, R.st2)
    gain4 = column(R.g4[...])
    gain5 = column(R.g5[...])

    @pl.loop(0, 8, unroll=4)
    def _(j):
        hat, _ = norm(lane_group(R.st2, j), 0)
        nb4 = (hat * gain4).astype(BF16)
        R.nb4[:, chunk_at(j)] = nb4
        update = dot_nn(R.wo1t[...], nb4)
        gate = sigmoid(dot_nn(R.w1t[512:, :], R.nb3[:, chunk_at(j)]))
        pair2 = R.pair1[:, chunk_at(j)] + gate * update
        R.pair2[:, chunk_at(j)] = pair2
        entry_chunk(R, pair2, gain5, R.w2t, R.nb5, j)

    pack_both(R, R.lrs)


def p_tri2(R, D):
    tri_forward(R, D, R.lr2r, R.mats2, R.t2r, dot_tn, nothing)


def chunk_rows(D, j):
    lane = iota((1, CHUNK), 1)
    local = 16 * ((lane % LANES) // 64) + 2 * j + lane // LANES
    return local, hot_bf16(iota((256, CHUNK), 0) == 32 * D.s + local)


def near_rows(D):
    return hot_bf16(iota((256, CHUNK), 0) == 64 * D.r + iota((256, CHUNK), 1) % 64)


def p_still(R, D):
    dist = column(R.w_ds[...])
    inv_k = 1.0 / R.ca.shape[1]
    R.at8[...] = jnp.zeros((8, 256), F32)
    R.at8[0:3, :] = R.at[...]
    R.la8[...] = jnp.zeros((8, 32), F32)
    R.la8[0:3, :] = R.adj_l[...]
    R.nodet[...] = dot_tn(R.vet[...].astype(BF16), R.w_nd[...]).T
    R.dmean[...] = dot_nt(R.w_up[...], R.adj_v[...].astype(BF16))
    near = near_rows(D)
    R.nbase[...] = pick_nn(R.nodet[64:, :], near, 2)
    R.cbase[...] = pick_nn(R.at8[...], near, 3)
    R.nb_f[...] = R.ca[...].astype(F32)

    @pl.loop(0, 8, unroll=2)
    def _(j):
        here = chunk_at(j)
        local, row = chunk_rows(D, j)
        mine = hot_bf16(iota((32, CHUNK), 0) == local)
        named = dot_tn(R.nb_f[...].astype(BF16), mine)
        target = (64 * D.r + iota((1, CHUNK), 1) % 64).astype(F32)
        mask = jnp.max(jnp.where(named == target, 1.0, 0.0), 0, keepdims=True) * inv_k
        diff = pick_nn(R.at8[...], row, 3) - R.cbase[...]
        square = 1.0 + jnp.sum(diff * diff, 0, keepdims=True)
        radial = jnp.log(square)
        R.geo[0:8, here] = diff
        R.geo[8:16, here] = pick_nn(R.la8[...], mine, 3)
        R.geo[16:17, here] = radial
        R.geo[17:18, here] = mask
        R.geo[18:19, here] = 2.0 / square
        R.pre[0:64, here] = pick_nn(R.nodet[0:64, :], row, 2) + R.nbase[...] + radial * dist
        R.pre[64:128, here] = pick_nn(R.dmean[...], mine, 2) * mask
        for q in range(2):
            m = 2 * j + q
            both = jnp.concatenate([R.adj_c[m], R.adj_c[16 + m]], 0).astype(F32)
            R.dpair[:, pl.ds(pl.multiple_of(m * LANES, LANES), LANES)] = both.T


def p_turn(R, D):
    stage_single(R.t2r, R.st2)
    gain6 = column(R.g6[...])
    dist = column(R.w_ds[...])
    turn_weight = column(R.w_sl[...])
    R.a_g6[...] = jnp.zeros((128, CHUNK), F32)

    @pl.loop(0, 8, unroll=4)
    def _(j):
        here = chunk_at(j)
        hat, rstd = norm(lane_group(R.st2, j), 0)
        nb6 = (hat * gain6).astype(BF16)
        R.nb6[:, here] = nb6
        update2 = dot_nn(R.wo2t[...], nb6)
        gate2 = sigmoid(dot_nn(R.w2t[512:, :], R.nb5[:, here]))
        pair3 = R.pair2[:, here] + gate2 * update2
        po_b = pair3.astype(BF16)
        R.po[:, here] = po_b
        pre = R.pre[0:64, here] + dot_nn(R.w_edt[...], po_b)
        sig_pre = sigmoid(pre)
        hidden = (pre * sig_pre).astype(BF16)
        R.hid[:, here] = hidden
        msg = dot_tn(R.w_ms[...], hidden)
        sig_msg = sigmoid(msg)
        message = msg * sig_msg
        turn = jnp.tanh(jnp.sum(message * turn_weight, 0, keepdims=True))
        diff = R.geo[0:8, here]
        locadj = R.geo[8:16, here]
        mask = R.geo[17:18, here]
        d_turn = jnp.sum(locadj * diff, 0, keepdims=True) * mask * (1.0 - turn * turn)
        d_message = R.pre[64:128, here] + turn_weight * d_turn
        d_msg = (d_message * sig_msg * (1.0 + msg * (1.0 - sig_msg))).astype(BF16)
        R.dmsg[:, here] = d_msg
        d_pre = dot_nn(R.w_ms[...], d_msg) * sig_pre * (1.0 + pre * (1.0 - sig_pre))
        d_edge = d_pre.astype(BF16)
        R.dedge[:, here] = d_edge
        d_radial = jnp.sum(d_pre * dist, 0, keepdims=True)
        R.pre[0:64, here] = message
        R.pre[64:128, here] = d_pre
        R.geo[19:20, here] = turn * mask
        R.geo[20:21, here] = d_turn
        R.geo[24:32, here] = (d_radial * R.geo[18:19, here]) * diff + locadj * (turn * mask)
        d_pair3 = R.dpair[:, here] + dot_tn(R.w_edt[...], d_edge)
        R.dpair[:, here] = d_pair3
        d_up = (d_pair3 * gate2).astype(BF16)
        R.dup2[:, here] = d_up
        R.dtri2[512:, here] = (d_pair3 * update2 * gate2 * (1.0 - gate2)).astype(BF16)
        d_nb = dot_nn(R.w_io[...], d_up)
        R.a_g6[...] += d_nb * hat
        lane_ungroup(R.st0, j, norm_back(d_nb, gain6, hat, rstd, 0))

    pack_single(R, R.ts)


def p_turn_grads(R, D):
    R.g_io[...] = dot_nt(R.nb6[...], R.dup2[...])
    R.g_ed[...] = dot_nt(R.dedge[...], R.po[...])
    R.g_ms[...] = dot_nt(R.hid[...], R.dmsg[...])
    R.gg6[...] = jnp.sum(R.a_g6[...], 1, keepdims=True)
    R.g_ds[...] = jnp.sum(R.pre[64:128, :] * R.geo[16:17, :], 1, keepdims=True)
    R.g_sl[...] = jnp.sum(R.pre[0:64, :] * R.geo[20:21, :], 1, keepdims=True)
    for acc in (R.s_mean, R.s_own, R.s_other):
        acc[...] = jnp.zeros(acc.shape, F32)
    R.s_xyz[...] = jnp.zeros((16, 256), F32)

    @pl.loop(0, 8, unroll=2)
    def _(j):
        here = chunk_at(j)
        _, row = chunk_rows(D, j)
        near = near_rows(D)
        d_pre = R.pre[64:128, here]
        d_diff = R.geo[24:32, here]
        R.s_mean[...] += pick_nt(R.pre[0:64, here] * R.geo[17:18, here], row, 2)
        R.s_own[...] += pick_nt(d_pre, row, 2)
        R.s_other[...] += pick_nt(d_pre, near, 2)
        R.s_xyz[0:8, :] += pick_nt(R.geo[0:8, here] * R.geo[19:20, here], row, 2)
        R.s_xyz[8:16, :] += pick_nt(d_diff, row, 2) - pick_nt(d_diff, near, 2)
        for q in range(2):
            m = 2 * j + q
            at = pl.ds(pl.multiple_of(m * LANES, LANES), LANES)
            out = R.po[:, at].astype(F32).T.astype(BF16)
            R.pair_out[m] = out[:64]
            R.pair_out[16 + m] = out[64:]

    R.leave("pair_out")


def pack_single(R, send):
    @pl.loop(0, 32, unroll=4)
    def _(d):
        send[d] = R.st0[pl.ds(pl.multiple_of(64 * d, 64), 64), :].astype(BF16)


def p_back2(R, D):
    tri_backward(
        R,
        D,
        R.dt2r,
        R.mats2,
        R.dlr2r,
        (lambda a, b, d: dot_nt(b, d), lambda a, b, d: dot_nn(a, d)),
        p_turn_grads,
    )


def gates_back(R, d_tri, w_t, nb_here, j):
    here = chunk_at(j)
    for k, stage in ((0, R.st0), (1, R.st1)):
        grad = lane_group(stage, j)
        linear = dot_nn(w_t[256 * k : 256 * k + 256, :], nb_here)
        gate = sigmoid(linear[128:])
        d_first = grad * gate
        d_tri[256 * k : 256 * k + 128, here] = d_first.astype(BF16)
        d_tri[256 * k + 128 : 256 * k + 256, here] = (
            d_first * linear[:128] * (1.0 - gate)
        ).astype(BF16)


def p_between(R, D):
    stage_both(R.dlr2r, R.st0, R.st1)
    stage_single(R.t1r, R.st2)
    gain4 = column(R.g4[...])
    gain5 = column(R.g5[...])
    R.a_g4[...] = jnp.zeros((128, CHUNK), F32)
    R.a_g5[...] = jnp.zeros((128, CHUNK), F32)

    @pl.loop(0, 8, unroll=4)
    def _(j):
        here = chunk_at(j)
        gates_back(R, R.dtri2, R.w2t, R.nb5[:, here], j)
        d_nb5 = dot_nn(R.w_ii[...], R.dtri2[:, here])
        hat5, rstd5 = norm(R.pair2[:, here], 0)
        R.a_g5[...] += d_nb5 * hat5
        d_pair2 = R.dpair[:, here] + norm_back(d_nb5, gain5, hat5, rstd5, 0)
        R.dpair[:, here] = d_pair2
        gate = sigmoid(dot_nn(R.w1t[512:, :], R.nb3[:, here]))
        update = dot_nn(R.wo1t[...], R.nb4[:, here])
        d_up = (d_pair2 * gate).astype(BF16)
        R.dup1[:, here] = d_up
        R.dtri1[512:, here] = (d_pair2 * update * gate * (1.0 - gate)).astype(BF16)
        d_nb4 = dot_nn(R.w_to[...], d_up)
        hat4, rstd4 = norm(lane_group(R.st2, j), 0)
        R.a_g4[...] += d_nb4 * hat4
        lane_ungroup(R.st3, j, norm_back(d_nb4, gain4, hat4, rstd4, 0))

    @pl.loop(0, 32, unroll=4)
    def _(d):
        R.ts[d] = R.st3[pl.ds(pl.multiple_of(64 * d, 64), 64), :].astype(BF16)


def p_between_grads(R, D):
    R.g_ii[...] = dot_nt(R.nb5[...], R.dtri2[...])
    R.g_to[...] = dot_nt(R.nb4[...], R.dup1[...])
    R.gg5[...] = jnp.sum(R.a_g5[...], 1, keepdims=True)
    R.gg4[...] = jnp.sum(R.a_g4[...], 1, keepdims=True)


def p_back1(R, D):
    tri_backward(
        R,
        D,
        R.dt1r,
        R.mats1,
        R.dlr1r,
        (lambda a, b, d: dot_nn(d, b), lambda a, b, d: dot_tn(d, a)),
        p_between_grads,
    )


def p_pair_end(R, D):
    stage_both(R.dlr1r, R.st0, R.st1)
    gain3 = column(R.g3[...])
    R.a_g3[...] = jnp.zeros((128, CHUNK), F32)
    inverse = 1.0 / count_of(R)

    @pl.loop(0, 8, unroll=4)
    def _(j):
        here = chunk_at(j)
        gates_back(R, R.dtri1, R.w1t, R.nb3[:, here], j)
        d_nb3 = dot_nn(R.w_ti[...], R.dtri1[:, here])
        hat3, rstd3 = norm(R.pair1[:, here], 0)
        R.a_g3[...] += d_nb3 * hat3
        d_pair1 = R.dpair[:, here] + norm_back(d_nb3, gain3, hat3, rstd3, 0)
        for q in range(2):
            m = 2 * j + q
            out = d_pair1[:, q * LANES : (q + 1) * LANES].T
            R.pair_grad[m] = out[:64]
            R.pair_grad[16 + m] = out[64:]
            small = (out * inverse).astype(BF16)
            R.dopm[m] = small[:64]
            R.dopm[16 + m] = small[64:]

    R.leave("pair_grad")


def p_pair_grads(R, D):
    R.g_ti[...] = dot_nt(R.nb3[...], R.dtri1[...])
    R.gg3[...] = jnp.sum(R.a_g3[...], 1, keepdims=True)


def p_outer_back(R, D):
    R.rt[...] = R.rall[...].T.astype(BF16)
    R.dright[...] = jnp.zeros((64, 1024), F32)
    R.dleft[...] = jnp.zeros((32, 1024), F32)

    @pl.loop(0, 4)
    def _(k):
        grad = jnp.concatenate([R.dopm[8 * k + u] for u in range(8)], 1)
        R.dright[...] += dot_nt(grad, jnp.concatenate([R.zb[8 * k + u] for u in range(8)], 1))

    @pl.loop(0, 4)
    def _(g):
        right = R.rt[pl.ds(pl.multiple_of(256 * g, 256), 256), :]

        @pl.loop(0, 16, unroll=16)
        def _(k):
            grad = jnp.concatenate([R.dopm[2 * k], R.dopm[2 * k + 1]], 1)
            both = dot_nn(right, grad).astype(BF16)
            for h in range(2):
                at = pl.ds(pl.multiple_of(64 * k + 32 * h, 32), 32)
                for u in range(8):
                    block = both[32 * u : 32 * u + 32, LANES * h : LANES * h + LANES]
                    R.zb[8 * g + u, at, :] = block

        weights = jnp.concatenate([outer_weight(R, 8 * g + u) for u in range(8)], 1)
        R.dleft[...] += dot_nt(weights, jnp.concatenate([R.zb[8 * g + u] for u in range(8)], 1))

    for q in range(4):
        R.dls[q] = R.dleft[:, 256 * q : 256 * q + 256].astype(BF16)


def p_outer_grads(R, D):
    @pl.loop(0, 4)
    def _(g):
        rows = jnp.concatenate([R.zb[8 * g + u] for u in range(8)], 1)
        total = dot_nn(R.lt[...], rows)
        for u in range(8):
            R.st1[pl.ds(8 * g + u, 32, stride=32), :] = total[:, LANES * u : LANES * u + LANES]

    R.g_oo[...] = R.st1[0:1024, :]


def p_outer_return(R, D):
    send, recv = R.back_send, R.back_recv
    column_res = D.s // 2
    owner = 2 * D.r + D.s // 4

    def left(q, slot):
        peer = (4 * (D.s % 2) + q, column_res)
        return remote(R.dls.at[q], R.dlr.at[slot], send.at[q], recv.at[slot], peer)

    for q in range(4):
        mine = (4 * (D.s % 2) + q == D.s) & (column_res == D.r)

        @pl.when(jnp.logical_not(mine))
        def _():
            left(q, D.r).start()

        @pl.when(mine)
        def _():
            R.dlr[D.r] = R.dls[q]

    def right(t):
        peer = seq_peers(D, t)
        at = pl.ds(pl.multiple_of(8 * peer[0], 8), 8)
        return remote(R.dright.at[at], R.drr.at[D.s], send.at[4 + t], recv.at[4 + t], peer)

    @pl.loop(1, 8)
    def _(t):
        right(t).start()

    R.drr[D.s] = R.dright[pl.ds(pl.multiple_of(8 * D.s, 8), 8), :]
    p_pair_grads(R, D)
    p_sum0(R, D)
    p_outer_grads(R, D)
    p_sum1(R, D)

    for q in range(4):
        mine = (4 * (D.s % 2) + q == D.s) & (column_res == D.r)
        theirs = (owner == D.s) & (D.r == q)

        @pl.when(jnp.logical_not(mine))
        def _():
            left(q, q).wait_send()

        @pl.when(jnp.logical_not(theirs))
        def _():
            left(q, q).wait_recv()

    @pl.loop(1, 8)
    def _(t):
        right(t).wait()


def p_attention_back(R, D):
    flag_rows = flag_column(R.fl[...].astype(F32))
    live = (flag_rows > 0).astype(F32)
    left = R.dlr[0].astype(F32)
    for k in range(1, 4):
        left += R.dlr[k].astype(F32)
    right = R.drr[0]
    for k in range(1, 8):
        right += R.drr[k]
    wide = jnp.concatenate([left, jnp.zeros((96, 256), F32)], 0).T
    spread = dot_nn(
        hot_bf16(iota((256, 8), 0) // 32 == iota((256, 8), 1)), right.astype(BF16)
    )
    kept = iota((256, 1024), 0) % 32 == iota((256, 1024), 1) % 32
    spread = jnp.where(kept, spread, 0.0).astype(BF16)
    back = hot_bf16(32 + iota((1024, LANES), 0) // 32 == iota((1024, LANES), 1))
    d_in = ((wide + dot_nn(spread, back)) * live).astype(BF16)[:, :64]
    hat2, rstd2 = norm(R.msan[...], -1)
    normed2 = (hat2 * R.g2[...]).astype(BF16)
    R.g_oi[...] = dot_tn(d_in, normed2)
    d_normed2 = dot_nn(d_in, R.w_oit[...])
    R.gg2[...] = jnp.sum(d_normed2 * hat2, 0, keepdims=True)
    d_later = R.ac[...] + norm_back(d_normed2, R.g2[...], hat2, rstd2, -1)
    R.dlater[...] = d_later
    d_exit = d_later.astype(BF16)
    gate = sigmoid(R.gl[...])
    gated = (gate * R.att[...]).astype(BF16)
    R.g_ao[...] = dot_tn(gated, d_exit)
    d_gated = dot_nt(d_exit, R.w_ao[...])
    R.datt[...] = (d_gated * gate).astype(BF16)
    R.dproj[:, 768:] = (d_gated * R.att[...] * gate * (1.0 - gate)).astype(BF16)
    R.dqkv[...] = jnp.zeros((256, 768), F32)

    @pl.loop(0, 8, unroll=4)
    def _(head):
        lanes = iota((1, 256), 1) // 32
        mine = lanes == head
        hot = hot_bf16(mine)
        query = R.qkv[:, 0:256]
        keys = R.qkv[:, 256:512]
        probs = head_probs(keys, query, flag_rows, head)
        d_att = R.datt[...]
        d_probs = dot_nt(R.qkv[:, 512:768], d_att * hot)
        total = jnp.sum(probs * d_probs, 0, keepdims=True)
        d_scores = (probs * (d_probs - total) * (32 ** (-0.5))).astype(BF16)
        R.dqkv[:, 0:256] += jnp.where(mine, dot_tn(d_scores, keys), 0.0)
        R.dqkv[:, 256:512] += jnp.where(mine, dot_nn(d_scores, query), 0.0)
        R.dqkv[:, 512:768] += jnp.where(mine, dot_nn(probs.astype(BF16), d_att), 0.0)

    R.dproj[:, :768] = R.dqkv[...].astype(BF16)
    hat, rstd = norm(R.xc[...], -1)
    normed = (hat * R.g1[...]).astype(BF16)
    R.g_qkvg[...] = dot_tn(normed, R.dproj[...])
    d_normed = dot_nt(R.dproj[...], R.w_qkvg[...])
    R.gg1[...] = jnp.sum(d_normed * hat, 0, keepdims=True)
    R.dlater[...] += norm_back(d_normed, R.g1[...], hat, rstd, -1)
    group_columns(R, R.dlater, R.gsend)


def group_columns(R, value, send):
    R.sp0[...] = value[:, :LANES]
    R.sp1[...] = value[:, LANES:]
    for d in range(8):
        for q in range(2):
            parts = []
            for k in range(2):
                rows = pl.ds(4 * d + 2 * q + k, 8, stride=32)
                parts.append(jnp.concatenate([R.sp0[rows, :], R.sp1[rows, :]], 1))
            send[d, q] = jnp.concatenate(parts, 0).astype(BF16)


def ungroup_columns(recv, target):
    for q in range(2):
        blocks = [recv[d, q].astype(F32) for d in range(8)]
        for k in range(2):
            rows = jnp.concatenate([block[8 * k : 8 * k + 8] for block in blocks], 0)
            target[2 * q + k] = rows.astype(target.dtype)


def p_send_value(R, D):
    group_columns(R, R.msan, R.osend)
    R.wait_value = start_columns(D, R.osend, R.orecv)


def p_take_value(R, D):
    R.wait_value()
    ungroup_columns(R.orecv, R.msa_out)
    R.leave("msa_out")
    R.wait_adjoint()
    unpack_columns(R, R.arecv, R.ac)


SEGMENTS = (
    dict(
        g_ti=(128, 640),
        g_ii=(128, 640),
        g_to=(128, 128),
        g_io=(128, 128),
        s_mean=(64, 256),
        s_own=(64, 256),
        s_other=(64, 256),
        s_vadj=(64, 256),
        s_xyz=(16, 256),
        g_ed=(64, 128),
        g_ms=(64, 64),
        small0=(16, 128),
    ),
    dict(g_oo=(1024, 128)),
    dict(g_qkvg=(256, 1024), g_ao=(256, 256), g_oi=(64, 256), small1=(16, 128)),
)


def segment_layout(index):
    layout = []
    start = 0
    for name, (rows, cols) in SEGMENTS[index].items():
        for lane in range(0, cols, LANES):
            layout.append((name, start, rows, lane, min(LANES, cols - lane)))
            start += rows
    return layout, -(-start // 512) * 512


def pack_segment(R, index):
    layout, total = segment_layout(index)
    pay = R.pay[index]
    for name, start, count, lane, width in layout:
        value = getattr(R, name)[:, lane : lane + width]
        pay[start : start + count, 0:width] = value.astype(BF16)
    end = layout[-1][1] + layout[-1][2]
    if end < total:
        pay[end:total, :] = jnp.zeros((total - end, LANES), BF16)


def rows_of(index, size):
    return pl.ds(pl.multiple_of(index * size, size), size)


def sum_segment(R, D, index):
    pay, full = R.pay[index], R.full[index]
    first, second, third, fourth = (table[index] for table in R.parts)
    eighth = pay.shape[0] // 8
    part = eighth // 4
    pack_segment(R, index)
    first[D.s] = pay[rows_of(D.s, eighth), :]
    most = pl.ds(0, eighth * (D.ns - 1))
    wait = start_seq(
        D, lambda i: pay.at[rows_of(i, eighth)], lambda i: first.at[i], pay.at[most]
    )
    yield
    wait()
    total = first[0].astype(F32)
    for k in range(1, 8):
        total += first[k].astype(F32)
    second[...] = total.astype(BF16)
    third[D.r] = second[rows_of(D.r, part), :]
    some = pl.ds(0, part * (D.nr - 1))
    wait = start_res(
        D, lambda i: second.at[rows_of(i, part)], lambda i: third.at[i], second.at[some]
    )
    yield
    wait()
    total = third[0].astype(F32)
    for k in range(1, 4):
        total += third[k].astype(F32)
    fourth[...] = total.astype(BF16)
    mine = pl.ds(pl.multiple_of(D.s * eighth + D.r * part, part), part)
    full[mine, :] = fourth[...]
    wait = start_res(D, lambda i: fourth, lambda i: full.at[mine], full.at[some])
    yield
    wait()
    wait = start_seq(
        D,
        lambda i: full.at[rows_of(D.s, eighth)],
        lambda i: full.at[rows_of(i, eighth)],
        full.at[most],
    )
    yield
    wait()
    R.leave(index)


def p_sum0(R, D):
    place = hot_bf16(iota((32, 256), 1) == 32 * D.s + iota((32, 256), 0))
    first = jnp.where(D.r == 0, 1.0, 0.0)
    R.s_vadj[...] = dot_tn(R.adj_v[...].astype(BF16), place) * first
    R.small[...] = jnp.zeros((128, LANES), F32)
    for k, value in enumerate((R.gg3, R.gg4, R.gg5, R.gg6, R.g_ds, R.g_sl)):
        R.small[0 : value.shape[0], k : k + 1] = value[...]
    R.small0[...] = R.small[...].T[:16]
    R.sum0 = sum_segment(R, D, 0)
    next(R.sum0)


def p_sum1(R, D):
    R.sum1 = sum_segment(R, D, 1)
    next(R.sum1)


def p_sum2(R, D):
    R.small1[...] = jnp.zeros((16, LANES), F32)
    for k, value in enumerate((R.gg1, R.gg2)):
        for half in range(2):
            at = 2 * k + half
            R.small1[at : at + 1, :] = value[:, LANES * half : LANES * half + LANES]
    R.sum2 = sum_segment(R, D, 2)
    next(R.sum2)


def p_sums(R, D):
    wait = start_columns(D, R.gsend, R.grecv)
    sums = [R.sum0, R.sum1, R.sum2]
    while sums:
        sums = [each for each in sums if next(each, D) is not D]
        if wait:
            wait()
            ungroup_columns(R.grecv, R.msa_grad)
            R.leave("msa_grad")
            wait = None


def unpack_segment(R, index):
    held = {}
    for name, start, count, lane, width in segment_layout(index)[0]:
        value = R.full[index][start : start + count, 0:width].astype(F32)
        if name.startswith("g_"):
            getattr(R, "o_" + name)[:, lane : lane + width] = value
        else:
            held.setdefault(name, []).append(value)
    return {name: jnp.concatenate(parts, 1) for name, parts in held.items()}


def p_finish_first(R, D):
    unpack_segment(R, 1)
    held = unpack_segment(R, 2)
    small = held["small1"]
    for k, target in enumerate((R.o_gg1, R.o_gg2)):
        for half in range(2):
            at = 2 * k + half
            target[:, LANES * half : LANES * half + LANES] = small[at : at + 1]


def p_finish(R, D):
    held = unpack_segment(R, 0)
    small = held["small0"]
    for k, target in enumerate((R.o_gg3, R.o_gg4, R.o_gg5, R.o_gg6)):
        target[...] = small[k : k + 1, :]
    R.o_g_ds[...] = small[4:5, :64]
    R.o_g_sl[...] = small[5:6, :64]
    mean_b = held["s_mean"].astype(BF16)
    R.o_g_up[...] = dot_nt(mean_b, held["s_vadj"].astype(BF16))
    d_node = jnp.concatenate([held["s_own"], held["s_other"]], 0).astype(BF16)
    R.o_g_nd[...] = dot_nt(R.vet[...].astype(BF16), d_node)
    step = dot_tn(R.w_up[...], mean_b)
    grad = dot_nn(R.w_nd[...], d_node)
    R.rows_f[...] = jnp.concatenate([step + R.vet[...], grad], 0).T
    here = pl.ds(pl.multiple_of(32 * D.s, 32), 32)
    mine = R.rows_f[here, :]
    R.single_out[...] = mine[:, :64]
    R.single_grad[...] = R.adj_v[...] + mine[:, 64:]
    R.xyz[...] = jnp.zeros((128, 256), F32)
    R.xyz[0:16, :] = held["s_xyz"]
    R.xyz[16:19, :] = R.at[...]
    R.rows_g[...] = R.xyz[...].T
    turned = R.rows_g[here, :]
    back = jnp.concatenate([turned, jnp.zeros((96, 128), F32)], 0).T
    R.coords_out[...] = back[16:19, 0:32] + back[0:3, 0:32]
    R.coords_grad[...] = R.adj_l[...] + back[8:11, 0:32]


KEPT = dict(
    xsend=((8, 2, 16, 256), BF16),
    xrecv=((8, 2, 16, 256), BF16),
    asend=((8, 2, 16, 256), BF16),
    arecv=((8, 2, 16, 256), BF16),
    osend=((8, 2, 16, 256), BF16),
    orecv=((8, 2, 16, 256), BF16),
    gsend=((8, 2, 16, 256), BF16),
    grecv=((8, 2, 16, 256), BF16),
    wst=((1024, 128), F32),
    lt=((32, 1024), BF16),
    tm=((4, 256, 256), BF16),
    geo=((32, 2048), F32),
    pre=((128, 2048), F32),
    small0=((16, 128), F32),
    small1=((16, 128), F32),
    xc=((256, 256), F32),
    ac=((256, 256), F32),
    sp0=((256, 128), F32),
    sp1=((256, 128), F32),
    qkv=((256, 768), BF16),
    gl=((256, 256), F32),
    att=((256, 256), F32),
    msan=((256, 256), F32),
    lsend=((32, 256), BF16),
    rsend=((8, 1024), F32),
    lall=((4, 32, 256), BF16),
    rall=((64, 1024), F32),
    st0=((2048, 128), F32),
    st1=((2048, 128), F32),
    st2=((2048, 128), F32),
    st3=((2048, 128), F32),
    l2=((1024, 32), BF16),
    zb=((32, 1024, 128), BF16),
    pair1=((128, 2048), F32),
    pair2=((128, 2048), F32),
    dpair=((128, 2048), F32),
    w1t=((640, 128), BF16),
    w2t=((640, 128), BF16),
    wo1t=((128, 128), BF16),
    wo2t=((128, 128), BF16),
    nb3=((128, 2048), BF16),
    nb4=((128, 2048), BF16),
    nb5=((128, 2048), BF16),
    nb6=((128, 2048), BF16),
    po=((128, 2048), BF16),
    hid=((64, 2048), BF16),
    dmsg=((64, 2048), BF16),
    dedge=((64, 2048), BF16),
    dup1=((128, 2048), BF16),
    dup2=((128, 2048), BF16),
    dtri1=((640, 2048), BF16),
    dtri2=((640, 2048), BF16),
    mats1=((8, 256, 256), BF16),
    mats2=((8, 256, 256), BF16),
    dm=((4, 256, 256), BF16),
    lrs=((32, 128, 128), BF16),
    lr1r=((32, 128, 128), BF16),
    lr2r=((32, 128, 128), BF16),
    dlr1r=((32, 128, 128), BF16),
    dlr2r=((32, 128, 128), BF16),
    ts=((32, 64, 128), BF16),
    t1r=((32, 64, 128), BF16),
    t2r=((32, 64, 128), BF16),
    dt1r=((32, 64, 128), BF16),
    dt2r=((32, 64, 128), BF16),
    at8=((8, 256), F32),
    la8=((8, 32), F32),
    nodet=((128, 256), F32),
    dmean=((64, 32), F32),
    nbase=((64, 256), F32),
    cbase=((8, 256), F32),
    nb_f=((32, 64), F32),
    s_mean=((64, 256), F32),
    s_own=((64, 256), F32),
    s_other=((64, 256), F32),
    s_vadj=((64, 256), F32),
    s_xyz=((16, 256), F32),
    a_g3=((128, 256), F32),
    a_g4=((128, 256), F32),
    a_g5=((128, 256), F32),
    a_g6=((128, 256), F32),
    gg3=((128, 1), F32),
    gg4=((128, 1), F32),
    gg5=((128, 1), F32),
    gg6=((128, 1), F32),
    gg1=((1, 256), F32),
    gg2=((1, 256), F32),
    g_ds=((64, 1), F32),
    g_sl=((64, 1), F32),
    g_io=((128, 128), F32),
    g_to=((128, 128), F32),
    g_ti=((128, 640), F32),
    g_ii=((128, 640), F32),
    g_ed=((64, 128), F32),
    g_ms=((64, 64), F32),
    g_oo=((1024, 128), F32),
    g_oi=((64, 256), F32),
    g_ao=((256, 256), F32),
    g_qkvg=((256, 1024), F32),
    small=((128, 128), F32),
    dopm=((32, 64, 128), BF16),
    rt=((1024, 64), BF16),
    dright=((64, 1024), F32),
    dleft=((32, 1024), F32),
    dls=((4, 32, 256), BF16),
    dlr=((4, 32, 256), BF16),
    drr=((8, 8, 1024), F32),
    dlater=((256, 256), F32),
    datt=((256, 256), BF16),
    dproj=((256, 1024), BF16),
    dqkv=((256, 768), F32),
)
SIZES = [segment_layout(index)[1] for index in range(len(SEGMENTS))]
PAYLOADS = [((size, 128), BF16) for size in SIZES]
PARTIAL = (
    [((8, size // 8, 128), BF16) for size in SIZES]
    + [((size // 8, 128), BF16) for size in SIZES]
    + [((4, size // 32, 128), BF16) for size in SIZES]
    + [((size // 32, 128), BF16) for size in SIZES]
)
LARGE = ("msa_out", "pair_out", "msa_grad", "pair_grad")
MOVED_IN = ("adj_a", "w_qkvg", "w_ao", "w_oo", "w_ti", "w_ii", "pe", "adj_c")
FINISH = ("vet", "w_up", "w_nd", "adj_v", "at", "adj_l")
FINISH_KEPT = dict(
    rows_f=((256, 128), F32), rows_g=((256, 128), F32), xyz=((128, 256), F32)
)
RESULTS = dict(
    msa_out=((4, 64, 256), BF16),
    pair_out=((32, 64, 128), BF16),
    single_out=((32, 64), F32),
    coords_out=((3, 32), F32),
    msa_grad=((4, 64, 256), F32),
    pair_grad=((32, 64, 128), F32),
    single_grad=((32, 64), F32),
    coords_grad=((3, 32), F32),
    o_gg1=((1, 256), F32),
    o_g_qkvg=((256, 1024), F32),
    o_g_ao=((256, 256), F32),
    o_gg2=((1, 256), F32),
    o_g_oi=((64, 256), F32),
    o_g_oo=((1024, 128), F32),
    o_gg3=((1, 128), F32),
    o_g_ti=((128, 640), F32),
    o_gg4=((1, 128), F32),
    o_g_to=((128, 128), F32),
    o_gg5=((1, 128), F32),
    o_g_ii=((128, 640), F32),
    o_gg6=((1, 128), F32),
    o_g_io=((128, 128), F32),
    o_g_nd=((64, 128), F32),
    o_g_ed=((64, 128), F32),
    o_g_ds=((1, 64), F32),
    o_g_ms=((64, 64), F32),
    o_g_sl=((1, 64), F32),
    o_g_up=((64, 64), F32),
)

STEPS = (
    p_spread,
    p_attention,
    p_outer_exchange,
    p_send_value,
    p_outer,
    p_take_value,
    p_entry1,
    p_tri1,
    p_middle,
    p_tri2,
    p_turn,
    p_back2,
    p_between,
    p_back1,
    p_pair_end,
    p_outer_back,
    p_outer_return,
    p_attention_back,
    p_sum2,
    p_sums,
)
PARTS = 4
EXCHANGES = 16 + 8 * PARTS


class Device:
    def __init__(self, n_seq, n_res, sems, rows_in):
        self.s, self.r = lax.axis_index("seq"), lax.axis_index("res")
        self.ns, self.nr = n_seq, n_res
        self.sems = sems
        self.rows_in = rows_in
        self.used = 0

    def take(self):
        self.used += 2
        assert self.used <= 2 * EXCHANGES
        return self.sems.at[self.used - 2], self.sems.at[self.used - 1]

    def ready(self):
        pl.semaphore_wait(pltpu.get_barrier_semaphore(), self.ns + self.nr - 2)

        @pl.loop(1, self.nr)
        def _(t):
            pl.semaphore_signal(self.rows_in, inc=1, device_id=res_peers(self, t), device_id_type=MESH)

    def all_ready(self):
        pl.semaphore_wait(self.rows_in, self.nr - 1)


def first_kernel(n_seq, n_res, names, *refs):
    refs = list(refs)
    far = {name: refs.pop(0) for name in names}
    far_full = [refs.pop(0) for _ in SIZES]
    R = SimpleNamespace(**far)
    R.__dict__.update({name: refs.pop(0) for name in (*KEPT, *MOVED_IN, *LARGE)})
    tables = [[refs.pop(0) for _ in SIZES] for _ in range(6)]
    R.full, R.pay, R.parts = tables[0], tables[1], tables[2:]
    R.out_send, R.out_recv, R.back_send, R.back_recv, R.move = refs[2:]
    D = Device(n_seq, n_res, refs[0], refs[1])
    barrier = pltpu.get_barrier_semaphore()

    for peers, count in ((seq_peers, n_seq), (res_peers, n_res)):

        @pl.loop(1, count)
        def _(t):
            pl.semaphore_signal(barrier, inc=1, device_id=peers(D, t), device_id_type=MESH)

    moves = {}
    for name in MOVED_IN:
        moves[name] = pltpu.make_async_copy(far[name], getattr(R, name), R.move.at[len(moves)])
        moves[name].start()
    R.arrived = lambda *wanted: [moves.pop(name).wait() for name in wanted]
    base = len(moves)
    out = []

    def leave(name):
        if name in far:
            source, target, at = getattr(R, name), far[name], LARGE.index(name)
        else:
            source, target, at = R.full[name], far_full[name], len(LARGE) + name
        out.append(pltpu.make_async_copy(source, target, R.move.at[base + at]))
        out[-1].start()

    R.leave = leave
    for step in STEPS:
        step(R, D)
    for copy in out:
        copy.wait()


def last_kernel(n_seq, n_res, names, *refs):
    refs = list(refs)
    full = [refs.pop(0) for _ in SIZES]
    near = [refs.pop(0) for _ in LARGE]
    R = SimpleNamespace(**{name: refs.pop(0) for name in names[: len(FINISH)]}, full=full)
    away = [refs.pop(0) for _ in LARGE]
    *refs, sems = refs
    held = refs[-len(LARGE) :]
    R.__dict__.update(zip(names[len(FINISH) :], refs))

    def move(index, source, target):
        copy = pltpu.make_async_copy(source, target, sems.at[index])
        copy.start()
        return copy

    coming = [move(k, near[k], held[k]) for k in range(len(LARGE))]
    D = Device(n_seq, n_res, None, None)
    p_finish_first(R, D)
    for copy in coming:
        copy.wait()
    going = [move(len(LARGE) + k, held[k], away[k]) for k in range(len(LARGE))]
    p_finish(R, D)
    for copy in going:
        copy.wait()


ARGS = dict(
    x=(4, 64, 256),
    pe=(32, 64, 128),
    vet=(256, 64),
    at=(3, 256),
    fl=(32,),
    ca=(32, 64),
    g1=(256,),
    w_qkvg=(256, 1024),
    w_ao=(256, 256),
    g2=(256,),
    w_oit=(256, 64),
    w_oo=(1024, 128),
    g3=(128,),
    w_ti=(128, 640),
    g4=(128,),
    w_to=(128, 128),
    g5=(128,),
    w_ii=(128, 640),
    g6=(128,),
    w_io=(128, 128),
    w_nd=(64, 128),
    w_edt=(128, 64),
    w_ds=(64,),
    w_ms=(64, 64),
    w_sl=(64,),
    w_up=(64, 64),
    adj_a=(4, 64, 256),
    adj_c=(32, 64, 128),
    adj_v=(32, 64),
    adj_l=(3, 32),
)


def fits(n_seq, n_res, args):
    shapes = tuple(tuple(arg.shape) for arg in args)
    return (n_seq, n_res) == (8, 4) and shapes == tuple(ARGS.values())


def fast_shards(n_seq, n_res, *args):
    env = dict(zip(ARGS, args))
    for name, value in tuple(env.items()):
        if value.ndim == 1:
            env[name] = value.reshape(1, -1)
    env.update(vet=env["vet"].T, w_oit=env["w_oit"].T, w_edt=env["w_edt"].T)
    space = pl.BlockSpec(memory_space=pltpu.VMEM)

    def shapes(entries):
        return [jax.ShapeDtypeStruct(*entry) for entry in entries]

    large = {name: RESULTS[name] for name in LARGE}
    anywhere = pl.BlockSpec(memory_space=pl.ANY)
    held = [(ARGS[name], BF16) for name in MOVED_IN] + [RESULTS[name] for name in LARGE]
    values = pl.pallas_call(
        functools.partial(first_kernel, n_seq, n_res, (*env, *large)),
        out_shape=shapes((*large.values(), *PAYLOADS)),
        in_specs=[anywhere if name in MOVED_IN else space for name in env],
        out_specs=[anywhere] * (len(large) + len(PAYLOADS)),
        scratch_shapes=[
            pltpu.VMEM(*entry) for entry in (*KEPT.values(), *held, *PAYLOADS, *PAYLOADS, *PARTIAL)
        ]
        + [pltpu.SemaphoreType.DMA((2 * EXCHANGES,)), pltpu.SemaphoreType.REGULAR]
        + [pltpu.SemaphoreType.DMA((12,))] * 4
        + [pltpu.SemaphoreType.DMA((len(MOVED_IN) + len(LARGE) + len(SIZES),))],
        compiler_params=pltpu.CompilerParams(
            vmem_limit_bytes=62 * 2**20, collective_id=0, has_side_effects=True
        ),
    )(*env.values())
    full = values[len(large) :]
    env.update(zip(large, values))
    small = {name: entry for name, entry in RESULTS.items() if name not in large}
    values = pl.pallas_call(
        functools.partial(last_kernel, n_seq, n_res, (*FINISH, *small, *FINISH_KEPT)),
        out_shape=shapes((*large.values(), *small.values())),
        in_specs=[space] * len(full) + [anywhere] * len(LARGE) + [space] * len(FINISH),
        out_specs=[anywhere] * len(LARGE) + [space] * len(small),
        scratch_shapes=[pltpu.VMEM(*entry) for entry in FINISH_KEPT.values()]
        + [pltpu.VMEM(*RESULTS[name]) for name in LARGE]
        + [pltpu.SemaphoreType.DMA((2 * len(LARGE),))],
        compiler_params=pltpu.CompilerParams(vmem_limit_bytes=60 * 2**20),
    )(*full, *[env[name] for name in LARGE], *[env[name] for name in FINISH])
    env.update(zip((*large, *small), values))
    results = [env[name] for name in RESULTS]
    for index, value in enumerate(results):
        if value.shape[0] == 1:
            results[index] = value.reshape(-1)
    for index in (12, 23):
        results[index] = results[index].T
    return tuple(results)


def solution(mesh):
    n_seq, n_res = mesh.shape["seq"], mesh.shape["res"]

    def body(*args):
        if fits(n_seq, n_res, args):
            return fast_shards(n_seq, n_res, *args)
        return shards(*args)

    return jax.shard_map(
        body,
        mesh=mesh,
        in_specs=(
            P("seq", "res", None),
            P("seq", "res", None),
            P(),
            P(),
            P(),
            P("seq", None),
            P(),
            P(),
            P(),
            P(),
            P(),
            P(),
            P(),
            P(),
            P(),
            P(),
            P(),
            P(),
            P(),
            P(),
            P(),
            P(),
            P(),
            P(),
            P(),
            P(),
            P("seq", "res", None),
            P("seq", "res", None),
            P("seq", None),
            P(None, "seq"),
        ),
        out_specs=(
            P("seq", "res", None),
            P("seq", "res", None),
            P("seq", None),
            P(None, "seq"),
            P("seq", "res", None),
            P("seq", "res", None),
            P("seq", None),
            P(None, "seq"),
            P(),
            P(),
            P(),
            P(),
            P(),
            P(),
            P(),
            P(),
            P(),
            P(),
            P(),
            P(),
            P(),
            P(),
            P(),
            P(),
            P(),
            P(),
            P(),
            P(),
        ),
        check_vma=False,
    )
```

```python
import functools
from types import SimpleNamespace

import jax
import jax.numpy as jnp
from jax import lax
from jax.experimental import pallas as pl
from jax.experimental.pallas import tpu as pltpu
from jax.sharding import PartitionSpec as P

HEADS = 8


EPS = 1e-05
HIGH = lax.Precision.HIGHEST


def spread_2(value, axis, source):
    kept = jnp.where(lax.axis_index(axis) == source, value, 0).astype(value.dtype)
    return lax.psum(kept, axis)


def standardize_lines(value, gain):
    row_mean = jnp.mean(value, -1, keepdims=True)
    centred = value - row_mean
    spread = jnp.mean(centred * centred, -1, keepdims=True)
    return centred * lax.rsqrt(spread + EPS) * gain


def tensor_mean_answer(left, right):
    return jnp.einsum("...c,cd->...d", left, right, preferred_element_type=jnp.float32)


def product_back(grad, right):
    return jnp.einsum("...d,cd->...c", grad, right, preferred_element_type=jnp.float32)


def weight_back(left, grad):
    flat_left = left.reshape(-1, left.shape[-1])
    flat_grad = grad.reshape(-1, grad.shape[-1])
    return jnp.einsum("nc,nd->cd", flat_left, flat_grad, preferred_element_type=jnp.float32)


def attn_scores(query, keys, allowed, scale):
    raw_scores = (
        jnp.einsum("qlhd,klhd->lhqk", query, keys, preferred_element_type=jnp.float32) * scale
    )
    return jnp.where(allowed, raw_scores, -1e30)


def tri_gates(tri_lin):
    quarter = tri_lin.shape[-1] // 4
    left_part = jax.nn.sigmoid(tri_lin[..., quarter : 2 * quarter]) * tri_lin[..., :quarter]
    right_part = (
        jax.nn.sigmoid(tri_lin[..., 3 * quarter :]) * tri_lin[..., 2 * quarter : 3 * quarter]
    )
    return (left_part, right_part)


def edge_front(own_rows, other_near, edge_lin, diff, distance_basis_matrix):
    radial = jnp.log(1.0 + jnp.sum(diff * diff, 0))
    return jax.nn.silu(
        own_rows[:, None, :] + other_near + edge_lin + radial[..., None] * distance_basis_matrix
    )


def edge_finish(msg_lin, signal_location_matrix, diff):
    message = jax.nn.silu(msg_lin)
    turn = jnp.tanh(jnp.einsum("ikc,c->ik", message, signal_location_matrix, precision=HIGH))
    return (jnp.mean(message, 1), jnp.mean(diff * turn[None], 2))


def gather_rows(value):
    return lax.all_gather(value, "seq", axis=0, tiled=True)


def across_res(value):
    return lax.psum(value.astype(jnp.bfloat16), "res").astype(jnp.float32)


def owners_sum(value):
    return lax.psum_scatter(value, "seq", scatter_dimension=0, tiled=True)


def place_home(rows_part, col_width, offset, keep_home):
    empty = jnp.zeros((rows_part.shape[0], col_width, rows_part.shape[2]), jnp.float32)
    return lax.dynamic_update_slice_in_dim(empty, rows_part, offset, 1) * keep_home


def sum_flat(parts):
    flat = jnp.concatenate([jnp.ravel(member) for member in parts])
    summed = lax.psum(flat, ("seq", "res"))
    pieces = []
    offset = 0
    for member in parts:
        pieces.append(summed[offset : offset + member.size].reshape(member.shape))
        offset = offset + member.size
    return pieces


def shards(
    alignment_embedding,
    coupling_embedding,
    vertex_embedding,
    atom_locations,
    chain_existence_flags,
    closest_aminos,
    softmax_mixer_scale_factor,
    attender_stacked_matrix,
    softmax_mixer_exit_matrix,
    tensor_mean_scale_factor,
    tensor_mean_entry_matrix,
    tensor_mean_exit_matrix,
    outbound_entry_scale,
    outbound_entry_matrix,
    outbound_exit_scale,
    outbound_exit_matrix,
    inbound_entry_scale,
    inbound_entry_matrix,
    inbound_exit_scale,
    inbound_exit_matrix,
    vertex_mapping_matrix,
    bond_mapping_matrix,
    distance_basis_matrix,
    signal_matrix,
    signal_location_matrix,
    vertex_change_matrix,
    alignment_adjoint,
    coupling_adjoint,
    vertex_adjoint,
    location_adjoint,
):
    seq_index = lax.axis_index("seq")
    res_index = lax.axis_index("res")
    n_seq = lax.axis_size("seq")
    n_res = lax.axis_size("res")
    chain_shard_piece, vertical_shard_piece, breadth_overall = alignment_embedding.shape
    rows_dev = coupling_embedding.shape[0]
    span_overall, node_width = vertex_embedding.shape
    block_tally = chain_existence_flags.shape[0]
    head_size = breadth_overall // HEADS
    scale = head_size ** (-0.5)
    opm_width = tensor_mean_entry_matrix.shape[1] // 2
    tri_width = outbound_exit_matrix.shape[0]
    chain_exists = (chain_existence_flags > 0).astype(jnp.float32)
    line_indicator_entries = lax.dynamic_slice_in_dim(
        chain_exists, seq_index * chain_shard_piece, chain_shard_piece
    )
    first_res = (res_index == 0).astype(jnp.float32)
    home = seq_index * rows_dev // vertical_shard_piece
    offset = seq_index * rows_dev - home * vertical_shard_piece
    keep_home = (home == res_index).astype(jnp.float32)
    alignment_real_lines = alignment_embedding.astype(jnp.float32)
    standardized_lines, standardize_reverse_alpha = jax.vjp(
        standardize_lines, alignment_real_lines, softmax_mixer_scale_factor
    )
    normed_b = standardized_lines.astype(jnp.bfloat16)
    projected = tensor_mean_answer(normed_b, attender_stacked_matrix)
    query = projected[..., :breadth_overall].astype(jnp.bfloat16)
    keyval = projected[..., breadth_overall : 3 * breadth_overall].astype(jnp.bfloat16)
    attn_gate = jax.nn.sigmoid(projected[..., 3 * breadth_overall :])
    all_keyval = lax.all_gather(keyval, "seq", axis=0, tiled=True)
    query4 = query.reshape(chain_shard_piece, vertical_shard_piece, HEADS, head_size)
    keys4 = all_keyval[..., :breadth_overall].reshape(
        block_tally, vertical_shard_piece, HEADS, head_size
    )
    values4 = all_keyval[..., breadth_overall:].reshape(
        block_tally, vertical_shard_piece, HEADS, head_size
    )
    allowed = chain_exists[None, None, None, :] > 0
    scores = attn_scores(query4, keys4, allowed, scale)
    score_peak = jnp.max(scores, -1, keepdims=True)
    exp_scores = jnp.exp(scores - score_peak)
    exp_total = jnp.sum(exp_scores, -1, keepdims=True)
    log_total = score_peak + jnp.log(exp_total)
    probs_b = (exp_scores / exp_total).astype(jnp.bfloat16)
    attended = jnp.einsum(
        "lhqk,klhd->qlhd", probs_b, values4, preferred_element_type=jnp.float32
    ).reshape(chain_shard_piece, vertical_shard_piece, breadth_overall)
    sigmoid_scaled_lines = (attn_gate * attended).astype(jnp.bfloat16)
    alignment_later = alignment_real_lines + tensor_mean_answer(
        sigmoid_scaled_lines, softmax_mixer_exit_matrix
    )
    standardized_lines2, standardize_reverse_beta = jax.vjp(
        standardize_lines, alignment_later, tensor_mean_scale_factor
    )
    normed2_b = standardized_lines2.astype(jnp.bfloat16)
    outer_in = (
        tensor_mean_answer(normed2_b, tensor_mean_entry_matrix)
        * line_indicator_entries[:, None, None]
    ).astype(jnp.bfloat16)
    everyone = lax.all_gather(outer_in, ("seq", "res"), axis=0, tiled=True)
    blocks = everyone.reshape(n_seq, n_res, chain_shard_piece, vertical_shard_piece, 2 * opm_width)
    home_block = lax.dynamic_index_in_dim(blocks, home, 1, keepdims=False)
    left_rows = lax.dynamic_slice_in_dim(home_block, offset, rows_dev, 2)[..., :opm_width]
    left_rows = left_rows.reshape(block_tally, rows_dev, opm_width)
    right_cols = lax.dynamic_index_in_dim(blocks, res_index, 1, keepdims=False)[..., opm_width:]
    right_cols = right_cols.reshape(block_tally, vertical_shard_piece, opm_width)
    outer_b = jnp.einsum("sic,sjd->ijcd", left_rows, right_cols, preferred_element_type=jnp.float32)
    outer_b = outer_b.reshape(rows_dev, vertical_shard_piece, opm_width * opm_width).astype(
        jnp.bfloat16
    )
    count = jnp.sum(chain_exists)
    pair1 = (
        coupling_embedding.astype(jnp.float32)
        + tensor_mean_answer(outer_b, tensor_mean_exit_matrix) / count
    )
    normed3, norm_back3 = jax.vjp(standardize_lines, pair1, outbound_entry_scale)
    normed3_b = normed3.astype(jnp.bfloat16)
    tri = tensor_mean_answer(normed3_b, outbound_entry_matrix)
    (left_t, right_t), gates_back = jax.vjp(tri_gates, tri[..., : 4 * tri_width])
    left_b = left_t.astype(jnp.bfloat16)
    right_b = right_t.astype(jnp.bfloat16)
    right_all = gather_rows(right_b)
    partial_tri = jnp.einsum("ikc,jkc->ijc", left_b, right_all, preferred_element_type=jnp.float32)
    triangle = lax.psum_scatter(
        partial_tri.astype(jnp.bfloat16), "res", scatter_dimension=1, tiled=True
    ).astype(jnp.float32)
    normed4, norm_back4 = jax.vjp(standardize_lines, triangle, outbound_exit_scale)
    normed4_b = normed4.astype(jnp.bfloat16)
    update = tensor_mean_answer(normed4_b, outbound_exit_matrix)
    out_gate = jax.nn.sigmoid(tri[..., 4 * tri_width :])
    pair2 = pair1 + out_gate * update
    normed5, norm_back5 = jax.vjp(standardize_lines, pair2, inbound_entry_scale)
    normed5_b = normed5.astype(jnp.bfloat16)
    tri2 = tensor_mean_answer(normed5_b, inbound_entry_matrix)
    (left_i, right_i), gates_back2 = jax.vjp(tri_gates, tri2[..., : 4 * tri_width])
    both_local = jnp.concatenate([left_i.astype(jnp.bfloat16), right_i.astype(jnp.bfloat16)], -1)
    both_all = gather_rows(both_local)
    right_all2 = both_all[..., tri_width:]
    left_cand = lax.dynamic_slice_in_dim(both_all[..., :tri_width], offset, rows_dev, 1)
    left_sel = spread_2(left_cand, "res", home)
    triangle2 = jnp.einsum("kic,kjc->ijc", left_sel, right_all2, preferred_element_type=jnp.float32)
    normed6, norm_back6 = jax.vjp(standardize_lines, triangle2, inbound_exit_scale)
    normed6_b = normed6.astype(jnp.bfloat16)
    update2 = tensor_mean_answer(normed6_b, inbound_exit_matrix)
    out_gate2 = jax.nn.sigmoid(tri2[..., 4 * tri_width :])
    coupling_later3 = pair2 + out_gate2 * update2
    pair3_b = coupling_later3.astype(jnp.bfloat16)
    rows_all = lax.all_gather(pair3_b, "res", axis=1, tiled=True)
    nbr_hot = closest_aminos[:, :, None] == jnp.arange(span_overall, dtype=jnp.int32)[None, None, :]
    hot_float = nbr_hot.astype(jnp.float32)
    edges_b = jnp.einsum(
        "ikl,ilc->ikc", nbr_hot.astype(jnp.bfloat16), rows_all, preferred_element_type=jnp.float32
    ).astype(jnp.bfloat16)
    single_b = vertex_embedding.astype(jnp.bfloat16)
    node_proj = tensor_mean_answer(single_b, vertex_mapping_matrix)
    own_rows = lax.dynamic_slice_in_dim(node_proj[:, :node_width], seq_index * rows_dev, rows_dev)
    other_near = jnp.einsum("ikl,lc->ikc", hot_float, node_proj[:, node_width:], precision=HIGH)
    coords_own = lax.dynamic_slice_in_dim(atom_locations, seq_index * rows_dev, rows_dev, 1)
    coords_near = jnp.einsum("ikl,xl->xik", hot_float, atom_locations, precision=HIGH)
    diff = coords_own[:, :, None] - coords_near
    edge_lin = tensor_mean_answer(edges_b, bond_mapping_matrix)
    hidden, front_back = jax.vjp(
        edge_front, own_rows, other_near, edge_lin, diff, distance_basis_matrix
    )
    hidden_b = hidden.astype(jnp.bfloat16)
    msg_lin = tensor_mean_answer(hidden_b, signal_matrix)
    (mean_msg, shift), finish_back = jax.vjp(edge_finish, msg_lin, signal_location_matrix, diff)
    mean_b = mean_msg.astype(jnp.bfloat16)
    single_rows = lax.dynamic_slice_in_dim(vertex_embedding, seq_index * rows_dev, rows_dev)
    single_out = single_rows + tensor_mean_answer(mean_b, vertex_change_matrix)
    coords_out = coords_own + shift
    d_update_b = vertex_adjoint.astype(jnp.bfloat16)
    g_update = weight_back(mean_b, d_update_b)
    d_mean = product_back(d_update_b, vertex_change_matrix)
    d_msg_lin, g_coord, d_diff_finish = finish_back((d_mean, location_adjoint))
    d_msg_b = d_msg_lin.astype(jnp.bfloat16)
    g_msg = weight_back(hidden_b, d_msg_b)
    d_hidden = product_back(d_msg_b, signal_matrix)
    d_own, d_other_near, d_edge_lin, d_diff_front, g_dist = front_back(d_hidden)
    d_edge_b = d_edge_lin.astype(jnp.bfloat16)
    g_edge = weight_back(edges_b, d_edge_b)
    d_edges = product_back(d_edge_b, bond_mapping_matrix)
    d_rows = jnp.einsum("ikl,ikc->ilc", hot_float, d_edges, precision=HIGH)
    d_pair3 = coupling_adjoint.astype(jnp.float32) + lax.dynamic_slice_in_dim(
        d_rows, res_index * vertical_shard_piece, vertical_shard_piece, 1
    )
    d_diff = d_diff_front + d_diff_finish
    d_coords_own = jnp.sum(d_diff, 2)
    d_coords_near = jnp.einsum("ikl,xik->xl", hot_float, -d_diff, precision=HIGH)
    d_other_all = jnp.einsum("ikl,ikc->lc", hot_float, d_other_near, precision=HIGH)
    d_other_rows, d_near_rows = (
        lax.psum_scatter(d_other_all, "seq", scatter_dimension=0, tiled=True),
        lax.psum_scatter(d_coords_near, "seq", scatter_dimension=1, tiled=True),
    )
    d_node_b = jnp.concatenate([d_own, d_other_rows], -1).astype(jnp.bfloat16)
    g_node = weight_back(
        lax.dynamic_slice_in_dim(single_b, seq_index * rows_dev, rows_dev), d_node_b
    )
    single_grad = vertex_adjoint + product_back(d_node_b, vertex_mapping_matrix)
    coords_grad = location_adjoint + d_coords_own + d_near_rows
    layer_two = [
        g_node * first_res,
        g_edge * first_res,
        g_dist * first_res,
        g_msg * first_res,
        g_coord * first_res,
        g_update * first_res,
    ]
    d_inc_b = (d_pair3 * out_gate2).astype(jnp.bfloat16)
    d_gate_out2 = d_pair3 * update2 * out_gate2 * (1.0 - out_gate2)
    g_inc_out = weight_back(normed6_b, d_inc_b)
    d_normed6 = product_back(d_inc_b, inbound_exit_matrix)
    d_triangle2, g_inc_out_gain = norm_back6(d_normed6)
    d_tri2_b = d_triangle2.astype(jnp.bfloat16)
    d_left_sel = jnp.einsum(
        "ijc,kjc->kic", d_tri2_b, right_all2, preferred_element_type=jnp.float32
    )
    d_right_all2 = jnp.einsum(
        "ijc,kic->kjc", d_tri2_b, left_sel, preferred_element_type=jnp.float32
    )
    d_left_total = across_res(d_left_sel)
    d_both2 = owners_sum(
        jnp.concatenate(
            [place_home(d_left_total, vertical_shard_piece, offset, keep_home), d_right_all2], -1
        )
    )
    (d_gates2,) = gates_back2((d_both2[..., :tri_width], d_both2[..., tri_width:]))
    d_tri2_in_b = jnp.concatenate([d_gates2, d_gate_out2], -1).astype(jnp.bfloat16)
    g_inc_in = weight_back(normed5_b, d_tri2_in_b)
    d_normed5 = product_back(d_tri2_in_b, inbound_entry_matrix)
    d_pair2_norm, g_inc_gain = norm_back5(d_normed5)
    d_pair2 = d_pair3 + d_pair2_norm
    d_tri_out_b = (d_pair2 * out_gate).astype(jnp.bfloat16)
    d_gate_out = d_pair2 * update * out_gate * (1.0 - out_gate)
    g_tri_out = weight_back(normed4_b, d_tri_out_b)
    d_normed4 = product_back(d_tri_out_b, outbound_exit_matrix)
    d_triangle, g_tri_out_gain = norm_back4(d_normed4)
    d_triangle_b = d_triangle.astype(jnp.bfloat16)
    d_tri_all = lax.all_gather(d_triangle_b, "res", axis=1, tiled=True)
    d_left = jnp.einsum("ijc,jkc->ikc", d_tri_all, right_all, preferred_element_type=jnp.float32)
    d_right_part = jnp.einsum("ijc,ikc->jkc", d_tri_all, left_b, preferred_element_type=jnp.float32)
    d_right = owners_sum(d_right_part)
    (d_gates_in,) = gates_back((d_left, d_right))
    d_tri_b = jnp.concatenate([d_gates_in, d_gate_out], -1).astype(jnp.bfloat16)
    g_tri_in = weight_back(normed3_b, d_tri_b)
    d_normed3 = product_back(d_tri_b, outbound_entry_matrix)
    d_pair1_norm, g_tri_gain = norm_back3(d_normed3)
    pair_grad = d_pair2 + d_pair1_norm
    d_opm_b = (pair_grad / count).astype(jnp.bfloat16)
    g_opm_out = weight_back(outer_b, d_opm_b)
    d_outer = product_back(d_opm_b, tensor_mean_exit_matrix).astype(jnp.bfloat16)
    d_outer = d_outer.reshape(rows_dev, vertical_shard_piece, opm_width, opm_width)
    d_left_rows = jnp.einsum(
        "ijcd,sjd->sic", d_outer, right_cols, preferred_element_type=jnp.float32
    )
    d_right_cols = jnp.einsum(
        "ijcd,sic->sjd", d_outer, left_rows, preferred_element_type=jnp.float32
    )
    d_left_sum = across_res(d_left_rows)
    d_outer_in = owners_sum(
        jnp.concatenate(
            [place_home(d_left_sum, vertical_shard_piece, offset, keep_home), d_right_cols], -1
        )
    )
    d_outer_in_b = (d_outer_in * line_indicator_entries[:, None, None]).astype(jnp.bfloat16)
    g_opm_in = weight_back(normed2_b, d_outer_in_b)
    standardized_sens2 = product_back(d_outer_in_b, tensor_mean_entry_matrix)
    alignment_standard_sens, tensor_mean_scale_sens = standardize_reverse_beta(standardized_sens2)
    alignment_later_sens = alignment_adjoint.astype(jnp.float32) + alignment_standard_sens
    softmax_mixer_sens_lines = alignment_later_sens.astype(jnp.bfloat16)
    g_attn_out = weight_back(sigmoid_scaled_lines, softmax_mixer_sens_lines)
    d_gated = product_back(softmax_mixer_sens_lines, softmax_mixer_exit_matrix)
    d_attended_b = (d_gated * attn_gate).astype(jnp.bfloat16)
    d_gate_lin = d_gated * attended * attn_gate * (1.0 - attn_gate)
    probs_full = jnp.exp(attn_scores(query4, keys4, allowed, scale) - log_total)
    d_attended4 = d_attended_b.reshape(chain_shard_piece, vertical_shard_piece, HEADS, head_size)
    d_probs = jnp.einsum(
        "qlhd,klhd->lhqk", d_attended4, values4, preferred_element_type=jnp.float32
    )
    softmax_total = jnp.sum(probs_full * d_probs, -1, keepdims=True)
    d_scores_b = (probs_full * (d_probs - softmax_total) * scale).astype(jnp.bfloat16)
    d_query = jnp.einsum(
        "lhqk,klhd->qlhd", d_scores_b, keys4, preferred_element_type=jnp.float32
    ).reshape(chain_shard_piece, vertical_shard_piece, breadth_overall)
    d_keys = jnp.einsum("lhqk,qlhd->klhd", d_scores_b, query4, preferred_element_type=jnp.float32)
    d_values = jnp.einsum(
        "lhqk,qlhd->klhd",
        probs_full.astype(jnp.bfloat16),
        d_attended4,
        preferred_element_type=jnp.float32,
    )
    d_keyval = jnp.concatenate(
        [
            d_keys.reshape(block_tally, vertical_shard_piece, breadth_overall),
            d_values.reshape(block_tally, vertical_shard_piece, breadth_overall),
        ],
        -1,
    )
    d_keyval_own = lax.psum_scatter(d_keyval, "seq", scatter_dimension=0, tiled=True)
    d_proj_b = jnp.concatenate([d_query, d_keyval_own, d_gate_lin], -1).astype(jnp.bfloat16)
    g_qkvg = weight_back(normed_b, d_proj_b)
    standardized_sens = product_back(d_proj_b, attender_stacked_matrix)
    alignment_early_sens, alignment_scale_sens = standardize_reverse_alpha(standardized_sens)
    alignment_sensitivity = alignment_later_sens + alignment_early_sens
    layer_one = [
        alignment_scale_sens,
        g_qkvg,
        g_attn_out,
        tensor_mean_scale_sens,
        g_opm_in,
        g_opm_out,
        g_tri_gain,
        g_tri_in,
        g_tri_out_gain,
        g_tri_out,
        g_inc_gain,
        g_inc_in,
        g_inc_out_gain,
        g_inc_out,
    ]
    summed_all = sum_flat(layer_one + layer_two)
    layer_one = summed_all[:14]
    layer_two = summed_all[14:]
    return (
        alignment_later.astype(jnp.bfloat16),
        pair3_b,
        single_out,
        coords_out,
        alignment_sensitivity,
        pair_grad,
        single_grad,
        coords_grad,
        layer_one[0],
        layer_one[1],
        layer_one[2],
        layer_one[3],
        layer_one[4],
        layer_one[5],
        layer_one[6],
        layer_one[7],
        layer_one[8],
        layer_one[9],
        layer_one[10],
        layer_one[11],
        layer_one[12],
        layer_one[13],
        layer_two[0],
        layer_two[1],
        layer_two[2],
        layer_two[3],
        layer_two[4],
        layer_two[5],
    )


F32 = jnp.float32
BF16 = jnp.bfloat16
MESH = pl.DeviceIdType.MESH
LANES = 128
CHUNK = 256


def dot_nn(a, b):
    return jnp.dot(a, b, preferred_element_type=F32)


def dot_nt(a, b):
    return lax.dot_general(a, b, (((1,), (1,)), ((), ())), preferred_element_type=F32)


def dot_tn(a, b):
    return lax.dot_general(a, b, (((0,), (0,)), ((), ())), preferred_element_type=F32)


def split_terms(value, terms):
    parts = []
    for _ in range(terms):
        part = value.astype(BF16)
        parts.append(part)
        value = value - part.astype(F32)
    return parts


def pick_nn(value, hot, terms):
    return sum(dot_nn(part, hot) for part in split_terms(value, terms))


def pick_nt(value, hot, terms):
    return sum(dot_nt(part, hot) for part in split_terms(value, terms))


def iota(shape, axis):
    return lax.broadcasted_iota(jnp.int32, shape, axis)


def hot_bf16(cond):
    return jnp.where(cond, 1.0, 0.0).astype(BF16)


def sigmoid(value):
    return 0.5 * jnp.tanh(0.5 * value) + 0.5


def norm(value, axis):
    centred = value - jnp.mean(value, axis, keepdims=True)
    rstd = lax.rsqrt(jnp.mean(centred * centred, axis, keepdims=True) + EPS)
    return centred * rstd, rstd


def norm_back(grad, gain, hat, rstd, axis):
    scaled = grad * gain
    first = jnp.mean(scaled, axis, keepdims=True)
    second = jnp.mean(scaled * hat, axis, keepdims=True)
    return rstd * (scaled - first - hat * second)


def column(row):
    size = row.shape[1]
    eye = iota((size, size), 0) == iota((size, size), 1)
    return jnp.sum(jnp.where(eye, row, 0.0), 1, keepdims=True)


def lane_group(ref, j):
    return jnp.concatenate(
        [ref[pl.ds(2 * j + q, LANES, stride=16), :] for q in range(2)], axis=1
    )


def lane_ungroup(ref, j, value):
    for q in range(2):
        ref[pl.ds(2 * j + q, LANES, stride=16), :] = value[:, q * LANES : (q + 1) * LANES]


def chunk_at(j):
    return pl.ds(pl.multiple_of(j * CHUNK, CHUNK), CHUNK)


def all_peers(D, t):
    return lax.rem(D.s + t % D.ns, D.ns), lax.rem(D.r + t // D.ns, D.nr)


def seq_peers(D, t):
    return lax.rem(D.s + t, D.ns), D.r


def res_peers(D, t):
    return D.s, lax.rem(D.r + t, D.nr)


def remote(src, dst, send, recv, peer):
    return pltpu.make_async_remote_copy(
        src_ref=src,
        dst_ref=dst,
        send_sem=send,
        recv_sem=recv,
        device_id=peer,
        device_id_type=MESH,
    )


def swap(D, src_at, dst_at, count, peers, index, me, like):
    send, recv = D.take()

    @pl.loop(1, count)
    def _(t):
        peer = peers(D, t)
        remote(src_at(index(*peer)), dst_at(me), send, recv, peer).start()

    def wait():
        done = remote(like, like, send, recv, peers(D, 1))
        done.wait_send()
        done.wait_recv()

    return wait


def start_all(D, src, dst, first, size):
    n = D.ns * D.nr
    me = D.s * D.nr + D.r
    rows = pl.ds(first, size)
    dst[me, rows, :] = src[me, rows, :]
    return swap(
        D,
        lambda i: src.at[i, rows],
        lambda i: dst.at[i, rows],
        n,
        all_peers,
        lambda ps, pr: ps * D.nr + pr,
        me,
        dst.at[pl.ds(0, n - 1), rows],
    )


def start_seq(D, src_at, dst_at, like):
    return swap(D, src_at, dst_at, D.ns, seq_peers, lambda ps, pr: ps, D.s, like)


def start_res(D, src_at, dst_at, like):
    return swap(D, src_at, dst_at, D.nr, res_peers, lambda ps, pr: pr, D.r, like)


def pack_columns(value, send):
    for q in range(2):
        first = value[2 * q].astype(F32)
        second = value[2 * q + 1].astype(F32)
        for d in range(8):
            at = slice(8 * d, 8 * d + 8)
            send[d, q] = jnp.concatenate([first[at], second[at]], 0).astype(BF16)


def start_columns(D, send, recv):
    recv[D.s] = send[D.s]
    return start_seq(D, lambda i: send.at[i], lambda i: recv.at[i], recv.at[pl.ds(0, D.ns - 1)])


def unpack_columns(R, recv, target):
    for d in range(8):
        for q in range(2):
            both = recv[d, q].astype(F32)
            for k in range(2):
                rows = pl.ds(4 * d + 2 * q + k, 8, stride=32)
                R.sp0[rows, :] = both[8 * k : 8 * k + 8, :LANES]
                R.sp1[rows, :] = both[8 * k : 8 * k + 8, LANES:]
    target[...] = jnp.concatenate([R.sp0[...], R.sp1[...]], 1)


def p_spread(R, D):
    pack_columns(R.x, R.xsend)
    D.ready()
    wait = start_columns(D, R.xsend, R.xrecv)
    R.arrived("adj_a")
    pack_columns(R.adj_a, R.asend)
    R.wait_adjoint = start_columns(D, R.asend, R.arecv)
    R.arrived("w_ti", "w_ii", "w_oo", "w_qkvg", "w_ao", "pe", "adj_c")
    R.w1t[...] = R.w_ti[...].astype(F32).T.astype(BF16)
    R.w2t[...] = R.w_ii[...].astype(F32).T.astype(BF16)
    R.wo1t[...] = R.w_to[...].astype(F32).T.astype(BF16)
    R.wo2t[...] = R.w_io[...].astype(F32).T.astype(BF16)
    stage_outer_weight(R)
    wait()
    unpack_columns(R, R.xrecv, R.xc)


def flag_column(flags):
    here = iota((256, 32), 0) % 32 == iota((256, 32), 1)
    return jnp.sum(jnp.where(here, flags, 0.0), 1, keepdims=True)


def head_probs(keys, query, flag_rows, head):
    lanes = iota((1, 256), 1) // 32
    mine = hot_bf16(lanes == head)
    scores = dot_nt(keys, query * mine) * (32 ** (-0.5))
    same = iota((256, 256), 0) // 32 == iota((256, 256), 1) // 32
    scores = jnp.where(same, jnp.where(flag_rows > 0, scores, -1e30), -3e38)
    weights = jnp.exp(scores - jnp.max(scores, 0, keepdims=True))
    return weights / jnp.sum(weights, 0, keepdims=True)


def p_attention(R, D):
    flag_rows = flag_column(R.fl[...].astype(F32))
    hat, _ = norm(R.xc[...], -1)
    normed = (hat * R.g1[...]).astype(BF16)
    projected = dot_nn(normed, R.w_qkvg[...])
    R.qkv[...] = projected[:, :768].astype(BF16)
    R.gl[...] = projected[:, 768:]
    R.att[...] = jnp.zeros((256, 256), F32)

    @pl.loop(0, 8, unroll=4)
    def _(head):
        probs = head_probs(R.qkv[:, 256:512], R.qkv[:, :256], flag_rows, head).astype(BF16)
        lanes = iota((1, 256), 1) // 32
        R.att[...] += jnp.where(lanes == head, dot_tn(probs, R.qkv[:, 512:768]), 0.0)

    gated = (sigmoid(R.gl[...]) * R.att[...]).astype(BF16)
    later = R.xc[...] + dot_nn(gated, R.w_ao[...])
    R.msan[...] = later
    hat2, _ = norm(later, -1)
    normed2 = (hat2 * R.g2[...]).astype(BF16)
    outer_in = (dot_nt(normed2, R.w_oit[...]) * (flag_rows > 0).astype(F32)).astype(BF16)
    wide = jnp.concatenate([outer_in.astype(F32), jnp.zeros((256, 64), F32)], 1)
    R.lsend[...] = wide.T[:32].astype(BF16)
    spread = hot_bf16(iota((64, 1024), 0) == 32 + iota((64, 1024), 1) // 32)
    kept = iota((256, 1024), 0) % 32 == iota((256, 1024), 1) % 32
    rows = jnp.where(kept, dot_nn(outer_in, spread), 0.0).astype(BF16)
    R.rsend[...] = dot_nn(hot_bf16(iota((8, 256), 0) == iota((8, 256), 1) // 32), rows)


def p_outer_exchange(R, D):
    send, recv = R.out_send, R.out_recv
    D.all_ready()
    owner = 2 * D.r + D.s // 4
    slot = D.s % 4

    def left(k, to):
        return remote(R.lsend, R.lall.at[to], send.at[k], recv.at[to], (owner, k))

    for k in range(4):
        mine = (owner == D.s) & (D.r == k)

        @pl.when(jnp.logical_not(mine))
        def _():
            left(k, slot).start()

        @pl.when(mine)
        def _():
            R.lall[slot] = R.lsend[...]

    here = pl.ds(pl.multiple_of(8 * D.s, 8), 8)

    def right(t):
        return remote(R.rsend, R.rall.at[here], send.at[4 + t], recv.at[4 + t], seq_peers(D, t))

    @pl.loop(1, 8)
    def _(t):
        right(t).start()

    R.rall[here, :] = R.rsend[...]

    for k in range(4):
        mine = (owner == D.s) & (D.r == k)
        theirs = (4 * (D.s % 2) + k == D.s) & (D.s // 2 == D.r)

        @pl.when(jnp.logical_not(mine))
        def _():
            left(k, k).wait_send()

        @pl.when(jnp.logical_not(theirs))
        def _():
            left(k, k).wait_recv()

    @pl.loop(1, 8)
    def _(t):
        right(t).wait()


def stage_outer_weight(R):
    R.wst[...] = R.w_oo[...].astype(F32)


def outer_weight(R, d):
    return R.wst[pl.ds(d, 32, stride=32), :].astype(BF16)


def count_of(R):
    return jnp.sum(R.fl[...].astype(F32), 1, keepdims=True)


def p_outer(R, D):
    for q in range(4):
        wide = jnp.concatenate([R.lall[q].astype(F32), jnp.zeros((96, 256), F32)], 0)
        R.l2[256 * q : 256 * q + 256, :] = wide.T[:, :32].astype(BF16)
        R.lt[:, 256 * q : 256 * q + 256] = R.lall[q]

    @pl.loop(0, 8)
    def _(e):
        weights = jnp.concatenate([outer_weight(R, 4 * e + u) for u in range(4)], 1)
        part = dot_nn(R.l2[...], weights).astype(BF16)
        for u in range(4):
            at = pl.ds(pl.multiple_of(32 * (4 * e + u), 32), 32)
            for i in range(32):
                R.zb[i, at, :] = part[32 * i : 32 * i + 32, LANES * u : LANES * u + LANES]


def outer_rows(R, half):
    inverse = 1.0 / count_of(R)
    right = R.rall[...].astype(BF16)

    @pl.loop(8 * half, 8 * half + 8, unroll=4)
    def _(m):
        both = dot_nn(right, jnp.concatenate([R.zb[m], R.zb[16 + m]], 1)) * inverse
        rows = [
            both[:, LANES * h : LANES * h + LANES] + R.pe[16 * h + m].astype(F32) for h in range(2)
        ]
        R.pair1[:, pl.ds(pl.multiple_of(m * LANES, LANES), LANES)] = jnp.concatenate(rows, 0).T


def pack_both(R, half):
    @pl.loop(0, 32, unroll=4)
    def _(d):
        for pair in range(2):
            for k, stage in ((0, R.st0), (1, R.st1)):
                rows = tile_rows(stage, 64 * d + 32 * pair + 8 * half)
                first = 64 * half + 32 * pair + 16 * k
                R.lrs[d, first : first + 16, :] = rows.astype(BF16)


def pack_single(R, stage, half):
    @pl.loop(0, 32, unroll=4)
    def _(d):
        for pair in range(2):
            first = 32 * half + 16 * pair
            rows = tile_rows(stage, 64 * d + 32 * pair + 8 * half)
            R.ts[d, first : first + 16, :] = rows.astype(BF16)


def tile_rows(stage, start):
    start = pl.multiple_of(start, 8)
    return jnp.concatenate([stage[pl.ds(start, 8), :], stage[pl.ds(start + 16, 8), :]], 0)


def untile(stage, start, rows):
    start = pl.multiple_of(start, 8)
    stage[pl.ds(start, 8), :] = rows[:8]
    stage[pl.ds(start + 16, 8), :] = rows[8:]


def stage_single(recv, stage, half):
    @pl.loop(0, 32, unroll=4)
    def _(d):
        for pair in range(2):
            first = 32 * half + 16 * pair
            rows = recv[d, first : first + 16, :].astype(F32)
            untile(stage, 64 * d + 32 * pair + 8 * half, rows)


def stage_both(R, recv, half):
    @pl.loop(0, 32, unroll=4)
    def _(d):
        for pair in range(2):
            for k, stage in ((0, R.st0), (1, R.st1)):
                first = 64 * half + 32 * pair + 16 * k
                rows = recv[d, first : first + 16, :].astype(F32)
                untile(stage, 64 * d + 32 * pair + 8 * half, rows)


def send_part(D, src, dst, table, half, pair):
    size = src.shape[1] // 4
    table[half, pair] = start_all(D, src, dst, size * (2 * half + pair), size)


def send_half(D, src, dst, table, half):
    for pair in range(2):
        send_part(D, src, dst, table, half, pair)


def wait_half(table, half):
    for pair in range(2):
        table[half, pair]()


def entry_chunk(R, pair, gain, w_t, nb, j):
    hat, _ = norm(pair, 0)
    nb_here = (hat * gain).astype(BF16)
    nb[:, chunk_at(j)] = nb_here
    for k, stage in ((0, R.st0), (1, R.st1)):
        linear = dot_nn(w_t[256 * k : 256 * k + 256, :], nb_here)
        lane_ungroup(stage, j, sigmoid(linear[128:]) * linear[:128])


def p_entry1(R, D):
    gain = column(R.g3[...])
    for half in range(2):
        outer_rows(R, half)

        @pl.loop(4 * half, 4 * half + 4, unroll=4)
        def _(j):
            entry_chunk(R, R.pair1[:, chunk_at(j)], gain, R.w1t, R.nb3, j)

        pack_both(R, half)
        send_half(D, R.lrs, R.lr1r, R.waits, half)


def gather_pair(recv, pair, k, mats, at):
    size = recv.shape[1] // 4

    @pl.loop(0, 8, unroll=4)
    def _(s):
        top = pl.ds(pl.multiple_of(32 * s, 32), 16)
        low = pl.ds(pl.multiple_of(32 * s + 16, 16), 16)
        for p in range(2):
            tiles = []
            for q in range(2):
                halves = []
                for half in range(2):
                    first = size * (2 * half + pair) + 16 * k
                    block = recv[4 * s + 2 * p + q, first : first + 16, :]
                    halves.append(block.astype(F32))
                tiles.append(halves)
            lanes = slice(LANES * p, LANES * p + LANES)
            for c in range(2):
                rows = slice(8 * c, 8 * c + 8)
                a, b = (jnp.concatenate([h[rows] for h in halves], 0) for halves in tiles)
                mats[at + c, top, lanes] = jnp.concatenate([a[:, :64], b[:, :64]], 1).astype(BF16)
                mats[at + c, low, lanes] = jnp.concatenate([a[:, 64:], b[:, 64:]], 1).astype(BF16)


def scatter_pair(mats, send, pair, k):
    size = send.shape[1] // 4

    @pl.loop(0, 8, unroll=4)
    def _(s):
        for p in range(2):
            lanes = slice(LANES * p, LANES * p + LANES)
            tiles = [[], []]
            for c in range(2):
                a = mats[c, pl.ds(pl.multiple_of(32 * s, 32), 16), lanes]
                b = mats[c, pl.ds(pl.multiple_of(32 * s + 16, 16), 16), lanes]
                tiles[0].append(jnp.concatenate([a[:, :64], b[:, :64]], 1))
                tiles[1].append(jnp.concatenate([a[:, 64:], b[:, 64:]], 1))
            for q in range(2):
                for half in range(2):
                    first = size * (2 * half + pair) + 16 * k
                    rows = slice(8 * half, 8 * half + 8)
                    block = jnp.concatenate([tile[rows] for tile in tiles[q]], 0)
                    send[4 * s + 2 * p + q, first : first + 16, :] = block.astype(BF16)


def tri_forward(R, D, recv, mats, back, product, meanwhile):
    meanwhile(R, D)
    for pair in range(2):
        R.waits[0, pair]()
        R.waits[1, pair]()
        gather_pair(recv, pair, 0, mats, 2 * pair)
        gather_pair(recv, pair, 1, mats, 4 + 2 * pair)
        for c in range(2):
            R.tm[c] = product(mats[2 * pair + c], mats[4 + 2 * pair + c])
        scatter_pair(R.tm, R.ts, pair, 0)
        send_part(D, R.ts, back, R.later, 0, pair)
    for pair in range(2):
        send_part(D, R.ts, back, R.later, 1, pair)


def tri_backward(R, D, recv, mats, back, products, meanwhile):
    meanwhile(R, D)
    for pair in range(2):
        R.waits[0, pair]()
        R.waits[1, pair]()
        gather_pair(recv, pair, 0, R.dm, 0)
        for k in range(2):
            for c in range(2):
                at = 2 * pair + c
                R.tm[c] = products[k](mats[at], mats[4 + at], R.dm[c])
            scatter_pair(R.tm, R.lrs, pair, k)
        send_part(D, R.lrs, back, R.later, 0, pair)
    for pair in range(2):
        send_part(D, R.lrs, back, R.later, 1, pair)


def p_tri1(R, D):
    tri_forward(R, D, R.lr1r, R.mats1, R.t1r, dot_nt, p_still)


def p_middle(R, D):
    gain4 = column(R.g4[...])
    gain5 = column(R.g5[...])
    for half in range(2):
        wait_half(R.later, half)
        stage_single(R.t1r, R.st2, half)

        @pl.loop(4 * half, 4 * half + 4, unroll=4)
        def _(j):
            hat, _ = norm(lane_group(R.st2, j), 0)
            nb4 = (hat * gain4).astype(BF16)
            R.nb4[:, chunk_at(j)] = nb4
            update = dot_nn(R.wo1t[...], nb4)
            gate = sigmoid(dot_nn(R.w1t[512:, :], R.nb3[:, chunk_at(j)]))
            pair2 = R.pair1[:, chunk_at(j)] + gate * update
            R.pair2[:, chunk_at(j)] = pair2
            entry_chunk(R, pair2, gain5, R.w2t, R.nb5, j)

        pack_both(R, half)
        send_half(D, R.lrs, R.lr2r, R.waits, half)


def p_tri2(R, D):
    tri_forward(R, D, R.lr2r, R.mats2, R.t2r, dot_tn, p_values)


def chunk_rows(D, j):
    lane = iota((1, CHUNK), 1)
    local = 16 * ((lane % LANES) // 64) + 2 * j + lane // LANES
    return local, hot_bf16(iota((256, CHUNK), 0) == 32 * D.s + local)


def near_rows(D):
    return hot_bf16(iota((256, CHUNK), 0) == 64 * D.r + iota((256, CHUNK), 1) % 64)


def p_still(R, D):
    dist = column(R.w_ds[...])
    inv_k = 1.0 / R.ca.shape[1]
    R.at8[...] = jnp.zeros((8, 256), F32)
    R.at8[0:3, :] = R.at[...]
    R.la8[...] = jnp.zeros((8, 32), F32)
    R.la8[0:3, :] = R.adj_l[...]
    R.nodet[...] = dot_tn(R.vet[...].astype(BF16), R.w_nd[...]).T
    R.dmean[...] = dot_nt(R.w_up[...], R.adj_v[...].astype(BF16))
    near = near_rows(D)
    R.nbase[...] = pick_nn(R.nodet[64:, :], near, 2)
    R.cbase[...] = pick_nn(R.at8[...], near, 3)
    R.nb_f[...] = R.ca[...].astype(F32)

    @pl.loop(0, 8, unroll=2)
    def _(j):
        here = chunk_at(j)
        local, row = chunk_rows(D, j)
        mine = hot_bf16(iota((32, CHUNK), 0) == local)
        named = dot_tn(R.nb_f[...].astype(BF16), mine)
        target = (64 * D.r + iota((1, CHUNK), 1) % 64).astype(F32)
        mask = jnp.max(jnp.where(named == target, 1.0, 0.0), 0, keepdims=True) * inv_k
        diff = pick_nn(R.at8[...], row, 3) - R.cbase[...]
        square = 1.0 + jnp.sum(diff * diff, 0, keepdims=True)
        radial = jnp.log(square)
        R.geo[0:8, here] = diff
        R.geo[8:16, here] = pick_nn(R.la8[...], mine, 3)
        R.geo[16:17, here] = radial
        R.geo[17:18, here] = mask
        R.geo[18:19, here] = 2.0 / square
        R.pre[0:64, here] = pick_nn(R.nodet[0:64, :], row, 2) + R.nbase[...] + radial * dist
        R.pre[64:128, here] = pick_nn(R.dmean[...], mine, 2) * mask
        for q in range(2):
            m = 2 * j + q
            both = jnp.concatenate([R.adj_c[m], R.adj_c[16 + m]], 0).astype(F32)
            R.dpair[:, pl.ds(pl.multiple_of(m * LANES, LANES), LANES)] = both.T


def p_turn(R, D):
    gain6 = column(R.g6[...])
    dist = column(R.w_ds[...])
    turn_weight = column(R.w_sl[...])
    R.a_g6[...] = jnp.zeros((128, CHUNK), F32)

    def chunk(j):
        here = chunk_at(j)
        hat, rstd = norm(lane_group(R.st2, j), 0)
        nb6 = (hat * gain6).astype(BF16)
        R.nb6[:, here] = nb6
        update2 = dot_nn(R.wo2t[...], nb6)
        gate2 = sigmoid(dot_nn(R.w2t[512:, :], R.nb5[:, here]))
        pair3 = R.pair2[:, here] + gate2 * update2
        po_b = pair3.astype(BF16)
        R.po[:, here] = po_b
        pre = R.pre[0:64, here] + dot_nn(R.w_edt[...], po_b)
        sig_pre = sigmoid(pre)
        hidden = (pre * sig_pre).astype(BF16)
        R.hid[:, here] = hidden
        msg = dot_tn(R.w_ms[...], hidden)
        sig_msg = sigmoid(msg)
        message = msg * sig_msg
        turn = jnp.tanh(jnp.sum(message * turn_weight, 0, keepdims=True))
        diff = R.geo[0:8, here]
        locadj = R.geo[8:16, here]
        mask = R.geo[17:18, here]
        d_turn = jnp.sum(locadj * diff, 0, keepdims=True) * mask * (1.0 - turn * turn)
        d_message = R.pre[64:128, here] + turn_weight * d_turn
        d_msg = (d_message * sig_msg * (1.0 + msg * (1.0 - sig_msg))).astype(BF16)
        R.dmsg[:, here] = d_msg
        d_pre = dot_nn(R.w_ms[...], d_msg) * sig_pre * (1.0 + pre * (1.0 - sig_pre))
        d_edge = d_pre.astype(BF16)
        R.dedge[:, here] = d_edge
        d_radial = jnp.sum(d_pre * dist, 0, keepdims=True)
        R.pre[0:64, here] = message
        R.pre[64:128, here] = d_pre
        R.geo[19:20, here] = turn * mask
        R.geo[20:21, here] = d_turn
        R.geo[24:32, here] = (d_radial * R.geo[18:19, here]) * diff + locadj * (turn * mask)
        d_pair3 = R.dpair[:, here] + dot_tn(R.w_edt[...], d_edge)
        R.dpair[:, here] = d_pair3
        d_up = (d_pair3 * gate2).astype(BF16)
        R.dup2[:, here] = d_up
        R.dtri2[512:, here] = (d_pair3 * update2 * gate2 * (1.0 - gate2)).astype(BF16)
        d_nb = dot_nn(R.w_io[...], d_up)
        R.a_g6[...] += d_nb * hat
        lane_ungroup(R.st0, j, norm_back(d_nb, gain6, hat, rstd, 0))

    for half in range(2):
        wait_half(R.later, half)
        stage_single(R.t2r, R.st2, half)
        pl.loop(4 * half, 4 * half + 4, unroll=4)(chunk)
        pack_single(R, R.st0, half)
        send_half(D, R.ts, R.dt2r, R.waits, half)


def p_turn_grads(R, D):
    R.g_io[...] = dot_nt(R.nb6[...], R.dup2[...])
    R.g_ed[...] = dot_nt(R.dedge[...], R.po[...])
    R.g_ms[...] = dot_nt(R.hid[...], R.dmsg[...])
    R.gg6[...] = jnp.sum(R.a_g6[...], 1, keepdims=True)
    R.g_ds[...] = jnp.sum(R.pre[64:128, :] * R.geo[16:17, :], 1, keepdims=True)
    R.g_sl[...] = jnp.sum(R.pre[0:64, :] * R.geo[20:21, :], 1, keepdims=True)
    for acc in (R.s_mean, R.s_own, R.s_other):
        acc[...] = jnp.zeros(acc.shape, F32)
    R.s_xyz[...] = jnp.zeros((16, 256), F32)

    @pl.loop(0, 8, unroll=2)
    def _(j):
        here = chunk_at(j)
        _, row = chunk_rows(D, j)
        near = near_rows(D)
        d_pre = R.pre[64:128, here]
        d_diff = R.geo[24:32, here]
        R.s_mean[...] += pick_nt(R.pre[0:64, here] * R.geo[17:18, here], row, 2)
        R.s_own[...] += pick_nt(d_pre, row, 2)
        R.s_other[...] += pick_nt(d_pre, near, 2)
        R.s_xyz[0:8, :] += pick_nt(R.geo[0:8, here] * R.geo[19:20, here], row, 2)
        R.s_xyz[8:16, :] += pick_nt(d_diff, row, 2) - pick_nt(d_diff, near, 2)
        for q in range(2):
            m = 2 * j + q
            at = pl.ds(pl.multiple_of(m * LANES, LANES), LANES)
            out = R.po[:, at].astype(F32).T.astype(BF16)
            R.pair_out[m] = out[:64]
            R.pair_out[16 + m] = out[64:]

    R.leave("pair_out")


def p_turn_rest(R, D):
    p_turn_grads(R, D)
    p_sum0(R, D)
    for half in range(2):
        stage_single(R.t1r, R.st2, half)


def p_back2(R, D):
    tri_backward(
        R,
        D,
        R.dt2r,
        R.mats2,
        R.dlr2r,
        (lambda a, b, d: dot_nt(b, d), lambda a, b, d: dot_nn(a, d)),
        p_turn_rest,
    )


def gates_back(R, d_tri, w_t, nb_here, j):
    here = chunk_at(j)
    for k, stage in ((0, R.st0), (1, R.st1)):
        grad = lane_group(stage, j)
        linear = dot_nn(w_t[256 * k : 256 * k + 256, :], nb_here)
        gate = sigmoid(linear[128:])
        d_first = grad * gate
        d_tri[256 * k : 256 * k + 128, here] = d_first.astype(BF16)
        d_tri[256 * k + 128 : 256 * k + 256, here] = (
            d_first * linear[:128] * (1.0 - gate)
        ).astype(BF16)


def p_between(R, D):
    gain4 = column(R.g4[...])
    gain5 = column(R.g5[...])
    R.a_g4[...] = jnp.zeros((128, CHUNK), F32)
    R.a_g5[...] = jnp.zeros((128, CHUNK), F32)
    next(R.sum0)

    def chunk(j):
        here = chunk_at(j)
        gates_back(R, R.dtri2, R.w2t, R.nb5[:, here], j)
        d_nb5 = dot_nn(R.w_ii[...], R.dtri2[:, here])
        hat5, rstd5 = norm(R.pair2[:, here], 0)
        R.a_g5[...] += d_nb5 * hat5
        d_pair2 = R.dpair[:, here] + norm_back(d_nb5, gain5, hat5, rstd5, 0)
        R.dpair[:, here] = d_pair2
        gate = sigmoid(dot_nn(R.w1t[512:, :], R.nb3[:, here]))
        update = dot_nn(R.wo1t[...], R.nb4[:, here])
        d_up = (d_pair2 * gate).astype(BF16)
        R.dup1[:, here] = d_up
        R.dtri1[512:, here] = (d_pair2 * update * gate * (1.0 - gate)).astype(BF16)
        d_nb4 = dot_nn(R.w_to[...], d_up)
        hat4, rstd4 = norm(lane_group(R.st2, j), 0)
        R.a_g4[...] += d_nb4 * hat4
        lane_ungroup(R.st3, j, norm_back(d_nb4, gain4, hat4, rstd4, 0))

    for half in range(2):
        wait_half(R.later, half)
        stage_both(R, R.dlr2r, half)
        pl.loop(4 * half, 4 * half + 4, unroll=4)(chunk)
        pack_single(R, R.st3, half)
        send_half(D, R.ts, R.dt1r, R.waits, half)


def p_between_grads(R, D):
    R.g_ii[...] = dot_nt(R.nb5[...], R.dtri2[...])
    R.g_to[...] = dot_nt(R.nb4[...], R.dup1[...])
    R.gg5[...] = jnp.sum(R.a_g5[...], 1, keepdims=True)
    R.gg4[...] = jnp.sum(R.a_g4[...], 1, keepdims=True)
    p_sum1(R, D)
    next(R.sum0)


def p_back1(R, D):
    tri_backward(
        R,
        D,
        R.dt1r,
        R.mats1,
        R.dlr1r,
        (lambda a, b, d: dot_nn(d, b), lambda a, b, d: dot_tn(d, a)),
        p_between_grads,
    )


def p_pair_end(R, D):
    next(R.sum0)
    next(R.sum1)
    gain3 = column(R.g3[...])
    R.a_g3[...] = jnp.zeros((128, CHUNK), F32)
    inverse = 1.0 / count_of(R)

    def chunk(j):
        here = chunk_at(j)
        gates_back(R, R.dtri1, R.w1t, R.nb3[:, here], j)
        d_nb3 = dot_nn(R.w_ti[...], R.dtri1[:, here])
        hat3, rstd3 = norm(R.pair1[:, here], 0)
        R.a_g3[...] += d_nb3 * hat3
        d_pair1 = R.dpair[:, here] + norm_back(d_nb3, gain3, hat3, rstd3, 0)
        for q in range(2):
            m = 2 * j + q
            out = d_pair1[:, q * LANES : (q + 1) * LANES].T
            R.pair_grad[m] = out[:64]
            R.pair_grad[16 + m] = out[64:]
            small = (out * inverse).astype(BF16)
            R.dopm[m] = small[:64]
            R.dopm[16 + m] = small[64:]

    for half in range(2):
        wait_half(R.later, half)
        stage_both(R, R.dlr1r, half)
        pl.loop(4 * half, 4 * half + 4, unroll=4)(chunk)
    R.leave("pair_grad")


def p_pair_grads(R, D):
    R.g_ti[...] = dot_nt(R.nb3[...], R.dtri1[...])
    R.gg3[...] = jnp.sum(R.a_g3[...], 1, keepdims=True)


def p_outer_back(R, D):
    R.rt[...] = R.rall[...].T.astype(BF16)
    R.dright[...] = jnp.zeros((64, 1024), F32)
    R.dleft[...] = jnp.zeros((32, 1024), F32)

    @pl.loop(0, 4)
    def _(k):
        grad = jnp.concatenate([R.dopm[8 * k + u] for u in range(8)], 1)
        R.dright[...] += dot_nt(grad, jnp.concatenate([R.zb[8 * k + u] for u in range(8)], 1))

    @pl.loop(0, 4)
    def _(g):
        right = R.rt[pl.ds(pl.multiple_of(256 * g, 256), 256), :]

        @pl.loop(0, 16, unroll=16)
        def _(k):
            grad = jnp.concatenate([R.dopm[2 * k], R.dopm[2 * k + 1]], 1)
            both = dot_nn(right, grad).astype(BF16)
            for h in range(2):
                at = pl.ds(pl.multiple_of(64 * k + 32 * h, 32), 32)
                for u in range(8):
                    block = both[32 * u : 32 * u + 32, LANES * h : LANES * h + LANES]
                    R.zb[8 * g + u, at, :] = block

        weights = jnp.concatenate([outer_weight(R, 8 * g + u) for u in range(8)], 1)
        R.dleft[...] += dot_nt(weights, jnp.concatenate([R.zb[8 * g + u] for u in range(8)], 1))

    for q in range(4):
        R.dls[q] = R.dleft[:, 256 * q : 256 * q + 256].astype(BF16)


def p_outer_grads(R, D):
    @pl.loop(0, 4)
    def _(g):
        rows = jnp.concatenate([R.zb[8 * g + u] for u in range(8)], 1)
        total = dot_nn(R.lt[...], rows)
        for u in range(8):
            R.st1[pl.ds(8 * g + u, 32, stride=32), :] = total[:, LANES * u : LANES * u + LANES]

    R.g_oo[...] = R.st1[0:1024, :]


def p_outer_return(R, D):
    send, recv = R.back_send, R.back_recv
    column_res = D.s // 2
    owner = 2 * D.r + D.s // 4

    def left(q, slot):
        peer = (4 * (D.s % 2) + q, column_res)
        return remote(R.dls.at[q], R.dlr.at[slot], send.at[q], recv.at[slot], peer)

    for q in range(4):
        mine = (4 * (D.s % 2) + q == D.s) & (column_res == D.r)

        @pl.when(jnp.logical_not(mine))
        def _():
            left(q, D.r).start()

        @pl.when(mine)
        def _():
            R.dlr[D.r] = R.dls[q]

    def right(t):
        peer = seq_peers(D, t)
        at = pl.ds(pl.multiple_of(8 * peer[0], 8), 8)
        return remote(R.dright.at[at], R.drr.at[D.s], send.at[4 + t], recv.at[4 + t], peer)

    @pl.loop(1, 8)
    def _(t):
        right(t).start()

    R.drr[D.s] = R.dright[pl.ds(pl.multiple_of(8 * D.s, 8), 8), :]
    p_pair_grads(R, D)
    p_outer_grads(R, D)
    p_sum2(R, D)
    next(R.sum0, D)
    next(R.sum1)

    for q in range(4):
        mine = (4 * (D.s % 2) + q == D.s) & (column_res == D.r)
        theirs = (owner == D.s) & (D.r == q)

        @pl.when(jnp.logical_not(mine))
        def _():
            left(q, q).wait_send()

        @pl.when(jnp.logical_not(theirs))
        def _():
            left(q, q).wait_recv()

    @pl.loop(1, 8)
    def _(t):
        right(t).wait()


def p_attention_back(R, D):
    flag_rows = flag_column(R.fl[...].astype(F32))
    live = (flag_rows > 0).astype(F32)
    left = R.dlr[0].astype(F32)
    for k in range(1, 4):
        left += R.dlr[k].astype(F32)
    right = R.drr[0]
    for k in range(1, 8):
        right += R.drr[k]
    wide = jnp.concatenate([left, jnp.zeros((96, 256), F32)], 0).T
    spread = dot_nn(
        hot_bf16(iota((256, 8), 0) // 32 == iota((256, 8), 1)), right.astype(BF16)
    )
    kept = iota((256, 1024), 0) % 32 == iota((256, 1024), 1) % 32
    spread = jnp.where(kept, spread, 0.0).astype(BF16)
    back = hot_bf16(32 + iota((1024, LANES), 0) // 32 == iota((1024, LANES), 1))
    d_in = ((wide + dot_nn(spread, back)) * live).astype(BF16)[:, :64]
    hat2, rstd2 = norm(R.msan[...], -1)
    normed2 = (hat2 * R.g2[...]).astype(BF16)
    R.g_oi[...] = dot_tn(d_in, normed2)
    d_normed2 = dot_nn(d_in, R.w_oit[...])
    R.gg2[...] = jnp.sum(d_normed2 * hat2, 0, keepdims=True)
    d_later = R.ac[...] + norm_back(d_normed2, R.g2[...], hat2, rstd2, -1)
    R.dlater[...] = d_later
    d_exit = d_later.astype(BF16)
    gate = sigmoid(R.gl[...])
    gated = (gate * R.att[...]).astype(BF16)
    R.g_ao[...] = dot_tn(gated, d_exit)
    d_gated = dot_nt(d_exit, R.w_ao[...])
    R.datt[...] = (d_gated * gate).astype(BF16)
    R.dproj[:, 768:] = (d_gated * R.att[...] * gate * (1.0 - gate)).astype(BF16)
    hat, rstd = norm(R.xc[...], -1)
    R.normed[...] = (hat * R.g1[...]).astype(BF16)
    R.c_gate[...] = dot_tn(R.normed[...], R.dproj[:, 768:])
    p_sum3(R, D)
    R.dqkv[...] = jnp.zeros((256, 768), F32)
    next(R.sum2)

    @pl.loop(0, 8, unroll=4)
    def _(head):
        lanes = iota((1, 256), 1) // 32
        mine = lanes == head
        hot = hot_bf16(mine)
        query = R.qkv[:, 0:256]
        keys = R.qkv[:, 256:512]
        probs = head_probs(keys, query, flag_rows, head)
        d_att = R.datt[...]
        d_probs = dot_nt(R.qkv[:, 512:768], d_att * hot)
        total = jnp.sum(probs * d_probs, 0, keepdims=True)
        d_scores = (probs * (d_probs - total) * (32 ** (-0.5))).astype(BF16)
        R.dqkv[:, 0:256] += jnp.where(mine, dot_tn(d_scores, keys), 0.0)
        R.dqkv[:, 256:512] += jnp.where(mine, dot_nn(d_scores, query), 0.0)
        R.dqkv[:, 512:768] += jnp.where(mine, dot_nn(probs.astype(BF16), d_att), 0.0)

    R.dproj[:, :768] = R.dqkv[...].astype(BF16)
    R.c_qkv[...] = dot_tn(R.normed[...], R.dproj[:, :768])
    d_normed = dot_nt(R.dproj[...], R.w_qkvg[...])
    hat, rstd = norm(R.xc[...], -1)
    R.dlater[...] += norm_back(d_normed, R.g1[...], hat, rstd, -1)
    group_columns(R, R.dlater, R.gsend)


def group_columns(R, value, send):
    R.sp0[...] = value[:, :LANES]
    R.sp1[...] = value[:, LANES:]
    for d in range(8):
        for q in range(2):
            parts = []
            for k in range(2):
                rows = pl.ds(4 * d + 2 * q + k, 8, stride=32)
                parts.append(jnp.concatenate([R.sp0[rows, :], R.sp1[rows, :]], 1))
            send[d, q] = jnp.concatenate(parts, 0).astype(BF16)


def ungroup_columns(recv, target):
    for q in range(2):
        blocks = [recv[d, q].astype(F32) for d in range(8)]
        for k in range(2):
            rows = jnp.concatenate([block[8 * k : 8 * k + 8] for block in blocks], 0)
            target[2 * q + k] = rows.astype(target.dtype)


def p_send_value(R, D):
    group_columns(R, R.msan, R.osend)
    R.wait_value = start_columns(D, R.osend, R.orecv)


def p_values(R, D):
    p_send_value(R, D)
    R.wait_value()
    ungroup_columns(R.orecv, R.msa_out)
    R.leave("msa_out")
    R.wait_adjoint()
    unpack_columns(R, R.arecv, R.ac)


SEGMENTS = (
    dict(
        g_io=(128, 128),
        s_mean=(64, 256),
        s_own=(64, 256),
        s_other=(64, 256),
        s_vadj=(64, 256),
        s_xyz=(16, 256),
        g_ed=(64, 128),
        g_ms=(64, 64),
        small0=(16, 128),
    ),
    dict(g_ii=(128, 640), g_to=(128, 128), small1=(16, 128)),
    dict(g_ti=(128, 640), g_oo=(1024, 128), small2=(16, 128)),
    dict(g_ao=(256, 256), c_gate=(256, 256), g_oi=(64, 256), small3=(16, 128)),
    dict(c_qkv=(256, 768)),
)


def segment_layout(index):
    layout = []
    start = 0
    for name, (rows, cols) in SEGMENTS[index].items():
        for lane in range(0, cols, LANES):
            layout.append((name, start, rows, lane, min(LANES, cols - lane)))
            start += rows
    return layout, -(-start // 512) * 512


def pack_segment(R, index):
    layout, total = segment_layout(index)
    pay = R.pay[index]
    for name, start, count, lane, width in layout:
        value = getattr(R, name)[:, lane : lane + width]
        pay[start : start + count, 0:width] = value.astype(BF16)
    end = layout[-1][1] + layout[-1][2]
    if end < total:
        pay[end:total, :] = jnp.zeros((total - end, LANES), BF16)


def rows_of(index, size):
    return pl.ds(pl.multiple_of(index * size, size), size)


def sum_segment(R, D, index):
    pay, full = R.pay[index], R.full[index]
    first, second, third, fourth = (table[index] for table in R.parts)
    eighth = pay.shape[0] // 8
    part = eighth // 4
    pack_segment(R, index)
    first[D.s] = pay[rows_of(D.s, eighth), :]
    most = pl.ds(0, eighth * (D.ns - 1))
    wait = start_seq(
        D, lambda i: pay.at[rows_of(i, eighth)], lambda i: first.at[i], pay.at[most]
    )
    yield
    wait()
    total = first[0].astype(F32)
    for k in range(1, 8):
        total += first[k].astype(F32)
    second[...] = total.astype(BF16)
    third[D.r] = second[rows_of(D.r, part), :]
    some = pl.ds(0, part * (D.nr - 1))
    wait = start_res(
        D, lambda i: second.at[rows_of(i, part)], lambda i: third.at[i], second.at[some]
    )
    yield
    wait()
    total = third[0].astype(F32)
    for k in range(1, 4):
        total += third[k].astype(F32)
    fourth[...] = total.astype(BF16)
    mine = pl.ds(pl.multiple_of(D.s * eighth + D.r * part, part), part)
    full[mine, :] = fourth[...]
    wait = start_res(D, lambda i: fourth, lambda i: full.at[mine], full.at[some])
    yield
    wait()
    wait = start_seq(
        D,
        lambda i: full.at[rows_of(D.s, eighth)],
        lambda i: full.at[rows_of(i, eighth)],
        full.at[most],
    )
    yield
    wait()
    R.leave(index)


def p_sum0(R, D):
    place = hot_bf16(iota((32, 256), 1) == 32 * D.s + iota((32, 256), 0))
    first = jnp.where(D.r == 0, 1.0, 0.0)
    R.s_vadj[...] = dot_tn(R.adj_v[...].astype(BF16), place) * first
    small_rows(R, R.small0, (R.gg6, R.g_ds, R.g_sl))
    R.sum0 = sum_segment(R, D, 0)
    next(R.sum0)


def small_rows(R, target, values):
    R.small[...] = jnp.zeros((128, LANES), F32)
    for k, value in enumerate(values):
        R.small[0 : value.shape[0], k : k + 1] = value[...]
    target[...] = R.small[...].T[:16]


def p_sum1(R, D):
    small_rows(R, R.small1, (R.gg5, R.gg4))
    R.sum1 = sum_segment(R, D, 1)
    next(R.sum1)


def p_sum2(R, D):
    small_rows(R, R.small2, (R.gg3,))
    R.sum2 = sum_segment(R, D, 2)
    next(R.sum2)


def p_sum3(R, D):
    R.small3[...] = jnp.zeros((16, LANES), F32)
    for half in range(2):
        R.small3[half : half + 1, :] = R.gg2[:, LANES * half : LANES * half + LANES]
    R.sum3 = sum_segment(R, D, 3)
    next(R.sum3)


def p_sums(R, D):
    R.sum4 = sum_segment(R, D, 4)
    next(R.sum4)
    wait = start_columns(D, R.gsend, R.grecv)
    next(R.sum1)
    next(R.sum2)
    next(R.sum3)
    next(R.sum1, D)
    next(R.sum2)
    next(R.sum3)
    wait()
    ungroup_columns(R.grecv, R.msa_grad)
    R.leave("msa_grad")
    next(R.sum4)
    next(R.sum2, D)
    next(R.sum3)
    next(R.sum4)
    next(R.sum3, D)
    next(R.sum4)
    next(R.sum4, D)


def unpack_segment(R, index):
    held = {}
    for name, start, count, lane, width in segment_layout(index)[0]:
        value = R.full[index][start : start + count, 0:width].astype(F32)
        if name.startswith("g_"):
            getattr(R, "o_" + name)[:, lane : lane + width] = value
        else:
            held.setdefault(name, []).append(value)
    return {name: jnp.concatenate(parts, 1) for name, parts in held.items()}


def p_finish(R, D):
    R.arrived(1)
    small = unpack_segment(R, 1)["small1"]
    R.o_gg5[...] = small[0:1]
    R.o_gg4[...] = small[1:2]
    R.leave(R.o_g_ii)
    R.arrived(2)
    R.o_gg3[...] = unpack_segment(R, 2)["small2"][0:1]
    R.leave(R.o_g_ti, R.o_g_oo)
    R.arrived(3)
    held = unpack_segment(R, 3)
    R.leave(R.o_g_ao)
    for half in range(2):
        R.o_gg2[:, LANES * half : LANES * half + LANES] = held["small3"][half : half + 1]
    R.o_g_qkvg[:, 768:] = held["c_gate"]
    R.arrived(4)
    R.o_g_qkvg[:, :768] = unpack_segment(R, 4)["c_qkv"]
    R.leave(R.o_g_qkvg)
    R.pass_on()
    R.arrived(5)
    total = jnp.sum(R.w_far[...].astype(F32) * R.o_g_qkvg[...], 1, keepdims=True)
    eye = iota((256, 256), 0) == iota((256, 256), 1)
    R.o_gg1[...] = jnp.sum(jnp.where(eye, total, 0.0), 0, keepdims=True) / R.g1[...]
    R.arrived(0)
    held = unpack_segment(R, 0)
    small = held["small0"]
    R.o_gg6[...] = small[0:1]
    R.o_g_ds[...] = small[1:2, :64]
    R.o_g_sl[...] = small[2:3, :64]
    mean_b = held["s_mean"].astype(BF16)
    R.o_g_up[...] = dot_nt(mean_b, held["s_vadj"].astype(BF16))
    d_node = jnp.concatenate([held["s_own"], held["s_other"]], 0).astype(BF16)
    R.o_g_nd[...] = dot_nt(R.vet[...].astype(BF16), d_node)
    step = dot_tn(R.w_up[...], mean_b)
    grad = dot_nn(R.w_nd[...], d_node)
    R.rows_f[...] = jnp.concatenate([step + R.vet[...], grad], 0).T
    here = pl.ds(pl.multiple_of(32 * D.s, 32), 32)
    mine = R.rows_f[here, :]
    R.single_out[...] = mine[:, :64]
    R.single_grad[...] = R.adj_v[...] + mine[:, 64:]
    R.xyz[...] = jnp.zeros((128, 256), F32)
    R.xyz[0:16, :] = held["s_xyz"]
    R.xyz[16:19, :] = R.at[...]
    R.rows_g[...] = R.xyz[...].T
    turned = R.rows_g[here, :]
    back = jnp.concatenate([turned, jnp.zeros((96, 128), F32)], 0).T
    R.coords_out[...] = back[16:19, 0:32] + back[0:3, 0:32]
    R.coords_grad[...] = R.adj_l[...] + back[8:11, 0:32]


KEPT = dict(
    xsend=((8, 2, 16, 256), BF16),
    xrecv=((8, 2, 16, 256), BF16),
    asend=((8, 2, 16, 256), BF16),
    arecv=((8, 2, 16, 256), BF16),
    osend=((8, 2, 16, 256), BF16),
    orecv=((8, 2, 16, 256), BF16),
    gsend=((8, 2, 16, 256), BF16),
    grecv=((8, 2, 16, 256), BF16),
    wst=((1024, 128), F32),
    lt=((32, 1024), BF16),
    tm=((2, 256, 256), F32),
    geo=((32, 2048), F32),
    pre=((128, 2048), F32),
    small0=((16, 128), F32),
    small1=((16, 128), F32),
    small2=((16, 128), F32),
    small3=((16, 128), F32),
    xc=((256, 256), F32),
    ac=((256, 256), F32),
    sp0=((256, 128), F32),
    sp1=((256, 128), F32),
    qkv=((256, 768), BF16),
    gl=((256, 256), F32),
    att=((256, 256), F32),
    msan=((256, 256), F32),
    lsend=((32, 256), BF16),
    rsend=((8, 1024), F32),
    lall=((4, 32, 256), BF16),
    rall=((64, 1024), F32),
    st0=((2048, 128), F32),
    st1=((2048, 128), F32),
    st2=((2048, 128), F32),
    st3=((2048, 128), F32),
    l2=((1024, 32), BF16),
    zb=((32, 1024, 128), BF16),
    pair1=((128, 2048), F32),
    pair2=((128, 2048), F32),
    dpair=((128, 2048), F32),
    w1t=((640, 128), BF16),
    w2t=((640, 128), BF16),
    wo1t=((128, 128), BF16),
    wo2t=((128, 128), BF16),
    nb3=((128, 2048), BF16),
    nb4=((128, 2048), BF16),
    nb5=((128, 2048), BF16),
    nb6=((128, 2048), BF16),
    po=((128, 2048), BF16),
    hid=((64, 2048), BF16),
    dmsg=((64, 2048), BF16),
    dedge=((64, 2048), BF16),
    dup1=((128, 2048), BF16),
    dup2=((128, 2048), BF16),
    dtri1=((640, 2048), BF16),
    dtri2=((640, 2048), BF16),
    mats1=((8, 256, 256), BF16),
    mats2=((8, 256, 256), BF16),
    dm=((2, 256, 256), BF16),
    lrs=((32, 128, 128), BF16),
    lr1r=((32, 128, 128), BF16),
    lr2r=((32, 128, 128), BF16),
    dlr1r=((32, 128, 128), BF16),
    dlr2r=((32, 128, 128), BF16),
    ts=((32, 64, 128), BF16),
    t1r=((32, 64, 128), BF16),
    t2r=((32, 64, 128), BF16),
    dt1r=((32, 64, 128), BF16),
    dt2r=((32, 64, 128), BF16),
    at8=((8, 256), F32),
    la8=((8, 32), F32),
    nodet=((128, 256), F32),
    dmean=((64, 32), F32),
    nbase=((64, 256), F32),
    cbase=((8, 256), F32),
    nb_f=((32, 64), F32),
    s_mean=((64, 256), F32),
    s_own=((64, 256), F32),
    s_other=((64, 256), F32),
    s_vadj=((64, 256), F32),
    s_xyz=((16, 256), F32),
    a_g3=((128, 256), F32),
    a_g4=((128, 256), F32),
    a_g5=((128, 256), F32),
    a_g6=((128, 256), F32),
    gg3=((128, 1), F32),
    gg4=((128, 1), F32),
    gg5=((128, 1), F32),
    gg6=((128, 1), F32),
    gg2=((1, 256), F32),
    g_ds=((64, 1), F32),
    g_sl=((64, 1), F32),
    g_io=((128, 128), F32),
    g_to=((128, 128), F32),
    g_ti=((128, 640), F32),
    g_ii=((128, 640), F32),
    g_ed=((64, 128), F32),
    g_ms=((64, 64), F32),
    g_oo=((1024, 128), F32),
    g_oi=((64, 256), F32),
    g_ao=((256, 256), F32),
    c_gate=((256, 256), F32),
    c_qkv=((256, 768), F32),
    normed=((256, 256), BF16),
    small=((128, 128), F32),
    dopm=((32, 64, 128), BF16),
    rt=((1024, 64), BF16),
    dright=((64, 1024), F32),
    dleft=((32, 1024), F32),
    dls=((4, 32, 256), BF16),
    dlr=((4, 32, 256), BF16),
    drr=((8, 8, 1024), F32),
    dlater=((256, 256), F32),
    datt=((256, 256), BF16),
    dproj=((256, 1024), BF16),
    dqkv=((256, 768), F32),
)
SIZES = [segment_layout(index)[1] for index in range(len(SEGMENTS))]
PAYLOADS = [((size, 128), BF16) for size in SIZES]
PARTIAL = (
    [((8, size // 8, 128), BF16) for size in SIZES]
    + [((size // 8, 128), BF16) for size in SIZES]
    + [((4, size // 32, 128), BF16) for size in SIZES]
    + [((size // 32, 128), BF16) for size in SIZES]
)
LARGE = ("msa_out", "pair_out", "msa_grad", "pair_grad")
MOVED_IN = ("adj_a", "w_qkvg", "w_ao", "w_oo", "w_ti", "w_ii", "pe", "adj_c")
BIG = ("o_g_ii", "o_g_ti", "o_g_oo", "o_g_ao", "o_g_qkvg")
FINISH = ("g1", "vet", "w_up", "w_nd", "adj_v", "at", "adj_l")
FINISH_KEPT = dict(
    rows_f=((256, 128), F32), rows_g=((256, 128), F32), xyz=((128, 256), F32)
)
RESULTS = dict(
    msa_out=((4, 64, 256), BF16),
    pair_out=((32, 64, 128), BF16),
    single_out=((32, 64), F32),
    coords_out=((3, 32), F32),
    msa_grad=((4, 64, 256), F32),
    pair_grad=((32, 64, 128), F32),
    single_grad=((32, 64), F32),
    coords_grad=((3, 32), F32),
    o_gg1=((1, 256), F32),
    o_g_qkvg=((256, 1024), F32),
    o_g_ao=((256, 256), F32),
    o_gg2=((1, 256), F32),
    o_g_oi=((64, 256), F32),
    o_g_oo=((1024, 128), F32),
    o_gg3=((1, 128), F32),
    o_g_ti=((128, 640), F32),
    o_gg4=((1, 128), F32),
    o_g_to=((128, 128), F32),
    o_gg5=((1, 128), F32),
    o_g_ii=((128, 640), F32),
    o_gg6=((1, 128), F32),
    o_g_io=((128, 128), F32),
    o_g_nd=((64, 128), F32),
    o_g_ed=((64, 128), F32),
    o_g_ds=((1, 64), F32),
    o_g_ms=((64, 64), F32),
    o_g_sl=((1, 64), F32),
    o_g_up=((64, 64), F32),
)

STEPS = (
    p_spread,
    p_attention,
    p_outer_exchange,
    p_outer,
    p_entry1,
    p_tri1,
    p_middle,
    p_tri2,
    p_turn,
    p_back2,
    p_between,
    p_back1,
    p_pair_end,
    p_outer_back,
    p_outer_return,
    p_attention_back,
    p_sums,
)
EXCHANGES = 56


class Device:
    def __init__(self, n_seq, n_res, sems, rows_in):
        self.s, self.r = lax.axis_index("seq"), lax.axis_index("res")
        self.ns, self.nr = n_seq, n_res
        self.sems = sems
        self.rows_in = rows_in
        self.used = 0

    def take(self):
        self.used += 2
        assert self.used <= 2 * EXCHANGES
        return self.sems.at[self.used - 2], self.sems.at[self.used - 1]

    def ready(self):
        pl.semaphore_wait(pltpu.get_barrier_semaphore(), self.ns + self.nr - 2)

        @pl.loop(1, self.nr)
        def _(t):
            pl.semaphore_signal(self.rows_in, inc=1, device_id=res_peers(self, t), device_id_type=MESH)

    def all_ready(self):
        pl.semaphore_wait(self.rows_in, self.nr - 1)


def first_kernel(n_seq, n_res, names, *refs):
    refs = list(refs)
    far = {name: refs.pop(0) for name in names}
    far_full = [refs.pop(0) for _ in SIZES]
    R = SimpleNamespace(**far)
    R.__dict__.update({name: refs.pop(0) for name in (*KEPT, *MOVED_IN, *LARGE)})
    tables = [[refs.pop(0) for _ in SIZES] for _ in range(6)]
    R.full, R.pay, R.parts = tables[0], tables[1], tables[2:]
    R.waits, R.later = {}, {}
    R.out_send, R.out_recv, R.back_send, R.back_recv, R.move = refs[2:]
    D = Device(n_seq, n_res, refs[0], refs[1])
    barrier = pltpu.get_barrier_semaphore()

    for peers, count in ((seq_peers, n_seq), (res_peers, n_res)):

        @pl.loop(1, count)
        def _(t):
            pl.semaphore_signal(barrier, inc=1, device_id=peers(D, t), device_id_type=MESH)

    moves = {}
    for name in MOVED_IN:
        moves[name] = pltpu.make_async_copy(far[name], getattr(R, name), R.move.at[len(moves)])
        moves[name].start()
    R.arrived = lambda *wanted: [moves.pop(name).wait() for name in wanted]
    base = len(moves)
    out = []

    def leave(name):
        if name in far:
            source, target, at = getattr(R, name), far[name], LARGE.index(name)
        else:
            source, target, at = R.full[name], far_full[name], len(LARGE) + name
        out.append(pltpu.make_async_copy(source, target, R.move.at[base + at]))
        out[-1].start()

    R.leave = leave
    for step in STEPS:
        step(R, D)
    for copy in out:
        copy.wait()


def last_kernel(n_seq, n_res, names, *refs):
    refs = list(refs)

    def some(wanted):
        return {name: refs.pop(0) for name in wanted}

    far_in = [refs.pop(0) for _ in range(len(SIZES) + 1)]
    far_large = some(LARGE)
    R = SimpleNamespace(**some(FINISH))
    away = some((*LARGE, *BIG))
    R.__dict__.update(some(names))
    R.__dict__.update(some((*FINISH_KEPT, *LARGE, *BIG)))
    near_in = [refs.pop(0) for _ in far_in]
    (sems,) = refs
    R.full, R.w_far = near_in[:-1], near_in[-1]
    used = []

    def move(source, target):
        copy = pltpu.make_async_copy(source, target, sems.at[len(used)])
        copy.start()
        used.append(copy)
        return copy

    order = (1, 2, 3, 4, 5, 0)
    coming = {k: move(far_in[k], near_in[k]) for k in order}
    passing = [(name, move(far_large[name], getattr(R, name))) for name in LARGE]
    going = []

    def leave(*values):
        for name in BIG:
            if any(getattr(R, name) is value for value in values):
                going.append(move(getattr(R, name), away[name]))

    def pass_on():
        for name, copy in passing:
            copy.wait()
            going.append(move(getattr(R, name), away[name]))

    R.arrived, R.leave, R.pass_on = lambda k: coming[k].wait(), leave, pass_on
    p_finish(R, Device(n_seq, n_res, None, None))
    for copy in going:
        copy.wait()


ARGS = dict(
    x=(4, 64, 256),
    pe=(32, 64, 128),
    vet=(256, 64),
    at=(3, 256),
    fl=(32,),
    ca=(32, 64),
    g1=(256,),
    w_qkvg=(256, 1024),
    w_ao=(256, 256),
    g2=(256,),
    w_oit=(256, 64),
    w_oo=(1024, 128),
    g3=(128,),
    w_ti=(128, 640),
    g4=(128,),
    w_to=(128, 128),
    g5=(128,),
    w_ii=(128, 640),
    g6=(128,),
    w_io=(128, 128),
    w_nd=(64, 128),
    w_edt=(128, 64),
    w_ds=(64,),
    w_ms=(64, 64),
    w_sl=(64,),
    w_up=(64, 64),
    adj_a=(4, 64, 256),
    adj_c=(32, 64, 128),
    adj_v=(32, 64),
    adj_l=(3, 32),
)


def fits(n_seq, n_res, args):
    shapes = tuple(tuple(arg.shape) for arg in args)
    return (n_seq, n_res) == (8, 4) and shapes == tuple(ARGS.values())


def fast_shards(n_seq, n_res, *args):
    env = dict(zip(ARGS, args))
    for name, value in tuple(env.items()):
        if value.ndim == 1:
            env[name] = value.reshape(1, -1)
    env.update(vet=env["vet"].T, w_oit=env["w_oit"].T, w_edt=env["w_edt"].T)
    space = pl.BlockSpec(memory_space=pltpu.VMEM)

    def shapes(entries):
        return [jax.ShapeDtypeStruct(*entry) for entry in entries]

    large = {name: RESULTS[name] for name in LARGE}
    anywhere = pl.BlockSpec(memory_space=pl.ANY)
    held = [(ARGS[name], BF16) for name in MOVED_IN] + [RESULTS[name] for name in LARGE]
    values = pl.pallas_call(
        functools.partial(first_kernel, n_seq, n_res, (*env, *large)),
        out_shape=shapes((*large.values(), *PAYLOADS)),
        in_specs=[anywhere if name in MOVED_IN else space for name in env],
        out_specs=[anywhere] * (len(large) + len(PAYLOADS)),
        scratch_shapes=[
            pltpu.VMEM(*entry) for entry in (*KEPT.values(), *held, *PAYLOADS, *PAYLOADS, *PARTIAL)
        ]
        + [pltpu.SemaphoreType.DMA((2 * EXCHANGES,)), pltpu.SemaphoreType.REGULAR]
        + [pltpu.SemaphoreType.DMA((12,))] * 4
        + [pltpu.SemaphoreType.DMA((len(MOVED_IN) + len(LARGE) + len(SIZES),))],
        compiler_params=pltpu.CompilerParams(
            vmem_limit_bytes=62 * 2**20, collective_id=0, has_side_effects=True
        ),
    )(*env.values())
    full = values[len(large) :]
    env.update(zip(large, values))
    apart = {name: RESULTS[name] for name in (*LARGE, *BIG)}
    small = {name: entry for name, entry in RESULTS.items() if name not in apart}
    brought = [*PAYLOADS, (ARGS["w_qkvg"], BF16)]
    values = pl.pallas_call(
        functools.partial(last_kernel, n_seq, n_res, tuple(small)),
        out_shape=shapes((*apart.values(), *small.values())),
        in_specs=[anywhere] * (len(brought) + len(LARGE)) + [space] * len(FINISH),
        out_specs=[anywhere] * len(apart) + [space] * len(small),
        scratch_shapes=[
            pltpu.VMEM(*entry) for entry in (*FINISH_KEPT.values(), *apart.values(), *brought)
        ]
        + [pltpu.SemaphoreType.DMA((len(brought) + len(apart) + len(LARGE),))],
        compiler_params=pltpu.CompilerParams(vmem_limit_bytes=60 * 2**20),
    )(*full, env["w_qkvg"], *[env[name] for name in LARGE], *[env[name] for name in FINISH])
    env.update(zip((*apart, *small), values))
    results = [env[name] for name in RESULTS]
    for index, value in enumerate(results):
        if value.shape[0] == 1:
            results[index] = value.reshape(-1)
    for index in (12, 23):
        results[index] = results[index].T
    return tuple(results)


def solution(mesh):
    n_seq, n_res = mesh.shape["seq"], mesh.shape["res"]

    def body(*args):
        if fits(n_seq, n_res, args):
            return fast_shards(n_seq, n_res, *args)
        return shards(*args)

    return jax.shard_map(
        body,
        mesh=mesh,
        in_specs=(
            P("seq", "res", None),
            P("seq", "res", None),
            P(),
            P(),
            P(),
            P("seq", None),
            P(),
            P(),
            P(),
            P(),
            P(),
            P(),
            P(),
            P(),
            P(),
            P(),
            P(),
            P(),
            P(),
            P(),
            P(),
            P(),
            P(),
            P(),
            P(),
            P(),
            P("seq", "res", None),
            P("seq", "res", None),
            P("seq", None),
            P(None, "seq"),
        ),
        out_specs=(
            P("seq", "res", None),
            P("seq", "res", None),
            P("seq", None),
            P(None, "seq"),
            P("seq", "res", None),
            P("seq", "res", None),
            P("seq", None),
            P(None, "seq"),
            P(),
            P(),
            P(),
            P(),
            P(),
            P(),
            P(),
            P(),
            P(),
            P(),
            P(),
            P(),
            P(),
            P(),
            P(),
            P(),
            P(),
            P(),
            P(),
            P(),
        ),
        check_vma=False,
    )
```

```python
import functools
from types import SimpleNamespace

import jax
import jax.numpy as jnp
from jax import lax
from jax.experimental import pallas as pl
from jax.experimental.pallas import tpu as pltpu
from jax.sharding import PartitionSpec as P

HEADS = 8


EPS = 1e-05
HIGH = lax.Precision.HIGHEST


def spread_2(value, axis, source):
    kept = jnp.where(lax.axis_index(axis) == source, value, 0).astype(value.dtype)
    return lax.psum(kept, axis)


def standardize_lines(value, gain):
    row_mean = jnp.mean(value, -1, keepdims=True)
    centred = value - row_mean
    spread = jnp.mean(centred * centred, -1, keepdims=True)
    return centred * lax.rsqrt(spread + EPS) * gain


def tensor_mean_answer(left, right):
    return jnp.einsum("...c,cd->...d", left, right, preferred_element_type=jnp.float32)


def product_back(grad, right):
    return jnp.einsum("...d,cd->...c", grad, right, preferred_element_type=jnp.float32)


def weight_back(left, grad):
    flat_left = left.reshape(-1, left.shape[-1])
    flat_grad = grad.reshape(-1, grad.shape[-1])
    return jnp.einsum("nc,nd->cd", flat_left, flat_grad, preferred_element_type=jnp.float32)


def attn_scores(query, keys, allowed, scale):
    raw_scores = (
        jnp.einsum("qlhd,klhd->lhqk", query, keys, preferred_element_type=jnp.float32) * scale
    )
    return jnp.where(allowed, raw_scores, -1e30)


def tri_gates(tri_lin):
    quarter = tri_lin.shape[-1] // 4
    left_part = jax.nn.sigmoid(tri_lin[..., quarter : 2 * quarter]) * tri_lin[..., :quarter]
    right_part = (
        jax.nn.sigmoid(tri_lin[..., 3 * quarter :]) * tri_lin[..., 2 * quarter : 3 * quarter]
    )
    return (left_part, right_part)


def edge_front(own_rows, other_near, edge_lin, diff, distance_basis_matrix):
    radial = jnp.log(1.0 + jnp.sum(diff * diff, 0))
    return jax.nn.silu(
        own_rows[:, None, :] + other_near + edge_lin + radial[..., None] * distance_basis_matrix
    )


def edge_finish(msg_lin, signal_location_matrix, diff):
    message = jax.nn.silu(msg_lin)
    turn = jnp.tanh(jnp.einsum("ikc,c->ik", message, signal_location_matrix, precision=HIGH))
    return (jnp.mean(message, 1), jnp.mean(diff * turn[None], 2))


def gather_rows(value):
    return lax.all_gather(value, "seq", axis=0, tiled=True)


def across_res(value):
    return lax.psum(value.astype(jnp.bfloat16), "res").astype(jnp.float32)


def owners_sum(value):
    return lax.psum_scatter(value, "seq", scatter_dimension=0, tiled=True)


def place_home(rows_part, col_width, offset, keep_home):
    empty = jnp.zeros((rows_part.shape[0], col_width, rows_part.shape[2]), jnp.float32)
    return lax.dynamic_update_slice_in_dim(empty, rows_part, offset, 1) * keep_home


def sum_flat(parts):
    flat = jnp.concatenate([jnp.ravel(member) for member in parts])
    summed = lax.psum(flat, ("seq", "res"))
    pieces = []
    offset = 0
    for member in parts:
        pieces.append(summed[offset : offset + member.size].reshape(member.shape))
        offset = offset + member.size
    return pieces


def shards(
    alignment_embedding,
    coupling_embedding,
    vertex_embedding,
    atom_locations,
    chain_existence_flags,
    closest_aminos,
    softmax_mixer_scale_factor,
    attender_stacked_matrix,
    softmax_mixer_exit_matrix,
    tensor_mean_scale_factor,
    tensor_mean_entry_matrix,
    tensor_mean_exit_matrix,
    outbound_entry_scale,
    outbound_entry_matrix,
    outbound_exit_scale,
    outbound_exit_matrix,
    inbound_entry_scale,
    inbound_entry_matrix,
    inbound_exit_scale,
    inbound_exit_matrix,
    vertex_mapping_matrix,
    bond_mapping_matrix,
    distance_basis_matrix,
    signal_matrix,
    signal_location_matrix,
    vertex_change_matrix,
    alignment_adjoint,
    coupling_adjoint,
    vertex_adjoint,
    location_adjoint,
):
    seq_index = lax.axis_index("seq")
    res_index = lax.axis_index("res")
    n_seq = lax.axis_size("seq")
    n_res = lax.axis_size("res")
    chain_shard_piece, vertical_shard_piece, breadth_overall = alignment_embedding.shape
    rows_dev = coupling_embedding.shape[0]
    span_overall, node_width = vertex_embedding.shape
    block_tally = chain_existence_flags.shape[0]
    head_size = breadth_overall // HEADS
    scale = head_size ** (-0.5)
    opm_width = tensor_mean_entry_matrix.shape[1] // 2
    tri_width = outbound_exit_matrix.shape[0]
    chain_exists = (chain_existence_flags > 0).astype(jnp.float32)
    line_indicator_entries = lax.dynamic_slice_in_dim(
        chain_exists, seq_index * chain_shard_piece, chain_shard_piece
    )
    first_res = (res_index == 0).astype(jnp.float32)
    home = seq_index * rows_dev // vertical_shard_piece
    offset = seq_index * rows_dev - home * vertical_shard_piece
    keep_home = (home == res_index).astype(jnp.float32)
    alignment_real_lines = alignment_embedding.astype(jnp.float32)
    standardized_lines, standardize_reverse_alpha = jax.vjp(
        standardize_lines, alignment_real_lines, softmax_mixer_scale_factor
    )
    normed_b = standardized_lines.astype(jnp.bfloat16)
    projected = tensor_mean_answer(normed_b, attender_stacked_matrix)
    query = projected[..., :breadth_overall].astype(jnp.bfloat16)
    keyval = projected[..., breadth_overall : 3 * breadth_overall].astype(jnp.bfloat16)
    attn_gate = jax.nn.sigmoid(projected[..., 3 * breadth_overall :])
    all_keyval = lax.all_gather(keyval, "seq", axis=0, tiled=True)
    query4 = query.reshape(chain_shard_piece, vertical_shard_piece, HEADS, head_size)
    keys4 = all_keyval[..., :breadth_overall].reshape(
        block_tally, vertical_shard_piece, HEADS, head_size
    )
    values4 = all_keyval[..., breadth_overall:].reshape(
        block_tally, vertical_shard_piece, HEADS, head_size
    )
    allowed = chain_exists[None, None, None, :] > 0
    scores = attn_scores(query4, keys4, allowed, scale)
    score_peak = jnp.max(scores, -1, keepdims=True)
    exp_scores = jnp.exp(scores - score_peak)
    exp_total = jnp.sum(exp_scores, -1, keepdims=True)
    log_total = score_peak + jnp.log(exp_total)
    probs_b = (exp_scores / exp_total).astype(jnp.bfloat16)
    attended = jnp.einsum(
        "lhqk,klhd->qlhd", probs_b, values4, preferred_element_type=jnp.float32
    ).reshape(chain_shard_piece, vertical_shard_piece, breadth_overall)
    sigmoid_scaled_lines = (attn_gate * attended).astype(jnp.bfloat16)
    alignment_later = alignment_real_lines + tensor_mean_answer(
        sigmoid_scaled_lines, softmax_mixer_exit_matrix
    )
    standardized_lines2, standardize_reverse_beta = jax.vjp(
        standardize_lines, alignment_later, tensor_mean_scale_factor
    )
    normed2_b = standardized_lines2.astype(jnp.bfloat16)
    outer_in = (
        tensor_mean_answer(normed2_b, tensor_mean_entry_matrix)
        * line_indicator_entries[:, None, None]
    ).astype(jnp.bfloat16)
    everyone = lax.all_gather(outer_in, ("seq", "res"), axis=0, tiled=True)
    blocks = everyone.reshape(n_seq, n_res, chain_shard_piece, vertical_shard_piece, 2 * opm_width)
    home_block = lax.dynamic_index_in_dim(blocks, home, 1, keepdims=False)
    left_rows = lax.dynamic_slice_in_dim(home_block, offset, rows_dev, 2)[..., :opm_width]
    left_rows = left_rows.reshape(block_tally, rows_dev, opm_width)
    right_cols = lax.dynamic_index_in_dim(blocks, res_index, 1, keepdims=False)[..., opm_width:]
    right_cols = right_cols.reshape(block_tally, vertical_shard_piece, opm_width)
    outer_b = jnp.einsum("sic,sjd->ijcd", left_rows, right_cols, preferred_element_type=jnp.float32)
    outer_b = outer_b.reshape(rows_dev, vertical_shard_piece, opm_width * opm_width).astype(
        jnp.bfloat16
    )
    count = jnp.sum(chain_exists)
    pair1 = (
        coupling_embedding.astype(jnp.float32)
        + tensor_mean_answer(outer_b, tensor_mean_exit_matrix) / count
    )
    normed3, norm_back3 = jax.vjp(standardize_lines, pair1, outbound_entry_scale)
    normed3_b = normed3.astype(jnp.bfloat16)
    tri = tensor_mean_answer(normed3_b, outbound_entry_matrix)
    (left_t, right_t), gates_back = jax.vjp(tri_gates, tri[..., : 4 * tri_width])
    left_b = left_t.astype(jnp.bfloat16)
    right_b = right_t.astype(jnp.bfloat16)
    right_all = gather_rows(right_b)
    partial_tri = jnp.einsum("ikc,jkc->ijc", left_b, right_all, preferred_element_type=jnp.float32)
    triangle = lax.psum_scatter(
        partial_tri.astype(jnp.bfloat16), "res", scatter_dimension=1, tiled=True
    ).astype(jnp.float32)
    normed4, norm_back4 = jax.vjp(standardize_lines, triangle, outbound_exit_scale)
    normed4_b = normed4.astype(jnp.bfloat16)
    update = tensor_mean_answer(normed4_b, outbound_exit_matrix)
    out_gate = jax.nn.sigmoid(tri[..., 4 * tri_width :])
    pair2 = pair1 + out_gate * update
    normed5, norm_back5 = jax.vjp(standardize_lines, pair2, inbound_entry_scale)
    normed5_b = normed5.astype(jnp.bfloat16)
    tri2 = tensor_mean_answer(normed5_b, inbound_entry_matrix)
    (left_i, right_i), gates_back2 = jax.vjp(tri_gates, tri2[..., : 4 * tri_width])
    both_local = jnp.concatenate([left_i.astype(jnp.bfloat16), right_i.astype(jnp.bfloat16)], -1)
    both_all = gather_rows(both_local)
    right_all2 = both_all[..., tri_width:]
    left_cand = lax.dynamic_slice_in_dim(both_all[..., :tri_width], offset, rows_dev, 1)
    left_sel = spread_2(left_cand, "res", home)
    triangle2 = jnp.einsum("kic,kjc->ijc", left_sel, right_all2, preferred_element_type=jnp.float32)
    normed6, norm_back6 = jax.vjp(standardize_lines, triangle2, inbound_exit_scale)
    normed6_b = normed6.astype(jnp.bfloat16)
    update2 = tensor_mean_answer(normed6_b, inbound_exit_matrix)
    out_gate2 = jax.nn.sigmoid(tri2[..., 4 * tri_width :])
    coupling_later3 = pair2 + out_gate2 * update2
    pair3_b = coupling_later3.astype(jnp.bfloat16)
    rows_all = lax.all_gather(pair3_b, "res", axis=1, tiled=True)
    nbr_hot = closest_aminos[:, :, None] == jnp.arange(span_overall, dtype=jnp.int32)[None, None, :]
    hot_float = nbr_hot.astype(jnp.float32)
    edges_b = jnp.einsum(
        "ikl,ilc->ikc", nbr_hot.astype(jnp.bfloat16), rows_all, preferred_element_type=jnp.float32
    ).astype(jnp.bfloat16)
    single_b = vertex_embedding.astype(jnp.bfloat16)
    node_proj = tensor_mean_answer(single_b, vertex_mapping_matrix)
    own_rows = lax.dynamic_slice_in_dim(node_proj[:, :node_width], seq_index * rows_dev, rows_dev)
    other_near = jnp.einsum("ikl,lc->ikc", hot_float, node_proj[:, node_width:], precision=HIGH)
    coords_own = lax.dynamic_slice_in_dim(atom_locations, seq_index * rows_dev, rows_dev, 1)
    coords_near = jnp.einsum("ikl,xl->xik", hot_float, atom_locations, precision=HIGH)
    diff = coords_own[:, :, None] - coords_near
    edge_lin = tensor_mean_answer(edges_b, bond_mapping_matrix)
    hidden, front_back = jax.vjp(
        edge_front, own_rows, other_near, edge_lin, diff, distance_basis_matrix
    )
    hidden_b = hidden.astype(jnp.bfloat16)
    msg_lin = tensor_mean_answer(hidden_b, signal_matrix)
    (mean_msg, shift), finish_back = jax.vjp(edge_finish, msg_lin, signal_location_matrix, diff)
    mean_b = mean_msg.astype(jnp.bfloat16)
    single_rows = lax.dynamic_slice_in_dim(vertex_embedding, seq_index * rows_dev, rows_dev)
    single_out = single_rows + tensor_mean_answer(mean_b, vertex_change_matrix)
    coords_out = coords_own + shift
    d_update_b = vertex_adjoint.astype(jnp.bfloat16)
    g_update = weight_back(mean_b, d_update_b)
    d_mean = product_back(d_update_b, vertex_change_matrix)
    d_msg_lin, g_coord, d_diff_finish = finish_back((d_mean, location_adjoint))
    d_msg_b = d_msg_lin.astype(jnp.bfloat16)
    g_msg = weight_back(hidden_b, d_msg_b)
    d_hidden = product_back(d_msg_b, signal_matrix)
    d_own, d_other_near, d_edge_lin, d_diff_front, g_dist = front_back(d_hidden)
    d_edge_b = d_edge_lin.astype(jnp.bfloat16)
    g_edge = weight_back(edges_b, d_edge_b)
    d_edges = product_back(d_edge_b, bond_mapping_matrix)
    d_rows = jnp.einsum("ikl,ikc->ilc", hot_float, d_edges, precision=HIGH)
    d_pair3 = coupling_adjoint.astype(jnp.float32) + lax.dynamic_slice_in_dim(
        d_rows, res_index * vertical_shard_piece, vertical_shard_piece, 1
    )
    d_diff = d_diff_front + d_diff_finish
    d_coords_own = jnp.sum(d_diff, 2)
    d_coords_near = jnp.einsum("ikl,xik->xl", hot_float, -d_diff, precision=HIGH)
    d_other_all = jnp.einsum("ikl,ikc->lc", hot_float, d_other_near, precision=HIGH)
    d_other_rows, d_near_rows = (
        lax.psum_scatter(d_other_all, "seq", scatter_dimension=0, tiled=True),
        lax.psum_scatter(d_coords_near, "seq", scatter_dimension=1, tiled=True),
    )
    d_node_b = jnp.concatenate([d_own, d_other_rows], -1).astype(jnp.bfloat16)
    g_node = weight_back(
        lax.dynamic_slice_in_dim(single_b, seq_index * rows_dev, rows_dev), d_node_b
    )
    single_grad = vertex_adjoint + product_back(d_node_b, vertex_mapping_matrix)
    coords_grad = location_adjoint + d_coords_own + d_near_rows
    layer_two = [
        g_node * first_res,
        g_edge * first_res,
        g_dist * first_res,
        g_msg * first_res,
        g_coord * first_res,
        g_update * first_res,
    ]
    d_inc_b = (d_pair3 * out_gate2).astype(jnp.bfloat16)
    d_gate_out2 = d_pair3 * update2 * out_gate2 * (1.0 - out_gate2)
    g_inc_out = weight_back(normed6_b, d_inc_b)
    d_normed6 = product_back(d_inc_b, inbound_exit_matrix)
    d_triangle2, g_inc_out_gain = norm_back6(d_normed6)
    d_tri2_b = d_triangle2.astype(jnp.bfloat16)
    d_left_sel = jnp.einsum(
        "ijc,kjc->kic", d_tri2_b, right_all2, preferred_element_type=jnp.float32
    )
    d_right_all2 = jnp.einsum(
        "ijc,kic->kjc", d_tri2_b, left_sel, preferred_element_type=jnp.float32
    )
    d_left_total = across_res(d_left_sel)
    d_both2 = owners_sum(
        jnp.concatenate(
            [place_home(d_left_total, vertical_shard_piece, offset, keep_home), d_right_all2], -1
        )
    )
    (d_gates2,) = gates_back2((d_both2[..., :tri_width], d_both2[..., tri_width:]))
    d_tri2_in_b = jnp.concatenate([d_gates2, d_gate_out2], -1).astype(jnp.bfloat16)
    g_inc_in = weight_back(normed5_b, d_tri2_in_b)
    d_normed5 = product_back(d_tri2_in_b, inbound_entry_matrix)
    d_pair2_norm, g_inc_gain = norm_back5(d_normed5)
    d_pair2 = d_pair3 + d_pair2_norm
    d_tri_out_b = (d_pair2 * out_gate).astype(jnp.bfloat16)
    d_gate_out = d_pair2 * update * out_gate * (1.0 - out_gate)
    g_tri_out = weight_back(normed4_b, d_tri_out_b)
    d_normed4 = product_back(d_tri_out_b, outbound_exit_matrix)
    d_triangle, g_tri_out_gain = norm_back4(d_normed4)
    d_triangle_b = d_triangle.astype(jnp.bfloat16)
    d_tri_all = lax.all_gather(d_triangle_b, "res", axis=1, tiled=True)
    d_left = jnp.einsum("ijc,jkc->ikc", d_tri_all, right_all, preferred_element_type=jnp.float32)
    d_right_part = jnp.einsum("ijc,ikc->jkc", d_tri_all, left_b, preferred_element_type=jnp.float32)
    d_right = owners_sum(d_right_part)
    (d_gates_in,) = gates_back((d_left, d_right))
    d_tri_b = jnp.concatenate([d_gates_in, d_gate_out], -1).astype(jnp.bfloat16)
    g_tri_in = weight_back(normed3_b, d_tri_b)
    d_normed3 = product_back(d_tri_b, outbound_entry_matrix)
    d_pair1_norm, g_tri_gain = norm_back3(d_normed3)
    pair_grad = d_pair2 + d_pair1_norm
    d_opm_b = (pair_grad / count).astype(jnp.bfloat16)
    g_opm_out = weight_back(outer_b, d_opm_b)
    d_outer = product_back(d_opm_b, tensor_mean_exit_matrix).astype(jnp.bfloat16)
    d_outer = d_outer.reshape(rows_dev, vertical_shard_piece, opm_width, opm_width)
    d_left_rows = jnp.einsum(
        "ijcd,sjd->sic", d_outer, right_cols, preferred_element_type=jnp.float32
    )
    d_right_cols = jnp.einsum(
        "ijcd,sic->sjd", d_outer, left_rows, preferred_element_type=jnp.float32
    )
    d_left_sum = across_res(d_left_rows)
    d_outer_in = owners_sum(
        jnp.concatenate(
            [place_home(d_left_sum, vertical_shard_piece, offset, keep_home), d_right_cols], -1
        )
    )
    d_outer_in_b = (d_outer_in * line_indicator_entries[:, None, None]).astype(jnp.bfloat16)
    g_opm_in = weight_back(normed2_b, d_outer_in_b)
    standardized_sens2 = product_back(d_outer_in_b, tensor_mean_entry_matrix)
    alignment_standard_sens, tensor_mean_scale_sens = standardize_reverse_beta(standardized_sens2)
    alignment_later_sens = alignment_adjoint.astype(jnp.float32) + alignment_standard_sens
    softmax_mixer_sens_lines = alignment_later_sens.astype(jnp.bfloat16)
    g_attn_out = weight_back(sigmoid_scaled_lines, softmax_mixer_sens_lines)
    d_gated = product_back(softmax_mixer_sens_lines, softmax_mixer_exit_matrix)
    d_attended_b = (d_gated * attn_gate).astype(jnp.bfloat16)
    d_gate_lin = d_gated * attended * attn_gate * (1.0 - attn_gate)
    probs_full = jnp.exp(attn_scores(query4, keys4, allowed, scale) - log_total)
    d_attended4 = d_attended_b.reshape(chain_shard_piece, vertical_shard_piece, HEADS, head_size)
    d_probs = jnp.einsum(
        "qlhd,klhd->lhqk", d_attended4, values4, preferred_element_type=jnp.float32
    )
    softmax_total = jnp.sum(probs_full * d_probs, -1, keepdims=True)
    d_scores_b = (probs_full * (d_probs - softmax_total) * scale).astype(jnp.bfloat16)
    d_query = jnp.einsum(
        "lhqk,klhd->qlhd", d_scores_b, keys4, preferred_element_type=jnp.float32
    ).reshape(chain_shard_piece, vertical_shard_piece, breadth_overall)
    d_keys = jnp.einsum("lhqk,qlhd->klhd", d_scores_b, query4, preferred_element_type=jnp.float32)
    d_values = jnp.einsum(
        "lhqk,qlhd->klhd",
        probs_full.astype(jnp.bfloat16),
        d_attended4,
        preferred_element_type=jnp.float32,
    )
    d_keyval = jnp.concatenate(
        [
            d_keys.reshape(block_tally, vertical_shard_piece, breadth_overall),
            d_values.reshape(block_tally, vertical_shard_piece, breadth_overall),
        ],
        -1,
    )
    d_keyval_own = lax.psum_scatter(d_keyval, "seq", scatter_dimension=0, tiled=True)
    d_proj_b = jnp.concatenate([d_query, d_keyval_own, d_gate_lin], -1).astype(jnp.bfloat16)
    g_qkvg = weight_back(normed_b, d_proj_b)
    standardized_sens = product_back(d_proj_b, attender_stacked_matrix)
    alignment_early_sens, alignment_scale_sens = standardize_reverse_alpha(standardized_sens)
    alignment_sensitivity = alignment_later_sens + alignment_early_sens
    layer_one = [
        alignment_scale_sens,
        g_qkvg,
        g_attn_out,
        tensor_mean_scale_sens,
        g_opm_in,
        g_opm_out,
        g_tri_gain,
        g_tri_in,
        g_tri_out_gain,
        g_tri_out,
        g_inc_gain,
        g_inc_in,
        g_inc_out_gain,
        g_inc_out,
    ]
    summed_all = sum_flat(layer_one + layer_two)
    layer_one = summed_all[:14]
    layer_two = summed_all[14:]
    return (
        alignment_later.astype(jnp.bfloat16),
        pair3_b,
        single_out,
        coords_out,
        alignment_sensitivity,
        pair_grad,
        single_grad,
        coords_grad,
        layer_one[0],
        layer_one[1],
        layer_one[2],
        layer_one[3],
        layer_one[4],
        layer_one[5],
        layer_one[6],
        layer_one[7],
        layer_one[8],
        layer_one[9],
        layer_one[10],
        layer_one[11],
        layer_one[12],
        layer_one[13],
        layer_two[0],
        layer_two[1],
        layer_two[2],
        layer_two[3],
        layer_two[4],
        layer_two[5],
    )


F32 = jnp.float32
BF16 = jnp.bfloat16
MESH = pl.DeviceIdType.MESH
LANES = 128
CHUNK = 256


def dot_nn(a, b):
    return jnp.dot(a, b, preferred_element_type=F32)


def dot_nt(a, b):
    return lax.dot_general(a, b, (((1,), (1,)), ((), ())), preferred_element_type=F32)


def dot_tn(a, b):
    return lax.dot_general(a, b, (((0,), (0,)), ((), ())), preferred_element_type=F32)


def split_terms(value, terms):
    parts = []
    for _ in range(terms):
        part = value.astype(BF16)
        parts.append(part)
        value = value - part.astype(F32)
    return parts


def pick_nn(value, hot, terms):
    return sum(dot_nn(part, hot) for part in split_terms(value, terms))


def pick_nt(value, hot, terms):
    return sum(dot_nt(part, hot) for part in split_terms(value, terms))


def iota(shape, axis):
    return lax.broadcasted_iota(jnp.int32, shape, axis)


def hot_bf16(cond):
    return jnp.where(cond, 1.0, 0.0).astype(BF16)


def sigmoid(value):
    return 0.5 * jnp.tanh(0.5 * value) + 0.5


def norm(value, axis):
    centred = value - jnp.mean(value, axis, keepdims=True)
    rstd = lax.rsqrt(jnp.mean(centred * centred, axis, keepdims=True) + EPS)
    return centred * rstd, rstd


def norm_back(grad, gain, hat, rstd, axis):
    scaled = grad * gain
    first = jnp.mean(scaled, axis, keepdims=True)
    second = jnp.mean(scaled * hat, axis, keepdims=True)
    return rstd * (scaled - first - hat * second)


def column(row):
    size = row.shape[1]
    eye = iota((size, size), 0) == iota((size, size), 1)
    return jnp.sum(jnp.where(eye, row, 0.0), 1, keepdims=True)


def lane_group(ref, j):
    return jnp.concatenate(
        [ref[pl.ds(2 * j + q, LANES, stride=16), :] for q in range(2)], axis=1
    )


def lane_ungroup(ref, j, value):
    for q in range(2):
        ref[pl.ds(2 * j + q, LANES, stride=16), :] = value[:, q * LANES : (q + 1) * LANES]


def chunk_at(j):
    return pl.ds(pl.multiple_of(j * CHUNK, CHUNK), CHUNK)


def all_peers(D, t):
    return lax.rem(D.s + t % D.ns, D.ns), lax.rem(D.r + t // D.ns, D.nr)


def seq_peers(D, t):
    return lax.rem(D.s + t, D.ns), D.r


def res_peers(D, t):
    return D.s, lax.rem(D.r + t, D.nr)


def sibling(D, t):
    return D.s + 1 - 2 * (D.s % 2), D.r


def chip_peers(D, t):
    return lax.rem(D.s + 2 * t, D.ns), D.r


def remote(src, dst, send, recv, peer):
    return pltpu.make_async_remote_copy(
        src_ref=src,
        dst_ref=dst,
        send_sem=send,
        recv_sem=recv,
        device_id=peer,
        device_id_type=MESH,
    )


def swap(D, src_at, dst_at, count, peers, index, me, like):
    send, recv = D.take()

    @pl.loop(1, count)
    def _(t):
        peer = peers(D, t)
        remote(src_at(index(*peer)), dst_at(me), send, recv, peer).start()

    def wait():
        done = remote(like, like, send, recv, peers(D, 1))
        done.wait_send()
        done.wait_recv()

    return wait


def start_all(D, src, dst, first, size):
    n = D.ns * D.nr
    me = D.s * D.nr + D.r
    rows = pl.ds(first, size)
    dst[me, rows, :] = src[me, rows, :]
    return swap(
        D,
        lambda i: src.at[i, rows],
        lambda i: dst.at[i, rows],
        n,
        all_peers,
        lambda ps, pr: ps * D.nr + pr,
        me,
        dst.at[pl.ds(0, n - 1), rows],
    )


def start_seq(D, src_at, dst_at, like):
    return swap(D, src_at, dst_at, D.ns, seq_peers, lambda ps, pr: ps, D.s, like)


def start_res(D, src_at, dst_at, like):
    return swap(D, src_at, dst_at, D.nr, res_peers, lambda ps, pr: pr, D.r, like)


def pack_columns(value, send):
    for q in range(2):
        first = value[2 * q].astype(F32)
        second = value[2 * q + 1].astype(F32)
        for d in range(8):
            at = slice(8 * d, 8 * d + 8)
            send[d, q] = jnp.concatenate([first[at], second[at]], 0).astype(BF16)


def start_columns(D, send, recv):
    recv[D.s] = send[D.s]
    return start_seq(D, lambda i: send.at[i], lambda i: recv.at[i], recv.at[pl.ds(0, D.ns - 1)])


def unpack_columns(R, recv, target):
    for d in range(8):
        for q in range(2):
            both = recv[d, q].astype(F32)
            for k in range(2):
                rows = pl.ds(4 * d + 2 * q + k, 8, stride=32)
                R.sp0[rows, :] = both[8 * k : 8 * k + 8, :LANES]
                R.sp1[rows, :] = both[8 * k : 8 * k + 8, LANES:]
    target[...] = jnp.concatenate([R.sp0[...], R.sp1[...]], 1)


def p_spread(R, D):
    pack_columns(R.x, R.xsend)
    D.ready()
    wait = start_columns(D, R.xsend, R.xrecv)
    R.arrived("adj_a")
    pack_columns(R.adj_a, R.asend)
    R.wait_adjoint = start_columns(D, R.asend, R.arecv)
    R.arrived("w_ti", "w_ii", "w_oo", "w_qkvg", "w_ao", "pe", "adj_c")
    R.w1t[...] = R.w_ti[...].astype(F32).T.astype(BF16)
    R.w2t[...] = R.w_ii[...].astype(F32).T.astype(BF16)
    R.wo1t[...] = R.w_to[...].astype(F32).T.astype(BF16)
    R.wo2t[...] = R.w_io[...].astype(F32).T.astype(BF16)
    stage_outer_weight(R)
    wait()
    unpack_columns(R, R.xrecv, R.xc)


def flag_column(flags):
    here = iota((256, 32), 0) % 32 == iota((256, 32), 1)
    return jnp.sum(jnp.where(here, flags, 0.0), 1, keepdims=True)


def head_probs(keys, query, flag_rows, head):
    lanes = iota((1, 256), 1) // 32
    mine = hot_bf16(lanes == head)
    scores = dot_nt(keys, query * mine) * (32 ** (-0.5))
    same = iota((256, 256), 0) // 32 == iota((256, 256), 1) // 32
    scores = jnp.where(same, jnp.where(flag_rows > 0, scores, -1e30), -3e38)
    weights = jnp.exp(scores - jnp.max(scores, 0, keepdims=True))
    return weights / jnp.sum(weights, 0, keepdims=True)


def p_attention(R, D):
    flag_rows = flag_column(R.fl[...].astype(F32))
    hat, _ = norm(R.xc[...], -1)
    normed = (hat * R.g1[...]).astype(BF16)
    projected = dot_nn(normed, R.w_qkvg[...])
    R.qkv[...] = projected[:, :768].astype(BF16)
    R.gl[...] = projected[:, 768:]
    R.att[...] = jnp.zeros((256, 256), F32)

    @pl.loop(0, 8, unroll=4)
    def _(head):
        probs = head_probs(R.qkv[:, 256:512], R.qkv[:, :256], flag_rows, head).astype(BF16)
        lanes = iota((1, 256), 1) // 32
        R.att[...] += jnp.where(lanes == head, dot_tn(probs, R.qkv[:, 512:768]), 0.0)

    gated = (sigmoid(R.gl[...]) * R.att[...]).astype(BF16)
    later = R.xc[...] + dot_nn(gated, R.w_ao[...])
    R.msan[...] = later
    hat2, _ = norm(later, -1)
    normed2 = (hat2 * R.g2[...]).astype(BF16)
    outer_in = (dot_nt(normed2, R.w_oit[...]) * (flag_rows > 0).astype(F32)).astype(BF16)
    wide = jnp.concatenate([outer_in.astype(F32), jnp.zeros((256, 64), F32)], 1)
    R.lsend[...] = wide.T[:32].astype(BF16)
    spread = hot_bf16(iota((64, 1024), 0) == 32 + iota((64, 1024), 1) // 32)
    kept = iota((256, 1024), 0) % 32 == iota((256, 1024), 1) % 32
    rows = jnp.where(kept, dot_nn(outer_in, spread), 0.0).astype(BF16)
    R.rsend[...] = dot_nn(hot_bf16(iota((8, 256), 0) == iota((8, 256), 1) // 32), rows)


def p_outer_exchange(R, D):
    send, recv = R.out_send, R.out_recv
    D.all_ready()
    owner = 2 * D.r + D.s // 4
    slot = D.s % 4

    def left(k, to):
        return remote(R.lsend, R.lall.at[to], send.at[k], recv.at[to], (owner, k))

    for k in range(4):
        mine = (owner == D.s) & (D.r == k)

        @pl.when(jnp.logical_not(mine))
        def _():
            left(k, slot).start()

        @pl.when(mine)
        def _():
            R.lall[slot] = R.lsend[...]

    here = pl.ds(pl.multiple_of(8 * D.s, 8), 8)

    def right(t):
        return remote(R.rsend, R.rall.at[here], send.at[4 + t], recv.at[4 + t], seq_peers(D, t))

    @pl.loop(1, 8)
    def _(t):
        right(t).start()

    R.rall[here, :] = R.rsend[...]

    for k in range(4):
        mine = (owner == D.s) & (D.r == k)
        theirs = (4 * (D.s % 2) + k == D.s) & (D.s // 2 == D.r)

        @pl.when(jnp.logical_not(mine))
        def _():
            left(k, k).wait_send()

        @pl.when(jnp.logical_not(theirs))
        def _():
            left(k, k).wait_recv()

    @pl.loop(1, 8)
    def _(t):
        right(t).wait()


def stage_outer_weight(R):
    R.wst[...] = R.w_oo[...].astype(F32)


def outer_weight(R, d):
    return R.wst[pl.ds(d, 32, stride=32), :].astype(BF16)


def count_of(R):
    return jnp.sum(R.fl[...].astype(F32), 1, keepdims=True)


def p_outer(R, D):
    for q in range(4):
        wide = jnp.concatenate([R.lall[q].astype(F32), jnp.zeros((96, 256), F32)], 0)
        R.l2[256 * q : 256 * q + 256, :] = wide.T[:, :32].astype(BF16)
        R.lt[:, 256 * q : 256 * q + 256] = R.lall[q]

    @pl.loop(0, 8)
    def _(e):
        weights = jnp.concatenate([outer_weight(R, 4 * e + u) for u in range(4)], 1)
        part = dot_nn(R.l2[...], weights).astype(BF16)
        for u in range(4):
            at = pl.ds(pl.multiple_of(32 * (4 * e + u), 32), 32)
            for i in range(32):
                R.zb[i, at, :] = part[32 * i : 32 * i + 32, LANES * u : LANES * u + LANES]


def outer_rows(R, half):
    inverse = 1.0 / count_of(R)
    right = R.rall[...].astype(BF16)

    @pl.loop(8 * half, 8 * half + 8, unroll=4)
    def _(m):
        both = dot_nn(right, jnp.concatenate([R.zb[m], R.zb[16 + m]], 1)) * inverse
        rows = [
            both[:, LANES * h : LANES * h + LANES] + R.pe[16 * h + m].astype(F32) for h in range(2)
        ]
        R.pair1[:, pl.ds(pl.multiple_of(m * LANES, LANES), LANES)] = jnp.concatenate(rows, 0).T


def pack_both(R, half):
    @pl.loop(0, 32, unroll=4)
    def _(d):
        for pair in range(2):
            for k, stage in ((0, R.st0), (1, R.st1)):
                rows = tile_rows(stage, 64 * d + 32 * pair + 8 * half)
                first = 64 * half + 32 * pair + 16 * k
                R.lrs[d, first : first + 16, :] = rows.astype(BF16)


def pack_single(R, stage, half):
    @pl.loop(0, 32, unroll=4)
    def _(d):
        for pair in range(2):
            first = 32 * half + 16 * pair
            rows = tile_rows(stage, 64 * d + 32 * pair + 8 * half)
            R.ts[d, first : first + 16, :] = rows.astype(BF16)


def tile_rows(stage, start):
    start = pl.multiple_of(start, 8)
    return jnp.concatenate([stage[pl.ds(start, 8), :], stage[pl.ds(start + 16, 8), :]], 0)


def untile(stage, start, rows):
    start = pl.multiple_of(start, 8)
    stage[pl.ds(start, 8), :] = rows[:8]
    stage[pl.ds(start + 16, 8), :] = rows[8:]


def stage_single(recv, stage, half):
    @pl.loop(0, 32, unroll=4)
    def _(d):
        for pair in range(2):
            first = 32 * half + 16 * pair
            rows = recv[d, first : first + 16, :].astype(F32)
            untile(stage, 64 * d + 32 * pair + 8 * half, rows)


def stage_both(R, recv, half):
    @pl.loop(0, 32, unroll=4)
    def _(d):
        for pair in range(2):
            for k, stage in ((0, R.st0), (1, R.st1)):
                first = 64 * half + 32 * pair + 16 * k
                rows = recv[d, first : first + 16, :].astype(F32)
                untile(stage, 64 * d + 32 * pair + 8 * half, rows)


def send_part(D, src, dst, table, half, pair):
    size = src.shape[1] // 4
    table[half, pair] = start_all(D, src, dst, size * (2 * half + pair), size)


def send_half(D, src, dst, table, half):
    for pair in range(2):
        send_part(D, src, dst, table, half, pair)


def wait_half(table, half):
    for pair in range(2):
        table[half, pair]()


def entry_chunk(R, pair, gain, w_t, nb, j):
    hat, _ = norm(pair, 0)
    nb_here = (hat * gain).astype(BF16)
    nb[:, chunk_at(j)] = nb_here
    for k, stage in ((0, R.st0), (1, R.st1)):
        linear = dot_nn(w_t[256 * k : 256 * k + 256, :], nb_here)
        lane_ungroup(stage, j, sigmoid(linear[128:]) * linear[:128])


def p_entry1(R, D):
    gain = column(R.g3[...])
    for half in range(2):
        outer_rows(R, half)

        @pl.loop(4 * half, 4 * half + 4, unroll=4)
        def _(j):
            entry_chunk(R, R.pair1[:, chunk_at(j)], gain, R.w1t, R.nb3, j)

        pack_both(R, half)
        send_half(D, R.lrs, R.lr1r, R.waits, half)


def gather_pair(recv, pair, k, mats, at):
    size = recv.shape[1] // 4

    @pl.loop(0, 8, unroll=4)
    def _(s):
        top = pl.ds(pl.multiple_of(32 * s, 32), 16)
        low = pl.ds(pl.multiple_of(32 * s + 16, 16), 16)
        for p in range(2):
            tiles = []
            for q in range(2):
                halves = []
                for half in range(2):
                    first = size * (2 * half + pair) + 16 * k
                    block = recv[4 * s + 2 * p + q, first : first + 16, :]
                    halves.append(block.astype(F32))
                tiles.append(halves)
            lanes = slice(LANES * p, LANES * p + LANES)
            for c in range(2):
                rows = slice(8 * c, 8 * c + 8)
                a, b = (jnp.concatenate([h[rows] for h in halves], 0) for halves in tiles)
                mats[at + c, top, lanes] = jnp.concatenate([a[:, :64], b[:, :64]], 1).astype(BF16)
                mats[at + c, low, lanes] = jnp.concatenate([a[:, 64:], b[:, 64:]], 1).astype(BF16)


def scatter_pair(mats, send, pair, k):
    size = send.shape[1] // 4

    @pl.loop(0, 8, unroll=4)
    def _(s):
        for p in range(2):
            lanes = slice(LANES * p, LANES * p + LANES)
            tiles = [[], []]
            for c in range(2):
                a = mats[c, pl.ds(pl.multiple_of(32 * s, 32), 16), lanes]
                b = mats[c, pl.ds(pl.multiple_of(32 * s + 16, 16), 16), lanes]
                tiles[0].append(jnp.concatenate([a[:, :64], b[:, :64]], 1))
                tiles[1].append(jnp.concatenate([a[:, 64:], b[:, 64:]], 1))
            for q in range(2):
                for half in range(2):
                    first = size * (2 * half + pair) + 16 * k
                    rows = slice(8 * half, 8 * half + 8)
                    block = jnp.concatenate([tile[rows] for tile in tiles[q]], 0)
                    send[4 * s + 2 * p + q, first : first + 16, :] = block.astype(BF16)


def tri_forward(R, D, recv, mats, back, product, meanwhile):
    meanwhile(R, D)
    for pair in range(2):
        R.waits[0, pair]()
        R.waits[1, pair]()
        gather_pair(recv, pair, 0, mats, 2 * pair)
        gather_pair(recv, pair, 1, mats, 4 + 2 * pair)
        for c in range(2):
            R.tm[c] = product(mats[2 * pair + c], mats[4 + 2 * pair + c])
        scatter_pair(R.tm, R.ts, pair, 0)
        send_part(D, R.ts, back, R.later, 0, pair)
    for pair in range(2):
        send_part(D, R.ts, back, R.later, 1, pair)


def tri_backward(R, D, recv, mats, back, products, meanwhile):
    meanwhile(R, D)
    advance(R, D)
    for pair in range(2):
        R.waits[0, pair]()
        R.waits[1, pair]()
        gather_pair(recv, pair, 0, R.dm, 0)
        for k in range(2):
            for c in range(2):
                at = 2 * pair + c
                R.tm[c] = products[k](mats[at], mats[4 + at], R.dm[c])
            scatter_pair(R.tm, R.lrs, pair, k)
        send_part(D, R.lrs, back, R.later, 0, pair)
        if not pair:
            advance(R, D)
    for pair in range(2):
        send_part(D, R.lrs, back, R.later, 1, pair)
    advance(R, D)


def p_tri1(R, D):
    tri_forward(R, D, R.lr1r, R.mats1, R.t1r, dot_nt, p_still)


def p_middle(R, D):
    gain4 = column(R.g4[...])
    gain5 = column(R.g5[...])
    for half in range(2):
        wait_half(R.later, half)
        stage_single(R.t1r, R.st2, half)

        @pl.loop(4 * half, 4 * half + 4, unroll=4)
        def _(j):
            hat, _ = norm(lane_group(R.st2, j), 0)
            nb4 = (hat * gain4).astype(BF16)
            R.nb4[:, chunk_at(j)] = nb4
            update = dot_nn(R.wo1t[...], nb4)
            gate = sigmoid(dot_nn(R.w1t[512:, :], R.nb3[:, chunk_at(j)]))
            pair2 = R.pair1[:, chunk_at(j)] + gate * update
            R.pair2[:, chunk_at(j)] = pair2
            entry_chunk(R, pair2, gain5, R.w2t, R.nb5, j)

        pack_both(R, half)
        send_half(D, R.lrs, R.lr2r, R.waits, half)


def p_tri2(R, D):
    tri_forward(R, D, R.lr2r, R.mats2, R.t2r, dot_tn, p_values)


def chunk_rows(D, j):
    lane = iota((1, CHUNK), 1)
    local = 16 * ((lane % LANES) // 64) + 2 * j + lane // LANES
    return local, hot_bf16(iota((256, CHUNK), 0) == 32 * D.s + local)


def near_rows(D):
    return hot_bf16(iota((256, CHUNK), 0) == 64 * D.r + iota((256, CHUNK), 1) % 64)


def p_still(R, D):
    dist = column(R.w_ds[...])
    inv_k = 1.0 / R.ca.shape[1]
    R.at8[...] = jnp.zeros((8, 256), F32)
    R.at8[0:3, :] = R.at[...]
    R.la8[...] = jnp.zeros((8, 32), F32)
    R.la8[0:3, :] = R.adj_l[...]
    R.nodet[...] = dot_tn(R.vet[...].astype(BF16), R.w_nd[...]).T
    R.dmean[...] = dot_nt(R.w_up[...], R.adj_v[...].astype(BF16))
    near = near_rows(D)
    R.nbase[...] = pick_nn(R.nodet[64:, :], near, 2)
    R.cbase[...] = pick_nn(R.at8[...], near, 3)
    R.nb_f[...] = R.ca[...].astype(F32)

    @pl.loop(0, 8, unroll=2)
    def _(j):
        here = chunk_at(j)
        local, row = chunk_rows(D, j)
        mine = hot_bf16(iota((32, CHUNK), 0) == local)
        named = dot_tn(R.nb_f[...].astype(BF16), mine)
        target = (64 * D.r + iota((1, CHUNK), 1) % 64).astype(F32)
        mask = jnp.max(jnp.where(named == target, 1.0, 0.0), 0, keepdims=True) * inv_k
        diff = pick_nn(R.at8[...], row, 3) - R.cbase[...]
        square = 1.0 + jnp.sum(diff * diff, 0, keepdims=True)
        radial = jnp.log(square)
        R.geo[0:8, here] = diff
        R.geo[8:16, here] = pick_nn(R.la8[...], mine, 3)
        R.geo[16:17, here] = radial
        R.geo[17:18, here] = mask
        R.geo[18:19, here] = 2.0 / square
        R.pre[0:64, here] = pick_nn(R.nodet[0:64, :], row, 2) + R.nbase[...] + radial * dist
        R.pre[64:128, here] = pick_nn(R.dmean[...], mine, 2) * mask
        for q in range(2):
            m = 2 * j + q
            both = jnp.concatenate([R.adj_c[m], R.adj_c[16 + m]], 0).astype(F32)
            R.dpair[:, pl.ds(pl.multiple_of(m * LANES, LANES), LANES)] = both.T


def p_turn(R, D):
    gain6 = column(R.g6[...])
    dist = column(R.w_ds[...])
    turn_weight = column(R.w_sl[...])
    R.a_g6[...] = jnp.zeros((128, CHUNK), F32)

    def chunk(j):
        here = chunk_at(j)
        hat, rstd = norm(lane_group(R.st2, j), 0)
        nb6 = (hat * gain6).astype(BF16)
        R.nb6[:, here] = nb6
        update2 = dot_nn(R.wo2t[...], nb6)
        gate2 = sigmoid(dot_nn(R.w2t[512:, :], R.nb5[:, here]))
        pair3 = R.pair2[:, here] + gate2 * update2
        po_b = pair3.astype(BF16)
        R.po[:, here] = po_b
        pre = R.pre[0:64, here] + dot_nn(R.w_edt[...], po_b)
        sig_pre = sigmoid(pre)
        hidden = (pre * sig_pre).astype(BF16)
        R.hid[:, here] = hidden
        msg = dot_tn(R.w_ms[...], hidden)
        sig_msg = sigmoid(msg)
        message = msg * sig_msg
        turn = jnp.tanh(jnp.sum(message * turn_weight, 0, keepdims=True))
        diff = R.geo[0:8, here]
        locadj = R.geo[8:16, here]
        mask = R.geo[17:18, here]
        d_turn = jnp.sum(locadj * diff, 0, keepdims=True) * mask * (1.0 - turn * turn)
        d_message = R.pre[64:128, here] + turn_weight * d_turn
        d_msg = (d_message * sig_msg * (1.0 + msg * (1.0 - sig_msg))).astype(BF16)
        R.dmsg[:, here] = d_msg
        d_pre = dot_nn(R.w_ms[...], d_msg) * sig_pre * (1.0 + pre * (1.0 - sig_pre))
        d_edge = d_pre.astype(BF16)
        R.dedge[:, here] = d_edge
        d_radial = jnp.sum(d_pre * dist, 0, keepdims=True)
        R.pre[0:64, here] = message
        R.pre[64:128, here] = d_pre
        R.geo[19:20, here] = turn * mask
        R.geo[20:21, here] = d_turn
        R.geo[24:32, here] = (d_radial * R.geo[18:19, here]) * diff + locadj * (turn * mask)
        d_pair3 = R.dpair[:, here] + dot_tn(R.w_edt[...], d_edge)
        R.dpair[:, here] = d_pair3
        d_up = (d_pair3 * gate2).astype(BF16)
        R.dup2[:, here] = d_up
        R.dtri2[512:, here] = (d_pair3 * update2 * gate2 * (1.0 - gate2)).astype(BF16)
        d_nb = dot_nn(R.w_io[...], d_up)
        R.a_g6[...] += d_nb * hat
        lane_ungroup(R.st0, j, norm_back(d_nb, gain6, hat, rstd, 0))

    for half in range(2):
        wait_half(R.later, half)
        stage_single(R.t2r, R.st2, half)
        pl.loop(4 * half, 4 * half + 4, unroll=4)(chunk)
        pack_single(R, R.st0, half)
        send_half(D, R.ts, R.dt2r, R.waits, half)


def p_turn_grads(R, D):
    R.g_io[...] = dot_nt(R.nb6[...], R.dup2[...])
    R.g_ed[...] = dot_nt(R.dedge[...], R.po[...])
    R.g_ms[...] = dot_nt(R.hid[...], R.dmsg[...])
    R.gg6[...] = jnp.sum(R.a_g6[...], 1, keepdims=True)
    R.g_ds[...] = jnp.sum(R.pre[64:128, :] * R.geo[16:17, :], 1, keepdims=True)
    R.g_sl[...] = jnp.sum(R.pre[0:64, :] * R.geo[20:21, :], 1, keepdims=True)
    for acc in (R.s_mean, R.s_own, R.s_other):
        acc[...] = jnp.zeros(acc.shape, F32)
    R.s_xyz[...] = jnp.zeros((16, 256), F32)

    @pl.loop(0, 8, unroll=2)
    def _(j):
        here = chunk_at(j)
        _, row = chunk_rows(D, j)
        near = near_rows(D)
        d_pre = R.pre[64:128, here]
        d_diff = R.geo[24:32, here]
        R.s_mean[...] += pick_nt(R.pre[0:64, here] * R.geo[17:18, here], row, 2)
        R.s_own[...] += pick_nt(d_pre, row, 2)
        R.s_other[...] += pick_nt(d_pre, near, 2)
        R.s_xyz[0:8, :] += pick_nt(R.geo[0:8, here] * R.geo[19:20, here], row, 2)
        R.s_xyz[8:16, :] += pick_nt(d_diff, row, 2) - pick_nt(d_diff, near, 2)
        for q in range(2):
            m = 2 * j + q
            at = pl.ds(pl.multiple_of(m * LANES, LANES), LANES)
            out = R.po[:, at].astype(F32).T.astype(BF16)
            R.pair_out[m] = out[:64]
            R.pair_out[16 + m] = out[64:]

    R.leave("pair_out")


def p_turn_rest(R, D):
    p_turn_grads(R, D)
    p_sum0(R, D)
    for half in range(2):
        stage_single(R.t1r, R.st2, half)


def p_back2(R, D):
    tri_backward(
        R,
        D,
        R.dt2r,
        R.mats2,
        R.dlr2r,
        (lambda a, b, d: dot_nt(b, d), lambda a, b, d: dot_nn(a, d)),
        p_turn_rest,
    )


def gates_back(R, d_tri, w_t, nb_here, j):
    here = chunk_at(j)
    for k, stage in ((0, R.st0), (1, R.st1)):
        grad = lane_group(stage, j)
        linear = dot_nn(w_t[256 * k : 256 * k + 256, :], nb_here)
        gate = sigmoid(linear[128:])
        d_first = grad * gate
        d_tri[256 * k : 256 * k + 128, here] = d_first.astype(BF16)
        d_tri[256 * k + 128 : 256 * k + 256, here] = (
            d_first * linear[:128] * (1.0 - gate)
        ).astype(BF16)


def p_between(R, D):
    gain4 = column(R.g4[...])
    gain5 = column(R.g5[...])
    R.a_g4[...] = jnp.zeros((128, CHUNK), F32)
    R.a_g5[...] = jnp.zeros((128, CHUNK), F32)

    def chunk(j):
        here = chunk_at(j)
        gates_back(R, R.dtri2, R.w2t, R.nb5[:, here], j)
        d_nb5 = dot_nn(R.w_ii[...], R.dtri2[:, here])
        hat5, rstd5 = norm(R.pair2[:, here], 0)
        R.a_g5[...] += d_nb5 * hat5
        d_pair2 = R.dpair[:, here] + norm_back(d_nb5, gain5, hat5, rstd5, 0)
        R.dpair[:, here] = d_pair2
        gate = sigmoid(dot_nn(R.w1t[512:, :], R.nb3[:, here]))
        update = dot_nn(R.wo1t[...], R.nb4[:, here])
        d_up = (d_pair2 * gate).astype(BF16)
        R.dup1[:, here] = d_up
        R.dtri1[512:, here] = (d_pair2 * update * gate * (1.0 - gate)).astype(BF16)
        d_nb4 = dot_nn(R.w_to[...], d_up)
        hat4, rstd4 = norm(lane_group(R.st2, j), 0)
        R.a_g4[...] += d_nb4 * hat4
        lane_ungroup(R.st3, j, norm_back(d_nb4, gain4, hat4, rstd4, 0))

    for half in range(2):
        wait_half(R.later, half)
        stage_both(R, R.dlr2r, half)
        pl.loop(4 * half, 4 * half + 4, unroll=4)(chunk)
        pack_single(R, R.st3, half)
        send_half(D, R.ts, R.dt1r, R.waits, half)


def p_between_grads(R, D):
    R.g_ii[...] = dot_nt(R.nb5[...], R.dtri2[...])
    R.g_to[...] = dot_nt(R.nb4[...], R.dup1[...])
    R.gg5[...] = jnp.sum(R.a_g5[...], 1, keepdims=True)
    R.gg4[...] = jnp.sum(R.a_g4[...], 1, keepdims=True)
    p_sum1(R, D)


def p_back1(R, D):
    tri_backward(
        R,
        D,
        R.dt1r,
        R.mats1,
        R.dlr1r,
        (lambda a, b, d: dot_nn(d, b), lambda a, b, d: dot_tn(d, a)),
        p_between_grads,
    )


def p_pair_end(R, D):
    gain3 = column(R.g3[...])
    R.a_g3[...] = jnp.zeros((128, CHUNK), F32)
    inverse = 1.0 / count_of(R)

    def chunk(j):
        here = chunk_at(j)
        gates_back(R, R.dtri1, R.w1t, R.nb3[:, here], j)
        d_nb3 = dot_nn(R.w_ti[...], R.dtri1[:, here])
        hat3, rstd3 = norm(R.pair1[:, here], 0)
        R.a_g3[...] += d_nb3 * hat3
        d_pair1 = R.dpair[:, here] + norm_back(d_nb3, gain3, hat3, rstd3, 0)
        for q in range(2):
            m = 2 * j + q
            out = d_pair1[:, q * LANES : (q + 1) * LANES].T
            R.pair_grad[m] = out[:64]
            R.pair_grad[16 + m] = out[64:]
            small = (out * inverse).astype(BF16)
            R.dopm[m] = small[:64]
            R.dopm[16 + m] = small[64:]

    for half in range(2):
        wait_half(R.later, half)
        stage_both(R, R.dlr1r, half)
        pl.loop(4 * half, 4 * half + 4, unroll=4)(chunk)
        if not half:
            advance(R, D)
    R.leave("pair_grad")


def p_pair_grads(R, D):
    R.g_ti[...] = dot_nt(R.nb3[...], R.dtri1[...])
    R.gg3[...] = jnp.sum(R.a_g3[...], 1, keepdims=True)


def p_outer_back(R, D):
    R.rt[...] = R.rall[...].T.astype(BF16)
    R.dright[...] = jnp.zeros((64, 1024), F32)
    R.dleft[...] = jnp.zeros((32, 1024), F32)

    @pl.loop(0, 4)
    def _(k):
        grad = jnp.concatenate([R.dopm[8 * k + u] for u in range(8)], 1)
        R.dright[...] += dot_nt(grad, jnp.concatenate([R.zb[8 * k + u] for u in range(8)], 1))

    @pl.loop(0, 4)
    def _(g):
        right = R.rt[pl.ds(pl.multiple_of(256 * g, 256), 256), :]

        @pl.loop(0, 16, unroll=16)
        def _(k):
            grad = jnp.concatenate([R.dopm[2 * k], R.dopm[2 * k + 1]], 1)
            both = dot_nn(right, grad).astype(BF16)
            for h in range(2):
                at = pl.ds(pl.multiple_of(64 * k + 32 * h, 32), 32)
                for u in range(8):
                    block = both[32 * u : 32 * u + 32, LANES * h : LANES * h + LANES]
                    R.zb[8 * g + u, at, :] = block

        weights = jnp.concatenate([outer_weight(R, 8 * g + u) for u in range(8)], 1)
        R.dleft[...] += dot_nt(weights, jnp.concatenate([R.zb[8 * g + u] for u in range(8)], 1))

    for q in range(4):
        R.dls[q] = R.dleft[:, 256 * q : 256 * q + 256].astype(BF16)


def p_outer_grads(R, D):
    @pl.loop(0, 4)
    def _(g):
        rows = jnp.concatenate([R.zb[8 * g + u] for u in range(8)], 1)
        total = dot_nn(R.lt[...], rows)
        for u in range(8):
            R.st1[pl.ds(8 * g + u, 32, stride=32), :] = total[:, LANES * u : LANES * u + LANES]

    R.g_oo[...] = R.st1[0:1024, :]


def p_outer_return(R, D):
    send, recv = R.back_send, R.back_recv
    column_res = D.s // 2
    owner = 2 * D.r + D.s // 4

    def left(q, slot):
        peer = (4 * (D.s % 2) + q, column_res)
        return remote(R.dls.at[q], R.dlr.at[slot], send.at[q], recv.at[slot], peer)

    for q in range(4):
        mine = (4 * (D.s % 2) + q == D.s) & (column_res == D.r)

        @pl.when(jnp.logical_not(mine))
        def _():
            left(q, D.r).start()

        @pl.when(mine)
        def _():
            R.dlr[D.r] = R.dls[q]

    def right(t):
        peer = seq_peers(D, t)
        at = pl.ds(pl.multiple_of(8 * peer[0], 8), 8)
        return remote(R.dright.at[at], R.drr.at[D.s], send.at[4 + t], recv.at[4 + t], peer)

    @pl.loop(1, 8)
    def _(t):
        right(t).start()

    R.drr[D.s] = R.dright[pl.ds(pl.multiple_of(8 * D.s, 8), 8), :]
    p_pair_grads(R, D)
    p_outer_grads(R, D)
    advance(R, D)
    p_sum2(R, D)

    for q in range(4):
        mine = (4 * (D.s % 2) + q == D.s) & (column_res == D.r)
        theirs = (owner == D.s) & (D.r == q)

        @pl.when(jnp.logical_not(mine))
        def _():
            left(q, q).wait_send()

        @pl.when(jnp.logical_not(theirs))
        def _():
            left(q, q).wait_recv()

    @pl.loop(1, 8)
    def _(t):
        right(t).wait()


def p_attention_back(R, D):
    flag_rows = flag_column(R.fl[...].astype(F32))
    live = (flag_rows > 0).astype(F32)
    left = R.dlr[0].astype(F32)
    for k in range(1, 4):
        left += R.dlr[k].astype(F32)
    right = R.drr[0]
    for k in range(1, 8):
        right += R.drr[k]
    wide = jnp.concatenate([left, jnp.zeros((96, 256), F32)], 0).T
    spread = dot_nn(
        hot_bf16(iota((256, 8), 0) // 32 == iota((256, 8), 1)), right.astype(BF16)
    )
    kept = iota((256, 1024), 0) % 32 == iota((256, 1024), 1) % 32
    spread = jnp.where(kept, spread, 0.0).astype(BF16)
    back = hot_bf16(32 + iota((1024, LANES), 0) // 32 == iota((1024, LANES), 1))
    d_in = ((wide + dot_nn(spread, back)) * live).astype(BF16)[:, :64]
    hat2, rstd2 = norm(R.msan[...], -1)
    normed2 = (hat2 * R.g2[...]).astype(BF16)
    R.g_oi[...] = dot_tn(d_in, normed2)
    d_normed2 = dot_nn(d_in, R.w_oit[...])
    R.gg2[...] = jnp.sum(d_normed2 * hat2, 0, keepdims=True)
    d_later = R.ac[...] + norm_back(d_normed2, R.g2[...], hat2, rstd2, -1)
    R.dlater[...] = d_later
    d_exit = d_later.astype(BF16)
    gate = sigmoid(R.gl[...])
    gated = (gate * R.att[...]).astype(BF16)
    R.g_ao[...] = dot_tn(gated, d_exit)
    d_gated = dot_nt(d_exit, R.w_ao[...])
    R.datt[...] = (d_gated * gate).astype(BF16)
    R.dproj[:, 768:] = (d_gated * R.att[...] * gate * (1.0 - gate)).astype(BF16)
    hat, rstd = norm(R.xc[...], -1)
    R.normed[...] = (hat * R.g1[...]).astype(BF16)
    R.c_gate[...] = dot_tn(R.normed[...], R.dproj[:, 768:])
    advance(R, D)
    p_sum3(R, D)
    R.dqkv[...] = jnp.zeros((256, 768), F32)

    @pl.loop(0, 8, unroll=4)
    def _(head):
        lanes = iota((1, 256), 1) // 32
        mine = lanes == head
        hot = hot_bf16(mine)
        query = R.qkv[:, 0:256]
        keys = R.qkv[:, 256:512]
        probs = head_probs(keys, query, flag_rows, head)
        d_att = R.datt[...]
        d_probs = dot_nt(R.qkv[:, 512:768], d_att * hot)
        total = jnp.sum(probs * d_probs, 0, keepdims=True)
        d_scores = (probs * (d_probs - total) * (32 ** (-0.5))).astype(BF16)
        R.dqkv[:, 0:256] += jnp.where(mine, dot_tn(d_scores, keys), 0.0)
        R.dqkv[:, 256:512] += jnp.where(mine, dot_nn(d_scores, query), 0.0)
        R.dqkv[:, 512:768] += jnp.where(mine, dot_nn(probs.astype(BF16), d_att), 0.0)

    R.dproj[:, :768] = R.dqkv[...].astype(BF16)
    R.c_qkv[...] = dot_tn(R.normed[...], R.dproj[:, :768])
    d_normed = dot_nt(R.dproj[...], R.w_qkvg[...])
    hat, rstd = norm(R.xc[...], -1)
    R.dlater[...] += norm_back(d_normed, R.g1[...], hat, rstd, -1)
    group_columns(R, R.dlater, R.gsend)


def group_columns(R, value, send):
    R.sp0[...] = value[:, :LANES]
    R.sp1[...] = value[:, LANES:]
    for d in range(8):
        for q in range(2):
            parts = []
            for k in range(2):
                rows = pl.ds(4 * d + 2 * q + k, 8, stride=32)
                parts.append(jnp.concatenate([R.sp0[rows, :], R.sp1[rows, :]], 1))
            send[d, q] = jnp.concatenate(parts, 0).astype(BF16)


def ungroup_columns(recv, target):
    for q in range(2):
        blocks = [recv[d, q].astype(F32) for d in range(8)]
        for k in range(2):
            rows = jnp.concatenate([block[8 * k : 8 * k + 8] for block in blocks], 0)
            target[2 * q + k] = rows.astype(target.dtype)


def p_send_value(R, D):
    group_columns(R, R.msan, R.osend)
    R.wait_value = start_columns(D, R.osend, R.orecv)


def p_values(R, D):
    p_send_value(R, D)
    R.wait_value()
    ungroup_columns(R.orecv, R.msa_out)
    R.leave("msa_out")
    R.wait_adjoint()
    unpack_columns(R, R.arecv, R.ac)


SEGMENTS = (
    dict(
        g_io=(128, 128),
        s_mean=(64, 256),
        s_own=(64, 256),
        s_other=(64, 256),
        s_vadj=(64, 256),
        s_xyz=(16, 256),
        g_ed=(64, 128),
        g_ms=(64, 64),
        small0=(16, 128),
    ),
    dict(g_ii=(128, 640), g_to=(128, 128), small1=(16, 128)),
    dict(g_ti=(128, 640), g_oo=(1024, 128), small2=(16, 128)),
    dict(g_ao=(256, 256), c_gate=(256, 256), g_oi=(64, 256), small3=(16, 128)),
    dict(c_qkv=(256, 768)),
)


def segment_layout(index):
    layout = []
    start = 0
    for name, (rows, cols) in SEGMENTS[index].items():
        for lane in range(0, cols, LANES):
            layout.append((name, start, rows, lane, min(LANES, cols - lane)))
            start += rows
    return layout, -(-start // 512) * 512


def pack_segment(R, index):
    layout, total = segment_layout(index)
    pay = R.pay[index]
    for name, start, count, lane, width in layout:
        value = getattr(R, name)[:, lane : lane + width]
        pay[start : start + count, 0:width] = value.astype(BF16)
    end = layout[-1][1] + layout[-1][2]
    if end < total:
        pay[end:total, :] = jnp.zeros((total - end, LANES), BF16)


def rows_of(index, size):
    return pl.ds(pl.multiple_of(index * size, size), size)


def sum_segment(R, D, index):
    pay, full = R.pay[index], R.full[index]
    first, second, third, fourth, fifth, sixth = (table[index] for table in R.parts)
    half = pay.shape[0] // 2
    eighth = half // 4
    part = eighth // 4
    core, chip = D.s % 2, D.s // 2
    place = core * 4 + chip
    pack_segment(R, index)
    theirs = pay.at[rows_of(1 - core, half)]
    wait = swap(D, lambda i: theirs, lambda i: first, 2, sibling, lambda ps, pr: 0, 0, first)
    yield
    wait()
    total = pay[rows_of(core, half), :].astype(F32) + first[...].astype(F32)
    second[...] = total.astype(BF16)
    third[chip] = second[rows_of(chip, eighth), :]
    wait = swap(
        D,
        lambda i: second.at[rows_of(i, eighth)],
        lambda i: third.at[i],
        4,
        chip_peers,
        lambda ps, pr: ps // 2,
        chip,
        second.at[pl.ds(0, 3 * eighth)],
    )
    yield
    wait()
    total = third[0].astype(F32)
    for k in range(1, 4):
        total += third[k].astype(F32)
    fourth[...] = total.astype(BF16)
    fifth[D.r] = fourth[rows_of(D.r, part), :]
    some = pl.ds(0, part * (D.nr - 1))
    wait = start_res(
        D, lambda i: fourth.at[rows_of(i, part)], lambda i: fifth.at[i], fourth.at[some]
    )
    yield
    wait()
    total = fifth[0].astype(F32)
    for k in range(1, 4):
        total += fifth[k].astype(F32)
    sixth[...] = total.astype(BF16)
    mine = pl.ds(pl.multiple_of(place * eighth + D.r * part, part), part)
    full[mine, :] = sixth[...]
    wait = start_res(D, lambda i: sixth, lambda i: full.at[mine], full.at[some])
    yield
    wait()
    mine = full.at[rows_of(place, eighth)]
    most = full.at[pl.ds(0, 3 * eighth)]
    wait = swap(D, lambda i: mine, lambda i: mine, 4, chip_peers, lambda ps, pr: 0, 0, most)
    yield
    wait()
    mine = full.at[rows_of(core, half)]
    wait = swap(D, lambda i: mine, lambda i: mine, 2, sibling, lambda ps, pr: 0, 0, first)
    yield
    wait()
    R.leave(index)


def advance(R, D):
    R.chains = [chain for chain in R.chains if next(chain, D) is not D]


def begin(R, D, index):
    chain = sum_segment(R, D, index)
    next(chain)
    R.chains.append(chain)


def p_sum0(R, D):
    place = hot_bf16(iota((32, 256), 1) == 32 * D.s + iota((32, 256), 0))
    first = jnp.where(D.r == 0, 1.0, 0.0)
    R.s_vadj[...] = dot_tn(R.adj_v[...].astype(BF16), place) * first
    small_rows(R, R.small0, (R.gg6, R.g_ds, R.g_sl))
    begin(R, D, 0)


def small_rows(R, target, values):
    R.small[...] = jnp.zeros((128, LANES), F32)
    for k, value in enumerate(values):
        R.small[0 : value.shape[0], k : k + 1] = value[...]
    target[...] = R.small[...].T[:16]


def p_sum1(R, D):
    small_rows(R, R.small1, (R.gg5, R.gg4))
    begin(R, D, 1)


def p_sum2(R, D):
    small_rows(R, R.small2, (R.gg3,))
    begin(R, D, 2)


def p_sum3(R, D):
    R.small3[...] = jnp.zeros((16, LANES), F32)
    for half in range(2):
        R.small3[half : half + 1, :] = R.gg2[:, LANES * half : LANES * half + LANES]
    begin(R, D, 3)


def p_sums(R, D):
    wait = start_columns(D, R.gsend, R.grecv)
    advance(R, D)
    begin(R, D, 4)
    advance(R, D)
    wait()
    ungroup_columns(R.grecv, R.msa_grad)
    R.leave("msa_grad")
    while R.chains:
        advance(R, D)


def unpack_segment(R, index):
    held = {}
    for name, start, count, lane, width in segment_layout(index)[0]:
        value = R.full[index][start : start + count, 0:width].astype(F32)
        if name.startswith("g_"):
            getattr(R, "o_" + name)[:, lane : lane + width] = value
        else:
            held.setdefault(name, []).append(value)
    return {name: jnp.concatenate(parts, 1) for name, parts in held.items()}


def p_finish(R, D):
    R.arrived(1)
    small = unpack_segment(R, 1)["small1"]
    R.o_gg5[...] = small[0:1]
    R.o_gg4[...] = small[1:2]
    R.leave(R.o_g_ii)
    R.arrived(2)
    R.o_gg3[...] = unpack_segment(R, 2)["small2"][0:1]
    R.leave(R.o_g_ti, R.o_g_oo)
    R.arrived(3)
    held = unpack_segment(R, 3)
    R.leave(R.o_g_ao)
    for half in range(2):
        R.o_gg2[:, LANES * half : LANES * half + LANES] = held["small3"][half : half + 1]
    R.o_g_qkvg[:, 768:] = held["c_gate"]
    R.arrived(4)
    R.o_g_qkvg[:, :768] = unpack_segment(R, 4)["c_qkv"]
    R.leave(R.o_g_qkvg)
    R.pass_on()
    R.arrived(5)
    total = jnp.sum(R.w_far[...].astype(F32) * R.o_g_qkvg[...], 1, keepdims=True)
    eye = iota((256, 256), 0) == iota((256, 256), 1)
    R.o_gg1[...] = jnp.sum(jnp.where(eye, total, 0.0), 0, keepdims=True) / R.g1[...]
    R.arrived(0)
    held = unpack_segment(R, 0)
    small = held["small0"]
    R.o_gg6[...] = small[0:1]
    R.o_g_ds[...] = small[1:2, :64]
    R.o_g_sl[...] = small[2:3, :64]
    mean_b = held["s_mean"].astype(BF16)
    R.o_g_up[...] = dot_nt(mean_b, held["s_vadj"].astype(BF16))
    d_node = jnp.concatenate([held["s_own"], held["s_other"]], 0).astype(BF16)
    R.o_g_nd[...] = dot_nt(R.vet[...].astype(BF16), d_node)
    step = dot_tn(R.w_up[...], mean_b)
    grad = dot_nn(R.w_nd[...], d_node)
    R.rows_f[...] = jnp.concatenate([step + R.vet[...], grad], 0).T
    here = pl.ds(pl.multiple_of(32 * D.s, 32), 32)
    mine = R.rows_f[here, :]
    R.single_out[...] = mine[:, :64]
    R.single_grad[...] = R.adj_v[...] + mine[:, 64:]
    R.xyz[...] = jnp.zeros((128, 256), F32)
    R.xyz[0:16, :] = held["s_xyz"]
    R.xyz[16:19, :] = R.at[...]
    R.rows_g[...] = R.xyz[...].T
    turned = R.rows_g[here, :]
    back = jnp.concatenate([turned, jnp.zeros((96, 128), F32)], 0).T
    R.coords_out[...] = back[16:19, 0:32] + back[0:3, 0:32]
    R.coords_grad[...] = R.adj_l[...] + back[8:11, 0:32]


KEPT = dict(
    xsend=((8, 2, 16, 256), BF16),
    xrecv=((8, 2, 16, 256), BF16),
    asend=((8, 2, 16, 256), BF16),
    arecv=((8, 2, 16, 256), BF16),
    osend=((8, 2, 16, 256), BF16),
    orecv=((8, 2, 16, 256), BF16),
    gsend=((8, 2, 16, 256), BF16),
    grecv=((8, 2, 16, 256), BF16),
    wst=((1024, 128), F32),
    lt=((32, 1024), BF16),
    tm=((2, 256, 256), F32),
    geo=((32, 2048), F32),
    pre=((128, 2048), F32),
    small0=((16, 128), F32),
    small1=((16, 128), F32),
    small2=((16, 128), F32),
    small3=((16, 128), F32),
    xc=((256, 256), F32),
    ac=((256, 256), F32),
    sp0=((256, 128), F32),
    sp1=((256, 128), F32),
    qkv=((256, 768), BF16),
    gl=((256, 256), F32),
    att=((256, 256), F32),
    msan=((256, 256), F32),
    lsend=((32, 256), BF16),
    rsend=((8, 1024), F32),
    lall=((4, 32, 256), BF16),
    rall=((64, 1024), F32),
    st0=((2048, 128), F32),
    st1=((2048, 128), F32),
    st2=((2048, 128), F32),
    st3=((2048, 128), F32),
    l2=((1024, 32), BF16),
    zb=((32, 1024, 128), BF16),
    pair1=((128, 2048), F32),
    pair2=((128, 2048), F32),
    dpair=((128, 2048), F32),
    w1t=((640, 128), BF16),
    w2t=((640, 128), BF16),
    wo1t=((128, 128), BF16),
    wo2t=((128, 128), BF16),
    nb3=((128, 2048), BF16),
    nb4=((128, 2048), BF16),
    nb5=((128, 2048), BF16),
    nb6=((128, 2048), BF16),
    po=((128, 2048), BF16),
    hid=((64, 2048), BF16),
    dmsg=((64, 2048), BF16),
    dedge=((64, 2048), BF16),
    dup1=((128, 2048), BF16),
    dup2=((128, 2048), BF16),
    dtri1=((640, 2048), BF16),
    dtri2=((640, 2048), BF16),
    mats1=((8, 256, 256), BF16),
    mats2=((8, 256, 256), BF16),
    dm=((2, 256, 256), BF16),
    lrs=((32, 128, 128), BF16),
    lr1r=((32, 128, 128), BF16),
    lr2r=((32, 128, 128), BF16),
    dlr1r=((32, 128, 128), BF16),
    dlr2r=((32, 128, 128), BF16),
    ts=((32, 64, 128), BF16),
    t1r=((32, 64, 128), BF16),
    t2r=((32, 64, 128), BF16),
    dt1r=((32, 64, 128), BF16),
    dt2r=((32, 64, 128), BF16),
    at8=((8, 256), F32),
    la8=((8, 32), F32),
    nodet=((128, 256), F32),
    dmean=((64, 32), F32),
    nbase=((64, 256), F32),
    cbase=((8, 256), F32),
    nb_f=((32, 64), F32),
    s_mean=((64, 256), F32),
    s_own=((64, 256), F32),
    s_other=((64, 256), F32),
    s_vadj=((64, 256), F32),
    s_xyz=((16, 256), F32),
    a_g3=((128, 256), F32),
    a_g4=((128, 256), F32),
    a_g5=((128, 256), F32),
    a_g6=((128, 256), F32),
    gg3=((128, 1), F32),
    gg4=((128, 1), F32),
    gg5=((128, 1), F32),
    gg6=((128, 1), F32),
    gg2=((1, 256), F32),
    g_ds=((64, 1), F32),
    g_sl=((64, 1), F32),
    g_io=((128, 128), F32),
    g_to=((128, 128), F32),
    g_ti=((128, 640), F32),
    g_ii=((128, 640), F32),
    g_ed=((64, 128), F32),
    g_ms=((64, 64), F32),
    g_oo=((1024, 128), F32),
    g_oi=((64, 256), F32),
    g_ao=((256, 256), F32),
    c_gate=((256, 256), F32),
    c_qkv=((256, 768), F32),
    normed=((256, 256), BF16),
    small=((128, 128), F32),
    dopm=((32, 64, 128), BF16),
    rt=((1024, 64), BF16),
    dright=((64, 1024), F32),
    dleft=((32, 1024), F32),
    dls=((4, 32, 256), BF16),
    dlr=((4, 32, 256), BF16),
    drr=((8, 8, 1024), F32),
    dlater=((256, 256), F32),
    datt=((256, 256), BF16),
    dproj=((256, 1024), BF16),
    dqkv=((256, 768), F32),
)
SIZES = [segment_layout(index)[1] for index in range(len(SEGMENTS))]
PAYLOADS = [((size, 128), BF16) for size in SIZES]
PARTIAL = (
    [((size // 2, 128), BF16) for size in SIZES]
    + [((size // 2, 128), BF16) for size in SIZES]
    + [((4, size // 8, 128), BF16) for size in SIZES]
    + [((size // 8, 128), BF16) for size in SIZES]
    + [((4, size // 32, 128), BF16) for size in SIZES]
    + [((size // 32, 128), BF16) for size in SIZES]
)
LARGE = ("msa_out", "pair_out", "msa_grad", "pair_grad")
MOVED_IN = ("adj_a", "w_qkvg", "w_ao", "w_oo", "w_ti", "w_ii", "pe", "adj_c")
BIG = ("o_g_ii", "o_g_ti", "o_g_oo", "o_g_ao", "o_g_qkvg")
FINISH = ("g1", "vet", "w_up", "w_nd", "adj_v", "at", "adj_l")
FINISH_KEPT = dict(
    rows_f=((256, 128), F32), rows_g=((256, 128), F32), xyz=((128, 256), F32)
)
RESULTS = dict(
    msa_out=((4, 64, 256), BF16),
    pair_out=((32, 64, 128), BF16),
    single_out=((32, 64), F32),
    coords_out=((3, 32), F32),
    msa_grad=((4, 64, 256), F32),
    pair_grad=((32, 64, 128), F32),
    single_grad=((32, 64), F32),
    coords_grad=((3, 32), F32),
    o_gg1=((1, 256), F32),
    o_g_qkvg=((256, 1024), F32),
    o_g_ao=((256, 256), F32),
    o_gg2=((1, 256), F32),
    o_g_oi=((64, 256), F32),
    o_g_oo=((1024, 128), F32),
    o_gg3=((1, 128), F32),
    o_g_ti=((128, 640), F32),
    o_gg4=((1, 128), F32),
    o_g_to=((128, 128), F32),
    o_gg5=((1, 128), F32),
    o_g_ii=((128, 640), F32),
    o_gg6=((1, 128), F32),
    o_g_io=((128, 128), F32),
    o_g_nd=((64, 128), F32),
    o_g_ed=((64, 128), F32),
    o_g_ds=((1, 64), F32),
    o_g_ms=((64, 64), F32),
    o_g_sl=((1, 64), F32),
    o_g_up=((64, 64), F32),
)

STEPS = (
    p_spread,
    p_attention,
    p_outer_exchange,
    p_outer,
    p_entry1,
    p_tri1,
    p_middle,
    p_tri2,
    p_turn,
    p_back2,
    p_between,
    p_back1,
    p_pair_end,
    p_outer_back,
    p_outer_return,
    p_attention_back,
    p_sums,
)
EXCHANGES = 66


class Device:
    def __init__(self, n_seq, n_res, sems, rows_in):
        self.s, self.r = lax.axis_index("seq"), lax.axis_index("res")
        self.ns, self.nr = n_seq, n_res
        self.sems = sems
        self.rows_in = rows_in
        self.used = 0

    def take(self):
        self.used += 2
        assert self.used <= 2 * EXCHANGES
        return self.sems.at[self.used - 2], self.sems.at[self.used - 1]

    def ready(self):
        pl.semaphore_wait(pltpu.get_barrier_semaphore(), self.ns + self.nr - 2)

        @pl.loop(1, self.nr)
        def _(t):
            pl.semaphore_signal(self.rows_in, inc=1, device_id=res_peers(self, t), device_id_type=MESH)

    def all_ready(self):
        pl.semaphore_wait(self.rows_in, self.nr - 1)


def first_kernel(n_seq, n_res, names, *refs):
    refs = list(refs)
    far = {name: refs.pop(0) for name in names}
    far_full = [refs.pop(0) for _ in SIZES]
    R = SimpleNamespace(**far)
    R.__dict__.update({name: refs.pop(0) for name in (*KEPT, *MOVED_IN, *LARGE)})
    tables = [[refs.pop(0) for _ in SIZES] for _ in range(8)]
    R.full, R.pay, R.parts = tables[0], tables[1], tables[2:]
    R.waits, R.later, R.chains = {}, {}, []
    R.out_send, R.out_recv, R.back_send, R.back_recv, R.move = refs[2:]
    D = Device(n_seq, n_res, refs[0], refs[1])
    barrier = pltpu.get_barrier_semaphore()

    for peers, count in ((seq_peers, n_seq), (res_peers, n_res)):

        @pl.loop(1, count)
        def _(t):
            pl.semaphore_signal(barrier, inc=1, device_id=peers(D, t), device_id_type=MESH)

    moves = {}
    for name in MOVED_IN:
        moves[name] = pltpu.make_async_copy(far[name], getattr(R, name), R.move.at[len(moves)])
        moves[name].start()
    R.arrived = lambda *wanted: [moves.pop(name).wait() for name in wanted]
    base = len(moves)
    out = []

    def leave(name):
        if name in far:
            source, target, at = getattr(R, name), far[name], LARGE.index(name)
        else:
            source, target, at = R.full[name], far_full[name], len(LARGE) + name
        out.append(pltpu.make_async_copy(source, target, R.move.at[base + at]))
        out[-1].start()

    R.leave = leave
    for step in STEPS:
        step(R, D)
    for copy in out:
        copy.wait()


def last_kernel(n_seq, n_res, names, *refs):
    refs = list(refs)

    def some(wanted):
        return {name: refs.pop(0) for name in wanted}

    far_in = [refs.pop(0) for _ in range(len(SIZES) + 1)]
    far_large = some(LARGE)
    R = SimpleNamespace(**some(FINISH))
    away = some((*LARGE, *BIG))
    R.__dict__.update(some(names))
    R.__dict__.update(some((*FINISH_KEPT, *LARGE, *BIG)))
    near_in = [refs.pop(0) for _ in far_in]
    (sems,) = refs
    R.full, R.w_far = near_in[:-1], near_in[-1]
    used = []

    def move(source, target):
        copy = pltpu.make_async_copy(source, target, sems.at[len(used)])
        copy.start()
        used.append(copy)
        return copy

    order = (1, 2, 3, 4, 5, 0)
    coming = {k: move(far_in[k], near_in[k]) for k in order}
    passing = [(name, move(far_large[name], getattr(R, name))) for name in LARGE]
    going = []

    def leave(*values):
        for name in BIG:
            if any(getattr(R, name) is value for value in values):
                going.append(move(getattr(R, name), away[name]))

    def pass_on():
        for name, copy in passing:
            copy.wait()
            going.append(move(getattr(R, name), away[name]))

    R.arrived, R.leave, R.pass_on = lambda k: coming[k].wait(), leave, pass_on
    p_finish(R, Device(n_seq, n_res, None, None))
    for copy in going:
        copy.wait()


ARGS = dict(
    x=(4, 64, 256),
    pe=(32, 64, 128),
    vet=(256, 64),
    at=(3, 256),
    fl=(32,),
    ca=(32, 64),
    g1=(256,),
    w_qkvg=(256, 1024),
    w_ao=(256, 256),
    g2=(256,),
    w_oit=(256, 64),
    w_oo=(1024, 128),
    g3=(128,),
    w_ti=(128, 640),
    g4=(128,),
    w_to=(128, 128),
    g5=(128,),
    w_ii=(128, 640),
    g6=(128,),
    w_io=(128, 128),
    w_nd=(64, 128),
    w_edt=(128, 64),
    w_ds=(64,),
    w_ms=(64, 64),
    w_sl=(64,),
    w_up=(64, 64),
    adj_a=(4, 64, 256),
    adj_c=(32, 64, 128),
    adj_v=(32, 64),
    adj_l=(3, 32),
)


def fits(n_seq, n_res, args):
    shapes = tuple(tuple(arg.shape) for arg in args)
    return (n_seq, n_res) == (8, 4) and shapes == tuple(ARGS.values())


def fast_shards(n_seq, n_res, *args):
    env = dict(zip(ARGS, args))
    for name, value in tuple(env.items()):
        if value.ndim == 1:
            env[name] = value.reshape(1, -1)
    env.update(vet=env["vet"].T, w_oit=env["w_oit"].T, w_edt=env["w_edt"].T)
    space = pl.BlockSpec(memory_space=pltpu.VMEM)

    def shapes(entries):
        return [jax.ShapeDtypeStruct(*entry) for entry in entries]

    large = {name: RESULTS[name] for name in LARGE}
    anywhere = pl.BlockSpec(memory_space=pl.ANY)
    held = [(ARGS[name], BF16) for name in MOVED_IN] + [RESULTS[name] for name in LARGE]
    values = pl.pallas_call(
        functools.partial(first_kernel, n_seq, n_res, (*env, *large)),
        out_shape=shapes((*large.values(), *PAYLOADS)),
        in_specs=[anywhere if name in MOVED_IN else space for name in env],
        out_specs=[anywhere] * (len(large) + len(PAYLOADS)),
        scratch_shapes=[
            pltpu.VMEM(*entry) for entry in (*KEPT.values(), *held, *PAYLOADS, *PAYLOADS, *PARTIAL)
        ]
        + [pltpu.SemaphoreType.DMA((2 * EXCHANGES,)), pltpu.SemaphoreType.REGULAR]
        + [pltpu.SemaphoreType.DMA((12,))] * 4
        + [pltpu.SemaphoreType.DMA((len(MOVED_IN) + len(LARGE) + len(SIZES),))],
        compiler_params=pltpu.CompilerParams(
            vmem_limit_bytes=62 * 2**20, collective_id=0, has_side_effects=True
        ),
    )(*env.values())
    full = values[len(large) :]
    env.update(zip(large, values))
    apart = {name: RESULTS[name] for name in (*LARGE, *BIG)}
    small = {name: entry for name, entry in RESULTS.items() if name not in apart}
    brought = [*PAYLOADS, (ARGS["w_qkvg"], BF16)]
    values = pl.pallas_call(
        functools.partial(last_kernel, n_seq, n_res, tuple(small)),
        out_shape=shapes((*apart.values(), *small.values())),
        in_specs=[anywhere] * (len(brought) + len(LARGE)) + [space] * len(FINISH),
        out_specs=[anywhere] * len(apart) + [space] * len(small),
        scratch_shapes=[
            pltpu.VMEM(*entry) for entry in (*FINISH_KEPT.values(), *apart.values(), *brought)
        ]
        + [pltpu.SemaphoreType.DMA((len(brought) + len(apart) + len(LARGE),))],
        compiler_params=pltpu.CompilerParams(vmem_limit_bytes=60 * 2**20),
    )(*full, env["w_qkvg"], *[env[name] for name in LARGE], *[env[name] for name in FINISH])
    env.update(zip((*apart, *small), values))
    results = [env[name] for name in RESULTS]
    for index, value in enumerate(results):
        if value.shape[0] == 1:
            results[index] = value.reshape(-1)
    for index in (12, 23):
        results[index] = results[index].T
    return tuple(results)


def solution(mesh):
    n_seq, n_res = mesh.shape["seq"], mesh.shape["res"]

    def body(*args):
        if fits(n_seq, n_res, args):
            return fast_shards(n_seq, n_res, *args)
        return shards(*args)

    return jax.shard_map(
        body,
        mesh=mesh,
        in_specs=(
            P("seq", "res", None),
            P("seq", "res", None),
            P(),
            P(),
            P(),
            P("seq", None),
            P(),
            P(),
            P(),
            P(),
            P(),
            P(),
            P(),
            P(),
            P(),
            P(),
            P(),
            P(),
            P(),
            P(),
            P(),
            P(),
            P(),
            P(),
            P(),
            P(),
            P("seq", "res", None),
            P("seq", "res", None),
            P("seq", None),
            P(None, "seq"),
        ),
        out_specs=(
            P("seq", "res", None),
            P("seq", "res", None),
            P("seq", None),
            P(None, "seq"),
            P("seq", "res", None),
            P("seq", "res", None),
            P("seq", None),
            P(None, "seq"),
            P(),
            P(),
            P(),
            P(),
            P(),
            P(),
            P(),
            P(),
            P(),
            P(),
            P(),
            P(),
            P(),
            P(),
            P(),
            P(),
            P(),
            P(),
            P(),
            P(),
        ),
        check_vma=False,
    )
```

```python
import functools
from types import SimpleNamespace

import jax
import jax.numpy as jnp
from jax import lax
from jax.experimental import pallas as pl
from jax.experimental.pallas import tpu as pltpu
from jax.sharding import PartitionSpec as P

HEADS = 8


EPS = 1e-05
HIGH = lax.Precision.HIGHEST


def spread_2(value, axis, source):
    kept = jnp.where(lax.axis_index(axis) == source, value, 0).astype(value.dtype)
    return lax.psum(kept, axis)


def standardize_lines(value, gain):
    row_mean = jnp.mean(value, -1, keepdims=True)
    centred = value - row_mean
    spread = jnp.mean(centred * centred, -1, keepdims=True)
    return centred * lax.rsqrt(spread + EPS) * gain


def tensor_mean_answer(left, right):
    return jnp.einsum("...c,cd->...d", left, right, preferred_element_type=jnp.float32)


def product_back(grad, right):
    return jnp.einsum("...d,cd->...c", grad, right, preferred_element_type=jnp.float32)


def weight_back(left, grad):
    flat_left = left.reshape(-1, left.shape[-1])
    flat_grad = grad.reshape(-1, grad.shape[-1])
    return jnp.einsum("nc,nd->cd", flat_left, flat_grad, preferred_element_type=jnp.float32)


def attn_scores(query, keys, allowed, scale):
    raw_scores = (
        jnp.einsum("qlhd,klhd->lhqk", query, keys, preferred_element_type=jnp.float32) * scale
    )
    return jnp.where(allowed, raw_scores, -1e30)


def tri_gates(tri_lin):
    quarter = tri_lin.shape[-1] // 4
    left_part = jax.nn.sigmoid(tri_lin[..., quarter : 2 * quarter]) * tri_lin[..., :quarter]
    right_part = (
        jax.nn.sigmoid(tri_lin[..., 3 * quarter :]) * tri_lin[..., 2 * quarter : 3 * quarter]
    )
    return (left_part, right_part)


def edge_front(own_rows, other_near, edge_lin, diff, distance_basis_matrix):
    radial = jnp.log(1.0 + jnp.sum(diff * diff, 0))
    return jax.nn.silu(
        own_rows[:, None, :] + other_near + edge_lin + radial[..., None] * distance_basis_matrix
    )


def edge_finish(msg_lin, signal_location_matrix, diff):
    message = jax.nn.silu(msg_lin)
    turn = jnp.tanh(jnp.einsum("ikc,c->ik", message, signal_location_matrix, precision=HIGH))
    return (jnp.mean(message, 1), jnp.mean(diff * turn[None], 2))


def gather_rows(value):
    return lax.all_gather(value, "seq", axis=0, tiled=True)


def across_res(value):
    return lax.psum(value.astype(jnp.bfloat16), "res").astype(jnp.float32)


def owners_sum(value):
    return lax.psum_scatter(value, "seq", scatter_dimension=0, tiled=True)


def place_home(rows_part, col_width, offset, keep_home):
    empty = jnp.zeros((rows_part.shape[0], col_width, rows_part.shape[2]), jnp.float32)
    return lax.dynamic_update_slice_in_dim(empty, rows_part, offset, 1) * keep_home


def sum_flat(parts):
    flat = jnp.concatenate([jnp.ravel(member) for member in parts])
    summed = lax.psum(flat, ("seq", "res"))
    pieces = []
    offset = 0
    for member in parts:
        pieces.append(summed[offset : offset + member.size].reshape(member.shape))
        offset = offset + member.size
    return pieces


def shards(
    alignment_embedding,
    coupling_embedding,
    vertex_embedding,
    atom_locations,
    chain_existence_flags,
    closest_aminos,
    softmax_mixer_scale_factor,
    attender_stacked_matrix,
    softmax_mixer_exit_matrix,
    tensor_mean_scale_factor,
    tensor_mean_entry_matrix,
    tensor_mean_exit_matrix,
    outbound_entry_scale,
    outbound_entry_matrix,
    outbound_exit_scale,
    outbound_exit_matrix,
    inbound_entry_scale,
    inbound_entry_matrix,
    inbound_exit_scale,
    inbound_exit_matrix,
    vertex_mapping_matrix,
    bond_mapping_matrix,
    distance_basis_matrix,
    signal_matrix,
    signal_location_matrix,
    vertex_change_matrix,
    alignment_adjoint,
    coupling_adjoint,
    vertex_adjoint,
    location_adjoint,
):
    seq_index = lax.axis_index("seq")
    res_index = lax.axis_index("res")
    n_seq = lax.axis_size("seq")
    n_res = lax.axis_size("res")
    chain_shard_piece, vertical_shard_piece, breadth_overall = alignment_embedding.shape
    rows_dev = coupling_embedding.shape[0]
    span_overall, node_width = vertex_embedding.shape
    block_tally = chain_existence_flags.shape[0]
    head_size = breadth_overall // HEADS
    scale = head_size ** (-0.5)
    opm_width = tensor_mean_entry_matrix.shape[1] // 2
    tri_width = outbound_exit_matrix.shape[0]
    chain_exists = (chain_existence_flags > 0).astype(jnp.float32)
    line_indicator_entries = lax.dynamic_slice_in_dim(
        chain_exists, seq_index * chain_shard_piece, chain_shard_piece
    )
    first_res = (res_index == 0).astype(jnp.float32)
    home = seq_index * rows_dev // vertical_shard_piece
    offset = seq_index * rows_dev - home * vertical_shard_piece
    keep_home = (home == res_index).astype(jnp.float32)
    alignment_real_lines = alignment_embedding.astype(jnp.float32)
    standardized_lines, standardize_reverse_alpha = jax.vjp(
        standardize_lines, alignment_real_lines, softmax_mixer_scale_factor
    )
    normed_b = standardized_lines.astype(jnp.bfloat16)
    projected = tensor_mean_answer(normed_b, attender_stacked_matrix)
    query = projected[..., :breadth_overall].astype(jnp.bfloat16)
    keyval = projected[..., breadth_overall : 3 * breadth_overall].astype(jnp.bfloat16)
    attn_gate = jax.nn.sigmoid(projected[..., 3 * breadth_overall :])
    all_keyval = lax.all_gather(keyval, "seq", axis=0, tiled=True)
    query4 = query.reshape(chain_shard_piece, vertical_shard_piece, HEADS, head_size)
    keys4 = all_keyval[..., :breadth_overall].reshape(
        block_tally, vertical_shard_piece, HEADS, head_size
    )
    values4 = all_keyval[..., breadth_overall:].reshape(
        block_tally, vertical_shard_piece, HEADS, head_size
    )
    allowed = chain_exists[None, None, None, :] > 0
    scores = attn_scores(query4, keys4, allowed, scale)
    score_peak = jnp.max(scores, -1, keepdims=True)
    exp_scores = jnp.exp(scores - score_peak)
    exp_total = jnp.sum(exp_scores, -1, keepdims=True)
    log_total = score_peak + jnp.log(exp_total)
    probs_b = (exp_scores / exp_total).astype(jnp.bfloat16)
    attended = jnp.einsum(
        "lhqk,klhd->qlhd", probs_b, values4, preferred_element_type=jnp.float32
    ).reshape(chain_shard_piece, vertical_shard_piece, breadth_overall)
    sigmoid_scaled_lines = (attn_gate * attended).astype(jnp.bfloat16)
    alignment_later = alignment_real_lines + tensor_mean_answer(
        sigmoid_scaled_lines, softmax_mixer_exit_matrix
    )
    standardized_lines2, standardize_reverse_beta = jax.vjp(
        standardize_lines, alignment_later, tensor_mean_scale_factor
    )
    normed2_b = standardized_lines2.astype(jnp.bfloat16)
    outer_in = (
        tensor_mean_answer(normed2_b, tensor_mean_entry_matrix)
        * line_indicator_entries[:, None, None]
    ).astype(jnp.bfloat16)
    everyone = lax.all_gather(outer_in, ("seq", "res"), axis=0, tiled=True)
    blocks = everyone.reshape(n_seq, n_res, chain_shard_piece, vertical_shard_piece, 2 * opm_width)
    home_block = lax.dynamic_index_in_dim(blocks, home, 1, keepdims=False)
    left_rows = lax.dynamic_slice_in_dim(home_block, offset, rows_dev, 2)[..., :opm_width]
    left_rows = left_rows.reshape(block_tally, rows_dev, opm_width)
    right_cols = lax.dynamic_index_in_dim(blocks, res_index, 1, keepdims=False)[..., opm_width:]
    right_cols = right_cols.reshape(block_tally, vertical_shard_piece, opm_width)
    outer_b = jnp.einsum("sic,sjd->ijcd", left_rows, right_cols, preferred_element_type=jnp.float32)
    outer_b = outer_b.reshape(rows_dev, vertical_shard_piece, opm_width * opm_width).astype(
        jnp.bfloat16
    )
    count = jnp.sum(chain_exists)
    pair1 = (
        coupling_embedding.astype(jnp.float32)
        + tensor_mean_answer(outer_b, tensor_mean_exit_matrix) / count
    )
    normed3, norm_back3 = jax.vjp(standardize_lines, pair1, outbound_entry_scale)
    normed3_b = normed3.astype(jnp.bfloat16)
    tri = tensor_mean_answer(normed3_b, outbound_entry_matrix)
    (left_t, right_t), gates_back = jax.vjp(tri_gates, tri[..., : 4 * tri_width])
    left_b = left_t.astype(jnp.bfloat16)
    right_b = right_t.astype(jnp.bfloat16)
    right_all = gather_rows(right_b)
    partial_tri = jnp.einsum("ikc,jkc->ijc", left_b, right_all, preferred_element_type=jnp.float32)
    triangle = lax.psum_scatter(
        partial_tri.astype(jnp.bfloat16), "res", scatter_dimension=1, tiled=True
    ).astype(jnp.float32)
    normed4, norm_back4 = jax.vjp(standardize_lines, triangle, outbound_exit_scale)
    normed4_b = normed4.astype(jnp.bfloat16)
    update = tensor_mean_answer(normed4_b, outbound_exit_matrix)
    out_gate = jax.nn.sigmoid(tri[..., 4 * tri_width :])
    pair2 = pair1 + out_gate * update
    normed5, norm_back5 = jax.vjp(standardize_lines, pair2, inbound_entry_scale)
    normed5_b = normed5.astype(jnp.bfloat16)
    tri2 = tensor_mean_answer(normed5_b, inbound_entry_matrix)
    (left_i, right_i), gates_back2 = jax.vjp(tri_gates, tri2[..., : 4 * tri_width])
    both_local = jnp.concatenate([left_i.astype(jnp.bfloat16), right_i.astype(jnp.bfloat16)], -1)
    both_all = gather_rows(both_local)
    right_all2 = both_all[..., tri_width:]
    left_cand = lax.dynamic_slice_in_dim(both_all[..., :tri_width], offset, rows_dev, 1)
    left_sel = spread_2(left_cand, "res", home)
    triangle2 = jnp.einsum("kic,kjc->ijc", left_sel, right_all2, preferred_element_type=jnp.float32)
    normed6, norm_back6 = jax.vjp(standardize_lines, triangle2, inbound_exit_scale)
    normed6_b = normed6.astype(jnp.bfloat16)
    update2 = tensor_mean_answer(normed6_b, inbound_exit_matrix)
    out_gate2 = jax.nn.sigmoid(tri2[..., 4 * tri_width :])
    coupling_later3 = pair2 + out_gate2 * update2
    pair3_b = coupling_later3.astype(jnp.bfloat16)
    rows_all = lax.all_gather(pair3_b, "res", axis=1, tiled=True)
    nbr_hot = closest_aminos[:, :, None] == jnp.arange(span_overall, dtype=jnp.int32)[None, None, :]
    hot_float = nbr_hot.astype(jnp.float32)
    edges_b = jnp.einsum(
        "ikl,ilc->ikc", nbr_hot.astype(jnp.bfloat16), rows_all, preferred_element_type=jnp.float32
    ).astype(jnp.bfloat16)
    single_b = vertex_embedding.astype(jnp.bfloat16)
    node_proj = tensor_mean_answer(single_b, vertex_mapping_matrix)
    own_rows = lax.dynamic_slice_in_dim(node_proj[:, :node_width], seq_index * rows_dev, rows_dev)
    other_near = jnp.einsum("ikl,lc->ikc", hot_float, node_proj[:, node_width:], precision=HIGH)
    coords_own = lax.dynamic_slice_in_dim(atom_locations, seq_index * rows_dev, rows_dev, 1)
    coords_near = jnp.einsum("ikl,xl->xik", hot_float, atom_locations, precision=HIGH)
    diff = coords_own[:, :, None] - coords_near
    edge_lin = tensor_mean_answer(edges_b, bond_mapping_matrix)
    hidden, front_back = jax.vjp(
        edge_front, own_rows, other_near, edge_lin, diff, distance_basis_matrix
    )
    hidden_b = hidden.astype(jnp.bfloat16)
    msg_lin = tensor_mean_answer(hidden_b, signal_matrix)
    (mean_msg, shift), finish_back = jax.vjp(edge_finish, msg_lin, signal_location_matrix, diff)
    mean_b = mean_msg.astype(jnp.bfloat16)
    single_rows = lax.dynamic_slice_in_dim(vertex_embedding, seq_index * rows_dev, rows_dev)
    single_out = single_rows + tensor_mean_answer(mean_b, vertex_change_matrix)
    coords_out = coords_own + shift
    d_update_b = vertex_adjoint.astype(jnp.bfloat16)
    g_update = weight_back(mean_b, d_update_b)
    d_mean = product_back(d_update_b, vertex_change_matrix)
    d_msg_lin, g_coord, d_diff_finish = finish_back((d_mean, location_adjoint))
    d_msg_b = d_msg_lin.astype(jnp.bfloat16)
    g_msg = weight_back(hidden_b, d_msg_b)
    d_hidden = product_back(d_msg_b, signal_matrix)
    d_own, d_other_near, d_edge_lin, d_diff_front, g_dist = front_back(d_hidden)
    d_edge_b = d_edge_lin.astype(jnp.bfloat16)
    g_edge = weight_back(edges_b, d_edge_b)
    d_edges = product_back(d_edge_b, bond_mapping_matrix)
    d_rows = jnp.einsum("ikl,ikc->ilc", hot_float, d_edges, precision=HIGH)
    d_pair3 = coupling_adjoint.astype(jnp.float32) + lax.dynamic_slice_in_dim(
        d_rows, res_index * vertical_shard_piece, vertical_shard_piece, 1
    )
    d_diff = d_diff_front + d_diff_finish
    d_coords_own = jnp.sum(d_diff, 2)
    d_coords_near = jnp.einsum("ikl,xik->xl", hot_float, -d_diff, precision=HIGH)
    d_other_all = jnp.einsum("ikl,ikc->lc", hot_float, d_other_near, precision=HIGH)
    d_other_rows, d_near_rows = (
        lax.psum_scatter(d_other_all, "seq", scatter_dimension=0, tiled=True),
        lax.psum_scatter(d_coords_near, "seq", scatter_dimension=1, tiled=True),
    )
    d_node_b = jnp.concatenate([d_own, d_other_rows], -1).astype(jnp.bfloat16)
    g_node = weight_back(
        lax.dynamic_slice_in_dim(single_b, seq_index * rows_dev, rows_dev), d_node_b
    )
    single_grad = vertex_adjoint + product_back(d_node_b, vertex_mapping_matrix)
    coords_grad = location_adjoint + d_coords_own + d_near_rows
    layer_two = [
        g_node * first_res,
        g_edge * first_res,
        g_dist * first_res,
        g_msg * first_res,
        g_coord * first_res,
        g_update * first_res,
    ]
    d_inc_b = (d_pair3 * out_gate2).astype(jnp.bfloat16)
    d_gate_out2 = d_pair3 * update2 * out_gate2 * (1.0 - out_gate2)
    g_inc_out = weight_back(normed6_b, d_inc_b)
    d_normed6 = product_back(d_inc_b, inbound_exit_matrix)
    d_triangle2, g_inc_out_gain = norm_back6(d_normed6)
    d_tri2_b = d_triangle2.astype(jnp.bfloat16)
    d_left_sel = jnp.einsum(
        "ijc,kjc->kic", d_tri2_b, right_all2, preferred_element_type=jnp.float32
    )
    d_right_all2 = jnp.einsum(
        "ijc,kic->kjc", d_tri2_b, left_sel, preferred_element_type=jnp.float32
    )
    d_left_total = across_res(d_left_sel)
    d_both2 = owners_sum(
        jnp.concatenate(
            [place_home(d_left_total, vertical_shard_piece, offset, keep_home), d_right_all2], -1
        )
    )
    (d_gates2,) = gates_back2((d_both2[..., :tri_width], d_both2[..., tri_width:]))
    d_tri2_in_b = jnp.concatenate([d_gates2, d_gate_out2], -1).astype(jnp.bfloat16)
    g_inc_in = weight_back(normed5_b, d_tri2_in_b)
    d_normed5 = product_back(d_tri2_in_b, inbound_entry_matrix)
    d_pair2_norm, g_inc_gain = norm_back5(d_normed5)
    d_pair2 = d_pair3 + d_pair2_norm
    d_tri_out_b = (d_pair2 * out_gate).astype(jnp.bfloat16)
    d_gate_out = d_pair2 * update * out_gate * (1.0 - out_gate)
    g_tri_out = weight_back(normed4_b, d_tri_out_b)
    d_normed4 = product_back(d_tri_out_b, outbound_exit_matrix)
    d_triangle, g_tri_out_gain = norm_back4(d_normed4)
    d_triangle_b = d_triangle.astype(jnp.bfloat16)
    d_tri_all = lax.all_gather(d_triangle_b, "res", axis=1, tiled=True)
    d_left = jnp.einsum("ijc,jkc->ikc", d_tri_all, right_all, preferred_element_type=jnp.float32)
    d_right_part = jnp.einsum("ijc,ikc->jkc", d_tri_all, left_b, preferred_element_type=jnp.float32)
    d_right = owners_sum(d_right_part)
    (d_gates_in,) = gates_back((d_left, d_right))
    d_tri_b = jnp.concatenate([d_gates_in, d_gate_out], -1).astype(jnp.bfloat16)
    g_tri_in = weight_back(normed3_b, d_tri_b)
    d_normed3 = product_back(d_tri_b, outbound_entry_matrix)
    d_pair1_norm, g_tri_gain = norm_back3(d_normed3)
    pair_grad = d_pair2 + d_pair1_norm
    d_opm_b = (pair_grad / count).astype(jnp.bfloat16)
    g_opm_out = weight_back(outer_b, d_opm_b)
    d_outer = product_back(d_opm_b, tensor_mean_exit_matrix).astype(jnp.bfloat16)
    d_outer = d_outer.reshape(rows_dev, vertical_shard_piece, opm_width, opm_width)
    d_left_rows = jnp.einsum(
        "ijcd,sjd->sic", d_outer, right_cols, preferred_element_type=jnp.float32
    )
    d_right_cols = jnp.einsum(
        "ijcd,sic->sjd", d_outer, left_rows, preferred_element_type=jnp.float32
    )
    d_left_sum = across_res(d_left_rows)
    d_outer_in = owners_sum(
        jnp.concatenate(
            [place_home(d_left_sum, vertical_shard_piece, offset, keep_home), d_right_cols], -1
        )
    )
    d_outer_in_b = (d_outer_in * line_indicator_entries[:, None, None]).astype(jnp.bfloat16)
    g_opm_in = weight_back(normed2_b, d_outer_in_b)
    standardized_sens2 = product_back(d_outer_in_b, tensor_mean_entry_matrix)
    alignment_standard_sens, tensor_mean_scale_sens = standardize_reverse_beta(standardized_sens2)
    alignment_later_sens = alignment_adjoint.astype(jnp.float32) + alignment_standard_sens
    softmax_mixer_sens_lines = alignment_later_sens.astype(jnp.bfloat16)
    g_attn_out = weight_back(sigmoid_scaled_lines, softmax_mixer_sens_lines)
    d_gated = product_back(softmax_mixer_sens_lines, softmax_mixer_exit_matrix)
    d_attended_b = (d_gated * attn_gate).astype(jnp.bfloat16)
    d_gate_lin = d_gated * attended * attn_gate * (1.0 - attn_gate)
    probs_full = jnp.exp(attn_scores(query4, keys4, allowed, scale) - log_total)
    d_attended4 = d_attended_b.reshape(chain_shard_piece, vertical_shard_piece, HEADS, head_size)
    d_probs = jnp.einsum(
        "qlhd,klhd->lhqk", d_attended4, values4, preferred_element_type=jnp.float32
    )
    softmax_total = jnp.sum(probs_full * d_probs, -1, keepdims=True)
    d_scores_b = (probs_full * (d_probs - softmax_total) * scale).astype(jnp.bfloat16)
    d_query = jnp.einsum(
        "lhqk,klhd->qlhd", d_scores_b, keys4, preferred_element_type=jnp.float32
    ).reshape(chain_shard_piece, vertical_shard_piece, breadth_overall)
    d_keys = jnp.einsum("lhqk,qlhd->klhd", d_scores_b, query4, preferred_element_type=jnp.float32)
    d_values = jnp.einsum(
        "lhqk,qlhd->klhd",
        probs_full.astype(jnp.bfloat16),
        d_attended4,
        preferred_element_type=jnp.float32,
    )
    d_keyval = jnp.concatenate(
        [
            d_keys.reshape(block_tally, vertical_shard_piece, breadth_overall),
            d_values.reshape(block_tally, vertical_shard_piece, breadth_overall),
        ],
        -1,
    )
    d_keyval_own = lax.psum_scatter(d_keyval, "seq", scatter_dimension=0, tiled=True)
    d_proj_b = jnp.concatenate([d_query, d_keyval_own, d_gate_lin], -1).astype(jnp.bfloat16)
    g_qkvg = weight_back(normed_b, d_proj_b)
    standardized_sens = product_back(d_proj_b, attender_stacked_matrix)
    alignment_early_sens, alignment_scale_sens = standardize_reverse_alpha(standardized_sens)
    alignment_sensitivity = alignment_later_sens + alignment_early_sens
    layer_one = [
        alignment_scale_sens,
        g_qkvg,
        g_attn_out,
        tensor_mean_scale_sens,
        g_opm_in,
        g_opm_out,
        g_tri_gain,
        g_tri_in,
        g_tri_out_gain,
        g_tri_out,
        g_inc_gain,
        g_inc_in,
        g_inc_out_gain,
        g_inc_out,
    ]
    summed_all = sum_flat(layer_one + layer_two)
    layer_one = summed_all[:14]
    layer_two = summed_all[14:]
    return (
        alignment_later.astype(jnp.bfloat16),
        pair3_b,
        single_out,
        coords_out,
        alignment_sensitivity,
        pair_grad,
        single_grad,
        coords_grad,
        layer_one[0],
        layer_one[1],
        layer_one[2],
        layer_one[3],
        layer_one[4],
        layer_one[5],
        layer_one[6],
        layer_one[7],
        layer_one[8],
        layer_one[9],
        layer_one[10],
        layer_one[11],
        layer_one[12],
        layer_one[13],
        layer_two[0],
        layer_two[1],
        layer_two[2],
        layer_two[3],
        layer_two[4],
        layer_two[5],
    )


F32 = jnp.float32
BF16 = jnp.bfloat16
MESH = pl.DeviceIdType.MESH
LANES = 128
CHUNK = 256


def dot_nn(a, b):
    return jnp.dot(a, b, preferred_element_type=F32)


def dot_nt(a, b):
    return lax.dot_general(a, b, (((1,), (1,)), ((), ())), preferred_element_type=F32)


def dot_tn(a, b):
    return lax.dot_general(a, b, (((0,), (0,)), ((), ())), preferred_element_type=F32)


def split_terms(value, terms):
    parts = []
    for _ in range(terms):
        part = value.astype(BF16)
        parts.append(part)
        value = value - part.astype(F32)
    return parts


def pick_nn(value, hot, terms):
    return sum(dot_nn(part, hot) for part in split_terms(value, terms))


def pick_nt(value, hot, terms):
    return sum(dot_nt(part, hot) for part in split_terms(value, terms))


def iota(shape, axis):
    return lax.broadcasted_iota(jnp.int32, shape, axis)


def hot_bf16(cond):
    return jnp.where(cond, 1.0, 0.0).astype(BF16)


def sigmoid(value):
    return 0.5 * jnp.tanh(0.5 * value) + 0.5


def norm(value, axis):
    centred = value - jnp.mean(value, axis, keepdims=True)
    rstd = lax.rsqrt(jnp.mean(centred * centred, axis, keepdims=True) + EPS)
    return centred * rstd, rstd


def norm_back(grad, gain, hat, rstd, axis):
    scaled = grad * gain
    first = jnp.mean(scaled, axis, keepdims=True)
    second = jnp.mean(scaled * hat, axis, keepdims=True)
    return rstd * (scaled - first - hat * second)


def column(row):
    size = row.shape[1]
    eye = iota((size, size), 0) == iota((size, size), 1)
    return jnp.sum(jnp.where(eye, row, 0.0), 1, keepdims=True)


def lane_group(ref, j):
    return jnp.concatenate(
        [ref[pl.ds(2 * j + q, LANES, stride=16), :] for q in range(2)], axis=1
    )


def lane_ungroup(ref, j, value):
    for q in range(2):
        ref[pl.ds(2 * j + q, LANES, stride=16), :] = value[:, q * LANES : (q + 1) * LANES]


def chunk_at(j):
    return pl.ds(pl.multiple_of(j * CHUNK, CHUNK), CHUNK)


def all_peers(D, t):
    return lax.rem(D.s + t % D.ns, D.ns), lax.rem(D.r + t // D.ns, D.nr)


def seq_peers(D, t):
    return lax.rem(D.s + t, D.ns), D.r


def res_peers(D, t):
    return D.s, lax.rem(D.r + t, D.nr)


def sibling(D, t):
    return D.s + 1 - 2 * (D.s % 2), D.r


def chip_peers(D, t):
    return lax.rem(D.s + 2 * t, D.ns), D.r


def remote(src, dst, send, recv, peer):
    return pltpu.make_async_remote_copy(
        src_ref=src,
        dst_ref=dst,
        send_sem=send,
        recv_sem=recv,
        device_id=peer,
        device_id_type=MESH,
    )


def swap(D, src_at, dst_at, count, peers, index, me, like):
    send, recv = D.take()

    @pl.loop(1, count)
    def _(t):
        peer = peers(D, t)
        remote(src_at(index(*peer)), dst_at(me), send, recv, peer).start()

    def wait():
        done = remote(like, like, send, recv, peers(D, 1))
        done.wait_send()
        done.wait_recv()

    return wait


def start_all(D, src, dst, first, size):
    n = D.ns * D.nr
    me = D.s * D.nr + D.r
    rows = pl.ds(first, size)
    dst[me, rows, :] = src[me, rows, :]
    return swap(
        D,
        lambda i: src.at[i, rows],
        lambda i: dst.at[i, rows],
        n,
        all_peers,
        lambda ps, pr: ps * D.nr + pr,
        me,
        dst.at[pl.ds(0, n - 1), rows],
    )


def start_seq(D, src_at, dst_at, like):
    return swap(D, src_at, dst_at, D.ns, seq_peers, lambda ps, pr: ps, D.s, like)


def start_res(D, src_at, dst_at, like):
    return swap(D, src_at, dst_at, D.nr, res_peers, lambda ps, pr: pr, D.r, like)


def pack_columns(value, send):
    for q in range(2):
        first = value[2 * q].astype(F32)
        second = value[2 * q + 1].astype(F32)
        for d in range(8):
            at = slice(8 * d, 8 * d + 8)
            send[d, q] = jnp.concatenate([first[at], second[at]], 0).astype(BF16)


def start_columns(D, send, recv):
    recv[D.s] = send[D.s]
    return start_seq(D, lambda i: send.at[i], lambda i: recv.at[i], recv.at[pl.ds(0, D.ns - 1)])


def unpack_columns(R, recv, target):
    for d in range(8):
        for q in range(2):
            both = recv[d, q].astype(F32)
            for k in range(2):
                rows = pl.ds(4 * d + 2 * q + k, 8, stride=32)
                R.sp0[rows, :] = both[8 * k : 8 * k + 8, :LANES]
                R.sp1[rows, :] = both[8 * k : 8 * k + 8, LANES:]
    target[...] = jnp.concatenate([R.sp0[...], R.sp1[...]], 1)


def p_spread(R, D):
    pack_columns(R.x, R.xsend)
    D.ready()
    wait = start_columns(D, R.xsend, R.xrecv)
    R.arrived("adj_a")
    pack_columns(R.adj_a, R.asend)
    R.wait_adjoint = start_columns(D, R.asend, R.arecv)
    R.arrived("w_ti", "w_ii", "w_oo", "w_qkvg", "w_ao", "pe", "adj_c")
    R.w1t[...] = R.w_ti[...].astype(F32).T.astype(BF16)
    R.w2t[...] = R.w_ii[...].astype(F32).T.astype(BF16)
    R.wo1t[...] = R.w_to[...].astype(F32).T.astype(BF16)
    R.wo2t[...] = R.w_io[...].astype(F32).T.astype(BF16)
    stage_outer_weight(R)
    wait()
    unpack_columns(R, R.xrecv, R.xc)


def flag_column(flags):
    here = iota((256, 32), 0) % 32 == iota((256, 32), 1)
    return jnp.sum(jnp.where(here, flags, 0.0), 1, keepdims=True)


def head_probs(keys, query, flag_rows, head):
    lanes = iota((1, 256), 1) // 32
    mine = hot_bf16(lanes == head)
    scores = dot_nt(keys, query * mine) * (32 ** (-0.5))
    same = iota((256, 256), 0) // 32 == iota((256, 256), 1) // 32
    scores = jnp.where(same, jnp.where(flag_rows > 0, scores, -1e30), -3e38)
    weights = jnp.exp(scores - jnp.max(scores, 0, keepdims=True))
    return weights / jnp.sum(weights, 0, keepdims=True)


def p_attention(R, D):
    flag_rows = flag_column(R.fl[...].astype(F32))
    hat, _ = norm(R.xc[...], -1)
    normed = (hat * R.g1[...]).astype(BF16)
    projected = dot_nn(normed, R.w_qkvg[...])
    R.qkv[...] = projected[:, :768].astype(BF16)
    R.gl[...] = projected[:, 768:]
    R.att[...] = jnp.zeros((256, 256), F32)

    @pl.loop(0, 8, unroll=4)
    def _(head):
        probs = head_probs(R.qkv[:, 256:512], R.qkv[:, :256], flag_rows, head).astype(BF16)
        lanes = iota((1, 256), 1) // 32
        R.att[...] += jnp.where(lanes == head, dot_tn(probs, R.qkv[:, 512:768]), 0.0)

    gated = (sigmoid(R.gl[...]) * R.att[...]).astype(BF16)
    later = R.xc[...] + dot_nn(gated, R.w_ao[...])
    R.msan[...] = later
    hat2, _ = norm(later, -1)
    normed2 = (hat2 * R.g2[...]).astype(BF16)
    outer_in = (dot_nt(normed2, R.w_oit[...]) * (flag_rows > 0).astype(F32)).astype(BF16)
    wide = jnp.concatenate([outer_in.astype(F32), jnp.zeros((256, 64), F32)], 1)
    R.lsend[...] = wide.T[:32].astype(BF16)
    spread = hot_bf16(iota((64, 1024), 0) == 32 + iota((64, 1024), 1) // 32)
    kept = iota((256, 1024), 0) % 32 == iota((256, 1024), 1) % 32
    rows = jnp.where(kept, dot_nn(outer_in, spread), 0.0).astype(BF16)
    R.rsend[...] = dot_nn(hot_bf16(iota((8, 256), 0) == iota((8, 256), 1) // 32), rows)


def p_outer_exchange(R, D):
    send, recv = R.out_send, R.out_recv
    D.all_ready()
    owner = 2 * D.r + D.s // 4
    slot = D.s % 4

    def left(k, to):
        return remote(R.lsend, R.lall.at[to], send.at[k], recv.at[to], (owner, k))

    for k in range(4):
        mine = (owner == D.s) & (D.r == k)

        @pl.when(jnp.logical_not(mine))
        def _():
            left(k, slot).start()

        @pl.when(mine)
        def _():
            R.lall[slot] = R.lsend[...]

    here = pl.ds(pl.multiple_of(8 * D.s, 8), 8)

    def right(t):
        return remote(R.rsend, R.rall.at[here], send.at[4 + t], recv.at[4 + t], seq_peers(D, t))

    @pl.loop(1, 8)
    def _(t):
        right(t).start()

    R.rall[here, :] = R.rsend[...]

    for k in range(4):
        mine = (owner == D.s) & (D.r == k)
        theirs = (4 * (D.s % 2) + k == D.s) & (D.s // 2 == D.r)

        @pl.when(jnp.logical_not(mine))
        def _():
            left(k, k).wait_send()

        @pl.when(jnp.logical_not(theirs))
        def _():
            left(k, k).wait_recv()

    @pl.loop(1, 8)
    def _(t):
        right(t).wait()


def stage_outer_weight(R):
    R.wst[...] = R.w_oo[...].astype(F32)


def outer_weight(R, d):
    return R.wst[pl.ds(d, 32, stride=32), :].astype(BF16)


def count_of(R):
    return jnp.sum(R.fl[...].astype(F32), 1, keepdims=True)


def p_outer(R, D):
    for q in range(4):
        wide = jnp.concatenate([R.lall[q].astype(F32), jnp.zeros((96, 256), F32)], 0)
        R.l2[256 * q : 256 * q + 256, :] = wide.T[:, :32].astype(BF16)
        R.lt[:, 256 * q : 256 * q + 256] = R.lall[q]


def outer_left(R, half):
    left = jnp.concatenate(
        [R.l2[256 * (2 * h + half) : 256 * (2 * h + half) + 256, :] for h in range(2)], 0
    )

    @pl.loop(0, 8, unroll=2)
    def _(e):
        weights = jnp.concatenate([outer_weight(R, 4 * e + u) for u in range(4)], 1)
        part = dot_nn(left, weights).astype(BF16)
        for u in range(4):
            at = pl.ds(pl.multiple_of(32 * (4 * e + u), 32), 32)
            for i in range(16):
                row = 16 * (i // 8) + 8 * half + i % 8
                R.zb[row, at, :] = part[32 * i : 32 * i + 32, LANES * u : LANES * u + LANES]


def outer_rows(R, half):
    inverse = 1.0 / count_of(R)
    right = R.rall[...].astype(BF16)

    @pl.loop(8 * half, 8 * half + 8, unroll=4)
    def _(m):
        both = dot_nn(right, jnp.concatenate([R.zb[m], R.zb[16 + m]], 1)) * inverse
        rows = [
            both[:, LANES * h : LANES * h + LANES] + R.pe[16 * h + m].astype(F32) for h in range(2)
        ]
        R.pair1[:, pl.ds(pl.multiple_of(m * LANES, LANES), LANES)] = jnp.concatenate(rows, 0).T


def pack_both(R, half):
    @pl.loop(0, 32, unroll=4)
    def _(d):
        for pair in range(2):
            for k, stage in ((0, R.st0), (1, R.st1)):
                rows = tile_rows(stage, 64 * d + 32 * pair + 8 * half)
                first = 64 * half + 32 * pair + 16 * k
                R.lrs[d, first : first + 16, :] = rows.astype(BF16)


def pack_single(R, stage, half):
    @pl.loop(0, 32, unroll=4)
    def _(d):
        for pair in range(2):
            first = 32 * half + 16 * pair
            rows = tile_rows(stage, 64 * d + 32 * pair + 8 * half)
            R.ts[d, first : first + 16, :] = rows.astype(BF16)


def tile_rows(stage, start):
    start = pl.multiple_of(start, 8)
    return jnp.concatenate([stage[pl.ds(start, 8), :], stage[pl.ds(start + 16, 8), :]], 0)


def untile(stage, start, rows):
    start = pl.multiple_of(start, 8)
    stage[pl.ds(start, 8), :] = rows[:8]
    stage[pl.ds(start + 16, 8), :] = rows[8:]


def stage_single(recv, stage, half):
    @pl.loop(0, 32, unroll=4)
    def _(d):
        for pair in range(2):
            first = 32 * half + 16 * pair
            rows = recv[d, first : first + 16, :].astype(F32)
            untile(stage, 64 * d + 32 * pair + 8 * half, rows)


def stage_both(R, recv, half):
    @pl.loop(0, 32, unroll=4)
    def _(d):
        for pair in range(2):
            for k, stage in ((0, R.st0), (1, R.st1)):
                first = 64 * half + 32 * pair + 16 * k
                rows = recv[d, first : first + 16, :].astype(F32)
                untile(stage, 64 * d + 32 * pair + 8 * half, rows)


def send_part(D, src, dst, table, half, pair):
    size = src.shape[1] // 4
    table[half, pair] = start_all(D, src, dst, size * (2 * half + pair), size)


def send_half(D, src, dst, table, half):
    for pair in range(2):
        send_part(D, src, dst, table, half, pair)


def wait_half(table, half):
    for pair in range(2):
        table[half, pair]()


def entry_chunk(R, pair, gain, w_t, nb, j):
    hat, _ = norm(pair, 0)
    nb_here = (hat * gain).astype(BF16)
    nb[:, chunk_at(j)] = nb_here
    for k, stage in ((0, R.st0), (1, R.st1)):
        linear = dot_nn(w_t[256 * k : 256 * k + 256, :], nb_here)
        lane_ungroup(stage, j, sigmoid(linear[128:]) * linear[:128])


def p_entry1(R, D):
    gain = column(R.g3[...])
    for half in range(2):
        outer_left(R, half)
        outer_rows(R, half)

        @pl.loop(4 * half, 4 * half + 4, unroll=4)
        def _(j):
            entry_chunk(R, R.pair1[:, chunk_at(j)], gain, R.w1t, R.nb3, j)

        pack_both(R, half)
        send_half(D, R.lrs, R.lr1r, R.waits, half)


def gather_pair(recv, pair, k, mats, at):
    size = recv.shape[1] // 4

    @pl.loop(0, 8, unroll=4)
    def _(s):
        top = pl.ds(pl.multiple_of(32 * s, 32), 16)
        low = pl.ds(pl.multiple_of(32 * s + 16, 16), 16)
        for p in range(2):
            tiles = []
            for q in range(2):
                halves = []
                for half in range(2):
                    first = size * (2 * half + pair) + 16 * k
                    block = recv[4 * s + 2 * p + q, first : first + 16, :]
                    halves.append(block.astype(F32))
                tiles.append(halves)
            lanes = slice(LANES * p, LANES * p + LANES)
            for c in range(2):
                rows = slice(8 * c, 8 * c + 8)
                a, b = (jnp.concatenate([h[rows] for h in halves], 0) for halves in tiles)
                mats[at + c, top, lanes] = jnp.concatenate([a[:, :64], b[:, :64]], 1).astype(BF16)
                mats[at + c, low, lanes] = jnp.concatenate([a[:, 64:], b[:, 64:]], 1).astype(BF16)


def scatter_pair(mats, send, pair, k):
    size = send.shape[1] // 4

    @pl.loop(0, 8, unroll=4)
    def _(s):
        for p in range(2):
            lanes = slice(LANES * p, LANES * p + LANES)
            tiles = [[], []]
            for c in range(2):
                a = mats[c, pl.ds(pl.multiple_of(32 * s, 32), 16), lanes]
                b = mats[c, pl.ds(pl.multiple_of(32 * s + 16, 16), 16), lanes]
                tiles[0].append(jnp.concatenate([a[:, :64], b[:, :64]], 1))
                tiles[1].append(jnp.concatenate([a[:, 64:], b[:, 64:]], 1))
            for q in range(2):
                for half in range(2):
                    first = size * (2 * half + pair) + 16 * k
                    rows = slice(8 * half, 8 * half + 8)
                    block = jnp.concatenate([tile[rows] for tile in tiles[q]], 0)
                    send[4 * s + 2 * p + q, first : first + 16, :] = block.astype(BF16)


def tri_forward(R, D, recv, mats, back, product, meanwhile):
    meanwhile(R, D)
    for pair in range(2):
        R.waits[0, pair]()
        R.waits[1, pair]()
        gather_pair(recv, pair, 0, mats, 2 * pair)
        gather_pair(recv, pair, 1, mats, 4 + 2 * pair)
        for c in range(2):
            R.tm[c] = product(mats[2 * pair + c], mats[4 + 2 * pair + c])
        scatter_pair(R.tm, R.ts, pair, 0)
        send_part(D, R.ts, back, R.later, 0, pair)
    for pair in range(2):
        send_part(D, R.ts, back, R.later, 1, pair)


def tri_backward(R, D, recv, mats, back, products, meanwhile):
    meanwhile(R, D)
    advance(R, D)
    for pair in range(2):
        R.waits[0, pair]()
        R.waits[1, pair]()
        gather_pair(recv, pair, 0, R.dm, 0)
        for k in range(2):
            for c in range(2):
                at = 2 * pair + c
                R.tm[c] = products[k](mats[at], mats[4 + at], R.dm[c])
            scatter_pair(R.tm, R.lrs, pair, k)
        send_part(D, R.lrs, back, R.later, 0, pair)
        if not pair:
            advance(R, D)
    for pair in range(2):
        send_part(D, R.lrs, back, R.later, 1, pair)
    advance(R, D)


def p_tri1(R, D):
    tri_forward(R, D, R.lr1r, R.mats1, R.t1r, dot_nt, p_still)


def p_middle(R, D):
    gain4 = column(R.g4[...])
    gain5 = column(R.g5[...])
    for half in range(2):
        wait_half(R.later, half)
        stage_single(R.t1r, R.st2, half)

        @pl.loop(4 * half, 4 * half + 4, unroll=4)
        def _(j):
            hat, _ = norm(lane_group(R.st2, j), 0)
            nb4 = (hat * gain4).astype(BF16)
            R.nb4[:, chunk_at(j)] = nb4
            update = dot_nn(R.wo1t[...], nb4)
            gate = sigmoid(dot_nn(R.w1t[512:, :], R.nb3[:, chunk_at(j)]))
            pair2 = R.pair1[:, chunk_at(j)] + gate * update
            R.pair2[:, chunk_at(j)] = pair2
            entry_chunk(R, pair2, gain5, R.w2t, R.nb5, j)

        pack_both(R, half)
        send_half(D, R.lrs, R.lr2r, R.waits, half)


def p_tri2(R, D):
    tri_forward(R, D, R.lr2r, R.mats2, R.t2r, dot_tn, p_values)


def chunk_rows(D, j):
    lane = iota((1, CHUNK), 1)
    local = 16 * ((lane % LANES) // 64) + 2 * j + lane // LANES
    return local, hot_bf16(iota((256, CHUNK), 0) == 32 * D.s + local)


def near_rows(D):
    return hot_bf16(iota((256, CHUNK), 0) == 64 * D.r + iota((256, CHUNK), 1) % 64)


def p_still(R, D):
    dist = column(R.w_ds[...])
    inv_k = 1.0 / R.ca.shape[1]
    R.at8[...] = jnp.zeros((8, 256), F32)
    R.at8[0:3, :] = R.at[...]
    R.la8[...] = jnp.zeros((8, 32), F32)
    R.la8[0:3, :] = R.adj_l[...]
    R.nodet[...] = dot_tn(R.vet[...].astype(BF16), R.w_nd[...]).T
    R.dmean[...] = dot_nt(R.w_up[...], R.adj_v[...].astype(BF16))
    near = near_rows(D)
    R.nbase[...] = pick_nn(R.nodet[64:, :], near, 2)
    R.cbase[...] = pick_nn(R.at8[...], near, 3)
    R.nb_f[...] = R.ca[...].astype(F32)

    @pl.loop(0, 8, unroll=2)
    def _(j):
        here = chunk_at(j)
        local, row = chunk_rows(D, j)
        mine = hot_bf16(iota((32, CHUNK), 0) == local)
        named = dot_tn(R.nb_f[...].astype(BF16), mine)
        target = (64 * D.r + iota((1, CHUNK), 1) % 64).astype(F32)
        mask = jnp.max(jnp.where(named == target, 1.0, 0.0), 0, keepdims=True) * inv_k
        diff = pick_nn(R.at8[...], row, 3) - R.cbase[...]
        square = 1.0 + jnp.sum(diff * diff, 0, keepdims=True)
        radial = jnp.log(square)
        R.geo[0:8, here] = diff
        R.geo[8:16, here] = pick_nn(R.la8[...], mine, 3)
        R.geo[16:17, here] = radial
        R.geo[17:18, here] = mask
        R.geo[18:19, here] = 2.0 / square
        R.pre[0:64, here] = pick_nn(R.nodet[0:64, :], row, 2) + R.nbase[...] + radial * dist
        R.pre[64:128, here] = pick_nn(R.dmean[...], mine, 2) * mask
        for q in range(2):
            m = 2 * j + q
            both = jnp.concatenate([R.adj_c[m], R.adj_c[16 + m]], 0).astype(F32)
            R.dpair[:, pl.ds(pl.multiple_of(m * LANES, LANES), LANES)] = both.T


def p_turn(R, D):
    gain6 = column(R.g6[...])
    dist = column(R.w_ds[...])
    turn_weight = column(R.w_sl[...])
    R.a_g6[...] = jnp.zeros((128, CHUNK), F32)

    def chunk(j):
        here = chunk_at(j)
        hat, rstd = norm(lane_group(R.st2, j), 0)
        nb6 = (hat * gain6).astype(BF16)
        R.nb6[:, here] = nb6
        update2 = dot_nn(R.wo2t[...], nb6)
        gate2 = sigmoid(dot_nn(R.w2t[512:, :], R.nb5[:, here]))
        pair3 = R.pair2[:, here] + gate2 * update2
        po_b = pair3.astype(BF16)
        R.po[:, here] = po_b
        pre = R.pre[0:64, here] + dot_nn(R.w_edt[...], po_b)
        sig_pre = sigmoid(pre)
        hidden = (pre * sig_pre).astype(BF16)
        R.hid[:, here] = hidden
        msg = dot_tn(R.w_ms[...], hidden)
        sig_msg = sigmoid(msg)
        message = msg * sig_msg
        turn = jnp.tanh(jnp.sum(message * turn_weight, 0, keepdims=True))
        diff = R.geo[0:8, here]
        locadj = R.geo[8:16, here]
        mask = R.geo[17:18, here]
        d_turn = jnp.sum(locadj * diff, 0, keepdims=True) * mask * (1.0 - turn * turn)
        d_message = R.pre[64:128, here] + turn_weight * d_turn
        d_msg = (d_message * sig_msg * (1.0 + msg * (1.0 - sig_msg))).astype(BF16)
        R.dmsg[:, here] = d_msg
        d_pre = dot_nn(R.w_ms[...], d_msg) * sig_pre * (1.0 + pre * (1.0 - sig_pre))
        d_edge = d_pre.astype(BF16)
        R.dedge[:, here] = d_edge
        d_radial = jnp.sum(d_pre * dist, 0, keepdims=True)
        R.pre[0:64, here] = message
        R.pre[64:128, here] = d_pre
        R.geo[19:20, here] = turn * mask
        R.geo[20:21, here] = d_turn
        R.geo[24:32, here] = (d_radial * R.geo[18:19, here]) * diff + locadj * (turn * mask)
        d_pair3 = R.dpair[:, here] + dot_tn(R.w_edt[...], d_edge)
        R.dpair[:, here] = d_pair3
        d_up = (d_pair3 * gate2).astype(BF16)
        R.dup2[:, here] = d_up
        R.dtri2[512:, here] = (d_pair3 * update2 * gate2 * (1.0 - gate2)).astype(BF16)
        d_nb = dot_nn(R.w_io[...], d_up)
        R.a_g6[...] += d_nb * hat
        lane_ungroup(R.st0, j, norm_back(d_nb, gain6, hat, rstd, 0))

    for half in range(2):
        wait_half(R.later, half)
        stage_single(R.t2r, R.st2, half)
        pl.loop(4 * half, 4 * half + 4, unroll=4)(chunk)
        pack_single(R, R.st0, half)
        send_half(D, R.ts, R.dt2r, R.waits, half)


def p_turn_grads(R, D):
    R.g_io[...] = dot_nt(R.nb6[...], R.dup2[...])
    R.g_ed[...] = dot_nt(R.dedge[...], R.po[...])
    R.g_ms[...] = dot_nt(R.hid[...], R.dmsg[...])
    R.gg6[...] = jnp.sum(R.a_g6[...], 1, keepdims=True)
    R.g_ds[...] = jnp.sum(R.pre[64:128, :] * R.geo[16:17, :], 1, keepdims=True)
    R.g_sl[...] = jnp.sum(R.pre[0:64, :] * R.geo[20:21, :], 1, keepdims=True)
    for acc in (R.s_mean, R.s_own, R.s_other):
        acc[...] = jnp.zeros(acc.shape, F32)
    R.s_xyz[...] = jnp.zeros((16, 256), F32)

    @pl.loop(0, 8, unroll=2)
    def _(j):
        here = chunk_at(j)
        _, row = chunk_rows(D, j)
        near = near_rows(D)
        d_pre = R.pre[64:128, here]
        d_diff = R.geo[24:32, here]
        R.s_mean[...] += pick_nt(R.pre[0:64, here] * R.geo[17:18, here], row, 2)
        R.s_own[...] += pick_nt(d_pre, row, 2)
        R.s_other[...] += pick_nt(d_pre, near, 2)
        R.s_xyz[0:8, :] += pick_nt(R.geo[0:8, here] * R.geo[19:20, here], row, 2)
        R.s_xyz[8:16, :] += pick_nt(d_diff, row, 2) - pick_nt(d_diff, near, 2)
        for q in range(2):
            m = 2 * j + q
            at = pl.ds(pl.multiple_of(m * LANES, LANES), LANES)
            out = R.po[:, at].astype(F32).T.astype(BF16)
            R.pair_out[m] = out[:64]
            R.pair_out[16 + m] = out[64:]

    R.leave("pair_out")


def p_turn_rest(R, D):
    p_turn_grads(R, D)
    p_sum0(R, D)
    for half in range(2):
        stage_single(R.t1r, R.st2, half)


def p_back2(R, D):
    tri_backward(
        R,
        D,
        R.dt2r,
        R.mats2,
        R.dlr2r,
        (lambda a, b, d: dot_nt(b, d), lambda a, b, d: dot_nn(a, d)),
        p_turn_rest,
    )


def gates_back(R, d_tri, w_t, nb_here, j):
    here = chunk_at(j)
    for k, stage in ((0, R.st0), (1, R.st1)):
        grad = lane_group(stage, j)
        linear = dot_nn(w_t[256 * k : 256 * k + 256, :], nb_here)
        gate = sigmoid(linear[128:])
        d_first = grad * gate
        d_tri[256 * k : 256 * k + 128, here] = d_first.astype(BF16)
        d_tri[256 * k + 128 : 256 * k + 256, here] = (
            d_first * linear[:128] * (1.0 - gate)
        ).astype(BF16)


def p_between(R, D):
    gain4 = column(R.g4[...])
    gain5 = column(R.g5[...])
    R.a_g4[...] = jnp.zeros((128, CHUNK), F32)
    R.a_g5[...] = jnp.zeros((128, CHUNK), F32)

    def chunk(j):
        here = chunk_at(j)
        gates_back(R, R.dtri2, R.w2t, R.nb5[:, here], j)
        d_nb5 = dot_nn(R.w_ii[...], R.dtri2[:, here])
        hat5, rstd5 = norm(R.pair2[:, here], 0)
        R.a_g5[...] += d_nb5 * hat5
        d_pair2 = R.dpair[:, here] + norm_back(d_nb5, gain5, hat5, rstd5, 0)
        R.dpair[:, here] = d_pair2
        gate = sigmoid(dot_nn(R.w1t[512:, :], R.nb3[:, here]))
        update = dot_nn(R.wo1t[...], R.nb4[:, here])
        d_up = (d_pair2 * gate).astype(BF16)
        R.dup1[:, here] = d_up
        R.dtri1[512:, here] = (d_pair2 * update * gate * (1.0 - gate)).astype(BF16)
        d_nb4 = dot_nn(R.w_to[...], d_up)
        hat4, rstd4 = norm(lane_group(R.st2, j), 0)
        R.a_g4[...] += d_nb4 * hat4
        lane_ungroup(R.st3, j, norm_back(d_nb4, gain4, hat4, rstd4, 0))

    for half in range(2):
        wait_half(R.later, half)
        stage_both(R, R.dlr2r, half)
        pl.loop(4 * half, 4 * half + 4, unroll=4)(chunk)
        pack_single(R, R.st3, half)
        send_half(D, R.ts, R.dt1r, R.waits, half)


def p_between_grads(R, D):
    R.g_ii[...] = dot_nt(R.nb5[...], R.dtri2[...])
    R.g_to[...] = dot_nt(R.nb4[...], R.dup1[...])
    R.gg5[...] = jnp.sum(R.a_g5[...], 1, keepdims=True)
    R.gg4[...] = jnp.sum(R.a_g4[...], 1, keepdims=True)
    p_sum1(R, D)


def p_back1(R, D):
    tri_backward(
        R,
        D,
        R.dt1r,
        R.mats1,
        R.dlr1r,
        (lambda a, b, d: dot_nn(d, b), lambda a, b, d: dot_tn(d, a)),
        p_between_grads,
    )


def p_pair_end(R, D):
    gain3 = column(R.g3[...])
    R.a_g3[...] = jnp.zeros((128, CHUNK), F32)
    inverse = 1.0 / count_of(R)

    def chunk(j):
        here = chunk_at(j)
        gates_back(R, R.dtri1, R.w1t, R.nb3[:, here], j)
        d_nb3 = dot_nn(R.w_ti[...], R.dtri1[:, here])
        hat3, rstd3 = norm(R.pair1[:, here], 0)
        R.a_g3[...] += d_nb3 * hat3
        d_pair1 = R.dpair[:, here] + norm_back(d_nb3, gain3, hat3, rstd3, 0)
        for q in range(2):
            m = 2 * j + q
            out = d_pair1[:, q * LANES : (q + 1) * LANES].T
            R.pair_grad[m] = out[:64]
            R.pair_grad[16 + m] = out[64:]
            small = (out * inverse).astype(BF16)
            R.dopm[m] = small[:64]
            R.dopm[16 + m] = small[64:]

    for half in range(2):
        wait_half(R.later, half)
        stage_both(R, R.dlr1r, half)
        pl.loop(4 * half, 4 * half + 4, unroll=4)(chunk)
        if not half:
            advance(R, D)
            R.rt[...] = R.rall[...].T.astype(BF16)
            R.dright[...] = jnp.zeros((64, 1024), F32)
            outer_right_back(R, 0)
    R.leave("pair_grad")


def p_pair_grads(R, D):
    R.g_ti[...] = dot_nt(R.nb3[...], R.dtri1[...])
    R.gg3[...] = jnp.sum(R.a_g3[...], 1, keepdims=True)


def outer_right_back(R, half):
    @pl.loop(0, 2)
    def _(h):
        first = 16 * h + 8 * half
        grad = jnp.concatenate([R.dopm[first + u] for u in range(8)], 1)
        R.dright[...] += dot_nt(grad, jnp.concatenate([R.zb[first + u] for u in range(8)], 1))


def p_outer_back(R, D):
    outer_right_back(R, 1)

    @pl.loop(1, 8)
    def _(t):
        right_return(R, D, t).start()

    R.drr[D.s] = R.dright[pl.ds(pl.multiple_of(8 * D.s, 8), 8), :]
    R.dleft[...] = jnp.zeros((32, 1024), F32)

    @pl.loop(0, 4)
    def _(g):
        right = R.rt[pl.ds(pl.multiple_of(256 * g, 256), 256), :]

        @pl.loop(0, 16, unroll=16)
        def _(k):
            grad = jnp.concatenate([R.dopm[2 * k], R.dopm[2 * k + 1]], 1)
            both = dot_nn(right, grad).astype(BF16)
            for h in range(2):
                at = pl.ds(pl.multiple_of(64 * k + 32 * h, 32), 32)
                for u in range(8):
                    block = both[32 * u : 32 * u + 32, LANES * h : LANES * h + LANES]
                    R.zb[8 * g + u, at, :] = block

        weights = jnp.concatenate([outer_weight(R, 8 * g + u) for u in range(8)], 1)
        R.dleft[...] += dot_nt(weights, jnp.concatenate([R.zb[8 * g + u] for u in range(8)], 1))

    for q in range(4):
        R.dls[q] = R.dleft[:, 256 * q : 256 * q + 256].astype(BF16)


def right_return(R, D, t):
    peer = seq_peers(D, t)
    at = pl.ds(pl.multiple_of(8 * peer[0], 8), 8)
    sems = R.back_send.at[4 + t], R.back_recv.at[4 + t]
    return remote(R.dright.at[at], R.drr.at[D.s], *sems, peer)


def p_outer_grads(R, D):
    @pl.loop(0, 4)
    def _(g):
        rows = jnp.concatenate([R.zb[8 * g + u] for u in range(8)], 1)
        total = dot_nn(R.lt[...], rows)
        for u in range(8):
            R.st1[pl.ds(8 * g + u, 32, stride=32), :] = total[:, LANES * u : LANES * u + LANES]

    R.g_oo[...] = R.st1[0:1024, :]


def p_outer_return(R, D):
    send, recv = R.back_send, R.back_recv
    column_res = D.s // 2
    owner = 2 * D.r + D.s // 4

    def left(q, slot):
        peer = (4 * (D.s % 2) + q, column_res)
        return remote(R.dls.at[q], R.dlr.at[slot], send.at[q], recv.at[slot], peer)

    for q in range(4):
        mine = (4 * (D.s % 2) + q == D.s) & (column_res == D.r)

        @pl.when(jnp.logical_not(mine))
        def _():
            left(q, D.r).start()

        @pl.when(mine)
        def _():
            R.dlr[D.r] = R.dls[q]

    p_pair_grads(R, D)
    p_outer_grads(R, D)
    advance(R, D)
    p_sum2(R, D)

    for q in range(4):
        mine = (4 * (D.s % 2) + q == D.s) & (column_res == D.r)
        theirs = (owner == D.s) & (D.r == q)

        @pl.when(jnp.logical_not(mine))
        def _():
            left(q, q).wait_send()

        @pl.when(jnp.logical_not(theirs))
        def _():
            left(q, q).wait_recv()

    @pl.loop(1, 8)
    def _(t):
        right_return(R, D, t).wait()


def p_attention_back(R, D):
    flag_rows = flag_column(R.fl[...].astype(F32))
    live = (flag_rows > 0).astype(F32)
    left = R.dlr[0].astype(F32)
    for k in range(1, 4):
        left += R.dlr[k].astype(F32)
    right = R.drr[0]
    for k in range(1, 8):
        right += R.drr[k]
    wide = jnp.concatenate([left, jnp.zeros((96, 256), F32)], 0).T
    spread = dot_nn(
        hot_bf16(iota((256, 8), 0) // 32 == iota((256, 8), 1)), right.astype(BF16)
    )
    kept = iota((256, 1024), 0) % 32 == iota((256, 1024), 1) % 32
    spread = jnp.where(kept, spread, 0.0).astype(BF16)
    back = hot_bf16(32 + iota((1024, LANES), 0) // 32 == iota((1024, LANES), 1))
    d_in = ((wide + dot_nn(spread, back)) * live).astype(BF16)[:, :64]
    hat2, rstd2 = norm(R.msan[...], -1)
    normed2 = (hat2 * R.g2[...]).astype(BF16)
    R.g_oi[...] = dot_tn(d_in, normed2)
    d_normed2 = dot_nn(d_in, R.w_oit[...])
    R.gg2[...] = jnp.sum(d_normed2 * hat2, 0, keepdims=True)
    d_later = R.ac[...] + norm_back(d_normed2, R.g2[...], hat2, rstd2, -1)
    R.dlater[...] = d_later
    d_exit = d_later.astype(BF16)
    gate = sigmoid(R.gl[...])
    gated = (gate * R.att[...]).astype(BF16)
    R.g_ao[...] = dot_tn(gated, d_exit)
    d_gated = dot_nt(d_exit, R.w_ao[...])
    R.datt[...] = (d_gated * gate).astype(BF16)
    R.dproj[:, 768:] = (d_gated * R.att[...] * gate * (1.0 - gate)).astype(BF16)
    hat, rstd = norm(R.xc[...], -1)
    R.normed[...] = (hat * R.g1[...]).astype(BF16)
    R.c_gate[...] = dot_tn(R.normed[...], R.dproj[:, 768:])
    advance(R, D)
    p_sum3(R, D)
    R.dqkv[...] = jnp.zeros((256, 768), F32)

    @pl.loop(0, 8, unroll=4)
    def _(head):
        lanes = iota((1, 256), 1) // 32
        mine = lanes == head
        hot = hot_bf16(mine)
        query = R.qkv[:, 0:256]
        keys = R.qkv[:, 256:512]
        probs = head_probs(keys, query, flag_rows, head)
        d_att = R.datt[...]
        d_probs = dot_nt(R.qkv[:, 512:768], d_att * hot)
        total = jnp.sum(probs * d_probs, 0, keepdims=True)
        d_scores = (probs * (d_probs - total) * (32 ** (-0.5))).astype(BF16)
        R.dqkv[:, 0:256] += jnp.where(mine, dot_tn(d_scores, keys), 0.0)
        R.dqkv[:, 256:512] += jnp.where(mine, dot_nn(d_scores, query), 0.0)
        R.dqkv[:, 512:768] += jnp.where(mine, dot_nn(probs.astype(BF16), d_att), 0.0)

    R.dproj[:, :768] = R.dqkv[...].astype(BF16)
    R.c_qkv[...] = dot_tn(R.normed[...], R.dproj[:, :768])
    begin(R, D, 4)
    d_normed = dot_nt(R.dproj[...], R.w_qkvg[...])
    hat, rstd = norm(R.xc[...], -1)
    R.dlater[...] += norm_back(d_normed, R.g1[...], hat, rstd, -1)
    group_columns(R, R.dlater, R.gsend)


def group_columns(R, value, send):
    R.sp0[...] = value[:, :LANES]
    R.sp1[...] = value[:, LANES:]
    for d in range(8):
        for q in range(2):
            parts = []
            for k in range(2):
                rows = pl.ds(4 * d + 2 * q + k, 8, stride=32)
                parts.append(jnp.concatenate([R.sp0[rows, :], R.sp1[rows, :]], 1))
            send[d, q] = jnp.concatenate(parts, 0).astype(BF16)


def ungroup_columns(recv, target):
    for q in range(2):
        blocks = [recv[d, q].astype(F32) for d in range(8)]
        for k in range(2):
            rows = jnp.concatenate([block[8 * k : 8 * k + 8] for block in blocks], 0)
            target[2 * q + k] = rows.astype(target.dtype)


def p_send_value(R, D):
    group_columns(R, R.msan, R.osend)
    R.wait_value = start_columns(D, R.osend, R.orecv)


def p_values(R, D):
    p_send_value(R, D)
    R.wait_value()
    ungroup_columns(R.orecv, R.msa_out)
    R.leave("msa_out")
    R.wait_adjoint()
    unpack_columns(R, R.arecv, R.ac)


SEGMENTS = (
    dict(
        g_io=(128, 128),
        s_mean=(64, 256),
        s_own=(64, 256),
        s_other=(64, 256),
        s_vadj=(64, 256),
        s_xyz=(16, 256),
        g_ed=(64, 128),
        g_ms=(64, 64),
        small0=(16, 128),
    ),
    dict(g_ii=(128, 640), g_to=(128, 128), small1=(16, 128)),
    dict(g_ti=(128, 640), g_oo=(1024, 128), small2=(16, 128)),
    dict(g_ao=(256, 256), c_gate=(256, 256), g_oi=(64, 256), small3=(16, 128)),
    dict(c_qkv=(256, 768)),
)


def segment_layout(index):
    layout = []
    start = 0
    for name, (rows, cols) in SEGMENTS[index].items():
        for lane in range(0, cols, LANES):
            layout.append((name, start, rows, lane, min(LANES, cols - lane)))
            start += rows
    return layout, -(-start // 512) * 512


def pack_segment(R, index):
    layout, total = segment_layout(index)
    pay = R.pay[index]
    for name, start, count, lane, width in layout:
        value = getattr(R, name)[:, lane : lane + width]
        pay[start : start + count, 0:width] = value.astype(BF16)
    end = layout[-1][1] + layout[-1][2]
    if end < total:
        pay[end:total, :] = jnp.zeros((total - end, LANES), BF16)


def rows_of(index, size):
    return pl.ds(pl.multiple_of(index * size, size), size)


def sum_segment(R, D, index):
    pay, full = R.pay[index], R.full[index]
    first, second, third, fourth, fifth, sixth = (table[index] for table in R.parts)
    half = pay.shape[0] // 2
    eighth = half // 4
    part = eighth // 4
    core, chip = D.s % 2, D.s // 2
    place = core * 4 + chip
    pack_segment(R, index)
    theirs = pay.at[rows_of(1 - core, half)]
    wait = swap(D, lambda i: theirs, lambda i: first, 2, sibling, lambda ps, pr: 0, 0, first)
    yield
    wait()
    total = pay[rows_of(core, half), :].astype(F32) + first[...].astype(F32)
    second[...] = total.astype(BF16)
    third[chip] = second[rows_of(chip, eighth), :]
    wait = swap(
        D,
        lambda i: second.at[rows_of(i, eighth)],
        lambda i: third.at[i],
        4,
        chip_peers,
        lambda ps, pr: ps // 2,
        chip,
        second.at[pl.ds(0, 3 * eighth)],
    )
    yield
    wait()
    total = third[0].astype(F32)
    for k in range(1, 4):
        total += third[k].astype(F32)
    fourth[...] = total.astype(BF16)
    fifth[D.r] = fourth[rows_of(D.r, part), :]
    some = pl.ds(0, part * (D.nr - 1))
    wait = start_res(
        D, lambda i: fourth.at[rows_of(i, part)], lambda i: fifth.at[i], fourth.at[some]
    )
    yield
    wait()
    total = fifth[0].astype(F32)
    for k in range(1, 4):
        total += fifth[k].astype(F32)
    sixth[...] = total.astype(BF16)
    mine = pl.ds(pl.multiple_of(place * eighth + D.r * part, part), part)
    full[mine, :] = sixth[...]
    wait = start_res(D, lambda i: sixth, lambda i: full.at[mine], full.at[some])
    yield
    wait()
    mine = full.at[rows_of(place, eighth)]
    most = full.at[pl.ds(0, 3 * eighth)]
    wait = swap(D, lambda i: mine, lambda i: mine, 4, chip_peers, lambda ps, pr: 0, 0, most)
    yield
    wait()
    mine = full.at[rows_of(core, half)]
    wait = swap(D, lambda i: mine, lambda i: mine, 2, sibling, lambda ps, pr: 0, 0, first)
    yield
    wait()
    R.leave(index)


def advance(R, D):
    R.chains = [chain for chain in R.chains if next(chain, D) is not D]


def begin(R, D, index):
    chain = sum_segment(R, D, index)
    next(chain)
    R.chains.append(chain)


def p_sum0(R, D):
    place = hot_bf16(iota((32, 256), 1) == 32 * D.s + iota((32, 256), 0))
    first = jnp.where(D.r == 0, 1.0, 0.0)
    R.s_vadj[...] = dot_tn(R.adj_v[...].astype(BF16), place) * first
    small_rows(R, R.small0, (R.gg6, R.g_ds, R.g_sl))
    begin(R, D, 0)


def small_rows(R, target, values):
    R.small[...] = jnp.zeros((128, LANES), F32)
    for k, value in enumerate(values):
        R.small[0 : value.shape[0], k : k + 1] = value[...]
    target[...] = R.small[...].T[:16]


def p_sum1(R, D):
    small_rows(R, R.small1, (R.gg5, R.gg4))
    begin(R, D, 1)


def p_sum2(R, D):
    small_rows(R, R.small2, (R.gg3,))
    begin(R, D, 2)


def p_sum3(R, D):
    R.small3[...] = jnp.zeros((16, LANES), F32)
    for half in range(2):
        R.small3[half : half + 1, :] = R.gg2[:, LANES * half : LANES * half + LANES]
    begin(R, D, 3)


def p_sums(R, D):
    wait = start_columns(D, R.gsend, R.grecv)
    advance(R, D)
    advance(R, D)
    wait()
    ungroup_columns(R.grecv, R.msa_grad)
    R.leave("msa_grad")
    while R.chains:
        advance(R, D)


def unpack_segment(R, index):
    held = {}
    for name, start, count, lane, width in segment_layout(index)[0]:
        value = R.full[index][start : start + count, 0:width].astype(F32)
        if name.startswith("g_"):
            getattr(R, "o_" + name)[:, lane : lane + width] = value
        else:
            held.setdefault(name, []).append(value)
    return {name: jnp.concatenate(parts, 1) for name, parts in held.items()}


def p_finish(R, D):
    R.arrived(1)
    small = unpack_segment(R, 1)["small1"]
    R.o_gg5[...] = small[0:1]
    R.o_gg4[...] = small[1:2]
    R.leave(R.o_g_ii)
    R.arrived(2)
    R.o_gg3[...] = unpack_segment(R, 2)["small2"][0:1]
    R.leave(R.o_g_ti, R.o_g_oo)
    R.arrived(3)
    held = unpack_segment(R, 3)
    R.leave(R.o_g_ao)
    for half in range(2):
        R.o_gg2[:, LANES * half : LANES * half + LANES] = held["small3"][half : half + 1]
    R.o_g_qkvg[:, 768:] = held["c_gate"]
    R.arrived(4)
    R.o_g_qkvg[:, :768] = unpack_segment(R, 4)["c_qkv"]
    R.leave(R.o_g_qkvg)
    R.pass_on()
    R.arrived(5)
    total = jnp.sum(R.w_far[...].astype(F32) * R.o_g_qkvg[...], 1, keepdims=True)
    eye = iota((256, 256), 0) == iota((256, 256), 1)
    R.o_gg1[...] = jnp.sum(jnp.where(eye, total, 0.0), 0, keepdims=True) / R.g1[...]
    R.arrived(0)
    held = unpack_segment(R, 0)
    small = held["small0"]
    R.o_gg6[...] = small[0:1]
    R.o_g_ds[...] = small[1:2, :64]
    R.o_g_sl[...] = small[2:3, :64]
    mean_b = held["s_mean"].astype(BF16)
    R.o_g_up[...] = dot_nt(mean_b, held["s_vadj"].astype(BF16))
    d_node = jnp.concatenate([held["s_own"], held["s_other"]], 0).astype(BF16)
    R.o_g_nd[...] = dot_nt(R.vet[...].astype(BF16), d_node)
    step = dot_tn(R.w_up[...], mean_b)
    grad = dot_nn(R.w_nd[...], d_node)
    R.rows_f[...] = jnp.concatenate([step + R.vet[...], grad], 0).T
    here = pl.ds(pl.multiple_of(32 * D.s, 32), 32)
    mine = R.rows_f[here, :]
    R.single_out[...] = mine[:, :64]
    R.single_grad[...] = R.adj_v[...] + mine[:, 64:]
    R.xyz[...] = jnp.zeros((128, 256), F32)
    R.xyz[0:16, :] = held["s_xyz"]
    R.xyz[16:19, :] = R.at[...]
    R.rows_g[...] = R.xyz[...].T
    turned = R.rows_g[here, :]
    back = jnp.concatenate([turned, jnp.zeros((96, 128), F32)], 0).T
    R.coords_out[...] = back[16:19, 0:32] + back[0:3, 0:32]
    R.coords_grad[...] = R.adj_l[...] + back[8:11, 0:32]


KEPT = dict(
    xsend=((8, 2, 16, 256), BF16),
    xrecv=((8, 2, 16, 256), BF16),
    asend=((8, 2, 16, 256), BF16),
    arecv=((8, 2, 16, 256), BF16),
    osend=((8, 2, 16, 256), BF16),
    orecv=((8, 2, 16, 256), BF16),
    gsend=((8, 2, 16, 256), BF16),
    grecv=((8, 2, 16, 256), BF16),
    wst=((1024, 128), F32),
    lt=((32, 1024), BF16),
    tm=((2, 256, 256), F32),
    geo=((32, 2048), F32),
    pre=((128, 2048), F32),
    small0=((16, 128), F32),
    small1=((16, 128), F32),
    small2=((16, 128), F32),
    small3=((16, 128), F32),
    xc=((256, 256), F32),
    ac=((256, 256), F32),
    sp0=((256, 128), F32),
    sp1=((256, 128), F32),
    qkv=((256, 768), BF16),
    gl=((256, 256), F32),
    att=((256, 256), F32),
    msan=((256, 256), F32),
    lsend=((32, 256), BF16),
    rsend=((8, 1024), F32),
    lall=((4, 32, 256), BF16),
    rall=((64, 1024), F32),
    st0=((2048, 128), F32),
    st1=((2048, 128), F32),
    st2=((2048, 128), F32),
    st3=((2048, 128), F32),
    l2=((1024, 32), BF16),
    zb=((32, 1024, 128), BF16),
    pair1=((128, 2048), F32),
    pair2=((128, 2048), F32),
    dpair=((128, 2048), F32),
    w1t=((640, 128), BF16),
    w2t=((640, 128), BF16),
    wo1t=((128, 128), BF16),
    wo2t=((128, 128), BF16),
    nb3=((128, 2048), BF16),
    nb4=((128, 2048), BF16),
    nb5=((128, 2048), BF16),
    nb6=((128, 2048), BF16),
    po=((128, 2048), BF16),
    hid=((64, 2048), BF16),
    dmsg=((64, 2048), BF16),
    dedge=((64, 2048), BF16),
    dup1=((128, 2048), BF16),
    dup2=((128, 2048), BF16),
    dtri1=((640, 2048), BF16),
    dtri2=((640, 2048), BF16),
    mats1=((8, 256, 256), BF16),
    mats2=((8, 256, 256), BF16),
    dm=((2, 256, 256), BF16),
    lrs=((32, 128, 128), BF16),
    lr1r=((32, 128, 128), BF16),
    lr2r=((32, 128, 128), BF16),
    dlr1r=((32, 128, 128), BF16),
    dlr2r=((32, 128, 128), BF16),
    ts=((32, 64, 128), BF16),
    t1r=((32, 64, 128), BF16),
    t2r=((32, 64, 128), BF16),
    dt1r=((32, 64, 128), BF16),
    dt2r=((32, 64, 128), BF16),
    at8=((8, 256), F32),
    la8=((8, 32), F32),
    nodet=((128, 256), F32),
    dmean=((64, 32), F32),
    nbase=((64, 256), F32),
    cbase=((8, 256), F32),
    nb_f=((32, 64), F32),
    s_mean=((64, 256), F32),
    s_own=((64, 256), F32),
    s_other=((64, 256), F32),
    s_vadj=((64, 256), F32),
    s_xyz=((16, 256), F32),
    a_g3=((128, 256), F32),
    a_g4=((128, 256), F32),
    a_g5=((128, 256), F32),
    a_g6=((128, 256), F32),
    gg3=((128, 1), F32),
    gg4=((128, 1), F32),
    gg5=((128, 1), F32),
    gg6=((128, 1), F32),
    gg2=((1, 256), F32),
    g_ds=((64, 1), F32),
    g_sl=((64, 1), F32),
    g_io=((128, 128), F32),
    g_to=((128, 128), F32),
    g_ti=((128, 640), F32),
    g_ii=((128, 640), F32),
    g_ed=((64, 128), F32),
    g_ms=((64, 64), F32),
    g_oo=((1024, 128), F32),
    g_oi=((64, 256), F32),
    g_ao=((256, 256), F32),
    c_gate=((256, 256), F32),
    c_qkv=((256, 768), F32),
    normed=((256, 256), BF16),
    small=((128, 128), F32),
    dopm=((32, 64, 128), BF16),
    rt=((1024, 64), BF16),
    dright=((64, 1024), F32),
    dleft=((32, 1024), F32),
    dls=((4, 32, 256), BF16),
    dlr=((4, 32, 256), BF16),
    drr=((8, 8, 1024), F32),
    dlater=((256, 256), F32),
    datt=((256, 256), BF16),
    dproj=((256, 1024), BF16),
    dqkv=((256, 768), F32),
)
SIZES = [segment_layout(index)[1] for index in range(len(SEGMENTS))]
PAYLOADS = [((size, 128), BF16) for size in SIZES]
PARTIAL = (
    [((size // 2, 128), BF16) for size in SIZES]
    + [((size // 2, 128), BF16) for size in SIZES]
    + [((4, size // 8, 128), BF16) for size in SIZES]
    + [((size // 8, 128), BF16) for size in SIZES]
    + [((4, size // 32, 128), BF16) for size in SIZES]
    + [((size // 32, 128), BF16) for size in SIZES]
)
LARGE = ("msa_out", "pair_out", "msa_grad", "pair_grad")
MOVED_IN = ("adj_a", "w_qkvg", "w_ao", "w_oo", "w_ti", "w_ii", "pe", "adj_c")
BIG = ("o_g_ii", "o_g_ti", "o_g_oo", "o_g_ao", "o_g_qkvg")
FINISH = ("g1", "vet", "w_up", "w_nd", "adj_v", "at", "adj_l")
FINISH_KEPT = dict(
    rows_f=((256, 128), F32), rows_g=((256, 128), F32), xyz=((128, 256), F32)
)
RESULTS = dict(
    msa_out=((4, 64, 256), BF16),
    pair_out=((32, 64, 128), BF16),
    single_out=((32, 64), F32),
    coords_out=((3, 32), F32),
    msa_grad=((4, 64, 256), F32),
    pair_grad=((32, 64, 128), F32),
    single_grad=((32, 64), F32),
    coords_grad=((3, 32), F32),
    o_gg1=((1, 256), F32),
    o_g_qkvg=((256, 1024), F32),
    o_g_ao=((256, 256), F32),
    o_gg2=((1, 256), F32),
    o_g_oi=((64, 256), F32),
    o_g_oo=((1024, 128), F32),
    o_gg3=((1, 128), F32),
    o_g_ti=((128, 640), F32),
    o_gg4=((1, 128), F32),
    o_g_to=((128, 128), F32),
    o_gg5=((1, 128), F32),
    o_g_ii=((128, 640), F32),
    o_gg6=((1, 128), F32),
    o_g_io=((128, 128), F32),
    o_g_nd=((64, 128), F32),
    o_g_ed=((64, 128), F32),
    o_g_ds=((1, 64), F32),
    o_g_ms=((64, 64), F32),
    o_g_sl=((1, 64), F32),
    o_g_up=((64, 64), F32),
)

STEPS = (
    p_spread,
    p_attention,
    p_outer_exchange,
    p_outer,
    p_entry1,
    p_tri1,
    p_middle,
    p_tri2,
    p_turn,
    p_back2,
    p_between,
    p_back1,
    p_pair_end,
    p_outer_back,
    p_outer_return,
    p_attention_back,
    p_sums,
)
EXCHANGES = 66


class Device:
    def __init__(self, n_seq, n_res, sems, rows_in):
        self.s, self.r = lax.axis_index("seq"), lax.axis_index("res")
        self.ns, self.nr = n_seq, n_res
        self.sems = sems
        self.rows_in = rows_in
        self.used = 0

    def take(self):
        self.used += 2
        assert self.used <= 2 * EXCHANGES
        return self.sems.at[self.used - 2], self.sems.at[self.used - 1]

    def ready(self):
        pl.semaphore_wait(pltpu.get_barrier_semaphore(), self.ns + self.nr - 2)

        @pl.loop(1, self.nr)
        def _(t):
            pl.semaphore_signal(self.rows_in, inc=1, device_id=res_peers(self, t), device_id_type=MESH)

    def all_ready(self):
        pl.semaphore_wait(self.rows_in, self.nr - 1)


def first_kernel(n_seq, n_res, names, *refs):
    refs = list(refs)
    far = {name: refs.pop(0) for name in names}
    far_full = [refs.pop(0) for _ in SIZES]
    R = SimpleNamespace(**far)
    R.__dict__.update({name: refs.pop(0) for name in (*KEPT, *MOVED_IN, *LARGE)})
    tables = [[refs.pop(0) for _ in SIZES] for _ in range(8)]
    R.full, R.pay, R.parts = tables[0], tables[1], tables[2:]
    R.waits, R.later, R.chains = {}, {}, []
    R.out_send, R.out_recv, R.back_send, R.back_recv, R.move = refs[2:]
    D = Device(n_seq, n_res, refs[0], refs[1])
    barrier = pltpu.get_barrier_semaphore()

    for peers, count in ((seq_peers, n_seq), (res_peers, n_res)):

        @pl.loop(1, count)
        def _(t):
            pl.semaphore_signal(barrier, inc=1, device_id=peers(D, t), device_id_type=MESH)

    moves = {}
    for name in MOVED_IN:
        moves[name] = pltpu.make_async_copy(far[name], getattr(R, name), R.move.at[len(moves)])
        moves[name].start()
    R.arrived = lambda *wanted: [moves.pop(name).wait() for name in wanted]
    base = len(moves)
    out = []

    def leave(name):
        if name in far:
            source, target, at = getattr(R, name), far[name], LARGE.index(name)
        else:
            source, target, at = R.full[name], far_full[name], len(LARGE) + name
        out.append(pltpu.make_async_copy(source, target, R.move.at[base + at]))
        out[-1].start()

    R.leave = leave
    for step in STEPS:
        step(R, D)
    for copy in out:
        copy.wait()


def last_kernel(n_seq, n_res, names, *refs):
    refs = list(refs)

    def some(wanted):
        return {name: refs.pop(0) for name in wanted}

    far_in = [refs.pop(0) for _ in range(len(SIZES) + 1)]
    far_large = some(LARGE)
    R = SimpleNamespace(**some(FINISH))
    away = some((*LARGE, *BIG))
    R.__dict__.update(some(names))
    R.__dict__.update(some((*FINISH_KEPT, *LARGE, *BIG)))
    near_in = [refs.pop(0) for _ in far_in]
    (sems,) = refs
    R.full, R.w_far = near_in[:-1], near_in[-1]
    used = []

    def move(source, target):
        copy = pltpu.make_async_copy(source, target, sems.at[len(used)])
        copy.start()
        used.append(copy)
        return copy

    order = (1, 2, 3, 4, 5, 0)
    coming = {k: move(far_in[k], near_in[k]) for k in order}
    passing = [(name, move(far_large[name], getattr(R, name))) for name in LARGE]
    going = []

    def leave(*values):
        for name in BIG:
            if any(getattr(R, name) is value for value in values):
                going.append(move(getattr(R, name), away[name]))

    def pass_on():
        for name, copy in passing:
            copy.wait()
            going.append(move(getattr(R, name), away[name]))

    R.arrived, R.leave, R.pass_on = lambda k: coming[k].wait(), leave, pass_on
    p_finish(R, Device(n_seq, n_res, None, None))
    for copy in going:
        copy.wait()


ARGS = dict(
    x=(4, 64, 256),
    pe=(32, 64, 128),
    vet=(256, 64),
    at=(3, 256),
    fl=(32,),
    ca=(32, 64),
    g1=(256,),
    w_qkvg=(256, 1024),
    w_ao=(256, 256),
    g2=(256,),
    w_oit=(256, 64),
    w_oo=(1024, 128),
    g3=(128,),
    w_ti=(128, 640),
    g4=(128,),
    w_to=(128, 128),
    g5=(128,),
    w_ii=(128, 640),
    g6=(128,),
    w_io=(128, 128),
    w_nd=(64, 128),
    w_edt=(128, 64),
    w_ds=(64,),
    w_ms=(64, 64),
    w_sl=(64,),
    w_up=(64, 64),
    adj_a=(4, 64, 256),
    adj_c=(32, 64, 128),
    adj_v=(32, 64),
    adj_l=(3, 32),
)


def fits(n_seq, n_res, args):
    shapes = tuple(tuple(arg.shape) for arg in args)
    return (n_seq, n_res) == (8, 4) and shapes == tuple(ARGS.values())


def fast_shards(n_seq, n_res, *args):
    env = dict(zip(ARGS, args))
    for name, value in tuple(env.items()):
        if value.ndim == 1:
            env[name] = value.reshape(1, -1)
    env.update(vet=env["vet"].T, w_oit=env["w_oit"].T, w_edt=env["w_edt"].T)
    space = pl.BlockSpec(memory_space=pltpu.VMEM)

    def shapes(entries):
        return [jax.ShapeDtypeStruct(*entry) for entry in entries]

    large = {name: RESULTS[name] for name in LARGE}
    anywhere = pl.BlockSpec(memory_space=pl.ANY)
    held = [(ARGS[name], BF16) for name in MOVED_IN] + [RESULTS[name] for name in LARGE]
    values = pl.pallas_call(
        functools.partial(first_kernel, n_seq, n_res, (*env, *large)),
        out_shape=shapes((*large.values(), *PAYLOADS)),
        in_specs=[anywhere if name in MOVED_IN else space for name in env],
        out_specs=[anywhere] * (len(large) + len(PAYLOADS)),
        scratch_shapes=[
            pltpu.VMEM(*entry) for entry in (*KEPT.values(), *held, *PAYLOADS, *PAYLOADS, *PARTIAL)
        ]
        + [pltpu.SemaphoreType.DMA((2 * EXCHANGES,)), pltpu.SemaphoreType.REGULAR]
        + [pltpu.SemaphoreType.DMA((12,))] * 4
        + [pltpu.SemaphoreType.DMA((len(MOVED_IN) + len(LARGE) + len(SIZES),))],
        compiler_params=pltpu.CompilerParams(
            vmem_limit_bytes=62 * 2**20, collective_id=0, has_side_effects=True
        ),
    )(*env.values())
    full = values[len(large) :]
    env.update(zip(large, values))
    apart = {name: RESULTS[name] for name in (*LARGE, *BIG)}
    small = {name: entry for name, entry in RESULTS.items() if name not in apart}
    brought = [*PAYLOADS, (ARGS["w_qkvg"], BF16)]
    values = pl.pallas_call(
        functools.partial(last_kernel, n_seq, n_res, tuple(small)),
        out_shape=shapes((*apart.values(), *small.values())),
        in_specs=[anywhere] * (len(brought) + len(LARGE)) + [space] * len(FINISH),
        out_specs=[anywhere] * len(apart) + [space] * len(small),
        scratch_shapes=[
            pltpu.VMEM(*entry) for entry in (*FINISH_KEPT.values(), *apart.values(), *brought)
        ]
        + [pltpu.SemaphoreType.DMA((len(brought) + len(apart) + len(LARGE),))],
        compiler_params=pltpu.CompilerParams(vmem_limit_bytes=60 * 2**20),
    )(*full, env["w_qkvg"], *[env[name] for name in LARGE], *[env[name] for name in FINISH])
    env.update(zip((*apart, *small), values))
    results = [env[name] for name in RESULTS]
    for index, value in enumerate(results):
        if value.shape[0] == 1:
            results[index] = value.reshape(-1)
    for index in (12, 23):
        results[index] = results[index].T
    return tuple(results)


def solution(mesh):
    n_seq, n_res = mesh.shape["seq"], mesh.shape["res"]

    def body(*args):
        if fits(n_seq, n_res, args):
            return fast_shards(n_seq, n_res, *args)
        return shards(*args)

    return jax.shard_map(
        body,
        mesh=mesh,
        in_specs=(
            P("seq", "res", None),
            P("seq", "res", None),
            P(),
            P(),
            P(),
            P("seq", None),
            P(),
            P(),
            P(),
            P(),
            P(),
            P(),
            P(),
            P(),
            P(),
            P(),
            P(),
            P(),
            P(),
            P(),
            P(),
            P(),
            P(),
            P(),
            P(),
            P(),
            P("seq", "res", None),
            P("seq", "res", None),
            P("seq", None),
            P(None, "seq"),
        ),
        out_specs=(
            P("seq", "res", None),
            P("seq", "res", None),
            P("seq", None),
            P(None, "seq"),
            P("seq", "res", None),
            P("seq", "res", None),
            P("seq", None),
            P(None, "seq"),
            P(),
            P(),
            P(),
            P(),
            P(),
            P(),
            P(),
            P(),
            P(),
            P(),
            P(),
            P(),
            P(),
            P(),
            P(),
            P(),
            P(),
            P(),
            P(),
            P(),
        ),
        check_vma=False,
    )
```
